32 devices in a mesh: tm: 2 (over x), clip: 16 (over z, y, core).
Axes of the slice: x: 2, y: 2, z: 4, core: 2. Of those that a mesh axis runs over, the one named last changes fastest.
Arguments:
- tokens: bfloat16 [48, 1536, 384], P('clip', 'tm'), may hold values from -6 to 6
- masked: int32 [48, 1152], P('clip'), may hold values from 0 to 1535, as said below
- groups: int32 [48], P('clip'), may hold values from 0 to 23
- cotangent: bfloat16 [48, 1536, 384], P('clip', 'tm'), may hold values from -6 to 6
- mask_token: bfloat16 [384], replicated, may hold values from -6 to 6
- gain_one: bfloat16 [384], replicated, may hold values from 0.099609375 to 1.8984375
- shift_one: bfloat16 [384], replicated, may hold values from -4 to 4
- w_qkv: bfloat16 [384, 1152], replicated, may hold values from -0.3125 to 0.3125
- q_bias: bfloat16 [384], replicated, may hold values from -4 to 4
- v_bias: bfloat16 [384], replicated, may hold values from -0.4375 to 0.4375
- w_proj: bfloat16 [384, 384], replicated, may hold values from -4 to 4
- b_proj: bfloat16 [384], replicated, may hold values from -4 to 4
- gain_two: bfloat16 [384], replicated, may hold values from 0.099609375 to 1.8984375
- shift_two: bfloat16 [384], replicated, may hold values from -4 to 4
- w_up: bfloat16 [384, 1536], replicated, may hold values from -0.3125 to 0.3125
- b_up: bfloat16 [1536], replicated, may hold values from -6 to 6
- w_down: bfloat16 [1536, 384], replicated, may hold values from -0.15625 to 0.15625
- b_down: bfloat16 [384], replicated, may hold values from -4 to 4
Outputs:
- block_out: bfloat16 [48, 1536, 384], P('clip', 'tm')
- grad_tokens: bfloat16 [48, 1536, 384], P('clip', 'tm')
- grad_mask_token: float32 [384], replicated
- grad_gain_one: float32 [384], replicated
- grad_shift_one: float32 [384], replicated
- grad_w_qkv: float32 [384, 1152], replicated
- grad_q_bias: float32 [384], replicated
- grad_v_bias: float32 [384], replicated
- grad_w_proj: float32 [384, 384], replicated
- grad_b_proj: float32 [384], replicated
- grad_gain_two: float32 [384], replicated
- grad_shift_two: float32 [384], replicated
- grad_w_up: float32 [384, 1536], replicated
- grad_b_up: float32 [1536], replicated
- grad_w_down: float32 [1536, 384], replicated
- grad_b_down: float32 [384], replicated
The draws below stay inside these ranges and needn't reach their ends.
Inputs may be any that keep to these rules, and one draw needn't show every extreme that they name: `masked`: each row holds 1152 different positions of its copy.
All inputs are finite; a program needn't handle non-finite values.
Results may differ from the reference program's by a relative error of at most 0.04.
Values may be sent and summed in bfloat16 or wider, within the bound.
No kernel may reach another device: no remote copies, remote signals or barrier semaphores. Data moves between devices by JAX's collectives and lax.ppermute only.
A program may use at most 256 MiB of HBM per device.

```python
import jax
import jax.numpy as jnp
from jax import lax

D = 384
HEADS = 6
HEAD_DIM = 64
FF = 1536
SEQ_LEN = 1536
MASKED = 1152
COPIES = 48
GROUPS = 24


def draw_masked(key, part):
    key = jax.random.fold_in(key, 7)
    keys = jax.random.split(key, COPIES)
    orders = jax.vmap(lambda single: jax.random.permutation(single, SEQ_LEN))(keys)
    return orders[:, :MASKED].astype(jnp.int32)


def with_ends(values, key, least, largest):
    extent = values.shape
    place = [jax.random.randint(jax.random.fold_in(key, axis), (), 0, extent[axis]) for axis in range(len(extent))]
    values = values.at[tuple(place)].set(least)
    longest = extent.index(max(extent))
    place[longest] = (place[longest] + 1) % extent[longest]
    return values.at[tuple(place)].set(largest)


def level_of(key, extent, pieces, low, largest):
    level, own = 1.0, jax.random.fold_in(key, 6)
    for axis_at, shards_of in pieces:
        steps = jnp.exp(jax.random.uniform(jax.random.fold_in(own, axis_at), (shards_of,), jnp.float32, low / len(pieces), largest / len(pieces)))
        level = level * jnp.repeat(steps, extent[axis_at] // shards_of).reshape([-1 if axis == axis_at else 1 for axis in range(len(extent))])
    return level


def scatter_about(rng, shape, scale, reach, cuts=(), kind=jnp.bfloat16):
    level = level_of(rng, shape, cuts, -0.22, 0.18) if cuts else 1.0
    values = jax.random.normal(rng, shape, jnp.float32) * scale * level
    return jnp.minimum(jnp.maximum(values, -reach), reach).astype(kind)


def setup_inputs(seed: int = 0) -> dict:
    key_list = jax.random.split(jax.random.key(seed), 19)
    return {
        "tokens": scatter_about(key_list[0], (COPIES, SEQ_LEN, D), 1.0, 6.0, ((0, 16), (1, 2))),
        "masked": draw_masked(jax.random.fold_in(key_list[18], 71), 0),
        "groups": with_ends(jax.random.randint(key_list[2], (COPIES,), 0, GROUPS), jax.random.fold_in(key_list[2], 1), 0, GROUPS - 1).astype(jnp.int32),
        "cotangent": scatter_about(key_list[3], (COPIES, SEQ_LEN, D), 1.0, 6.0, ((0, 16), (1, 2))),
        "mask_token": scatter_about(key_list[4], (D,), 1.0, 6.0),
        "gain_one": jnp.clip(1.0 + 0.18 * jax.random.normal(key_list[5], (D,), jnp.float32), 0.099609375, 1.8984375).astype(jnp.bfloat16),
        "shift_one": scatter_about(key_list[6], (D,), 0.3, 4.0),
        "w_qkv": scatter_about(key_list[7], (D, 3 * D), D ** -0.5, 0.3125),
        "q_bias": scatter_about(key_list[8], (D,), 0.3, 4.0),
        "v_bias": scatter_about(key_list[9], (D,), 0.03, 0.4375),
        "w_proj": scatter_about(key_list[10], (D, D), 2 ** -0.5, 4.0),
        "b_proj": scatter_about(key_list[11], (D,), 0.3, 4.0),
        "gain_two": jnp.clip(1.0 + 0.18 * jax.random.normal(key_list[12], (D,), jnp.float32), 0.099609375, 1.8984375).astype(jnp.bfloat16),
        "shift_two": scatter_about(key_list[13], (D,), 0.3, 4.0),
        "w_up": scatter_about(key_list[14], (D, FF), D ** -0.5, 0.3125),
        "b_up": scatter_about(key_list[15], (FF,), 0.5, 6.0),
        "w_down": scatter_about(key_list[16], (FF, D), FF ** -0.5, 0.15625),
        "b_down": scatter_about(key_list[17], (D,), 0.3, 4.0),
    }


@jax.custom_vjp
def low(v):
    return lax.optimization_barrier(v.astype(jnp.bfloat16)).astype(jnp.float32)

@jax.custom_vjp
def low_back(v):
    return v

def low_keep(v):
    return (low(v), None)

def low_pass(kept, grad):
    return (grad,)

def back_keep(v):
    return (v, None)

def back_low(kept, grad):
    return (low(grad),)
low.defvjp(low_keep, low_pass)
low_back.defvjp(back_keep, back_low)
EPSILON = 1e-06

def matmul(left, right):
    return jnp.dot(left, right, precision=lax.Precision.HIGHEST)

def layer_norm(values, gain, shift):
    centre = lax.optimization_barrier(jnp.mean(values, axis=-1, keepdims=True))
    centred = values - centre
    spread = lax.optimization_barrier(jnp.mean(centred * centred, axis=-1, keepdims=True))
    return centred * lax.rsqrt(spread + EPSILON) * gain + shift

def one_copy(params, tokens, masked_row):
    mask_token, gain_one, shift_one, w_qkv, q_bias, v_bias, w_proj, b_proj, gain_two, shift_two, w_up, b_up, w_down, b_down = params
    indicator = jnp.zeros((SEQ_LEN,), jnp.float32).at[masked_row].set(1.0)
    inputs = jnp.where(indicator[:, None] > 0.5, mask_token[None, :], tokens)
    normed = low(layer_norm(inputs, gain_one, shift_one))
    mixed = matmul(normed, w_qkv)
    query = low_back(low(mixed[:, :D] + q_bias))
    key_rows = low_back(low(mixed[:, D:2 * D]))
    value = low_back(low(mixed[:, 2 * D:] + v_bias))
    scale = HEAD_DIM ** (-0.5)
    outputs = []
    for head_index in range(HEADS):
        first_col = head_index * HEAD_DIM
        query_head = query[:, first_col:first_col + HEAD_DIM]
        key_head = key_rows[:, first_col:first_col + HEAD_DIM]
        value_head = value[:, first_col:first_col + HEAD_DIM]
        scores = low_back(matmul(query_head, key_head.T) * scale)
        row_max = lax.optimization_barrier(jnp.max(scores, axis=1, keepdims=True))
        expo = jnp.exp(scores - row_max)
        total = lax.optimization_barrier(jnp.sum(expo, axis=1, keepdims=True))
        outputs.append(matmul(low(expo), value_head) / total)
    attended = low_back(low(jnp.concatenate(outputs, axis=1)))
    branch = low_back(matmul(attended, w_proj) + b_proj)
    middle = inputs + branch
    normed_two = low(layer_norm(middle, gain_two, shift_two))
    hidden = low_back(matmul(normed_two, w_up) + b_up)
    active = low(jax.nn.gelu(hidden, approximate=False))
    result = low_back(matmul(active, w_down) + b_down)
    return middle + result

def reference(tokens, masked, groups, cotangent, mask_token, gain_one, shift_one, w_qkv, q_bias, v_bias, w_proj, b_proj, gain_two, shift_two, w_up, b_up, w_down, b_down):
    params = tuple((item.astype(jnp.float32) for item in (mask_token, gain_one, shift_one, w_qkv, q_bias, v_bias, w_proj, b_proj, gain_two, shift_two, w_up, b_up, w_down, b_down)))
    labels = jnp.arange(GROUPS, dtype=jnp.int32)
    member = (groups[:, None] == labels[None, :]).astype(jnp.float32)
    group_count = lax.optimization_barrier(jnp.sum(member, axis=0))
    weighting = 1.0 / lax.optimization_barrier(jnp.sum(member * group_count[None, :], axis=1))

    def run(weights, inputs):

        def advance(carry, item):
            return (carry, jax.checkpoint(one_copy)(weights, item[0], item[1]))
        return lax.scan(advance, jnp.zeros((), jnp.float32), (inputs, masked))[1]
    outputs, pull = jax.vjp(run, params, tokens.astype(jnp.float32))
    grad_params, grad_inputs = pull(cotangent.astype(jnp.float32) * weighting[:, None, None])
    return (outputs.astype(jnp.bfloat16), grad_inputs.astype(jnp.bfloat16), grad_params[0], grad_params[1], grad_params[2], grad_params[3], grad_params[4], grad_params[5], grad_params[6], grad_params[7], grad_params[8], grad_params[9], grad_params[10], grad_params[11], grad_params[12], grad_params[13])
```

```python
import functools
import math

import jax
import jax.numpy as jnp
from jax import lax
from jax.experimental import pallas as pl
from jax.experimental.pallas import tpu as pltpu
from jax.sharding import PartitionSpec as P

HEADS = 6
HEAD_DIM = 64
LANES = 128
EXTRA = 16
EPSILON = 1e-06

BF = jnp.bfloat16
F32 = jnp.float32
VMEM = pl.BlockSpec(memory_space=pltpu.VMEM)
SMEM = pl.BlockSpec(memory_space=pltpu.SMEM)


def dot(left, right):
    return jnp.dot(left, right, preferred_element_type=F32)


def dot_last(left, right):
    return lax.dot_general(left, right, (((1,), (1,)), ((), ())), preferred_element_type=F32)


def dot_rows(left, right):
    return lax.dot_general(left, right, (((0,), (0,)), ((), ())), preferred_element_type=F32)


def iota(shape, axis):
    return lax.broadcasted_iota(jnp.int32, shape, axis)


def ones_where(condition):
    return jnp.where(condition, 1.0, 0.0).astype(BF)


def column_sums(values):
    return jnp.sum(values, axis=0, keepdims=True)


def shape(*dims, kind=BF):
    return jax.ShapeDtypeStruct(dims, kind)


def plain(kernel, outs):
    return pl.pallas_call(kernel, out_shape=outs, compiler_params=pltpu.CompilerParams(vmem_limit_bytes=16 << 20))


def one_hots(masked_row):
    low = ones_where(iota((LANES, masked_row.shape[1]), 0) == (masked_row & (LANES - 1)))
    high = ones_where(iota((16, masked_row.shape[1]), 0) == (masked_row >> 7))
    return low, high


def ranks(masked_row, tm, half, unmasked):
    low, high = one_hots(masked_row)
    marks = dot_last(high, low)
    valid = iota((16, LANES), 0) < 2 * half // LANES
    free = jnp.where(valid, 1.0 - marks, 0.0).astype(BF)
    before = ones_where(iota((LANES, LANES), 0) < iota((LANES, LANES), 1))
    within = dot(free, before)
    totals = dot(free, jnp.ones((LANES, LANES), BF)).astype(BF)
    earlier = ones_where(iota((16, 16), 1) < iota((16, 16), 0))
    rank = within + dot(earlier, totals)
    rank = jnp.where(marks > 0.5, float(unmasked), rank).astype(jnp.int32)
    blocks = half // LANES
    return jnp.where(tm == 0, rank[:blocks], rank[blocks : 2 * blocks])


def ranks_down(masked_row, tm, half, unmasked):
    low, high = one_hots(masked_row)
    marks = dot_last(low, high)
    valid = iota((LANES, 16), 1) < 2 * half // LANES
    free = jnp.where(valid, 1.0 - marks, 0.0).astype(BF)
    before = ones_where(iota((LANES, LANES), 1) < iota((LANES, LANES), 0))
    within = dot(before, free)
    totals = dot(jnp.ones((LANES, LANES), BF), free).astype(BF)
    earlier = ones_where(iota((16, 16), 0) < iota((16, 16), 1))
    rank = within + dot(totals, earlier)
    rank = jnp.where(marks > 0.5, float(unmasked), rank).astype(jnp.int32)
    blocks = half // LANES
    return jnp.where(tm == 0, rank[:, :blocks], rank[:, blocks : 2 * blocks])


def picks(rank, labels):
    wide = jnp.broadcast_to(labels, (labels.shape[0], LANES))
    return jnp.concatenate([ones_where(wide == rank[b : b + 1, :]) for b in range(rank.shape[0])], axis=1)


def prep_tokens_kernel(unmasked, place_ref, masked_ref, tokens_ref, mine_ref, theirs_ref, shared_ref, rank_ref):
    tm = place_ref[0]
    half = tokens_ref.shape[1]
    rows = unmasked + EXTRA
    labels = iota((rows, 1), 0)
    for role, (copy, out_ref) in enumerate(((1 - tm, theirs_ref), (2, shared_ref), (tm, mine_ref))):
        rank = ranks(masked_ref[copy], tm, half, unmasked)
        rank_ref[role] = jnp.concatenate([rank, jnp.zeros((8 - rank.shape[0], LANES), jnp.int32)], axis=0)
        out_ref[...] = dot(picks(rank, labels), tokens_ref[copy]).astype(BF)


def prep_grads_kernel(unmasked, place_ref, masked_ref, rank_ref, cotangent_ref, keep_ref, send_ref, down_ref):
    tm = place_ref[0]
    half = cotangent_ref.shape[1]
    blocks = half // LANES
    rows = unmasked + EXTRA
    part = unmasked // 2
    labels = iota((rows, 1), 0)
    send_ref[:rows, :] = dot(picks(rank_ref[0, :blocks], labels), cotangent_ref[1 - tm]).astype(BF)
    rank = rank_ref[1, :blocks]
    small = iota((part + EXTRA, 1), 0)
    theirs = jnp.where(small < part, small + part * (1 - tm), -1)
    send_ref[rows:, :] = dot(picks(rank, theirs), cotangent_ref[2]).astype(BF)
    own = jnp.where(small < part, small + part * tm, small + part)
    keep_ref[rows:, :] = dot(picks(rank, own), cotangent_ref[2]).astype(BF)
    keep_ref[:rows, :] = dot(picks(rank_ref[2, :blocks], labels), cotangent_ref[tm]).astype(BF)
    for role, copy in enumerate((1 - tm, 2, tm)):
        down = ranks_down(masked_ref[copy], tm, half, unmasked)
        down_ref[role] = jnp.concatenate([down, jnp.zeros((LANES, 8 - blocks), jnp.int32)], axis=1)


def normalise(values):
    centred = values - jnp.mean(values, axis=-1, keepdims=True)
    scale = lax.rsqrt(jnp.mean(centred * centred, axis=-1, keepdims=True) + EPSILON)
    return centred * scale, scale


def attention_kernel(
    unmasked, count, split, place_ref, own_ref, got_ref, small_ref, w_ref,
    x_ref, q_ref, k_ref, v_ref, p_ref, att_ref, *rest
):
    rows, width = own_ref.shape
    at = iota((rows, width), 0)
    x = own_ref[...].astype(F32) + got_ref[...].astype(F32)
    x = jnp.where(at == unmasked, small_ref[0:1, :], x)
    hat, _ = normalise(x)
    normed = (hat * small_ref[1:2, :] + small_ref[2:3, :]).astype(BF)
    mixed = dot(normed, w_ref[...])
    query = ((mixed[:, :width] + small_ref[3:4, :]).astype(BF).astype(F32) * HEAD_DIM ** (-0.5)).astype(BF)
    key = mixed[:, width : 2 * width].astype(BF)
    value = (mixed[:, 2 * width :] + small_ref[4:5, :]).astype(BF)
    k_ref[...] = key
    v_ref[...] = value
    x = x.astype(BF)
    if split:
        tm = place_ref[0]
        part = unmasked // 2

        def take(values):
            chosen = jnp.where(tm == 0, values[:part].astype(F32), values[part:unmasked].astype(F32)).astype(BF)
            return jnp.concatenate([chosen, values[unmasked:]], axis=0)

        rest[0][...] = x
        x, query = take(x), take(query)
    x_ref[...] = x
    q_ref[...] = query
    across = iota((1, rows), 1)
    bias = jnp.where(across < unmasked, 0.0, jnp.where(across == unmasked, math.log(count), -1e30))
    first = iota((1, LANES), 1) < HEAD_DIM
    for pair in range(width // LANES):
        cols = slice(pair * LANES, (pair + 1) * LANES)
        q_pair, k_pair, v_pair = query[:, cols], key[:, cols], value[:, cols]
        parts = []
        for side in range(2):
            mine = first if side == 0 else jnp.logical_not(first)
            scores = dot_last(jnp.where(mine, q_pair, jnp.zeros_like(q_pair)), k_pair) + bias
            expo = jnp.exp(scores - jnp.max(scores, axis=1, keepdims=True))
            probs = (expo * (1.0 / jnp.sum(expo, axis=1, keepdims=True))).astype(BF)
            p_ref[2 * pair + side] = probs
            parts.append(dot(probs, v_pair))
        att_ref[:, cols] = jnp.where(first, parts[0], parts[1]).astype(BF)


def gelu_terms(hidden):
    size = jnp.abs(hidden) * (0.5**0.5)
    t = 1.0 / (1.0 + 0.3275911 * size)
    bell = jnp.exp(hidden * hidden * -0.5)
    tail = t * (0.254829592 + t * (-0.284496736 + t * (1.421413741 + t * (-1.453152027 + t * 1.061405429))))
    tail = 0.5 * tail * bell
    below = jnp.where(hidden >= 0.0, 1.0 - tail, tail)
    return hidden * below, below + hidden * bell * (1.0 / math.sqrt(2.0 * math.pi))


def stacked(refs):
    return jnp.concatenate([ref[...] for ref in refs], axis=0)


def scatter_chunks(me, stage_ref, keep_ref, send_ref):
    depth = keep_ref.shape[2]
    for rel in range(2 * 4 * keep_ref.shape[1]):
        first = pl.multiple_of((me ^ rel) * depth, 16)
        target = send_ref if rel & 1 else keep_ref
        target[(rel >> 1) & 3, rel >> 3] = stage_ref[pl.ds(first, depth), :]


def stage_weight(stage_ref, first, grad):
    depth = grad.shape[0]
    for block in range(grad.shape[1] // LANES):
        stage_ref[first + block * depth : first + (block + 1) * depth, :] = grad[
            :, block * LANES : (block + 1) * LANES
        ].astype(BF)
    return first + grad.shape[0] * (grad.shape[1] // LANES)


def stage_rows(stage_ref, first, vectors):
    pieces = [v[:, b * LANES : (b + 1) * LANES] for v in vectors for b in range(v.shape[1] // LANES)]
    missing = -len(pieces) % 16
    if missing:
        pieces.append(jnp.zeros((missing, LANES), F32))
    block = jnp.concatenate(pieces, axis=0).astype(BF)
    stage_ref[first : first + block.shape[0], :] = block
    return first + block.shape[0]


def clear_rest(stage_ref, first):
    if first < stage_ref.shape[0]:
        stage_ref[first:, :] = jnp.zeros((stage_ref.shape[0] - first, LANES), BF)


def up_kernel(
    place_ref, weight_ref, att_a, att_b, x_a, x_b, cot_own, cot_got, small_ref, bias_up_ref, w_proj_ref, w_up_ref,
    middle_ref, normed_ref, active_ref, slope_ref, upstream_ref, keep_ref, send_ref, stage_ref
):
    rows_a, width = x_a.shape
    total = rows_a + x_b.shape[0]
    attended = stacked((att_a, att_b))
    x = stacked((x_a, x_b)).astype(F32)
    middle = x + dot(attended, w_proj_ref[...]) + small_ref[5:6, :]
    middle_ref[...] = middle
    hat, _ = normalise(middle)
    normed = (hat * small_ref[6:7, :] + small_ref[7:8, :]).astype(BF)
    normed_ref[...] = normed
    weight = jnp.where(iota((total, 1), 0) < rows_a, weight_ref[0], weight_ref[1])
    upstream = (cot_own[...].astype(F32) + cot_got[...].astype(F32)) * weight
    upstream_ref[...] = upstream
    grad_result = upstream.astype(BF)
    hidden = dot(normed, w_up_ref[...]) + bias_up_ref[...]
    active, slope = gelu_terms(hidden)
    active = active.astype(BF)
    active_ref[...] = active
    slope_ref[...] = slope.astype(BF)
    end = stage_weight(stage_ref, 0, dot_rows(active, grad_result))
    clear_rest(stage_ref, end)
    scatter_chunks(place_ref[1], stage_ref, keep_ref, send_ref)


def norm_back(grad, hat, scale, gain):
    inner = grad * gain
    mean = jnp.mean(inner, axis=-1, keepdims=True)
    along = jnp.mean(inner * hat, axis=-1, keepdims=True)
    return scale * (inner - mean - hat * along)


def down_kernel(
    place_ref, middle_ref, normed_ref, active_ref, slope_ref, upstream_ref, att_a, att_b, small_ref,
    w_proj_ref, w_up_ref, w_down_ref,
    out_ref, grad_middle_ref, grad_att_ref, keep_ref, send_ref, stage_ref
):
    middle = middle_ref[...]
    out_ref[...] = (middle + dot(active_ref[...], w_down_ref[...]) + small_ref[8:9, :]).astype(BF)
    upstream = upstream_ref[...]
    grad_result = upstream.astype(BF)
    grad_hidden = (dot_last(grad_result, w_down_ref[...]) * slope_ref[...].astype(F32)).astype(BF)
    end = stage_weight(stage_ref, 0, dot_rows(normed_ref[...], grad_hidden))
    grad_normed = dot_last(grad_hidden, w_up_ref[...])
    hat, scale = normalise(middle)
    grad_middle = upstream + norm_back(grad_normed, hat, scale, small_ref[6:7, :])
    grad_middle_ref[...] = grad_middle
    grad_branch = grad_middle.astype(BF)
    grad_att_ref[...] = dot_last(grad_branch, w_proj_ref[...]).astype(BF)
    end = stage_weight(stage_ref, end, dot_rows(stacked((att_a, att_b)), grad_branch))
    vectors = (
        column_sums(grad_hidden.astype(F32)),
        column_sums(grad_normed * hat),
        column_sums(grad_normed),
        column_sums(grad_branch.astype(F32)),
        column_sums(grad_result.astype(F32)),
    )
    end = stage_rows(stage_ref, end, vectors)
    clear_rest(stage_ref, end)
    scatter_chunks(place_ref[1], stage_ref, keep_ref, send_ref)


def attention_back_kernel(row_from, g_ref, att_ref, q_ref, k_ref, v_ref, p_ref, dq_ref, dk_ref, dv_ref):
    width = q_ref.shape[1]
    rows = q_ref.shape[0]
    first = iota((1, LANES), 1) < HEAD_DIM
    for pair in range(width // LANES):
        cols = slice(pair * LANES, (pair + 1) * LANES)
        g_pair = g_ref[row_from : row_from + rows, cols]
        q_pair, k_pair, v_pair = q_ref[:, cols], k_ref[:, cols], v_ref[:, cols]
        agree = g_pair.astype(F32) * att_ref[:, cols].astype(F32)
        dq, dk, dv = [], [], []
        for side in range(2):
            mine = first if side == 0 else jnp.logical_not(first)
            correction = jnp.sum(jnp.where(mine, agree, 0.0), axis=1, keepdims=True)
            probs = p_ref[2 * pair + side]
            grad_probs = dot_last(jnp.where(mine, g_pair, jnp.zeros_like(g_pair)), v_pair)
            grad_scores = (probs.astype(F32) * (grad_probs - correction)).astype(BF)
            dq.append(dot(grad_scores, k_pair))
            dk.append(dot_rows(grad_scores, q_pair))
            dv.append(dot_rows(probs, g_pair))
        dq_ref[:, cols] = (jnp.where(first, dq[0], dq[1]) * HEAD_DIM ** (-0.5)).astype(BF)
        dk_ref[:, cols] = jnp.where(first, dk[0], dk[1]).astype(BF)
        dv_ref[:, cols] = jnp.where(first, dv[0], dv[1]).astype(BF)


def inputs_back_kernel(
    unmasked, place_ref, x_a, x_b, dq_a, dq_b, dk_a, dk_b, dv_a, dv_b, grad_middle_ref, small_ref, w_ref,
    grad_ref, keep_ref, send_ref, stage_ref
):
    rows, width = x_a.shape
    part = unmasked // 2
    tm = place_ref[0]

    def spread(block):
        wide = block.astype(F32)
        left = jnp.where(tm == 0, wide[:part], 0.0)
        right = jnp.where(tm == 0, 0.0, wide[:part])
        return jnp.concatenate([left, right, wide[part:]], axis=0)

    x = stacked((x_a, x_b)).astype(F32)
    hat, scale = normalise(x)
    gain = small_ref[1:2, :]
    normed = (hat * gain + small_ref[2:3, :]).astype(BF)
    dq = jnp.concatenate([dq_a[...], spread(dq_b[...]).astype(BF)], axis=0)
    mixed = jnp.concatenate([dq, stacked((dk_a, dk_b)), stacked((dv_a, dv_b))], axis=1)
    end = stage_weight(stage_ref, 0, dot_rows(normed, mixed))
    grad_normed = dot_last(mixed, w_ref[...])
    grad = norm_back(grad_normed, hat, scale, gain)
    grad = grad + jnp.concatenate([grad_middle_ref[:rows], spread(grad_middle_ref[rows:])], axis=0)
    grad_ref[:unmasked] = grad[:unmasked].astype(BF)
    grad_ref[unmasked:] = grad[rows : rows + unmasked].astype(BF)
    vectors = (
        column_sums(mixed[:, :width].astype(F32)),
        column_sums(mixed[:, 2 * width :].astype(F32)),
        column_sums(grad_normed * hat),
        column_sums(grad_normed),
        grad[unmasked : unmasked + 1] + grad[rows + unmasked : rows + unmasked + 1],
    )
    end = stage_rows(stage_ref, end, vectors)
    clear_rest(stage_ref, end)
    scatter_chunks(place_ref[1], stage_ref, keep_ref, send_ref)


def place_back(down, rows, half):
    labels = jnp.broadcast_to(iota((1, rows), 1), (LANES, rows))
    return jnp.concatenate([ones_where(labels == down[:, b : b + 1]) for b in range(half // LANES)], axis=0)


def outputs_kernel(unmasked, place_ref, down_ref, own_ref, got_ref, out_ref):
    tm = place_ref[0]
    half = out_ref.shape[1]
    rows = unmasked + EXTRA
    part = unmasked // 2
    out_ref[tm] = dot(place_back(down_ref[2], rows, half), own_ref[:rows]).astype(BF)
    out_ref[1 - tm] = dot(place_back(down_ref[0], rows, half), got_ref[:rows]).astype(BF)
    own = own_ref[rows:].astype(F32)
    got = got_ref[rows:].astype(F32)
    left = jnp.where(tm == 0, own[:part], got[:part])
    right = jnp.where(tm == 0, got[:part], own[:part])
    whole = jnp.concatenate([left, right, own[part:]], axis=0).astype(BF)
    out_ref[2] = dot(place_back(down_ref[1], rows, half), whole).astype(BF)


def grads_out_kernel(unmasked, place_ref, down_ref, own_ref, got_ref, out_ref):
    tm = place_ref[0]
    half = out_ref.shape[1]
    out_ref[tm] = dot(place_back(down_ref[2], unmasked, half), own_ref[:unmasked]).astype(BF)
    out_ref[1 - tm] = dot(place_back(down_ref[0], unmasked, half), got_ref[:unmasked]).astype(BF)
    whole = (own_ref[unmasked:].astype(F32) + got_ref[unmasked:].astype(F32)).astype(BF)
    out_ref[2] = dot(place_back(down_ref[1], unmasked, half), whole).astype(BF)


def fold_kernel(keep_ref, got_ref, *out_refs):
    for step, out_ref in enumerate(out_refs):
        out_ref[...] = (keep_ref[step].astype(F32) + got_ref[step].astype(F32)).astype(BF)


def fold_four_kernel(*refs):
    total = refs[0][...].astype(F32)
    for ref in refs[1:4]:
        total = total + ref[...].astype(F32)
    total = total.astype(BF)
    if len(refs) == 5:
        refs[4][...] = total
        return
    for step, out_ref in enumerate(refs[4:]):
        for slot in range(out_ref.shape[0]):
            out_ref[slot] = total[4 * slot + step]


def join_kernel(*refs):
    for step in range(len(refs) - 1):
        refs[-1][step] = refs[step][...]


def clip_swap(values, distance):
    size = lax.axis_size("clip")
    return lax.ppermute(values, "clip", [(i, i ^ distance) for i in range(size)])


def near_swap(values, step):
    size = lax.axis_size("clip")
    pairs = [
        (t * size + i, (t ^ (step & 1)) * size + (i ^ ((step >> 1) << 1))) for t in range(2) for i in range(size)
    ]
    return lax.ppermute(values, ("tm", "clip"), pairs)


def sum_over_devices(keep, send):
    far = []
    distance = 4
    while distance < lax.axis_size("clip"):
        far.append(distance)
        distance *= 4
    _, groups, depth, _ = keep.shape
    got = clip_swap(send, 1)
    pieces = plain(fold_kernel, [shape(groups, depth, LANES)] * 4)(keep, got)
    pieces = [pieces[0]] + [near_swap(pieces[step], step) for step in (1, 2, 3)]
    left = groups
    for distance in far:
        left //= 4
        pieces = plain(fold_four_kernel, [shape(left, depth, LANES)] * 4)(*pieces)
        pieces = [pieces[0]] + [clip_swap(pieces[step], step * distance) for step in (1, 2, 3)]
    total = plain(fold_four_kernel, shape(left, depth, LANES))(*pieces)
    for distance in reversed(far):
        pieces = [total] + [clip_swap(total, step * distance) for step in (1, 2, 3)]
        total = jnp.stack(pieces, axis=1).reshape(-1, depth, LANES)
    pieces = [total] + [near_swap(total, step) for step in (1, 2, 3)]
    total = jnp.stack(pieces)
    return total, clip_swap(total, 1)


def gather_chunks(me, own_ref, got_ref, stage_ref):
    depth = own_ref.shape[2]
    for rel in range(2 * 4 * own_ref.shape[1]):
        first = pl.multiple_of((me ^ rel) * depth, 16)
        source = got_ref if rel & 1 else own_ref
        stage_ref[pl.ds(first, depth), :] = source[(rel >> 1) & 3, rel >> 3]


def unstage_kernel(weights, vectors, place_ref, own_ref, got_ref, *refs):
    outs, stage_ref = refs[:-1], refs[-1]
    gather_chunks(place_ref[1], own_ref, got_ref, stage_ref)
    first = 0
    for out_ref in outs[:weights]:
        depth, width = out_ref.shape
        for block in range(width // LANES):
            out_ref[:, block * LANES : (block + 1) * LANES] = stage_ref[first : first + depth, :].astype(F32)
            first += depth
    if vectors:
        count = sum(ref.shape[0] // LANES for ref in outs[weights:])
        rows = stage_ref[first : first + count + -count % 16, :].astype(F32)
        at = 0
        for out_ref in outs[weights:]:
            blocks = out_ref.shape[0] // LANES
            for block in range(blocks):
                out_ref[block * LANES : (block + 1) * LANES] = rows[at + block]
            at += blocks


def chunk_rows(count, devices):
    return -(-count // (devices * 16)) * 16


def body(
    tokens,
    masked,
    groups,
    cotangent,
    mask_token,
    gain_one,
    shift_one,
    w_qkv,
    q_bias,
    v_bias,
    w_proj,
    b_proj,
    gain_two,
    shift_two,
    w_up,
    b_up,
    w_down,
    b_down,
):
    copies, half, width = tokens.shape
    hidden = w_up.shape[1]
    hide = masked.shape[1]
    unmasked = 2 * half - hide
    rows = unmasked + EXTRA
    some = unmasked // 2 + EXTRA
    total = rows + some
    tm, clip = lax.axis_index("tm"), lax.axis_index("clip")
    clips = lax.axis_size("clip")
    devices = 2 * clips
    me = (clip & 1) | (tm << 1) | ((clip >> 1) << 2)
    place = jnp.stack([tm, me]).astype(jnp.int32)
    smem = pl.BlockSpec(memory_space=pltpu.SMEM)
    swap = functools.partial(lax.ppermute, axis_name="tm", perm=[(0, 1), (1, 0)])

    def run(kernel, args, outs, scratch=(), scalars=1, limit=48, flops=0):
        moved = sum(math.prod(a.shape) * a.dtype.itemsize for a in list(args) + jax.tree.leaves(outs))
        return pl.pallas_call(
            kernel,
            out_shape=outs,
            in_specs=[smem] * scalars + [VMEM] * (len(args) - scalars),
            out_specs=jax.tree.map(lambda _: VMEM, outs),
            scratch_shapes=list(scratch),
            compiler_params=pltpu.CompilerParams(vmem_limit_bytes=limit << 20),
            cost_estimate=pl.CostEstimate(flops=flops, bytes_accessed=moved, transcendentals=0),
        )(*args)

    def chunked(count):
        depth = chunk_rows(count, devices)
        halves = [shape(4, devices // 8, depth, LANES)] * 2
        return halves, [pltpu.VMEM((devices * depth, LANES), BF)]

    masked = masked.reshape(copies, 1, hide)
    small = jnp.stack(
        [mask_token, gain_one, shift_one, q_bias, v_bias, b_proj, gain_two, shift_two, b_down]
    ).astype(F32)
    bias_up = b_up.astype(F32).reshape(1, hidden)

    everyone = groups
    distance = 1
    while distance < clips:
        everyone = jnp.concatenate([everyone] + [clip_swap(everyone, step * distance) for step in (1, 2, 3)])
        distance *= 4
    counts = jnp.sum((groups[:, None] == everyone[None, :]).astype(F32), axis=1)
    weighting = 1.0 / counts
    weighting = jnp.stack([jnp.where(tm == 0, weighting[0], weighting[1]), weighting[2]])

    block = shape(rows, width)
    mine, theirs, shared, rank = run(
        functools.partial(prep_tokens_kernel, unmasked),
        (place, masked, tokens),
        [block, block, block, shape(copies, 8, LANES, kind=jnp.int32)],
        flops=2 * copies * rows * half * width,
    )
    got_mine = swap(theirs)
    got_shared = swap(shared)
    cot_own, cot_send, down = run(
        functools.partial(prep_grads_kernel, unmasked),
        (place, masked, rank, cotangent),
        [shape(total, width), shape(total, width), shape(copies, LANES, 8, kind=jnp.int32)],
        flops=2 * copies * rows * half * width,
    )
    cot_got = swap(cot_send)

    def attend(own, got, split):
        queries = some if split else rows
        outs = [
            shape(queries, width), shape(queries, width), block, block,
            shape(HEADS, queries, rows), shape(queries, width),
        ]
        if split:
            outs.append(block)
        return run(
            functools.partial(attention_kernel, unmasked, hide, split),
            (place, own, got, small, w_qkv),
            outs,
            flops=6 * rows * width * width + 4 * queries * rows * width,
        )

    x_a, q_a, k_a, v_a, p_a, att_a = attend(mine, got_mine, False)
    x_b, q_b, k_b, v_b, p_b, att_b, x_whole = attend(shared, got_shared, True)

    halves, stage = chunked(width // LANES * hidden)
    middle, normed_two, active, slope, upstream, keep, send = run(
        up_kernel,
        (place, weighting, att_a, att_b, x_a, x_b, cot_own, cot_got, small, bias_up, w_proj, w_up),
        [
            shape(total, width, kind=F32), shape(total, width), shape(total, hidden), shape(total, hidden),
            shape(total, width, kind=F32),
        ]
        + halves,
        stage,
        scalars=2,
        flops=2 * total * width * (width + 2 * hidden),
    )
    down_sums = sum_over_devices(keep, send)

    halves, stage = chunked(hidden // LANES * width + width // LANES * width + 32)
    out_rows, grad_middle, grad_att, keep, send = run(
        down_kernel,
        (place, middle, normed_two, active, slope, upstream, att_a, att_b, small, w_proj, w_up, w_down),
        [shape(total, width), shape(total, width, kind=F32), shape(total, width)] + halves,
        stage,
        flops=2 * total * width * (2 * width + 4 * hidden),
    )
    up_sums = sum_over_devices(keep, send)
    out_got = swap(out_rows)

    def attend_back(row_from, att, q, k, v, p):
        return run(
            functools.partial(attention_back_kernel, row_from),
            (grad_att, att, q, k, v, p),
            [shape(q.shape[0], width), block, block],
            scalars=0,
            flops=8 * q.shape[0] * rows * width,
        )

    dq_a, dk_a, dv_a = attend_back(0, att_a, q_a, k_a, v_a, p_a)
    dq_b, dk_b, dv_b = attend_back(rows, att_b, q_b, k_b, v_b, p_b)
    halves, stage = chunked(3 * width // LANES * width + 16)
    grad_rows, keep, send = run(
        functools.partial(inputs_back_kernel, unmasked),
        (place, x_a, x_whole, dq_a, dq_b, dk_a, dk_b, dv_a, dv_b, grad_middle, small, w_qkv),
        [shape(2 * unmasked, width)] + halves,
        stage,
        flops=2 * 2 * rows * width * 6 * width,
    )
    in_sums = sum_over_devices(keep, send)
    grad_got = swap(grad_rows)

    block_out = run(
        functools.partial(outputs_kernel, unmasked), (place, down, out_rows, out_got), shape(*tokens.shape)
    )
    grad_tokens = run(
        functools.partial(grads_out_kernel, unmasked), (place, down, grad_rows, grad_got), shape(*tokens.shape)
    )

    def unstage(sums, weights, vectors):
        depth = sums[0].shape[2]
        outs = [shape(*dims, kind=F32) for dims in weights] + [shape(dim, kind=F32) for dim in vectors]
        return run(
            functools.partial(unstage_kernel, len(weights), len(vectors)),
            (place,) + tuple(sums),
            outs,
            [pltpu.VMEM((devices * depth, LANES), BF)],
        )

    (grad_w_down,) = unstage(down_sums, [(hidden, width)], [])
    grad_w_up, grad_w_proj, grad_b_up, grad_gain_two, grad_shift_two, grad_b_proj, grad_b_down = unstage(
        up_sums, [(width, hidden), (width, width)], [hidden, width, width, width, width]
    )
    grad_w_qkv, grad_q_bias, grad_v_bias, grad_gain_one, grad_shift_one, grad_mask_token = unstage(
        in_sums, [(width, 3 * width)], [width] * 5
    )
    return (
        block_out,
        grad_tokens,
        grad_mask_token,
        grad_gain_one,
        grad_shift_one,
        grad_w_qkv,
        grad_q_bias,
        grad_v_bias,
        grad_w_proj,
        grad_b_proj,
        grad_gain_two,
        grad_shift_two,
        grad_w_up,
        grad_b_up,
        grad_w_down,
        grad_b_down,
    )


def solution(mesh):
    return jax.shard_map(
        body,
        mesh=mesh,
        in_specs=(P("clip", "tm", None), P("clip", None), P("clip"), P("clip", "tm", None)) + (P(),) * 14,
        out_specs=(P("clip", "tm", None), P("clip", "tm", None)) + (P(),) * 14,
        check_vma=False,
    )
```

```python
import functools
import math

import jax
import jax.numpy as jnp
from jax import lax
from jax.experimental import pallas as pl
from jax.experimental.pallas import tpu as pltpu
from jax.sharding import PartitionSpec as P

HEADS = 6
HEAD_DIM = 64
LANES = 128
EXTRA = 16
EPSILON = 1e-06

BF = jnp.bfloat16
F32 = jnp.float32
VMEM = pl.BlockSpec(memory_space=pltpu.VMEM)
SMEM = pl.BlockSpec(memory_space=pltpu.SMEM)


def dot(left, right):
    return jnp.dot(left, right, preferred_element_type=F32)


def dot_last(left, right):
    return lax.dot_general(left, right, (((1,), (1,)), ((), ())), preferred_element_type=F32)


def dot_rows(left, right):
    return lax.dot_general(left, right, (((0,), (0,)), ((), ())), preferred_element_type=F32)


def iota(shape, axis):
    return lax.broadcasted_iota(jnp.int32, shape, axis)


def ones_where(condition):
    return jnp.where(condition, 1.0, 0.0).astype(BF)


def column_sums(values):
    return jnp.sum(values, axis=0, keepdims=True)


def shape(*dims, kind=BF):
    return jax.ShapeDtypeStruct(dims, kind)


def plain(kernel, outs):
    return pl.pallas_call(kernel, out_shape=outs, compiler_params=pltpu.CompilerParams(vmem_limit_bytes=16 << 20))


def one_hots(masked_row):
    low = ones_where(iota((LANES, masked_row.shape[1]), 0) == (masked_row & (LANES - 1)))
    high = ones_where(iota((16, masked_row.shape[1]), 0) == (masked_row >> 7))
    return low, high


def ranks(masked_row, tm, half, unmasked):
    low, high = one_hots(masked_row)
    marks = dot_last(high, low)
    valid = iota((16, LANES), 0) < 2 * half // LANES
    free = jnp.where(valid, 1.0 - marks, 0.0).astype(BF)
    before = ones_where(iota((LANES, LANES), 0) < iota((LANES, LANES), 1))
    within = dot(free, before)
    totals = dot(free, jnp.ones((LANES, LANES), BF)).astype(BF)
    earlier = ones_where(iota((16, 16), 1) < iota((16, 16), 0))
    rank = within + dot(earlier, totals)
    rank = jnp.where(marks > 0.5, float(unmasked), rank).astype(jnp.int32)
    blocks = half // LANES
    return jnp.where(tm == 0, rank[:blocks], rank[blocks : 2 * blocks])


def ranks_down(masked_row, tm, half, unmasked):
    low, high = one_hots(masked_row)
    marks = dot_last(low, high)
    valid = iota((LANES, 16), 1) < 2 * half // LANES
    free = jnp.where(valid, 1.0 - marks, 0.0).astype(BF)
    before = ones_where(iota((LANES, LANES), 1) < iota((LANES, LANES), 0))
    within = dot(before, free)
    totals = dot(jnp.ones((LANES, LANES), BF), free).astype(BF)
    earlier = ones_where(iota((16, 16), 0) < iota((16, 16), 1))
    rank = within + dot(totals, earlier)
    rank = jnp.where(marks > 0.5, float(unmasked), rank).astype(jnp.int32)
    blocks = half // LANES
    return jnp.where(tm == 0, rank[:, :blocks], rank[:, blocks : 2 * blocks])


def picks(rank, labels):
    wide = jnp.broadcast_to(labels, (labels.shape[0], LANES))
    return jnp.concatenate([ones_where(wide == rank[b : b + 1, :]) for b in range(rank.shape[0])], axis=1)


def prep_theirs_kernel(unmasked, place_ref, masked_ref, tokens_ref, theirs_ref, rank_ref, half_ref, arrived):
    copy = 1 - place_ref[0]
    load = pltpu.make_async_copy(tokens_ref.at[copy], half_ref, arrived)
    load.start()
    half = tokens_ref.shape[1]
    rank = ranks(masked_ref[pl.ds(copy, 1), :], place_ref[0], half, unmasked)
    rank_ref[...] = jnp.concatenate([rank, jnp.zeros((8 - rank.shape[0], LANES), jnp.int32)], axis=0)
    chosen = picks(rank, iota((unmasked + EXTRA, 1), 0))
    load.wait()
    theirs_ref[...] = dot(chosen, half_ref[...]).astype(BF)


def prep_tokens_kernel(unmasked, place_ref, masked_ref, tokens_ref, shared_ref, mine_ref, rank_ref):
    tm = place_ref[0]
    half = tokens_ref.shape[1]
    labels = iota((unmasked + EXTRA, 1), 0)
    for role, (copy, out_ref) in enumerate(((2, shared_ref), (tm, mine_ref))):
        rank = ranks(masked_ref[pl.ds(copy, 1), :], tm, half, unmasked)
        rank_ref[role] = jnp.concatenate([rank, jnp.zeros((8 - rank.shape[0], LANES), jnp.int32)], axis=0)
        out_ref[...] = dot(picks(rank, labels), tokens_ref[copy]).astype(BF)


def prep_grads_kernel(
    unmasked, place_ref, masked_ref, rank_theirs_ref, rank_ref, cotangent_ref, keep_ref, send_ref, down_ref
):
    tm = place_ref[0]
    half = cotangent_ref.shape[1]
    blocks = half // LANES
    rows = unmasked + EXTRA
    part = unmasked // 2
    labels = iota((rows, 1), 0)
    send_ref[:rows, :] = dot(picks(rank_theirs_ref[:blocks], labels), cotangent_ref[1 - tm]).astype(BF)
    rank = rank_ref[0, :blocks]
    small = iota((part + EXTRA, 1), 0)
    theirs = jnp.where(small < part, small + part * (1 - tm), -1)
    send_ref[rows:, :] = dot(picks(rank, theirs), cotangent_ref[2]).astype(BF)
    own = jnp.where(small < part, small + part * tm, small + part)
    keep_ref[rows:, :] = dot(picks(rank, own), cotangent_ref[2]).astype(BF)
    keep_ref[:rows, :] = dot(picks(rank_ref[1, :blocks], labels), cotangent_ref[tm]).astype(BF)
    for role, copy in enumerate((1 - tm, 2, tm)):
        down = ranks_down(masked_ref[pl.ds(copy, 1), :], tm, half, unmasked)
        down_ref[role] = jnp.concatenate([down, jnp.zeros((LANES, 8 - blocks), jnp.int32)], axis=1)


def normalise(values):
    centred = values - jnp.mean(values, axis=-1, keepdims=True)
    scale = lax.rsqrt(jnp.mean(centred * centred, axis=-1, keepdims=True) + EPSILON)
    return centred * scale, scale


def attention_kernel(
    unmasked, count, split, place_ref, own_ref, got_ref, small_ref, w_ref,
    x_ref, q_ref, k_ref, v_ref, p_ref, att_ref, *rest
):
    rows, width = own_ref.shape
    at = iota((rows, width), 0)
    x = own_ref[...].astype(F32) + got_ref[...].astype(F32)
    x = jnp.where(at == unmasked, small_ref[0:1, :], x)
    hat, _ = normalise(x)
    normed = (hat * small_ref[1:2, :] + small_ref[2:3, :]).astype(BF)
    mixed = dot(normed, w_ref[...])
    query = ((mixed[:, :width] + small_ref[3:4, :]).astype(BF).astype(F32) * HEAD_DIM ** (-0.5)).astype(BF)
    key = mixed[:, width : 2 * width].astype(BF)
    value = (mixed[:, 2 * width :] + small_ref[4:5, :]).astype(BF)
    k_ref[...] = key
    v_ref[...] = value
    x = x.astype(BF)
    if split:
        tm = place_ref[0]
        part = unmasked // 2

        def take(values):
            chosen = jnp.where(tm == 0, values[:part].astype(F32), values[part:unmasked].astype(F32)).astype(BF)
            return jnp.concatenate([chosen, values[unmasked:]], axis=0)

        rest[0][...] = x
        x, query = take(x), take(query)
    x_ref[...] = x
    q_ref[...] = query
    across = iota((1, rows), 1)
    bias = jnp.where(across < unmasked, 0.0, jnp.where(across == unmasked, math.log(count), -1e30))
    first = iota((1, LANES), 1) < HEAD_DIM
    for pair in range(width // LANES):
        cols = slice(pair * LANES, (pair + 1) * LANES)
        q_pair, k_pair, v_pair = query[:, cols], key[:, cols], value[:, cols]
        parts = []
        for side in range(2):
            mine = first if side == 0 else jnp.logical_not(first)
            scores = dot_last(jnp.where(mine, q_pair, jnp.zeros_like(q_pair)), k_pair) + bias
            expo = jnp.exp(scores - jnp.max(scores, axis=1, keepdims=True))
            probs = (expo * (1.0 / jnp.sum(expo, axis=1, keepdims=True))).astype(BF)
            p_ref[2 * pair + side] = probs
            parts.append(dot(probs, v_pair))
        att_ref[:, cols] = jnp.where(first, parts[0], parts[1]).astype(BF)


def gelu_terms(hidden):
    size = jnp.abs(hidden) * (0.5**0.5)
    t = 1.0 / (1.0 + 0.3275911 * size)
    bell = jnp.exp(hidden * hidden * -0.5)
    tail = t * (0.254829592 + t * (-0.284496736 + t * (1.421413741 + t * (-1.453152027 + t * 1.061405429))))
    tail = 0.5 * tail * bell
    below = jnp.where(hidden >= 0.0, 1.0 - tail, tail)
    return hidden * below, below + hidden * bell * (1.0 / math.sqrt(2.0 * math.pi))


def stacked(refs):
    return jnp.concatenate([ref[...] for ref in refs], axis=0)


def scatter_chunks(me, stage_ref, keep_ref, send_ref, into=0):
    depth = keep_ref.shape[2] - into
    for rel in range(2 * 4 * keep_ref.shape[1]):
        first = pl.multiple_of((me ^ rel) * depth, 16)
        target = send_ref if rel & 1 else keep_ref
        target[(rel >> 1) & 3, rel >> 3, into:] = stage_ref[pl.ds(first, depth), :]


def stage_weight(stage_ref, first, grad):
    depth = grad.shape[0]
    for block in range(grad.shape[1] // LANES):
        stage_ref[first + block * depth : first + (block + 1) * depth, :] = grad[
            :, block * LANES : (block + 1) * LANES
        ].astype(BF)
    return first + grad.shape[0] * (grad.shape[1] // LANES)


def stage_rows(stage_ref, first, vectors):
    pieces = [v[:, b * LANES : (b + 1) * LANES] for v in vectors for b in range(v.shape[1] // LANES)]
    missing = -len(pieces) % 16
    if missing:
        pieces.append(jnp.zeros((missing, LANES), F32))
    block = jnp.concatenate(pieces, axis=0).astype(BF)
    stage_ref[first : first + block.shape[0], :] = block
    return first + block.shape[0]


def clear_rest(stage_ref, first):
    if first < stage_ref.shape[0]:
        stage_ref[first:, :] = jnp.zeros((stage_ref.shape[0] - first, LANES), BF)


def up_kernel(
    place_ref, groups_ref, everyone_ref, att_a, att_b, x_a, x_b, cot_own, cot_got, small_ref, bias_up_ref, w_proj_ref, w_up_ref,
    middle_ref, normed_ref, active_ref, slope_ref, upstream_ref, keep_ref, send_ref, stage_ref
):
    rows_a, width = x_a.shape
    total = rows_a + x_b.shape[0]
    attended = stacked((att_a, att_b))
    x = stacked((x_a, x_b)).astype(F32)
    middle = x + dot(attended, w_proj_ref[...]) + small_ref[5:6, :]
    middle_ref[...] = middle
    hat, _ = normalise(middle)
    normed = (hat * small_ref[6:7, :] + small_ref[7:8, :]).astype(BF)
    normed_ref[...] = normed
    everyone = everyone_ref[...]

    def weight_of(group):
        return 1.0 / jnp.sum(jnp.where(everyone == group, 1.0, 0.0), axis=1, keepdims=True)

    weight = jnp.where(
        iota((total, 1), 0) < rows_a, weight_of(groups_ref[place_ref[0]]), weight_of(groups_ref[2])
    )
    upstream = (cot_own[...].astype(F32) + cot_got[...].astype(F32)) * weight
    upstream_ref[...] = upstream
    grad_result = upstream.astype(BF)
    hidden = dot(normed, w_up_ref[...]) + bias_up_ref[...]
    active, slope = gelu_terms(hidden)
    active = active.astype(BF)
    active_ref[...] = active
    slope_ref[...] = slope.astype(BF)
    end = stage_weight(stage_ref, 0, dot_rows(active, grad_result))
    clear_rest(stage_ref, end)
    scatter_chunks(place_ref[1], stage_ref, keep_ref, send_ref)


def norm_back(grad, hat, scale, gain):
    inner = grad * gain
    mean = jnp.mean(inner, axis=-1, keepdims=True)
    along = jnp.mean(inner * hat, axis=-1, keepdims=True)
    return scale * (inner - mean - hat * along)


def down_kernel(
    place_ref, middle_ref, normed_ref, active_ref, slope_ref, upstream_ref, att_a, att_b, small_ref,
    w_proj_ref, w_up_ref, w_down_ref,
    out_ref, grad_middle_ref, grad_att_ref, keep_ref, send_ref, stage_ref
):
    middle = middle_ref[...]
    out_ref[...] = (middle + dot(active_ref[...], w_down_ref[...]) + small_ref[8:9, :]).astype(BF)
    upstream = upstream_ref[...]
    grad_result = upstream.astype(BF)
    grad_hidden = (dot_last(grad_result, w_down_ref[...]) * slope_ref[...].astype(F32)).astype(BF)
    end = stage_weight(stage_ref, 0, dot_rows(normed_ref[...], grad_hidden))
    grad_normed = dot_last(grad_hidden, w_up_ref[...])
    hat, scale = normalise(middle)
    grad_middle = upstream + norm_back(grad_normed, hat, scale, small_ref[6:7, :])
    grad_middle_ref[...] = grad_middle
    grad_branch = grad_middle.astype(BF)
    grad_att_ref[...] = dot_last(grad_branch, w_proj_ref[...]).astype(BF)
    end = stage_weight(stage_ref, end, dot_rows(stacked((att_a, att_b)), grad_branch))
    vectors = (
        column_sums(grad_hidden.astype(F32)),
        column_sums(grad_normed * hat),
        column_sums(grad_normed),
        column_sums(grad_branch.astype(F32)),
        column_sums(grad_result.astype(F32)),
    )
    end = stage_rows(stage_ref, end, vectors)
    clear_rest(stage_ref, end)
    scatter_chunks(place_ref[1], stage_ref, keep_ref, send_ref)


def attention_back_kernel(row_from, g_ref, att_ref, q_ref, k_ref, v_ref, p_ref, dq_ref, dk_ref, dv_ref):
    width = q_ref.shape[1]
    rows = q_ref.shape[0]
    first = iota((1, LANES), 1) < HEAD_DIM
    for pair in range(width // LANES):
        cols = slice(pair * LANES, (pair + 1) * LANES)
        g_pair = g_ref[row_from : row_from + rows, cols]
        q_pair, k_pair, v_pair = q_ref[:, cols], k_ref[:, cols], v_ref[:, cols]
        agree = g_pair.astype(F32) * att_ref[:, cols].astype(F32)
        dq, dk, dv = [], [], []
        for side in range(2):
            mine = first if side == 0 else jnp.logical_not(first)
            correction = jnp.sum(jnp.where(mine, agree, 0.0), axis=1, keepdims=True)
            probs = p_ref[2 * pair + side]
            grad_probs = dot_last(jnp.where(mine, g_pair, jnp.zeros_like(g_pair)), v_pair)
            grad_scores = (probs.astype(F32) * (grad_probs - correction)).astype(BF)
            dq.append(dot(grad_scores, k_pair))
            dk.append(dot_rows(grad_scores, q_pair))
            dv.append(dot_rows(probs, g_pair))
        dq_ref[:, cols] = (jnp.where(first, dq[0], dq[1]) * HEAD_DIM ** (-0.5)).astype(BF)
        dk_ref[:, cols] = jnp.where(first, dk[0], dk[1]).astype(BF)
        dv_ref[:, cols] = jnp.where(first, dv[0], dv[1]).astype(BF)


def inputs_back_kernel(
    unmasked, place_ref, x_a, x_b, dq_a, dq_b, dk_a, dk_b, dv_a, dv_b, grad_middle_ref, small_ref, w_ref,
    keep_one, send_one, keep_two, send_two,
    grad_ref, keep_ref, send_ref, stage_ref
):
    rows, width = x_a.shape
    part = unmasked // 2
    tm = place_ref[0]

    def spread(block):
        wide = block.astype(F32)
        left = jnp.where(tm == 0, wide[:part], 0.0)
        right = jnp.where(tm == 0, 0.0, wide[:part])
        return jnp.concatenate([left, right, wide[part:]], axis=0)

    x = stacked((x_a, x_b)).astype(F32)
    hat, scale = normalise(x)
    gain = small_ref[1:2, :]
    normed = (hat * gain + small_ref[2:3, :]).astype(BF)
    dq = jnp.concatenate([dq_a[...], spread(dq_b[...]).astype(BF)], axis=0)
    mixed = jnp.concatenate([dq, stacked((dk_a, dk_b)), stacked((dv_a, dv_b))], axis=1)
    end = stage_weight(stage_ref, 0, dot_rows(normed, mixed))
    grad_normed = dot_last(mixed, w_ref[...])
    grad = norm_back(grad_normed, hat, scale, gain)
    grad = grad + jnp.concatenate([grad_middle_ref[:rows], spread(grad_middle_ref[rows:])], axis=0)
    grad_ref[:unmasked] = grad[:unmasked].astype(BF)
    grad_ref[unmasked:] = grad[rows : rows + unmasked].astype(BF)
    vectors = (
        column_sums(mixed[:, :width].astype(F32)),
        column_sums(mixed[:, 2 * width :].astype(F32)),
        column_sums(grad_normed * hat),
        column_sums(grad_normed),
        grad[unmasked : unmasked + 1] + grad[rows + unmasked : rows + unmasked + 1],
    )
    end = stage_rows(stage_ref, end, vectors)
    clear_rest(stage_ref, end)
    one, two = keep_one.shape[2], keep_two.shape[2]
    keep_ref[:, :, :one] = keep_one[...]
    send_ref[:, :, :one] = send_one[...]
    keep_ref[:, :, one : one + two] = keep_two[...]
    send_ref[:, :, one : one + two] = send_two[...]
    scatter_chunks(place_ref[1], stage_ref, keep_ref, send_ref, one + two)


def place_back(down, rows, half):
    labels = jnp.broadcast_to(iota((1, rows), 1), (LANES, rows))
    return jnp.concatenate([ones_where(labels == down[:, b : b + 1]) for b in range(half // LANES)], axis=0)


def outputs_kernel(unmasked, place_ref, down_ref, own_ref, got_ref, out_ref):
    tm = place_ref[0]
    half = out_ref.shape[1]
    rows = unmasked + EXTRA
    part = unmasked // 2
    out_ref[tm] = dot(place_back(down_ref[2], rows, half), own_ref[:rows]).astype(BF)
    out_ref[1 - tm] = dot(place_back(down_ref[0], rows, half), got_ref[:rows]).astype(BF)
    own = own_ref[rows:].astype(F32)
    got = got_ref[rows:].astype(F32)
    left = jnp.where(tm == 0, own[:part], got[:part])
    right = jnp.where(tm == 0, got[:part], own[:part])
    whole = jnp.concatenate([left, right, own[part:]], axis=0).astype(BF)
    out_ref[2] = dot(place_back(down_ref[1], rows, half), whole).astype(BF)


def grads_out_kernel(unmasked, place_ref, down_ref, own_ref, got_ref, out_ref):
    tm = place_ref[0]
    half = out_ref.shape[1]
    out_ref[tm] = dot(place_back(down_ref[2], unmasked, half), own_ref[:unmasked]).astype(BF)
    out_ref[1 - tm] = dot(place_back(down_ref[0], unmasked, half), got_ref[:unmasked]).astype(BF)
    whole = (own_ref[unmasked:].astype(F32) + got_ref[unmasked:].astype(F32)).astype(BF)
    out_ref[2] = dot(place_back(down_ref[1], unmasked, half), whole).astype(BF)


def fold_kernel(keep_ref, got_ref, *out_refs):
    for step, out_ref in enumerate(out_refs):
        out_ref[...] = (keep_ref[step].astype(F32) + got_ref[step].astype(F32)).astype(BF)


def fold_four_kernel(*refs):
    total = refs[0][...].astype(F32)
    for ref in refs[1:4]:
        total = total + ref[...].astype(F32)
    total = total.astype(BF)
    if len(refs) == 5:
        refs[4][...] = total
        return
    for step, out_ref in enumerate(refs[4:]):
        for slot in range(out_ref.shape[0]):
            out_ref[slot] = total[4 * slot + step]


def join_kernel(*refs):
    for step in range(len(refs) - 1):
        refs[-1][step] = refs[step][...]


def clip_swap(values, distance):
    size = lax.axis_size("clip")
    return lax.ppermute(values, "clip", [(i, i ^ distance) for i in range(size)])


def near_swap(values, step):
    size = lax.axis_size("clip")
    pairs = [
        (t * size + i, (t ^ (step & 1)) * size + (i ^ ((step >> 1) << 1))) for t in range(2) for i in range(size)
    ]
    return lax.ppermute(values, ("tm", "clip"), pairs)


def sum_over_devices(keep, send, beside_near, send_far, beside_last):
    far = []
    distance = 4
    while distance < lax.axis_size("clip"):
        far.append(distance)
        distance *= 4
    _, groups, depth, _ = keep.shape
    got = clip_swap(send, 1)
    pieces = plain(fold_kernel, [shape(groups, depth, LANES)] * 4)(keep, got)
    pieces = [pieces[0]] + [near_swap(pieces[step], step) for step in (1, 2, 3)]
    first = beside_near()
    *pieces, first = lax.optimization_barrier((*pieces, first))
    left = groups
    sent = None
    for distance in far:
        left //= 4
        pieces = plain(fold_four_kernel, [shape(left, depth, LANES)] * 4)(*pieces)
        if sent is None:
            sent, pieces = send_far(pieces)
        pieces = [pieces[0]] + [clip_swap(pieces[step], step * distance) for step in (1, 2, 3)]
    total = plain(fold_four_kernel, shape(left, depth, LANES))(*pieces)
    for distance in reversed(far):
        pieces = [total] + [clip_swap(total, step * distance) for step in (1, 2, 3)]
        total = jnp.stack(pieces, axis=1).reshape(-1, depth, LANES)
    total, sent = lax.optimization_barrier((total, sent))
    pieces = [total] + [near_swap(total, step) for step in (1, 2, 3)]
    last = beside_last(sent)
    *pieces, last = lax.optimization_barrier((*pieces, last))
    total = jnp.stack(pieces)
    return total, clip_swap(total, 1), first, last


def gather_chunks(me, own_ref, got_ref, stage_ref, start, depth):
    for rel in range(2 * 4 * own_ref.shape[1]):
        first = pl.multiple_of((me ^ rel) * depth, 16)
        source = got_ref if rel & 1 else own_ref
        stage_ref[pl.ds(first, depth), :] = source[(rel >> 1) & 3, rel >> 3, start : start + depth]


def unstage_kernel(units, place_ref, own_ref, got_ref, *refs):
    stage_ref = refs[-1]
    start = at = 0
    for depth, weights, vectors in units:
        gather_chunks(place_ref[1], own_ref, got_ref, stage_ref, start, depth)
        unstage(weights, stage_ref, refs[at : at + weights + vectors])
        start += depth
        at += weights + vectors


def unstage(weights, stage_ref, outs):
    first = 0
    for out_ref in outs[:weights]:
        depth, width = out_ref.shape
        for block in range(width // LANES):
            out_ref[:, block * LANES : (block + 1) * LANES] = stage_ref[first : first + depth, :].astype(F32)
            first += depth
    if len(outs) > weights:
        count = sum(ref.shape[0] // LANES for ref in outs[weights:])
        rows = stage_ref[first : first + count + -count % 16, :].astype(F32)
        at = 0
        for out_ref in outs[weights:]:
            blocks = out_ref.shape[0] // LANES
            for block in range(blocks):
                out_ref[block * LANES : (block + 1) * LANES] = rows[at + block]
            at += blocks


def chunk_rows(count, devices):
    return -(-count // (devices * 16)) * 16


def body(
    tokens,
    masked,
    groups,
    cotangent,
    mask_token,
    gain_one,
    shift_one,
    w_qkv,
    q_bias,
    v_bias,
    w_proj,
    b_proj,
    gain_two,
    shift_two,
    w_up,
    b_up,
    w_down,
    b_down,
):
    copies, half, width = tokens.shape
    hidden = w_up.shape[1]
    hide = masked.shape[1]
    unmasked = 2 * half - hide
    rows = unmasked + EXTRA
    some = unmasked // 2 + EXTRA
    total = rows + some
    tm, clip = lax.axis_index("tm"), lax.axis_index("clip")
    clips = lax.axis_size("clip")
    devices = 2 * clips
    me = (clip & 1) | (tm << 1) | ((clip >> 1) << 2)
    place = jnp.stack([tm, me]).astype(jnp.int32)
    smem = pl.BlockSpec(memory_space=pltpu.SMEM)
    swap = functools.partial(lax.ppermute, axis_name="tm", perm=[(0, 1), (1, 0)])

    def run(kernel, args, outs, scratch=(), scalars=1, limit=48, flops=0, anywhere=()):
        moved = sum(math.prod(a.shape) * a.dtype.itemsize for a in list(args) + jax.tree.leaves(outs))
        return pl.pallas_call(
            kernel,
            out_shape=outs,
            in_specs=[
                smem if at < scalars else pl.BlockSpec(memory_space=pl.ANY) if at in anywhere else VMEM
                for at in range(len(args))
            ],
            out_specs=jax.tree.map(lambda _: VMEM, outs),
            scratch_shapes=list(scratch),
            compiler_params=pltpu.CompilerParams(vmem_limit_bytes=limit << 20),
            cost_estimate=pl.CostEstimate(flops=flops, bytes_accessed=moved, transcendentals=0),
        )(*args)

    counts = (width // LANES * hidden, hidden // LANES * width + width // LANES * width + 32, 3 * width // LANES * width + 16)
    depths = [chunk_rows(count, devices) for count in counts]

    def chunked(unit, together=False):
        depth = sum(depths) if together else depths[unit]
        halves = [shape(4, devices // 8, depth, LANES)] * 2
        return halves, [pltpu.VMEM((devices * depths[unit], LANES), BF)]

    small = jnp.stack(
        [mask_token, gain_one, shift_one, q_bias, v_bias, b_proj, gain_two, shift_two, b_down]
    ).astype(F32)
    bias_up = b_up.astype(F32).reshape(1, hidden)

    block = shape(rows, width)
    everyone = jnp.concatenate([groups, clip_swap(groups, 1)])
    theirs, rank_theirs = run(
        functools.partial(prep_theirs_kernel, unmasked),
        (place, masked, tokens),
        [block, shape(8, LANES, kind=jnp.int32)],
        [pltpu.VMEM((half, width), BF), pltpu.SemaphoreType.DMA],
        flops=2 * rows * half * width,
        anywhere=(2,),
    )
    everyone, theirs = lax.optimization_barrier((everyone, theirs))
    got_mine = swap(theirs)
    shared, mine, rank = run(
        functools.partial(prep_tokens_kernel, unmasked),
        (place, masked, tokens),
        [block, block, shape(2, 8, LANES, kind=jnp.int32)],
        flops=4 * rows * half * width,
    )
    got_shared = swap(shared)
    everyone, shared = lax.optimization_barrier((everyone, shared))
    everyone = jnp.concatenate([everyone, clip_swap(everyone, 2)])
    cot_own, cot_send, down = run(
        functools.partial(prep_grads_kernel, unmasked),
        (place, masked, rank_theirs, rank, cotangent),
        [shape(total, width), shape(total, width), shape(copies, LANES, 8, kind=jnp.int32)],
        flops=2 * copies * rows * half * width,
    )
    everyone, cot_send = lax.optimization_barrier((everyone, cot_send))
    everyone = jnp.concatenate([everyone, clip_swap(everyone, 4)])
    everyone, got_mine = lax.optimization_barrier((everyone, got_mine))
    distance = 8
    while distance < clips:
        everyone = jnp.concatenate([everyone, clip_swap(everyone, distance)])
        distance *= 2
    cot_got = swap(cot_send)

    def attend(own, got, split):
        queries = some if split else rows
        outs = [
            shape(queries, width), shape(queries, width), block, block,
            shape(HEADS, queries, rows), shape(queries, width),
        ]
        if split:
            outs.append(block)
        return run(
            functools.partial(attention_kernel, unmasked, hide, split),
            (place, own, got, small, w_qkv),
            outs,
            flops=6 * rows * width * width + 4 * queries * rows * width,
        )

    x_a, q_a, k_a, v_a, p_a, att_a = attend(mine, got_mine, False)
    x_b, q_b, k_b, v_b, p_b, att_b, x_whole = attend(shared, got_shared, True)

    halves, stage = chunked(0)
    middle, normed_two, active, slope, upstream, keep_one, send_one = run(
        up_kernel,
        (place, groups, everyone.reshape(1, -1), att_a, att_b, x_a, x_b, cot_own, cot_got, small, bias_up, w_proj, w_up),
        [
            shape(total, width, kind=F32), shape(total, width), shape(total, hidden), shape(total, hidden),
            shape(total, width, kind=F32),
        ]
        + halves,
        stage,
        scalars=2,
        flops=2 * total * width * (width + 2 * hidden),
    )

    halves, stage = chunked(1)
    out_rows, grad_middle, grad_att, keep_two, send_two = run(
        down_kernel,
        (place, middle, normed_two, active, slope, upstream, att_a, att_b, small, w_proj, w_up, w_down),
        [shape(total, width), shape(total, width, kind=F32), shape(total, width)] + halves,
        stage,
        flops=2 * total * width * (2 * width + 4 * hidden),
    )
    out_got = swap(out_rows)

    def attend_back(row_from, att, q, k, v, p):
        return run(
            functools.partial(attention_back_kernel, row_from),
            (grad_att, att, q, k, v, p),
            [shape(q.shape[0], width), block, block],
            scalars=0,
            flops=8 * q.shape[0] * rows * width,
        )

    dq_a, dk_a, dv_a = attend_back(0, att_a, q_a, k_a, v_a, p_a)
    dq_b, dk_b, dv_b = attend_back(rows, att_b, q_b, k_b, v_b, p_b)
    halves, stage = chunked(2, True)
    grad_rows, keep, send = run(
        functools.partial(inputs_back_kernel, unmasked),
        (place, x_a, x_whole, dq_a, dq_b, dk_a, dk_b, dv_a, dv_b, grad_middle, small, w_qkv, keep_one, send_one, keep_two, send_two),
        [shape(2 * unmasked, width)] + halves,
        stage,
        flops=2 * 2 * rows * width * 6 * width,
    )
    send, out_got = lax.optimization_barrier((send, out_got))

    def place_outputs():
        return run(functools.partial(outputs_kernel, unmasked), (place, down, out_rows, out_got), shape(*tokens.shape))

    def send_grads(pieces):
        *pieces, now = lax.optimization_barrier((*pieces, grad_rows))
        return swap(now), pieces

    def place_grads(got):
        return run(functools.partial(grads_out_kernel, unmasked), (place, down, grad_rows, got), shape(*tokens.shape))

    sums_own, sums_got, block_out, grad_tokens = sum_over_devices(
        keep, send, place_outputs, send_grads, place_grads
    )

    vector = shape(width, kind=F32)
    outs = [
        shape(hidden, width, kind=F32),
        shape(width, hidden, kind=F32), shape(width, width, kind=F32), shape(hidden, kind=F32),
        vector, vector, vector, vector,
        shape(width, 3 * width, kind=F32), vector, vector, vector, vector, vector,
    ]
    units = tuple(zip(depths, (1, 2, 1), (0, 5, 5)))
    (
        grad_w_down,
        grad_w_up, grad_w_proj, grad_b_up, grad_gain_two, grad_shift_two, grad_b_proj, grad_b_down,
        grad_w_qkv, grad_q_bias, grad_v_bias, grad_gain_one, grad_shift_one, grad_mask_token,
    ) = run(
        functools.partial(unstage_kernel, units),
        (place, sums_own, sums_got),
        outs,
        [pltpu.VMEM((devices * max(depths), LANES), BF)],
    )
    return (
        block_out,
        grad_tokens,
        grad_mask_token,
        grad_gain_one,
        grad_shift_one,
        grad_w_qkv,
        grad_q_bias,
        grad_v_bias,
        grad_w_proj,
        grad_b_proj,
        grad_gain_two,
        grad_shift_two,
        grad_w_up,
        grad_b_up,
        grad_w_down,
        grad_b_down,
    )


def solution(mesh):
    return jax.shard_map(
        body,
        mesh=mesh,
        in_specs=(P("clip", "tm", None), P("clip", None), P("clip"), P("clip", "tm", None)) + (P(),) * 14,
        out_specs=(P("clip", "tm", None), P("clip", "tm", None)) + (P(),) * 14,
        check_vma=False,
    )
```

```python
import functools
import math

import jax
import jax.numpy as jnp
from jax import lax
from jax.experimental import pallas as pl
from jax.experimental.pallas import tpu as pltpu
from jax.sharding import PartitionSpec as P

HEADS = 6
HEAD_DIM = 64
LANES = 128
EXTRA = 16
EPSILON = 1e-06

BF = jnp.bfloat16
F32 = jnp.float32
VMEM = pl.BlockSpec(memory_space=pltpu.VMEM)
SMEM = pl.BlockSpec(memory_space=pltpu.SMEM)
HBM = pl.BlockSpec(memory_space=pltpu.HBM)


def dot(left, right):
    return jnp.dot(left, right, preferred_element_type=F32)


def dot_last(left, right):
    return lax.dot_general(left, right, (((1,), (1,)), ((), ())), preferred_element_type=F32)


def dot_rows(left, right):
    return lax.dot_general(left, right, (((0,), (0,)), ((), ())), preferred_element_type=F32)


def iota(shape, axis):
    return lax.broadcasted_iota(jnp.int32, shape, axis)


def ones_where(condition):
    return jnp.where(condition, 1.0, 0.0).astype(BF)


def column_sums(values):
    return jnp.sum(values, axis=0, keepdims=True)


def shape(*dims, kind=BF):
    return jax.ShapeDtypeStruct(dims, kind)


def plain(kernel, outs):
    return pl.pallas_call(kernel, out_shape=outs, compiler_params=pltpu.CompilerParams(vmem_limit_bytes=8 << 20))


def all_ranks(masked_ref, tm, half, unmasked):
    copies, hide = masked_ref.shape
    blocks = half // LANES
    marks = []
    for copy in range(copies):
        row = masked_ref[copy : copy + 1, :]
        low = ones_where(iota((LANES, hide), 0) == (row & (LANES - 1)))
        high = ones_where(iota((16, hide), 0) == (row >> 7))
        marks.append(dot_last(high, low))
    marks = jnp.concatenate(marks, axis=0)
    count = 16 * copies
    block = iota((count, LANES), 0)
    free = jnp.where((block & 15) < 2 * blocks, 1.0 - marks, 0.0).astype(BF)
    before = ones_where(iota((LANES, LANES), 0) < iota((LANES, LANES), 1))
    within = dot(free, before)
    totals = dot(free, jnp.ones((LANES, LANES), BF)).astype(BF)
    row, column = iota((count, count), 0), iota((count, count), 1)
    earlier = ones_where(jnp.logical_and(column < row, (column >> 4) == (row >> 4)))
    rank = within + dot(earlier, totals)
    rank = jnp.where(marks > 0.5, float(unmasked), rank)
    rank = jnp.concatenate([rank, jnp.zeros((LANES - count, LANES), F32)], axis=0)
    down = jnp.transpose(rank).astype(jnp.int32)
    rank = rank.astype(jnp.int32)
    across = []
    for copy in range(copies):
        first = rank[16 * copy : 16 * copy + blocks]
        second = rank[16 * copy + blocks : 16 * copy + 2 * blocks]
        across.append(jnp.concatenate([jnp.where(tm == 0, first, second), rank[:8-blocks]], axis=0))
    return across, down


def picks(rank, labels):
    wide = jnp.broadcast_to(labels, (labels.shape[0], LANES))
    return jnp.concatenate([ones_where(wide == rank[b : b + 1, :]) for b in range(rank.shape[0])], axis=1)


def load_halves(copies, half_refs, arrived, source_ref):
    loads = [
        pltpu.make_async_copy(source_ref.at[copy], half_refs.at[at], arrived.at[at]) for at, copy in enumerate(copies)
    ]
    for load in loads:
        load.start()
    return loads


def prep_theirs_kernel(unmasked, place_ref, masked_ref, tokens_ref, theirs_ref, rank_ref, down_ref, half_refs, arrived):
    tm = place_ref[0]
    half = tokens_ref.shape[1]
    blocks = half // LANES
    (load,) = load_halves((1 - tm,), half_refs, arrived, tokens_ref)
    across, down = all_ranks(masked_ref, tm, half, unmasked)
    for copy, rank in enumerate(across):
        rank_ref[copy] = rank
    for copy in range(len(across)):
        first = 16 * copy
        down_ref[copy] = jnp.where(tm == 0, down[:, first : first + 8], down[:, first + blocks : first + blocks + 8])
    chosen = picks(rank_ref[1 - tm, :blocks], iota((unmasked + EXTRA, 1), 0))
    load.wait()
    theirs_ref[...] = dot(chosen, half_refs[0]).astype(BF)


def prep_tokens_kernel(unmasked, place_ref, rank_ref, tokens_ref, shared_ref, mine_ref, half_refs, arrived):
    tm = place_ref[0]
    copies = (2, tm)
    loads = load_halves(copies, half_refs, arrived, tokens_ref)
    labels = iota((unmasked + EXTRA, 1), 0)
    for role, out_ref in enumerate((shared_ref, mine_ref)):
        chosen = picks(rank_ref[copies[role], : tokens_ref.shape[1] // LANES], labels)
        loads[role].wait()
        out_ref[...] = dot(chosen, half_refs[role]).astype(BF)


def prep_grads_kernel(unmasked, place_ref, rank_ref, cotangent_ref, keep_ref, send_ref, half_refs, arrived):
    tm = place_ref[0]
    blocks = cotangent_ref.shape[1] // LANES
    rows = unmasked + EXTRA
    part = unmasked // 2
    loads = load_halves((1 - tm, 2, tm), half_refs, arrived, cotangent_ref)
    labels = iota((rows, 1), 0)
    chosen = picks(rank_ref[1 - tm, :blocks], labels)
    loads[0].wait()
    send_ref[:rows, :] = dot(chosen, half_refs[0]).astype(BF)
    small = iota((part + EXTRA, 1), 0)
    theirs = jnp.where(small < part, small + part * (1 - tm), -1)
    own = jnp.where(small < part, small + part * tm, small + part)
    chosen = picks(rank_ref[2, :blocks], jnp.concatenate([theirs, own], axis=0))
    loads[1].wait()
    both = dot(chosen, half_refs[1]).astype(BF)
    send_ref[rows:, :] = both[: part + EXTRA]
    keep_ref[rows:, :] = both[part + EXTRA :]
    chosen = picks(rank_ref[tm, :blocks], labels)
    loads[2].wait()
    keep_ref[:rows, :] = dot(chosen, half_refs[2]).astype(BF)


def normalise(values):
    centred = values - jnp.mean(values, axis=-1, keepdims=True)
    scale = lax.rsqrt(jnp.mean(centred * centred, axis=-1, keepdims=True) + EPSILON)
    return centred * scale, scale


def attention_kernel(
    unmasked, count, split, place_ref, own_ref, got_ref, small_ref, w_ref,
    x_ref, q_ref, k_ref, v_ref, p_ref, att_ref, *rest
):
    rows, width = own_ref.shape
    at = iota((rows, width), 0)
    x = own_ref[...].astype(F32) + got_ref[...].astype(F32)
    x = jnp.where(at == unmasked, small_ref[0:1, :], x)
    hat, _ = normalise(x)
    normed = (hat * small_ref[1:2, :] + small_ref[2:3, :]).astype(BF)
    mixed = dot(normed, w_ref[...])
    query = ((mixed[:, :width] + small_ref[3:4, :]).astype(BF).astype(F32) * HEAD_DIM ** (-0.5)).astype(BF)
    key = mixed[:, width : 2 * width].astype(BF)
    value = (mixed[:, 2 * width :] + small_ref[4:5, :]).astype(BF)
    k_ref[...] = key
    v_ref[...] = value
    x = x.astype(BF)
    if split:
        tm = place_ref[0]
        part = unmasked // 2

        def take(values):
            chosen = jnp.where(tm == 0, values[:part].astype(F32), values[part:unmasked].astype(F32)).astype(BF)
            return jnp.concatenate([chosen, values[unmasked:]], axis=0)

        rest[0][...] = x
        x, query = take(x), take(query)
    x_ref[...] = x
    q_ref[...] = query
    across = iota((1, rows), 1)
    bias = jnp.where(across < unmasked, 0.0, jnp.where(across == unmasked, math.log(count), -1e30))
    first = iota((1, LANES), 1) < HEAD_DIM
    for pair in range(width // LANES):
        cols = slice(pair * LANES, (pair + 1) * LANES)
        q_pair, k_pair, v_pair = query[:, cols], key[:, cols], value[:, cols]
        parts = []
        for side in range(2):
            mine = first if side == 0 else jnp.logical_not(first)
            scores = dot_last(jnp.where(mine, q_pair, jnp.zeros_like(q_pair)), k_pair) + bias
            expo = jnp.exp(scores - jnp.max(scores, axis=1, keepdims=True))
            probs = (expo * (1.0 / jnp.sum(expo, axis=1, keepdims=True))).astype(BF)
            p_ref[2 * pair + side] = probs
            parts.append(dot(probs, v_pair))
        att_ref[:, cols] = jnp.where(first, parts[0], parts[1]).astype(BF)


def gelu_terms(hidden):
    size = jnp.abs(hidden) * (0.5**0.5)
    t = 1.0 / (1.0 + 0.3275911 * size)
    bell = jnp.exp(hidden * hidden * -0.5)
    tail = t * (0.254829592 + t * (-0.284496736 + t * (1.421413741 + t * (-1.453152027 + t * 1.061405429))))
    tail = 0.5 * tail * bell
    below = jnp.where(hidden >= 0.0, 1.0 - tail, tail)
    return hidden * below, below + hidden * bell * (1.0 / math.sqrt(2.0 * math.pi))


def stacked(refs):
    return jnp.concatenate([ref[...] for ref in refs], axis=0)


def scatter_chunks(me, stage_ref, keep_ref, send_ref):
    depth = keep_ref.shape[2]
    for rel in range(2 * 4 * keep_ref.shape[1]):
        first = pl.multiple_of((me ^ rel) * depth, 16)
        target = send_ref if rel & 1 else keep_ref
        target[(rel >> 1) & 3, rel >> 3] = stage_ref[pl.ds(first, depth), :]


def stage_weight(stage_ref, first, grad, apart=None):
    depth = grad.shape[0]
    apart = apart or depth
    for block in range(grad.shape[1] // LANES):
        at = first + block * apart
        stage_ref[at : at + depth, :] = grad[:, block * LANES : (block + 1) * LANES].astype(BF)
    return first + apart * (grad.shape[1] // LANES)


def stage_rows(stage_ref, first, vectors):
    pieces = [v[:, b * LANES : (b + 1) * LANES] for v in vectors for b in range(v.shape[1] // LANES)]
    missing = -len(pieces) % 16
    if missing:
        pieces.append(jnp.zeros((missing, LANES), F32))
    block = jnp.concatenate(pieces, axis=0).astype(BF)
    stage_ref[first : first + block.shape[0], :] = block
    return first + block.shape[0]


def clear_rest(stage_ref, first):
    if first < stage_ref.shape[0]:
        stage_ref[first:, :] = jnp.zeros((stage_ref.shape[0] - first, LANES), BF)


def forward_kernel(
    att_a, att_b, x_a, x_b, small_ref, bias_up_ref, w_proj_ref, w_up_ref, w_down_ref,
    out_ref, middle_ref, normed_ref, active_ref, slope_ref
):
    attended = stacked((att_a, att_b))
    x = stacked((x_a, x_b)).astype(F32)
    middle = x + dot(attended, w_proj_ref[...]) + small_ref[5:6, :]
    middle_ref[...] = middle
    hat, _ = normalise(middle)
    normed = (hat * small_ref[6:7, :] + small_ref[7:8, :]).astype(BF)
    normed_ref[...] = normed
    result = middle + small_ref[8:9, :]
    step = 512
    for first in range(0, w_up_ref.shape[1], step):
        cols = slice(first, first + step)
        active, slope = gelu_terms(dot(normed, w_up_ref[:, cols]) + bias_up_ref[:, cols])
        active = active.astype(BF)
        active_ref[:, cols] = active
        slope_ref[:, cols] = slope.astype(BF)
        result = result + dot(active, w_down_ref[cols, :])
    out_ref[...] = result.astype(BF)


def norm_back(grad, hat, scale, gain):
    inner = grad * gain
    mean = jnp.mean(inner, axis=-1, keepdims=True)
    along = jnp.mean(inner * hat, axis=-1, keepdims=True)
    return scale * (inner - mean - hat * along)


def backward_kernel(
    place_ref, groups_ref, everyone_ref, cot_own, cot_got, middle_ref, normed_ref, active_ref, slope_ref, att_a, att_b,
    small_ref, w_proj_ref, w_up_ref, w_down_ref,
    grad_middle_ref, grad_att_ref, keep_ref, send_ref, stage_ref
):
    rows_a, total = att_a.shape[0], cot_own.shape[0]
    everyone = everyone_ref[...]

    def weight_of(group):
        return 1.0 / jnp.sum(jnp.where(everyone == group, 1.0, 0.0), axis=1, keepdims=True)

    weight = jnp.where(
        iota((total, 1), 0) < rows_a, weight_of(groups_ref[place_ref[0]]), weight_of(groups_ref[2])
    )
    upstream = (cot_own[...].astype(F32) + cot_got[...].astype(F32)) * weight
    grad_result = upstream.astype(BF)
    normed = normed_ref[...]
    hidden, step = active_ref.shape[1], 512
    grad_normed = None
    sums = []
    parts = []
    for first in range(0, hidden, step):
        cols = slice(first, first + step)
        grad_hidden = (dot_last(grad_result, w_down_ref[cols, :]) * slope_ref[:, cols].astype(F32)).astype(BF)
        stage_weight(stage_ref, first, dot_rows(active_ref[:, cols], grad_result), hidden)
        part = dot_last(grad_hidden, w_up_ref[:, cols])
        grad_normed = part if grad_normed is None else grad_normed + part
        sums.append(column_sums(grad_hidden.astype(F32)))
        parts.append(dot_rows(normed, grad_hidden))
    end = hidden * (grad_result.shape[1] // LANES)
    for part in parts:
        end = stage_weight(stage_ref, end, part)
    hat, scale = normalise(middle_ref[...])
    grad_middle = upstream + norm_back(grad_normed, hat, scale, small_ref[6:7, :])
    grad_middle_ref[...] = grad_middle
    grad_branch = grad_middle.astype(BF)
    grad_att_ref[...] = dot_last(grad_branch, w_proj_ref[...]).astype(BF)
    end = stage_weight(stage_ref, end, dot_rows(stacked((att_a, att_b)), grad_branch))
    vectors = sums + [
        column_sums(grad_normed * hat),
        column_sums(grad_normed),
        column_sums(grad_branch.astype(F32)),
        column_sums(grad_result.astype(F32)),
    ]
    end = stage_rows(stage_ref, end, vectors)
    clear_rest(stage_ref, end)
    scatter_chunks(place_ref[1], stage_ref, keep_ref, send_ref)


def attention_back_kernel(row_from, g_ref, att_ref, q_ref, k_ref, v_ref, p_ref, dq_ref, dk_ref, dv_ref):
    width = q_ref.shape[1]
    rows = q_ref.shape[0]
    first = iota((1, LANES), 1) < HEAD_DIM
    for pair in range(width // LANES):
        cols = slice(pair * LANES, (pair + 1) * LANES)
        g_pair = g_ref[row_from : row_from + rows, cols]
        q_pair, k_pair, v_pair = q_ref[:, cols], k_ref[:, cols], v_ref[:, cols]
        agree = g_pair.astype(F32) * att_ref[:, cols].astype(F32)
        dq, dk, dv = [], [], []
        for side in range(2):
            mine = first if side == 0 else jnp.logical_not(first)
            correction = jnp.sum(jnp.where(mine, agree, 0.0), axis=1, keepdims=True)
            probs = p_ref[2 * pair + side]
            grad_probs = dot_last(jnp.where(mine, g_pair, jnp.zeros_like(g_pair)), v_pair)
            grad_scores = (probs.astype(F32) * (grad_probs - correction)).astype(BF)
            dq.append(dot(grad_scores, k_pair))
            dk.append(dot_rows(grad_scores, q_pair))
            dv.append(dot_rows(probs, g_pair))
        dq_ref[:, cols] = (jnp.where(first, dq[0], dq[1]) * HEAD_DIM ** (-0.5)).astype(BF)
        dk_ref[:, cols] = jnp.where(first, dk[0], dk[1]).astype(BF)
        dv_ref[:, cols] = jnp.where(first, dv[0], dv[1]).astype(BF)


def inputs_back_kernel(
    unmasked, place_ref, x_a, x_b, dq_a, dq_b, dk_a, dk_b, dv_a, dv_b, grad_middle_ref, small_ref, w_ref,
    grad_ref, keep_ref, send_ref, stage_ref
):
    rows, width = x_a.shape
    part = unmasked // 2
    tm = place_ref[0]

    def spread(block):
        wide = block.astype(F32)
        left = jnp.where(tm == 0, wide[:part], 0.0)
        right = jnp.where(tm == 0, 0.0, wide[:part])
        return jnp.concatenate([left, right, wide[part:]], axis=0)

    x = stacked((x_a, x_b)).astype(F32)
    hat, scale = normalise(x)
    gain = small_ref[1:2, :]
    normed = (hat * gain + small_ref[2:3, :]).astype(BF)
    dq = jnp.concatenate([dq_a[...], spread(dq_b[...]).astype(BF)], axis=0)
    mixed = jnp.concatenate([dq, stacked((dk_a, dk_b)), stacked((dv_a, dv_b))], axis=1)
    end = stage_weight(stage_ref, 0, dot_rows(normed, mixed))
    grad_normed = dot_last(mixed, w_ref[...])
    grad = norm_back(grad_normed, hat, scale, gain)
    grad = grad + jnp.concatenate([grad_middle_ref[:rows], spread(grad_middle_ref[rows:])], axis=0)
    grad_ref[:unmasked] = grad[:unmasked].astype(BF)
    grad_ref[unmasked:] = grad[rows : rows + unmasked].astype(BF)
    vectors = (
        column_sums(mixed[:, :width].astype(F32)),
        column_sums(mixed[:, 2 * width :].astype(F32)),
        column_sums(grad_normed * hat),
        column_sums(grad_normed),
        grad[unmasked : unmasked + 1] + grad[rows + unmasked : rows + unmasked + 1],
    )
    end = stage_rows(stage_ref, end, vectors)
    clear_rest(stage_ref, end)
    scatter_chunks(place_ref[1], stage_ref, keep_ref, send_ref)


def place_back(down, rows, half):
    labels = jnp.broadcast_to(iota((1, rows), 1), (LANES, rows))
    return jnp.concatenate([ones_where(labels == down[:, b : b + 1]) for b in range(half // LANES)], axis=0)


def outputs_kernel(unmasked, place_ref, down_ref, own_ref, got_ref, out_ref):
    tm = place_ref[0]
    half = out_ref.shape[1]
    rows = unmasked + EXTRA
    part = unmasked // 2
    out_ref[tm] = dot(place_back(down_ref[tm], rows, half), own_ref[:rows]).astype(BF)
    out_ref[1 - tm] = dot(place_back(down_ref[1 - tm], rows, half), got_ref[:rows]).astype(BF)
    own = own_ref[rows:].astype(F32)
    got = got_ref[rows:].astype(F32)
    left = jnp.where(tm == 0, own[:part], got[:part])
    right = jnp.where(tm == 0, got[:part], own[:part])
    whole = jnp.concatenate([left, right, own[part:]], axis=0).astype(BF)
    out_ref[2] = dot(place_back(down_ref[2], rows, half), whole).astype(BF)


def grads_out_kernel(unmasked, place_ref, down_ref, own_ref, got_ref, out_ref):
    tm = place_ref[0]
    half = out_ref.shape[1]
    out_ref[tm] = dot(place_back(down_ref[tm], unmasked, half), own_ref[:unmasked]).astype(BF)
    out_ref[1 - tm] = dot(place_back(down_ref[1 - tm], unmasked, half), got_ref[:unmasked]).astype(BF)
    whole = (own_ref[unmasked:].astype(F32) + got_ref[unmasked:].astype(F32)).astype(BF)
    out_ref[2] = dot(place_back(down_ref[2], unmasked, half), whole).astype(BF)


def fold_kernel(keep_ref, got_ref, *out_refs):
    for step, out_ref in enumerate(out_refs):
        out_ref[...] = (keep_ref[step].astype(F32) + got_ref[step].astype(F32)).astype(BF)


def fold_four_kernel(units, *refs):
    outs = refs[4 * units :]
    first = 0
    for unit in range(units):
        total = refs[4 * unit][...].astype(F32)
        for ref in refs[4 * unit + 1 : 4 * unit + 4]:
            total = total + ref[...].astype(F32)
        total = total.astype(BF)
        rows = slice(first, first + total.shape[1])
        first += total.shape[1]
        if len(outs) == 1:
            outs[0][:, rows] = total
        else:
            for step, out_ref in enumerate(outs):
                for slot in range(out_ref.shape[0]):
                    out_ref[slot, rows] = total[4 * slot + step]


def clip_swap(values, distance):
    size = lax.axis_size("clip")
    return lax.ppermute(values, "clip", [(i, i ^ distance) for i in range(size)])


def near_swap(values, step):
    size = lax.axis_size("clip")
    pairs = [
        (t * size + i, (t ^ (step & 1)) * size + (i ^ ((step >> 1) << 1))) for t in range(2) for i in range(size)
    ]
    return lax.ppermute(values, ("tm", "clip"), pairs)


def sum_nearby(keep, send, after, before=()):
    _, groups, depth, _ = keep.shape
    got, after = lax.optimization_barrier((clip_swap(send, 1), after))
    pieces = plain(fold_kernel, [shape(groups, depth, LANES)] * 4)(keep, got)
    *pieces, before = lax.optimization_barrier((*pieces, before))
    return [pieces[0]] + [near_swap(pieces[step], step) for step in (1, 2, 3)], before


def sum_over_devices(first_pieces, second_pieces, send_far, beside_last):
    far = []
    distance = 4
    while distance < lax.axis_size("clip"):
        far.append(distance)
        distance *= 4
    pieces = [*first_pieces, *second_pieces]
    groups = pieces[0].shape[0]
    depth = pieces[0].shape[1] + pieces[4].shape[1]
    left = groups
    sent = None
    for distance in far:
        left //= 4
        fold = functools.partial(fold_four_kernel, len(pieces) // 4)
        pieces = plain(fold, [shape(left, depth, LANES)] * 4)(*pieces)
        if sent is None:
            sent, pieces = send_far(pieces)
        pieces = [pieces[0]] + [clip_swap(pieces[step], step * distance) for step in (1, 2, 3)]
    total = plain(functools.partial(fold_four_kernel, 1), shape(left, depth, LANES))(*pieces)
    for distance in reversed(far):
        pieces = [total] + [clip_swap(total, step * distance) for step in (1, 2, 3)]
        total = jnp.stack(pieces, axis=1).reshape(-1, depth, LANES)
    total, sent = lax.optimization_barrier((total, sent))
    pieces = [total] + [near_swap(total, step) for step in (1, 2, 3)]
    last = beside_last(sent)
    *pieces, last = lax.optimization_barrier((*pieces, last))
    total = jnp.stack(pieces)
    return total, clip_swap(total, 1), last


def gather_chunks(me, own_ref, got_ref, stage_ref, start, depth):
    for rel in range(2 * 4 * own_ref.shape[1]):
        first = pl.multiple_of((me ^ rel) * depth, 16)
        source = got_ref if rel & 1 else own_ref
        stage_ref[pl.ds(first, depth), :] = source[(rel >> 1) & 3, rel >> 3, start : start + depth]


def unstage_kernel(units, place_ref, own_ref, got_ref, *refs):
    stage_ref = refs[-1]
    start = at = 0
    for depth, weights, vectors in units:
        gather_chunks(place_ref[1], own_ref, got_ref, stage_ref, start, depth)
        unstage(weights, stage_ref, refs[at : at + weights + vectors])
        start += depth
        at += weights + vectors


def unstage(weights, stage_ref, outs):
    first = 0
    for out_ref in outs[:weights]:
        depth, width = out_ref.shape
        for block in range(width // LANES):
            out_ref[:, block * LANES : (block + 1) * LANES] = stage_ref[first : first + depth, :].astype(F32)
            first += depth
    if len(outs) > weights:
        count = sum(ref.shape[0] // LANES for ref in outs[weights:])
        rows = stage_ref[first : first + count + -count % 16, :].astype(F32)
        at = 0
        for out_ref in outs[weights:]:
            blocks = out_ref.shape[0] // LANES
            for block in range(blocks):
                out_ref[block * LANES : (block + 1) * LANES] = rows[at + block]
            at += blocks


def chunk_rows(count, devices):
    return -(-count // (devices * 16)) * 16


def body(
    tokens,
    masked,
    groups,
    cotangent,
    mask_token,
    gain_one,
    shift_one,
    w_qkv,
    q_bias,
    v_bias,
    w_proj,
    b_proj,
    gain_two,
    shift_two,
    w_up,
    b_up,
    w_down,
    b_down,
):
    copies, half, width = tokens.shape
    hidden = w_up.shape[1]
    hide = masked.shape[1]
    unmasked = 2 * half - hide
    rows = unmasked + EXTRA
    some = unmasked // 2 + EXTRA
    total = rows + some
    tm, clip = lax.axis_index("tm"), lax.axis_index("clip")
    clips = lax.axis_size("clip")
    devices = 2 * clips
    me = (clip & 1) | (tm << 1) | ((clip >> 1) << 2)
    place = jnp.stack([tm, me]).astype(jnp.int32)
    swap = functools.partial(lax.ppermute, axis_name="tm", perm=[(0, 1), (1, 0)])

    def run(kernel, args, outs, scratch=(), scalars=1, limit=20, flops=0, in_hbm=(), hides=True):
        moved = sum(math.prod(a.shape) * a.dtype.itemsize for a in list(args) + jax.tree.leaves(outs))
        return pl.pallas_call(
            kernel,
            out_shape=outs,
            in_specs=[
                SMEM if at < scalars else HBM if at in in_hbm else VMEM
                for at in range(len(args))
            ],
            out_specs=jax.tree.map(lambda _: VMEM, outs),
            scratch_shapes=list(scratch),
            compiler_params=pltpu.CompilerParams(vmem_limit_bytes=limit << 20),
            cost_estimate=pl.CostEstimate(
                flops=flops if hides else 1, bytes_accessed=moved if hides else 1, transcendentals=0
            ),
        )(*args)

    counts = (2 * width // LANES * hidden + width // LANES * width + 32, 3 * width // LANES * width + 16)
    depths = [chunk_rows(count, devices) for count in counts]

    def chunked(unit):
        halves = [shape(4, devices // 8, depths[unit], LANES)] * 2
        return halves, [pltpu.VMEM((devices * depths[unit], LANES), BF)]

    small = jnp.stack(
        [mask_token, gain_one, shift_one, q_bias, v_bias, b_proj, gain_two, shift_two, b_down]
    ).astype(F32)
    bias_up = b_up.astype(F32).reshape(1, hidden)

    block = shape(rows, width)
    def loads(count):
        return [pltpu.VMEM((count, half, width), BF), pltpu.SemaphoreType.DMA((count,))]

    everyone = jnp.concatenate([groups, clip_swap(groups, 1)])
    theirs, rank, down = run(
        functools.partial(prep_theirs_kernel, unmasked),
        (place, masked, tokens),
        [block, shape(copies, 8, LANES, kind=jnp.int32), shape(copies, LANES, 8, kind=jnp.int32)],
        loads(1),
        limit=60,
        flops=2 * rows * half * width,
        in_hbm=(2,),
    )
    got_mine = swap(theirs)
    everyone, theirs, rank = lax.optimization_barrier((everyone, theirs, rank))
    everyone = jnp.concatenate([everyone, clip_swap(everyone, 2)])
    shared, mine = run(
        functools.partial(prep_tokens_kernel, unmasked),
        (place, rank, tokens),
        [block, block],
        loads(2),
        limit=60,
        flops=4 * rows * half * width,
        in_hbm=(2,),
    )
    got_shared = swap(shared)
    everyone, shared, rank = lax.optimization_barrier((everyone, shared, rank))
    everyone = jnp.concatenate([everyone, clip_swap(everyone, 4)])
    cot_own, cot_send = run(
        functools.partial(prep_grads_kernel, unmasked),
        (place, rank, cotangent),
        [shape(total, width), shape(total, width)],
        loads(3),
        limit=60,
        flops=2 * copies * rows * half * width,
        in_hbm=(2,),
    )
    everyone, cot_send = lax.optimization_barrier((everyone, cot_send))
    distance = 8
    while distance < clips:
        everyone = jnp.concatenate([everyone, clip_swap(everyone, distance)])
        distance *= 2
    cot_got = swap(cot_send)

    def attend(own, got, split):
        queries = some if split else rows
        outs = [
            shape(queries, width), shape(queries, width), block, block,
            shape(HEADS, queries, rows), shape(queries, width),
        ]
        if split:
            outs.append(block)
        return run(
            functools.partial(attention_kernel, unmasked, hide, split),
            (place, own, got, small, w_qkv),
            outs,
            flops=6 * rows * width * width + 4 * queries * rows * width,
        )

    x_a, q_a, k_a, v_a, p_a, att_a = attend(mine, got_mine, False)
    x_b, q_b, k_b, v_b, p_b, att_b, x_whole = attend(shared, got_shared, True)

    out_rows, middle, normed_two, active, slope = run(
        forward_kernel,
        (att_a, att_b, x_a, x_b, small, bias_up, w_proj, w_up, w_down),
        [
            shape(total, width), shape(total, width, kind=F32), shape(total, width), shape(total, hidden),
            shape(total, hidden),
        ],
        scalars=0,
        flops=2 * total * width * (width + 2 * hidden),
    )
    halves, stage = chunked(0)
    grad_middle, grad_att, keep, send = run(
        backward_kernel,
        (
            place, groups, everyone.reshape(1, -1), cot_own, cot_got, middle, normed_two, active, slope, att_a, att_b,
            small, w_proj, w_up, w_down,
        ),
        [shape(total, width, kind=F32), shape(total, width)] + halves,
        stage,
        scalars=2,
        hides=False,
    )

    def attend_back(row_from, grads, att, q, k, v, p):
        return run(
            functools.partial(attention_back_kernel, row_from),
            (grads, att, q, k, v, p),
            [shape(q.shape[0], width), block, block],
            scalars=0,
            hides=False,
        )

    dq_b, dk_b, dv_b = attend_back(rows, grad_att, att_b, q_b, k_b, v_b, p_b)
    first_pieces, grad_att = sum_nearby(keep, send, dq_b, grad_att)
    dq_a, dk_a, dv_a = attend_back(0, grad_att, att_a, q_a, k_a, v_a, p_a)
    halves, stage = chunked(1)
    grad_rows, keep, send = run(
        functools.partial(inputs_back_kernel, unmasked),
        (place, x_a, x_whole, dq_a, dq_b, dk_a, dk_b, dv_a, dv_b, grad_middle, small, w_qkv),
        [shape(2 * unmasked, width)] + halves,
        stage,
        hides=False,
    )
    send, first_pieces = lax.optimization_barrier((send, first_pieces))
    second_pieces, _ = sum_nearby(keep, send, ())

    def send_rows(pieces):
        *pieces, grads, outs = lax.optimization_barrier((*pieces, grad_rows, out_rows))
        return (swap(grads), swap(outs)), pieces

    def place_rows(got):
        grads_got, out_got = got
        return (
            run(functools.partial(outputs_kernel, unmasked), (place, down, out_rows, out_got), shape(*tokens.shape)),
            run(functools.partial(grads_out_kernel, unmasked), (place, down, grad_rows, grads_got), shape(*tokens.shape)),
        )

    sums_own, sums_got, (block_out, grad_tokens) = sum_over_devices(first_pieces, second_pieces, send_rows, place_rows)

    vector = shape(width, kind=F32)
    outs = [
        shape(hidden, width, kind=F32), shape(width, hidden, kind=F32), shape(width, width, kind=F32), shape(hidden, kind=F32),
        vector, vector, vector, vector,
        shape(width, 3 * width, kind=F32), vector, vector, vector, vector, vector,
    ]
    units = tuple(zip(depths, (3, 1), (5, 5)))
    (
        grad_w_down, grad_w_up, grad_w_proj, grad_b_up, grad_gain_two, grad_shift_two, grad_b_proj, grad_b_down,
        grad_w_qkv, grad_q_bias, grad_v_bias, grad_gain_one, grad_shift_one, grad_mask_token,
    ) = run(
        functools.partial(unstage_kernel, units),
        (place, sums_own, sums_got),
        outs,
        [pltpu.VMEM((devices * max(depths), LANES), BF)],
    )
    return (
        block_out,
        grad_tokens,
        grad_mask_token,
        grad_gain_one,
        grad_shift_one,
        grad_w_qkv,
        grad_q_bias,
        grad_v_bias,
        grad_w_proj,
        grad_b_proj,
        grad_gain_two,
        grad_shift_two,
        grad_w_up,
        grad_b_up,
        grad_w_down,
        grad_b_down,
    )


def solution(mesh):
    return jax.shard_map(
        body,
        mesh=mesh,
        in_specs=(P("clip", "tm", None), P("clip", None), P("clip"), P("clip", "tm", None)) + (P(),) * 14,
        out_specs=(P("clip", "tm", None), P("clip", "tm", None)) + (P(),) * 14,
        check_vma=False,
    )
```

```python
import functools
import math

import jax
import jax.numpy as jnp
import numpy as np
from jax import lax
from jax.experimental import pallas as pl
from jax.experimental.pallas import tpu as pltpu
from jax.sharding import PartitionSpec as P

HEADS = 6
HEAD_DIM = 64
LANES = 128
EXTRA = 16
EPSILON = 1e-06

BF = jnp.bfloat16
F32 = jnp.float32
VMEM = pl.BlockSpec(memory_space=pltpu.VMEM)
SMEM = pl.BlockSpec(memory_space=pltpu.SMEM)
HBM = pl.BlockSpec(memory_space=pltpu.HBM)


def dot(left, right):
    return jnp.dot(left, right, preferred_element_type=F32)


def dot_last(left, right):
    return lax.dot_general(left, right, (((1,), (1,)), ((), ())), preferred_element_type=F32)


def dot_rows(left, right):
    return lax.dot_general(left, right, (((0,), (0,)), ((), ())), preferred_element_type=F32)


def iota(shape, axis):
    return lax.broadcasted_iota(jnp.int32, shape, axis)


def ones_where(condition):
    return jnp.where(condition, 1.0, 0.0).astype(BF)


def column_sums(values):
    return jnp.sum(values, axis=0, keepdims=True)


def shape(*dims, kind=BF):
    return jax.ShapeDtypeStruct(dims, kind)


def plain(kernel, outs):
    return pl.pallas_call(kernel, out_shape=outs, compiler_params=pltpu.CompilerParams(vmem_limit_bytes=8 << 20))


def all_ranks(masked_ref, tm, half, unmasked):
    copies, hide = masked_ref.shape
    blocks = half // LANES
    marks = []
    for copy in range(copies):
        row = masked_ref[copy : copy + 1, :]
        low = ones_where(iota((LANES, hide), 0) == (row & (LANES - 1)))
        high = ones_where(iota((16, hide), 0) == (row >> 7))
        marks.append(dot_last(high, low))
    marks = jnp.concatenate(marks, axis=0)
    count = 16 * copies
    block = iota((count, LANES), 0)
    free = jnp.where((block & 15) < 2 * blocks, 1.0 - marks, 0.0).astype(BF)
    before = ones_where(iota((LANES, LANES), 0) < iota((LANES, LANES), 1))
    within = dot(free, before)
    totals = dot(free, jnp.ones((LANES, LANES), BF)).astype(BF)
    row, column = iota((count, count), 0), iota((count, count), 1)
    earlier = ones_where(jnp.logical_and(column < row, (column >> 4) == (row >> 4)))
    rank = within + dot(earlier, totals)
    rank = jnp.where(marks > 0.5, float(unmasked), rank)
    across = []
    for first in range(0, count, 16):
        mine = jnp.where(tm == 0, rank[first : first + blocks], rank[first + blocks : first + 2 * blocks])
        across.append(jnp.concatenate([mine, jnp.zeros((16 - blocks, LANES), F32)], axis=0))
    return jnp.concatenate(across, axis=0)


def picks(rank, labels):
    wide = jnp.broadcast_to(labels.astype(F32), (labels.shape[0], LANES))
    return jnp.concatenate([ones_where(wide == rank[b : b + 1, :]) for b in range(rank.shape[0])], axis=1)


def ranks_of(rank_ref, copy, half):
    return rank_ref[pl.ds(pl.multiple_of(16 * copy, 16), 16), :][: half // LANES]


def prep_theirs_kernel(
    unmasked, place_ref, masked_ref, tokens_ref, theirs_ref, rank_ref, half_ref, arrived
):
    tm = place_ref[0]
    half = tokens_ref.shape[1]
    load = pltpu.make_async_copy(tokens_ref.at[1 - tm], half_ref, arrived)
    load.start()
    rank_ref[...] = all_ranks(masked_ref, tm, half, unmasked)
    chosen = picks(ranks_of(rank_ref, 1 - tm, half), iota((unmasked + EXTRA, 1), 0))
    load.wait()
    theirs_ref[...] = dot(chosen, half_ref[...]).astype(BF)


def prep_shared_kernel(unmasked, rank_ref, tokens_ref, shared_ref):
    chosen = picks(ranks_of(rank_ref, 2, tokens_ref.shape[1]), iota((unmasked + EXTRA, 1), 0))
    shared_ref[...] = dot(chosen, tokens_ref[2]).astype(BF)


def prep_grads_kernel(unmasked, place_ref, rank_ref, cotangent_ref, keep_ref, send_ref):
    tm = place_ref[0]
    half = cotangent_ref.shape[1]
    rows = unmasked + EXTRA
    part = unmasked // 2
    labels = iota((rows, 1), 0)
    small = iota((part + EXTRA, 1), 0)
    theirs = jnp.where(small < part, small + part * (1 - tm), -1)
    own = jnp.where(small < part, small + part * tm, small + part)
    send_ref[:rows, :] = dot(picks(ranks_of(rank_ref, 1 - tm, half), labels), cotangent_ref[1 - tm]).astype(BF)
    chosen = picks(ranks_of(rank_ref, 2, half), jnp.concatenate([theirs, own], axis=0))
    both = dot(chosen, cotangent_ref[2]).astype(BF)
    send_ref[rows:, :] = both[: part + EXTRA]
    keep_ref[rows:, :] = both[part + EXTRA :]
    keep_ref[:rows, :] = dot(picks(ranks_of(rank_ref, tm, half), labels), cotangent_ref[tm]).astype(BF)


def normalise(values):
    centred = values - jnp.mean(values, axis=-1, keepdims=True)
    scale = lax.rsqrt(jnp.mean(centred * centred, axis=-1, keepdims=True) + EPSILON)
    return centred * scale, scale


def bias_terms(count):
    terms, rest = [], math.log(count)
    for _ in range(3):
        terms.append(float(np.asarray(rest).astype(jnp.bfloat16)))
        rest -= terms[-1]
    return terms


def attention_kernel(unmasked, count, split, place_ref, *refs):
    tm = place_ref[0]
    if split:
        own_ref, got_ref, small_ref, w_ref, x_ref, q_ref, k_ref, v_ref, e_ref, inverse_ref, att_ref, whole_ref = refs
        own = own_ref[...].astype(F32)
    else:
        rank_ref, tokens_ref, got_ref, small_ref, w_ref, x_ref, q_ref, k_ref, v_ref, e_ref, inverse_ref, att_ref = refs
        chosen = picks(ranks_of(rank_ref, tm, tokens_ref.shape[1]), iota((unmasked + EXTRA, 1), 0))
        own = dot(chosen, tokens_ref[tm])
    rows, width = got_ref.shape
    x = own + got_ref[...].astype(F32)
    x = jnp.where(iota((rows, width), 0) == unmasked, small_ref[0:1, :], x)
    hat, _ = normalise(x)
    normed = (hat * small_ref[1:2, :] + small_ref[2:3, :]).astype(BF)
    mixed = dot(normed, w_ref[...])
    query = ((mixed[:, :width] + small_ref[3:4, :]).astype(BF).astype(F32) * HEAD_DIM ** (-0.5)).astype(BF)
    key = mixed[:, width : 2 * width].astype(BF)
    value = (mixed[:, 2 * width :] + small_ref[4:5, :]).astype(BF)
    k_ref[...] = key
    v_ref[...] = value
    x = x.astype(BF)
    if split:
        part = unmasked // 2

        def take(values):
            chosen = jnp.where(tm == 0, values[:part].astype(F32), values[part:unmasked].astype(F32)).astype(BF)
            return jnp.concatenate([chosen, values[unmasked:]], axis=0)

        whole_ref[...] = x
        x, query = take(x), take(query)
    x_ref[...] = x
    q_ref[...] = query
    lane = iota((1, LANES), 1)
    first = lane < HEAD_DIM
    at = iota((rows, LANES), 0)
    place = iota((rows, LANES), 1) & (HEAD_DIM - 1)
    log_count = jnp.zeros((rows, LANES), F32)
    for which, term in enumerate(bias_terms(count)):
        log_count = jnp.where(place == which, term, log_count)
    bias = jnp.where(at < unmasked, 0.0, jnp.where(at == unmasked, log_count, jnp.where(place == 0, -1e30, 0.0)))
    bias = bias.astype(BF)
    ones = jnp.where((lane & (HEAD_DIM - 1)) < 3, 1.0, 0.0).astype(BF)
    all_ones = jnp.ones((rows, LANES), BF)
    for pair in range(width // LANES):
        cols = slice(pair * LANES, (pair + 1) * LANES)
        q_pair, k_pair, v_pair = query[:, cols], key[:, cols], value[:, cols]
        v_wide = jnp.concatenate([v_pair, all_ones], axis=1)
        parts = []
        for side in range(2):
            mine = first if side == 0 else jnp.logical_not(first)
            scores = dot_last(jnp.where(mine, q_pair, ones), jnp.where(mine, k_pair, bias))
            expo = jnp.exp(scores - jnp.max(scores, axis=1, keepdims=True)).astype(BF)
            e_ref[2 * pair + side] = expo
            parts.append(dot(expo, v_wide))
        inverse = 1.0 / jnp.where(first, parts[0][:, LANES:], parts[1][:, LANES:])
        inverse_ref[:, cols] = inverse
        att_ref[:, cols] = (jnp.where(first, parts[0][:, :LANES], parts[1][:, :LANES]) * inverse).astype(BF)


def gelu_terms(hidden):
    size = jnp.abs(hidden) * (0.5**0.5)
    t = 1.0 / (1.0 + 0.3275911 * size)
    bell = jnp.exp(hidden * hidden * -0.5)
    tail = t * (0.254829592 + t * (-0.284496736 + t * (1.421413741 + t * (-1.453152027 + t * 1.061405429))))
    tail = 0.5 * tail * bell
    below = jnp.where(hidden >= 0.0, 1.0 - tail, tail)
    return hidden * below, below + hidden * bell * (1.0 / math.sqrt(2.0 * math.pi))


def stacked(refs):
    return jnp.concatenate([ref[...] for ref in refs], axis=0)


def scatter_chunks(me, stage_ref, keep_ref, send_refs):
    depth = keep_ref.shape[2]
    for rel in range(2 * 4 * keep_ref.shape[1]):
        first = pl.multiple_of((me ^ rel) * depth, 16)
        near, far = (rel >> 1) & 3, rel >> 3
        chunk = stage_ref[pl.ds(first, depth), :]
        if rel & 1 == 0:
            keep_ref[near, far] = chunk
        else:
            each = send_refs[0].shape[0]
            send_refs[near // each][near % each, far] = chunk


def stage_weight(stage_ref, first, grad, apart=None):
    depth = grad.shape[0]
    apart = apart or depth
    for block in range(grad.shape[1] // LANES):
        at = first + block * apart
        stage_ref[at : at + depth, :] = grad[:, block * LANES : (block + 1) * LANES].astype(BF)
    return first + apart * (grad.shape[1] // LANES)


def stage_rows(stage_ref, first, vectors):
    pieces = [v[:, b * LANES : (b + 1) * LANES] for v in vectors for b in range(v.shape[1] // LANES)]
    missing = -len(pieces) % 16
    if missing:
        pieces.append(jnp.zeros((missing, LANES), F32))
    block = jnp.concatenate(pieces, axis=0).astype(BF)
    stage_ref[first : first + block.shape[0], :] = block
    return first + block.shape[0]


def clear_rest(stage_ref, first):
    if first < stage_ref.shape[0]:
        stage_ref[first:, :] = jnp.zeros((stage_ref.shape[0] - first, LANES), BF)


def forward_kernel(
    att_a, att_b, x_a, x_b, small_ref, bias_up_ref, w_proj_ref, w_up_ref, w_down_ref,
    out_ref, middle_ref, normed_ref, active_ref, slope_ref
):
    attended = stacked((att_a, att_b))
    x = stacked((x_a, x_b)).astype(F32)
    middle = x + dot(attended, w_proj_ref[...]) + small_ref[5:6, :]
    middle_ref[...] = middle
    hat, _ = normalise(middle)
    normed = (hat * small_ref[6:7, :] + small_ref[7:8, :]).astype(BF)
    normed_ref[...] = normed
    result = middle + small_ref[8:9, :]
    step = 512
    for first in range(0, w_up_ref.shape[1], step):
        cols = slice(first, first + step)
        active, slope = gelu_terms(dot(normed, w_up_ref[:, cols]) + bias_up_ref[:, cols])
        active = active.astype(BF)
        active_ref[:, cols] = active
        slope_ref[:, cols] = slope.astype(BF)
        result = result + dot(active, w_down_ref[cols, :])
    out_ref[...] = result.astype(BF)


def norm_back(grad, hat, scale, gain):
    inner = grad * gain
    mean = jnp.mean(inner, axis=-1, keepdims=True)
    along = jnp.mean(inner * hat, axis=-1, keepdims=True)
    return scale * (inner - mean - hat * along)


def backward_kernel(
    place_ref, groups_ref, everyone_ref, cot_own, cot_got, middle_ref, normed_ref, active_ref, slope_ref, att_a, att_b,
    small_ref, w_proj_ref, w_up_ref, w_down_ref,
    grad_middle_ref, grad_att_ref, keep_ref, *send_refs
):
    *send_refs, stage_ref = send_refs
    rows_a, total = att_a.shape[0], cot_own.shape[0]
    everyone = everyone_ref[...]

    def weight_of(group):
        return 1.0 / jnp.sum(jnp.where(everyone == group, 1.0, 0.0), axis=1, keepdims=True)

    weight = jnp.where(
        iota((total, 1), 0) < rows_a, weight_of(groups_ref[place_ref[0]]), weight_of(groups_ref[2])
    )
    upstream = (cot_own[...].astype(F32) + cot_got[...].astype(F32)) * weight
    grad_result = upstream.astype(BF)
    normed = normed_ref[...]
    hidden, step = active_ref.shape[1], 512
    grad_normed = None
    sums = []
    parts = []
    for first in range(0, hidden, step):
        cols = slice(first, first + step)
        grad_hidden = (dot_last(grad_result, w_down_ref[cols, :]) * slope_ref[:, cols].astype(F32)).astype(BF)
        stage_weight(stage_ref, first, dot_rows(active_ref[:, cols], grad_result), hidden)
        part = dot_last(grad_hidden, w_up_ref[:, cols])
        grad_normed = part if grad_normed is None else grad_normed + part
        sums.append(column_sums(grad_hidden.astype(F32)))
        parts.append(dot_rows(normed, grad_hidden))
    end = hidden * (grad_result.shape[1] // LANES)
    for part in parts:
        end = stage_weight(stage_ref, end, part)
    hat, scale = normalise(middle_ref[...])
    grad_middle = upstream + norm_back(grad_normed, hat, scale, small_ref[6:7, :])
    grad_middle_ref[...] = grad_middle
    grad_branch = grad_middle.astype(BF)
    grad_att_ref[...] = dot_last(grad_branch, w_proj_ref[...]).astype(BF)
    end = stage_weight(stage_ref, end, dot_rows(stacked((att_a, att_b)), grad_branch))
    vectors = sums + [
        column_sums(grad_normed * hat),
        column_sums(grad_normed),
        column_sums(grad_branch.astype(F32)),
        column_sums(grad_result.astype(F32)),
    ]
    end = stage_rows(stage_ref, end, vectors)
    clear_rest(stage_ref, end)
    scatter_chunks(place_ref[1], stage_ref, keep_ref, send_refs)


def attention_back_kernel(row_from, g_ref, att_ref, q_ref, k_ref, v_ref, e_ref, inverse_ref, dq_ref, dk_ref, dv_ref):
    rows, width = q_ref.shape
    first = iota((1, LANES), 1) < HEAD_DIM
    for pair in range(width // LANES):
        cols = slice(pair * LANES, (pair + 1) * LANES)
        q_pair, k_pair, v_pair = q_ref[:, cols], k_ref[:, cols], v_ref[:, cols]
        g_pair = (g_ref[row_from : row_from + rows, cols].astype(F32) * inverse_ref[:, cols]).astype(BF)
        agree = g_pair.astype(F32) * att_ref[:, cols].astype(F32)
        dq, dk, dv = [], [], []
        for side in range(2):
            mine = first if side == 0 else jnp.logical_not(first)
            correction = jnp.sum(jnp.where(mine, agree, 0.0), axis=1, keepdims=True)
            expo = e_ref[2 * pair + side]
            grad_probs = dot_last(jnp.where(mine, g_pair, jnp.zeros_like(g_pair)), v_pair)
            grad_scores = expo * (grad_probs - correction).astype(BF)
            dq.append(dot(grad_scores, k_pair))
            dk.append(dot_rows(grad_scores, q_pair))
            dv.append(dot_rows(expo, g_pair))
        dq_ref[:, cols] = (jnp.where(first, dq[0], dq[1]) * HEAD_DIM ** (-0.5)).astype(BF)
        dk_ref[:, cols] = jnp.where(first, dk[0], dk[1]).astype(BF)
        dv_ref[:, cols] = jnp.where(first, dv[0], dv[1]).astype(BF)


def inputs_back_kernel(
    unmasked, place_ref, x_a, x_b, dq_a, dq_b, dk_a, dk_b, dv_a, dv_b, grad_middle_ref, small_ref, w_ref,
    grad_ref, keep_ref, *send_refs
):
    *send_refs, stage_ref = send_refs
    rows, width = x_a.shape
    part = unmasked // 2
    tm = place_ref[0]

    def spread(block):
        wide = block.astype(F32)
        left = jnp.where(tm == 0, wide[:part], 0.0)
        right = jnp.where(tm == 0, 0.0, wide[:part])
        return jnp.concatenate([left, right, wide[part:]], axis=0)

    x = stacked((x_a, x_b)).astype(F32)
    hat, scale = normalise(x)
    gain = small_ref[1:2, :]
    normed = (hat * gain + small_ref[2:3, :]).astype(BF)
    dq = jnp.concatenate([dq_a[...], spread(dq_b[...]).astype(BF)], axis=0)
    mixed = jnp.concatenate([dq, stacked((dk_a, dk_b)), stacked((dv_a, dv_b))], axis=1)
    end = stage_weight(stage_ref, 0, dot_rows(normed, mixed))
    grad_normed = dot_last(mixed, w_ref[...])
    grad = norm_back(grad_normed, hat, scale, gain)
    grad = grad + jnp.concatenate([grad_middle_ref[:rows], spread(grad_middle_ref[rows:])], axis=0)
    grad_ref[:unmasked] = grad[:unmasked].astype(BF)
    grad_ref[unmasked:] = grad[rows : rows + unmasked].astype(BF)
    vectors = (
        column_sums(mixed[:, :width].astype(F32)),
        column_sums(mixed[:, 2 * width :].astype(F32)),
        column_sums(grad_normed * hat),
        column_sums(grad_normed),
        grad[unmasked : unmasked + 1] + grad[rows + unmasked : rows + unmasked + 1],
    )
    end = stage_rows(stage_ref, end, vectors)
    clear_rest(stage_ref, end)
    scatter_chunks(place_ref[1], stage_ref, keep_ref, send_refs)


def place_back(rank_ref, copy, rows, half):
    down = jnp.transpose(ranks_of(rank_ref, copy, 16 * LANES))
    labels = jnp.broadcast_to(iota((1, rows), 1).astype(F32), (LANES, rows))
    return jnp.concatenate([ones_where(labels == down[:, b : b + 1]) for b in range(half // LANES)], axis=0)


def outputs_kernel(unmasked, place_ref, rank_ref, own_ref, got_ref, out_ref):
    tm = place_ref[0]
    half = out_ref.shape[1]
    rows = unmasked + EXTRA
    part = unmasked // 2
    out_ref[tm] = dot(place_back(rank_ref, tm, rows, half), own_ref[:rows]).astype(BF)
    out_ref[1 - tm] = dot(place_back(rank_ref, 1 - tm, rows, half), got_ref[:rows]).astype(BF)
    own = own_ref[rows:].astype(F32)
    got = got_ref[rows:].astype(F32)
    left = jnp.where(tm == 0, own[:part], got[:part])
    right = jnp.where(tm == 0, got[:part], own[:part])
    whole = jnp.concatenate([left, right, own[part:]], axis=0).astype(BF)
    out_ref[2] = dot(place_back(rank_ref, 2, rows, half), whole).astype(BF)


def grads_out_kernel(unmasked, place_ref, rank_ref, own_ref, got_ref, out_ref):
    tm = place_ref[0]
    half = out_ref.shape[1]
    out_ref[tm] = dot(place_back(rank_ref, tm, unmasked, half), own_ref[:unmasked]).astype(BF)
    out_ref[1 - tm] = dot(place_back(rank_ref, 1 - tm, unmasked, half), got_ref[:unmasked]).astype(BF)
    whole = (own_ref[unmasked:].astype(F32) + got_ref[unmasked:].astype(F32)).astype(BF)
    out_ref[2] = dot(place_back(rank_ref, 2, unmasked, half), whole).astype(BF)


def fold_kernel(keep_ref, *refs):
    got_refs, out_refs = refs[:-4], refs[-4:]
    each = got_refs[0].shape[0]
    for step, out_ref in enumerate(out_refs):
        got = got_refs[step // each][step % each]
        out_ref[...] = (keep_ref[step].astype(F32) + got.astype(F32)).astype(BF)


def fold_four_kernel(units, *refs):
    outs = refs[4 * units :]
    first = 0
    for unit in range(units):
        total = refs[4 * unit][...].astype(F32)
        for ref in refs[4 * unit + 1 : 4 * unit + 4]:
            total = total + ref[...].astype(F32)
        total = total.astype(BF)
        rows = slice(first, first + total.shape[1])
        first += total.shape[1]
        if len(outs) == 1:
            outs[0][:, rows] = total
        else:
            for step, out_ref in enumerate(outs):
                for slot in range(out_ref.shape[0]):
                    out_ref[slot, rows] = total[4 * slot + step]


def clip_swap(values, distance):
    size = lax.axis_size("clip")
    return lax.ppermute(values, "clip", [(i, i ^ distance) for i in range(size)])


def near_swap(values, step):
    size = lax.axis_size("clip")
    pairs = [
        (t * size + i, (t ^ (step & 1)) * size + (i ^ ((step >> 1) << 1))) for t in range(2) for i in range(size)
    ]
    return lax.ppermute(values, ("tm", "clip"), pairs)


def sum_cores(keep, send, after):
    _, groups, depth, _ = keep.shape
    got, after = lax.optimization_barrier(([clip_swap(part, 1) for part in send], after))
    return plain(fold_kernel, [shape(groups, depth, LANES)] * 4)(keep, *got)


def spread_near(pieces):
    return [pieces[0]] + [near_swap(pieces[step], step) for step in (1, 2, 3)]


def sum_over_devices(first_pieces, second_pieces, send_far, beside_last):
    far = []
    distance = 4
    while distance < lax.axis_size("clip"):
        far.append(distance)
        distance *= 4
    pieces = [*first_pieces, *second_pieces]
    groups = pieces[0].shape[0]
    depth = pieces[0].shape[1] + pieces[4].shape[1]
    left = groups
    sent = None
    for distance in far:
        left //= 4
        fold = functools.partial(fold_four_kernel, len(pieces) // 4)
        pieces = plain(fold, [shape(left, depth, LANES)] * 4)(*pieces)
        if sent is None:
            sent, pieces = send_far(pieces)
        pieces = [pieces[0]] + [clip_swap(pieces[step], step * distance) for step in (1, 2, 3)]
    total = plain(functools.partial(fold_four_kernel, 1), shape(left, depth, LANES))(*pieces)
    for distance in reversed(far):
        pieces = [total] + [clip_swap(total, step * distance) for step in (1, 2, 3)]
        total = jnp.stack(pieces, axis=1).reshape(-1, depth, LANES)
    total, sent = lax.optimization_barrier((total, sent))
    pieces = spread_near([total] * 4)
    last = beside_last(sent)
    *pieces, last = lax.optimization_barrier((*pieces, last))
    return pieces, [clip_swap(piece, 1) for piece in pieces], last


def gather_chunks(me, refs, stage_ref, start, depth):
    for rel in range(8 * refs[0].shape[0]):
        first = pl.multiple_of((me ^ rel) * depth, 16)
        source = refs[4 * (rel & 1) + ((rel >> 1) & 3)]
        stage_ref[pl.ds(first, depth), :] = source[rel >> 3, start : start + depth]


def unstage_kernel(units, place_ref, *refs):
    weights = sum(count for _, count, _ in units)
    vectors = sum(count for _, _, count in units)
    pieces, outs, vector_outs = refs[:8], refs[8 : 8 + weights], refs[8 + weights : 8 + weights + vectors]
    stage_ref, done, *wide_refs = refs[8 + weights + vectors :]
    stores = []
    start = at = vector_at = 0
    for depth, weights, vectors in units:
        gather_chunks(place_ref[1], pieces, stage_ref, start, depth)
        first = 0
        for each in range(at, at + weights):
            first = widen(stage_ref, first, wide_refs[each], outs[each], done, stores)
        widen_vectors(stage_ref, first, vector_outs[vector_at : vector_at + vectors])
        start, at, vector_at = start + depth, at + weights, vector_at + vectors
    for store in stores:
        store.wait()


def widen(stage_ref, first, wide_ref, out_ref, done, stores):
    depth, width = out_ref.shape
    for block in range(width // LANES):
        columns = slice(block * LANES, (block + 1) * LANES)
        wide_ref[:, columns] = stage_ref[first : first + depth, :].astype(F32)
        stores.append(pltpu.make_async_copy(wide_ref.at[:, columns], out_ref.at[:, columns], done.at[len(stores)]))
        stores[-1].start()
        first += depth
    return first


def widen_vectors(stage_ref, first, outs):
    count = sum(ref.shape[0] // LANES for ref in outs)
    rows = stage_ref[first : first + count + -count % 16, :].astype(F32)
    at = 0
    for out_ref in outs:
        blocks = out_ref.shape[0] // LANES
        for block in range(blocks):
            out_ref[block * LANES : (block + 1) * LANES] = rows[at + block]
        at += blocks


def chunk_rows(count, devices):
    return -(-count // (devices * 16)) * 16


def body(
    tokens,
    masked,
    groups,
    cotangent,
    mask_token,
    gain_one,
    shift_one,
    w_qkv,
    q_bias,
    v_bias,
    w_proj,
    b_proj,
    gain_two,
    shift_two,
    w_up,
    b_up,
    w_down,
    b_down,
):
    copies, half, width = tokens.shape
    hidden = w_up.shape[1]
    hide = masked.shape[1]
    unmasked = 2 * half - hide
    rows = unmasked + EXTRA
    some = unmasked // 2 + EXTRA
    total = rows + some
    tm, clip = lax.axis_index("tm"), lax.axis_index("clip")
    clips = lax.axis_size("clip")
    devices = 2 * clips
    me = (clip & 1) | (tm << 1) | ((clip >> 1) << 2)
    place = jnp.stack([tm, me]).astype(jnp.int32)
    swap = functools.partial(lax.ppermute, axis_name="tm", perm=[(0, 1), (1, 0)])

    def run(kernel, args, outs, scratch=(), scalars=1, limit=20, flops=0, in_hbm=(), out_hbm=(), hides=True):
        moved = sum(math.prod(a.shape) * a.dtype.itemsize for a in list(args) + jax.tree.leaves(outs))
        return pl.pallas_call(
            kernel,
            out_shape=outs,
            in_specs=[
                SMEM if at < scalars else HBM if at in in_hbm else VMEM
                for at in range(len(args))
            ],
            out_specs=[HBM if at in out_hbm else VMEM for at in range(len(outs))] if isinstance(outs, list) else VMEM,
            scratch_shapes=list(scratch),
            compiler_params=pltpu.CompilerParams(vmem_limit_bytes=limit << 20),
            cost_estimate=pl.CostEstimate(
                flops=flops if hides else 1, bytes_accessed=moved if hides else 1, transcendentals=0
            ),
        )(*args)

    counts = (2 * width // LANES * hidden + width // LANES * width + 32, 3 * width // LANES * width + 16)
    depths = [chunk_rows(count, devices) for count in counts]

    def chunked(unit, parts):
        halves = [shape(near, devices // 8, depths[unit], LANES) for near in [4] + [4 // parts] * parts]
        return halves, [pltpu.VMEM((devices * depths[unit], LANES), BF)]

    small = jnp.stack(
        [mask_token, gain_one, shift_one, q_bias, v_bias, b_proj, gain_two, shift_two, b_down]
    ).astype(F32)
    bias_up = b_up.astype(F32).reshape(1, hidden)

    block = shape(rows, width)
    everyone = jnp.concatenate([groups, clip_swap(groups, 1)])
    theirs, rank = run(
        functools.partial(prep_theirs_kernel, unmasked),
        (place, masked, pltpu.with_memory_space_constraint(tokens, pltpu.HBM)),
        [block, shape(16 * copies, LANES, kind=F32)],
        [pltpu.VMEM((half, width), BF), pltpu.SemaphoreType.DMA],
        flops=2 * rows * half * width,
        in_hbm=(2,),
    )
    got_mine = swap(theirs)
    everyone, theirs, rank = lax.optimization_barrier((everyone, theirs, rank))
    everyone = jnp.concatenate([everyone, clip_swap(everyone, 2)])
    shared = run(
        functools.partial(prep_shared_kernel, unmasked),
        (rank, tokens),
        block,
        scalars=0,
        flops=2 * rows * half * width,
    )
    got_shared = swap(shared)
    everyone, shared, rank = lax.optimization_barrier((everyone, shared, rank))
    everyone = jnp.concatenate([everyone, clip_swap(everyone, 4)])
    cot_own, cot_send = run(
        functools.partial(prep_grads_kernel, unmasked),
        (place, rank, cotangent),
        [shape(total, width), shape(total, width)],
        flops=2 * copies * rows * half * width,
    )
    everyone, cot_own, cot_send = lax.optimization_barrier((everyone, cot_own, cot_send))
    cot_got = swap(cot_send)

    def attend(sources, got, split):
        queries = some if split else rows
        outs = [
            shape(queries, width), shape(queries, width), block, block,
            shape(HEADS, queries, rows), shape(queries, width, kind=F32), shape(queries, width),
        ]
        if split:
            outs.append(block)
        return run(
            functools.partial(attention_kernel, unmasked, hide, split),
            (place, *sources, got, small, w_qkv),
            outs,
            flops=6 * rows * width * width + 4 * queries * rows * width,
        )

    x_a, q_a, k_a, v_a, e_a, inverse_a, att_a = attend((rank, tokens), got_mine, False)
    everyone, att_a = lax.optimization_barrier((everyone, att_a))
    distance = 8
    while distance < clips:
        everyone = jnp.concatenate([everyone, clip_swap(everyone, distance)])
        distance *= 2
    x_b, q_b, k_b, v_b, e_b, inverse_b, att_b, x_whole = attend((shared,), got_shared, True)

    out_rows, middle, normed_two, active, slope = run(
        forward_kernel,
        (att_a, att_b, x_a, x_b, small, bias_up, w_proj, w_up, w_down),
        [
            shape(total, width), shape(total, width, kind=F32), shape(total, width), shape(total, hidden),
            shape(total, hidden),
        ],
        scalars=0,
        flops=2 * total * width * (width + 2 * hidden),
    )
    out_got = swap(out_rows)
    halves, stage = chunked(0, 4)
    grad_middle, grad_att, keep, *send = run(
        backward_kernel,
        (
            place, groups, everyone.reshape(1, -1), cot_own, cot_got, middle, normed_two, active, slope, att_a, att_b,
            small, w_proj, w_up, w_down,
        ),
        [shape(total, width, kind=F32), shape(total, width)] + halves,
        stage,
        scalars=2,
        hides=False,
    )

    def attend_back(row_from, grads, att, q, k, v, e, inverse):
        return run(
            functools.partial(attention_back_kernel, row_from),
            (grads, att, q, k, v, e, inverse),
            [shape(q.shape[0], width), block, block],
            scalars=0,
            hides=False,
        )

    dq_b, dk_b, dv_b = attend_back(rows, grad_att, att_b, q_b, k_b, v_b, e_b, inverse_b)
    pieces, grad_att = lax.optimization_barrier((sum_cores(keep, send, dq_b), grad_att))
    first_pieces = spread_near(pieces)
    dq_a, dk_a, dv_a = attend_back(0, grad_att, att_a, q_a, k_a, v_a, e_a, inverse_a)
    dq_a, out_got = lax.optimization_barrier((dq_a, out_got))
    halves, stage = chunked(1, 2)
    grad_rows, keep, *send = run(
        functools.partial(inputs_back_kernel, unmasked),
        (place, x_a, x_whole, dq_a, dq_b, dk_a, dk_b, dv_a, dv_b, grad_middle, small, w_qkv),
        [shape(2 * unmasked, width)] + halves,
        stage,
        hides=False,
    )
    pieces, first_pieces = lax.optimization_barrier((sum_cores(keep, send, ()), first_pieces))
    second_pieces = spread_near(pieces)

    def send_rows(pieces):
        *pieces, grads = lax.optimization_barrier((*pieces, grad_rows))
        return swap(grads), pieces

    def place_rows(got):
        return (
            run(functools.partial(outputs_kernel, unmasked), (place, rank, out_rows, out_got), shape(*tokens.shape)),
            run(functools.partial(grads_out_kernel, unmasked), (place, rank, grad_rows, got), shape(*tokens.shape)),
        )

    own, got, (block_out, grad_tokens) = sum_over_devices(first_pieces, second_pieces, send_rows, place_rows)
    weights = [(hidden, width), (width, hidden), (width, width), (width, 3 * width)]
    vectors = [hidden] + [width] * 9
    (
        grad_w_down, grad_w_up, grad_w_proj, grad_w_qkv,
        grad_b_up, grad_gain_two, grad_shift_two, grad_b_proj, grad_b_down,
        grad_q_bias, grad_v_bias, grad_gain_one, grad_shift_one, grad_mask_token,
    ) = run(
        functools.partial(unstage_kernel, tuple(zip(depths, (3, 1), (5, 5)))),
        (place, *own, *got),
        [shape(*dims, kind=F32) for dims in weights] + [shape(dim, kind=F32) for dim in vectors],
        [pltpu.VMEM((devices * max(depths), LANES), BF), pltpu.SemaphoreType.DMA((sum(dims[1] for dims in weights) // LANES,))]
        + [pltpu.VMEM(dims, F32) for dims in weights],
        out_hbm=(0, 1, 2, 3),
    )
    return (
        block_out,
        grad_tokens,
        grad_mask_token,
        grad_gain_one,
        grad_shift_one,
        grad_w_qkv,
        grad_q_bias,
        grad_v_bias,
        grad_w_proj,
        grad_b_proj,
        grad_gain_two,
        grad_shift_two,
        grad_w_up,
        grad_b_up,
        grad_w_down,
        grad_b_down,
    )


def solution(mesh):
    return jax.shard_map(
        body,
        mesh=mesh,
        in_specs=(P("clip", "tm", None), P("clip", None), P("clip"), P("clip", "tm", None)) + (P(),) * 14,
        out_specs=(P("clip", "tm", None), P("clip", "tm", None)) + (P(),) * 14,
        check_vma=False,
    )
```

```python
import functools
import math

import jax
import jax.numpy as jnp
import numpy as np
from jax import lax
from jax.experimental import pallas as pl
from jax.experimental.pallas import tpu as pltpu
from jax.sharding import PartitionSpec as P

HEADS = 6
HEAD_DIM = 64
LANES = 128
EXTRA = 16
EPSILON = 1e-06

BF = jnp.bfloat16
F32 = jnp.float32
VMEM = pl.BlockSpec(memory_space=pltpu.VMEM)
SMEM = pl.BlockSpec(memory_space=pltpu.SMEM)
HBM = pl.BlockSpec(memory_space=pltpu.HBM)


def dot(left, right):
    return jnp.dot(left, right, preferred_element_type=F32)


def dot_last(left, right):
    return lax.dot_general(left, right, (((1,), (1,)), ((), ())), preferred_element_type=F32)


def dot_rows(left, right):
    return lax.dot_general(left, right, (((0,), (0,)), ((), ())), preferred_element_type=F32)


def iota(shape, axis):
    return lax.broadcasted_iota(jnp.int32, shape, axis)


def ones_where(condition):
    return jnp.where(condition, 1.0, 0.0).astype(BF)


def column_sums(values):
    return jnp.sum(values, axis=0, keepdims=True)


def shape(*dims, kind=BF):
    return jax.ShapeDtypeStruct(dims, kind)


def plain(kernel, outs):
    return pl.pallas_call(kernel, out_shape=outs, compiler_params=pltpu.CompilerParams(vmem_limit_bytes=8 << 20))


def all_ranks(masked_ref, tm, half, unmasked):
    copies, hide = masked_ref.shape
    blocks = half // LANES
    marks = []
    for copy in range(copies):
        row = masked_ref[copy : copy + 1, :]
        low = ones_where(iota((LANES, hide), 0) == (row & (LANES - 1)))
        high = ones_where(iota((16, hide), 0) == (row >> 7))
        marks.append(dot_last(high, low))
    marks = jnp.concatenate(marks, axis=0)
    count = 16 * copies
    block = iota((count, LANES), 0)
    free = jnp.where((block & 15) < 2 * blocks, 1.0 - marks, 0.0).astype(BF)
    before = ones_where(iota((LANES, LANES), 0) < iota((LANES, LANES), 1))
    within = dot(free, before)
    totals = dot(free, jnp.ones((LANES, LANES), BF)).astype(BF)
    row, column = iota((count, count), 0), iota((count, count), 1)
    earlier = ones_where(jnp.logical_and(column < row, (column >> 4) == (row >> 4)))
    rank = within + dot(earlier, totals)
    rank = jnp.where(marks > 0.5, float(unmasked), rank)
    across = []
    for first in range(0, count, 16):
        mine = jnp.where(tm == 0, rank[first : first + blocks], rank[first + blocks : first + 2 * blocks])
        across.append(jnp.concatenate([mine, jnp.zeros((16 - blocks, LANES), F32)], axis=0))
    return jnp.concatenate(across, axis=0)


def picks(rank, labels):
    wide = jnp.broadcast_to(labels.astype(F32), (labels.shape[0], LANES))
    return jnp.concatenate([ones_where(wide == rank[b : b + 1, :]) for b in range(rank.shape[0])], axis=1)


def ranks_of(rank_ref, copy, half):
    return rank_ref[pl.ds(pl.multiple_of(16 * copy, 16), 16), :][: half // LANES]


def prep_theirs_kernel(
    unmasked, place_ref, masked_ref, tokens_ref, theirs_ref, rank_ref, marks_ref, half_ref, arrived
):
    tm = place_ref[0]
    half = tokens_ref.shape[1]
    load_marks = pltpu.make_async_copy(masked_ref, marks_ref, arrived.at[0])
    load_marks.start()
    load = pltpu.make_async_copy(tokens_ref.at[1 - tm], half_ref, arrived.at[1])
    load.start()
    load_marks.wait()
    rank_ref[...] = all_ranks(marks_ref, tm, half, unmasked)
    chosen = picks(ranks_of(rank_ref, 1 - tm, half), iota((unmasked, 1), 0))
    load.wait()
    theirs_ref[...] = dot(chosen, half_ref[...]).astype(BF)


def prep_shared_kernel(unmasked, rank_ref, tokens_ref, shared_ref):
    chosen = picks(ranks_of(rank_ref, 2, tokens_ref.shape[1]), iota((unmasked, 1), 0))
    shared_ref[...] = dot(chosen, tokens_ref[2]).astype(BF)


def prep_grads_kernel(unmasked, place_ref, rank_ref, cotangent_ref, keep_ref, send_ref):
    tm = place_ref[0]
    half = cotangent_ref.shape[1]
    rows = unmasked + EXTRA
    part = unmasked // 2
    labels = iota((rows, 1), 0)
    small = iota((part + EXTRA, 1), 0)
    theirs = iota((part, 1), 0) + part * (1 - tm)
    own = jnp.where(small < part, small + part * tm, small + part)
    send_ref[:rows, :] = dot(picks(ranks_of(rank_ref, 1 - tm, half), labels), cotangent_ref[1 - tm]).astype(BF)
    chosen = picks(ranks_of(rank_ref, 2, half), jnp.concatenate([theirs, own], axis=0))
    both = dot(chosen, cotangent_ref[2]).astype(BF)
    send_ref[rows:, :] = both[:part]
    keep_ref[rows:, :] = both[part:]
    keep_ref[:rows, :] = dot(picks(ranks_of(rank_ref, tm, half), labels), cotangent_ref[tm]).astype(BF)


def normalise(values):
    centred = values - jnp.mean(values, axis=-1, keepdims=True)
    scale = lax.rsqrt(jnp.mean(centred * centred, axis=-1, keepdims=True) + EPSILON)
    return centred * scale, scale


def bias_terms(count):
    terms, rest = [], math.log(count)
    for _ in range(3):
        terms.append(float(np.asarray(rest).astype(jnp.bfloat16)))
        rest -= terms[-1]
    return terms


def attention_kernel(unmasked, count, split, place_ref, *refs):
    tm = place_ref[0]
    if split:
        own_ref, got_ref, small_ref, w_ref, x_ref, q_ref, k_ref, v_ref, e_ref, inverse_ref, att_ref, whole_ref = refs
        own = own_ref[...].astype(F32)
    else:
        rank_ref, tokens_ref, got_ref, small_ref, w_ref, x_ref, q_ref, k_ref, v_ref, e_ref, inverse_ref, att_ref = refs
        chosen = picks(ranks_of(rank_ref, tm, tokens_ref.shape[1]), iota((unmasked, 1), 0))
        own = dot(chosen, tokens_ref[tm])
    rows, width = k_ref.shape
    extra = jnp.where(iota((EXTRA, width), 0) == 0, small_ref[0:1, :], 0.0)
    x = jnp.concatenate([own + got_ref[...].astype(F32), extra], axis=0)
    hat, _ = normalise(x)
    normed = (hat * small_ref[1:2, :] + small_ref[2:3, :]).astype(BF)
    mixed = dot(normed, w_ref[...])
    query = ((mixed[:, :width] + small_ref[3:4, :]).astype(BF).astype(F32) * HEAD_DIM ** (-0.5)).astype(BF)
    key = mixed[:, width : 2 * width].astype(BF)
    value = (mixed[:, 2 * width :] + small_ref[4:5, :]).astype(BF)
    k_ref[...] = key
    v_ref[...] = value
    x = x.astype(BF)
    if split:
        part = unmasked // 2

        def take(values):
            chosen = jnp.where(tm == 0, values[:part].astype(F32), values[part:unmasked].astype(F32)).astype(BF)
            return jnp.concatenate([chosen, values[unmasked:]], axis=0)

        whole_ref[...] = x
        x, query = take(x), take(query)
    x_ref[...] = x
    q_ref[...] = query
    lane = iota((1, LANES), 1)
    first = lane < HEAD_DIM
    at = iota((rows, LANES), 0)
    place = iota((rows, LANES), 1) & (HEAD_DIM - 1)
    log_count = jnp.zeros((rows, LANES), F32)
    for which, term in enumerate(bias_terms(count)):
        log_count = jnp.where(place == which, term, log_count)
    bias = jnp.where(at < unmasked, 0.0, jnp.where(at == unmasked, log_count, jnp.where(place == 0, -1e30, 0.0)))
    bias = bias.astype(BF)
    ones = jnp.where((lane & (HEAD_DIM - 1)) < 3, 1.0, 0.0).astype(BF)
    all_ones = jnp.ones((rows, LANES), BF)
    for pair in range(width // LANES):
        cols = slice(pair * LANES, (pair + 1) * LANES)
        q_pair, k_pair, v_pair = query[:, cols], key[:, cols], value[:, cols]
        v_wide = jnp.concatenate([v_pair, all_ones], axis=1)
        parts = []
        for side in range(2):
            mine = first if side == 0 else jnp.logical_not(first)
            scores = dot_last(jnp.where(mine, q_pair, ones), jnp.where(mine, k_pair, bias))
            expo = jnp.exp(scores - jnp.max(scores, axis=1, keepdims=True)).astype(BF)
            e_ref[2 * pair + side] = expo
            parts.append(dot(expo, v_wide))
        inverse = 1.0 / jnp.where(first, parts[0][:, LANES:], parts[1][:, LANES:])
        inverse_ref[:, cols] = inverse
        att_ref[:, cols] = (jnp.where(first, parts[0][:, :LANES], parts[1][:, :LANES]) * inverse).astype(BF)


def gelu_terms(hidden):
    below = 0.5 * lax.erf(hidden * 0.5**0.5) + 0.5
    bell = jnp.exp2(hidden * hidden * (-0.5 * math.log2(math.e)))
    return hidden * below, below + hidden * bell * (1.0 / math.sqrt(2.0 * math.pi))


def stacked(refs):
    return jnp.concatenate([ref[...] for ref in refs], axis=0)


def eighth_at(place_ref, near, side):
    me = place_ref[1]
    return ((near ^ ((me >> 1) & 3)) << 1) | (side ^ (me & 1))


def chunk_rows_at(place_ref, far, depth):
    return pl.ds(pl.multiple_of((far ^ (place_ref[1] >> 3)) * depth, 16), depth)


def scatter_chunks(place_ref, stage_ref, keep_ref, send_refs):
    near_places, far_places, depth, _ = keep_ref.shape
    each = send_refs[0].shape[0]
    for near in range(near_places):
        for side in range(2):
            eighth = eighth_at(place_ref, near, side)
            for far in range(far_places):
                chunk = stage_ref[eighth, chunk_rows_at(place_ref, far, depth), :]
                if side:
                    send_refs[near // each][near % each, far] = chunk
                else:
                    keep_ref[near, far] = chunk


def stage_rows(stage_ref, base, grad, total, first=0):
    slab = total // 8
    step = math.gcd(slab, grad.shape[0])
    grad = grad.astype(BF)
    for row in range(0, grad.shape[0], step):
        eighth, offset = divmod(first + row, slab)
        for block in range(grad.shape[1] // LANES):
            at = base + block * slab + offset
            stage_ref[eighth, at : at + step, :] = grad[row : row + step, block * LANES : (block + 1) * LANES]


def stage_columns(stage_ref, base, grad, total, first):
    slab = grad.shape[0] // 2
    grad = grad.astype(BF)
    for block in range(grad.shape[1] // LANES):
        quarter, offset = divmod(first // LANES + block, total // 4 // LANES)
        at = base + offset * slab
        for half in range(2):
            stage_ref[2 * quarter + half, at : at + slab, :] = grad[
                half * slab : (half + 1) * slab, block * LANES : (block + 1) * LANES
            ]


def stage_vectors(stage_ref, base, vectors):
    pieces = [v[:, b * LANES : (b + 1) * LANES] for v in vectors for b in range(v.shape[1] // LANES)]
    each = -(-len(pieces) // 8)
    for eighth in range(8):
        rows = pieces[eighth * each : (eighth + 1) * each]
        rows = rows + [jnp.zeros((16 - len(rows), LANES), F32)]
        stage_ref[eighth, base : base + 16, :] = jnp.concatenate(rows, axis=0).astype(BF)
        rest = stage_ref.shape[1] - base - 16
        if rest:
            stage_ref[eighth, base + 16 :, :] = jnp.zeros((rest, LANES), BF)


def forward_kernel(
    att_a, att_b, x_a, x_b, small_ref, bias_up_ref, w_proj_ref, w_up_ref, w_down_ref,
    out_ref, middle_ref, normed_ref, active_ref, slope_ref
):
    attended = stacked((att_a, att_b))
    x = stacked((x_a, x_b)).astype(F32)
    middle = x + dot(attended, w_proj_ref[...]) + small_ref[5:6, :]
    middle_ref[...] = middle
    hat, _ = normalise(middle)
    normed = (hat * small_ref[6:7, :] + small_ref[7:8, :]).astype(BF)
    normed_ref[...] = normed
    result = middle + small_ref[8:9, :]
    width, step = w_up_ref.shape[1], 512
    ahead = dot(normed, w_up_ref[:, :step])
    for first in range(0, width, step):
        cols = slice(first, first + step)
        hidden = ahead + bias_up_ref[:, cols]
        if first + step < width:
            ahead = dot(normed, w_up_ref[:, first + step : first + 2 * step])
        active, slope = gelu_terms(hidden)
        active = active.astype(BF)
        active_ref[:, cols] = active
        slope_ref[:, cols] = slope.astype(BF)
        result = result + dot(active, w_down_ref[cols, :])
    out_ref[...] = result.astype(BF)


def norm_back(grad, hat, scale, gain):
    inner = grad * gain
    mean = jnp.mean(inner, axis=-1, keepdims=True)
    along = jnp.mean(inner * hat, axis=-1, keepdims=True)
    return scale * (inner - mean - hat * along)


def backward_kernel(
    place_ref, groups_ref, everyone_ref, cot_own, cot_got, middle_ref, normed_ref, active_ref, slope_ref, att_a, att_b,
    small_ref, w_proj_ref, w_up_ref, w_down_ref,
    grad_middle_ref, grad_att_ref, keep_ref, *send_refs
):
    *send_refs, stage_ref = send_refs
    rows_a, total = att_a.shape[0], cot_own.shape[0]
    everyone = everyone_ref[...]

    def weight_of(group):
        return 1.0 / jnp.sum(jnp.where(everyone == group, 1.0, 0.0), axis=1, keepdims=True)

    weight = jnp.where(
        iota((total, 1), 0) < rows_a, weight_of(groups_ref[place_ref[0]]), weight_of(groups_ref[2])
    )
    got = jnp.concatenate([cot_got[...].astype(F32), jnp.zeros((EXTRA, cot_got.shape[1]), F32)], axis=0)
    upstream = (cot_own[...].astype(F32) + got) * weight
    grad_result = upstream.astype(BF)
    normed = normed_ref[...]
    hidden, step = active_ref.shape[1], 512
    grad_normed = None
    sums = []
    slab = hidden // 8 * (grad_result.shape[1] // LANES)
    for first in range(0, hidden, step):
        cols = slice(first, first + step)
        grad_hidden = (dot_last(grad_result, w_down_ref[cols, :]) * slope_ref[:, cols].astype(F32)).astype(BF)
        stage_rows(stage_ref, 0, dot_rows(active_ref[:, cols], grad_result), hidden, first)
        part = dot_last(grad_hidden, w_up_ref[:, cols])
        grad_normed = part if grad_normed is None else grad_normed + part
        sums.append(column_sums(grad_hidden.astype(F32)))
        stage_columns(stage_ref, slab, dot_rows(normed, grad_hidden), hidden, first)
    hat, scale = normalise(middle_ref[...])
    grad_middle = upstream + norm_back(grad_normed, hat, scale, small_ref[6:7, :])
    grad_middle_ref[...] = grad_middle
    grad_branch = grad_middle.astype(BF)
    grad_att_ref[...] = dot_last(grad_branch, w_proj_ref[...]).astype(BF)
    width = grad_branch.shape[1]
    stage_rows(stage_ref, 2 * slab, dot_rows(stacked((att_a, att_b)), grad_branch), width)
    vectors = sums + [
        column_sums(grad_normed * hat),
        column_sums(grad_normed),
        column_sums(grad_branch.astype(F32)),
        column_sums(grad_result.astype(F32)),
    ]
    stage_vectors(stage_ref, 2 * slab + width // 8 * (width // LANES), vectors)
    scatter_chunks(place_ref, stage_ref, keep_ref, send_refs)


def attention_back_kernel(row_from, g_ref, att_ref, q_ref, k_ref, v_ref, e_ref, inverse_ref, dq_ref, dk_ref, dv_ref):
    rows, width = q_ref.shape
    first = iota((1, LANES), 1) < HEAD_DIM
    for pair in range(width // LANES):
        cols = slice(pair * LANES, (pair + 1) * LANES)
        q_pair, k_pair, v_pair = q_ref[:, cols], k_ref[:, cols], v_ref[:, cols]
        g_pair = (g_ref[row_from : row_from + rows, cols].astype(F32) * inverse_ref[:, cols]).astype(BF)
        agree = g_pair.astype(F32) * att_ref[:, cols].astype(F32)
        dq, dk, dv = [], [], []
        for side in range(2):
            mine = first if side == 0 else jnp.logical_not(first)
            correction = jnp.sum(jnp.where(mine, agree, 0.0), axis=1, keepdims=True)
            expo = e_ref[2 * pair + side]
            grad_probs = dot_last(jnp.where(mine, g_pair, jnp.zeros_like(g_pair)), v_pair)
            grad_scores = expo * (grad_probs - correction).astype(BF)
            dq.append(dot(grad_scores, k_pair))
            dk.append(dot_rows(grad_scores, q_pair))
            dv.append(dot_rows(expo, g_pair))
        dq_ref[:, cols] = (jnp.where(first, dq[0], dq[1]) * HEAD_DIM ** (-0.5)).astype(BF)
        dk_ref[:, cols] = jnp.where(first, dk[0], dk[1]).astype(BF)
        dv_ref[:, cols] = jnp.where(first, dv[0], dv[1]).astype(BF)


def inputs_back_kernel(
    unmasked, place_ref, x_a, x_b, dq_a, dq_b, dk_a, dk_b, dv_a, dv_b, grad_middle_ref, small_ref, w_ref,
    grad_ref, keep_ref, *send_refs
):
    *send_refs, stage_ref = send_refs
    rows, width = x_a.shape
    part = unmasked // 2
    tm = place_ref[0]

    def spread(block):
        wide = block.astype(F32)
        left = jnp.where(tm == 0, wide[:part], 0.0)
        right = jnp.where(tm == 0, 0.0, wide[:part])
        return jnp.concatenate([left, right, wide[part:]], axis=0)

    x = stacked((x_a, x_b)).astype(F32)
    hat, scale = normalise(x)
    gain = small_ref[1:2, :]
    normed = (hat * gain + small_ref[2:3, :]).astype(BF)
    dq = jnp.concatenate([dq_a[...], spread(dq_b[...]).astype(BF)], axis=0)
    mixed = jnp.concatenate([dq, stacked((dk_a, dk_b)), stacked((dv_a, dv_b))], axis=1)
    stage_rows(stage_ref, 0, dot_rows(normed, mixed), width)
    grad_normed = dot_last(mixed, w_ref[...])
    grad = norm_back(grad_normed, hat, scale, gain)
    grad = grad + jnp.concatenate([grad_middle_ref[:rows], spread(grad_middle_ref[rows:])], axis=0)
    grad_ref[:unmasked] = grad[:unmasked].astype(BF)
    grad_ref[unmasked:] = grad[rows : rows + unmasked].astype(BF)
    vectors = (
        column_sums(mixed[:, :width].astype(F32)),
        column_sums(mixed[:, 2 * width :].astype(F32)),
        column_sums(grad_normed * hat),
        column_sums(grad_normed),
        grad[unmasked : unmasked + 1] + grad[rows + unmasked : rows + unmasked + 1],
    )
    stage_vectors(stage_ref, width // 8 * (mixed.shape[1] // LANES), vectors)
    scatter_chunks(place_ref, stage_ref, keep_ref, send_refs)


def place_back(rank_ref, copy, rows, half):
    down = jnp.transpose(ranks_of(rank_ref, copy, 16 * LANES))
    labels = jnp.broadcast_to(iota((1, rows), 1).astype(F32), (LANES, rows))
    return jnp.concatenate([ones_where(labels == down[:, b : b + 1]) for b in range(half // LANES)], axis=0)


def outputs_kernel(unmasked, place_ref, rank_ref, own_ref, got_ref, out_ref):
    tm = place_ref[0]
    half = out_ref.shape[1]
    rows = unmasked + EXTRA
    part = unmasked // 2
    out_ref[tm] = dot(place_back(rank_ref, tm, rows, half), own_ref[:rows]).astype(BF)
    out_ref[1 - tm] = dot(place_back(rank_ref, 1 - tm, rows, half), got_ref[:rows]).astype(BF)
    own = own_ref[rows:].astype(F32)
    got = got_ref[rows:].astype(F32)
    left = jnp.where(tm == 0, own[:part], got[:part])
    right = jnp.where(tm == 0, got[:part], own[:part])
    whole = jnp.concatenate([left, right, own[part:]], axis=0).astype(BF)
    out_ref[2] = dot(place_back(rank_ref, 2, rows, half), whole).astype(BF)


def grads_out_kernel(unmasked, place_ref, rank_ref, own_ref, got_ref, out_ref):
    tm = place_ref[0]
    half = out_ref.shape[1]
    out_ref[tm] = dot(place_back(rank_ref, tm, unmasked, half), own_ref[:unmasked]).astype(BF)
    out_ref[1 - tm] = dot(place_back(rank_ref, 1 - tm, unmasked, half), got_ref[:unmasked]).astype(BF)
    whole = (own_ref[unmasked:].astype(F32) + got_ref[unmasked:].astype(F32)).astype(BF)
    out_ref[2] = dot(place_back(rank_ref, 2, unmasked, half), whole).astype(BF)


def fold_kernel(keep_ref, *refs):
    got_refs, out_refs = refs[:-4], refs[-4:]
    each = got_refs[0].shape[0]
    for step, out_ref in enumerate(out_refs):
        got = got_refs[step // each][step % each]
        out_ref[...] = (keep_ref[step].astype(F32) + got.astype(F32)).astype(BF)


def fold_four_kernel(units, *refs):
    outs = refs[4 * units :]
    first = 0
    for unit in range(units):
        total = refs[4 * unit][...].astype(F32)
        for ref in refs[4 * unit + 1 : 4 * unit + 4]:
            total = total + ref[...].astype(F32)
        total = total.astype(BF)
        rows = slice(first, first + total.shape[1])
        first += total.shape[1]
        if len(outs) == 1:
            outs[0][:, rows] = total
        else:
            for step, out_ref in enumerate(outs):
                for slot in range(out_ref.shape[0]):
                    out_ref[slot, rows] = total[4 * slot + step]


def clip_swap(values, distance):
    size = lax.axis_size("clip")
    return lax.ppermute(values, "clip", [(i, i ^ distance) for i in range(size)])


def near_swap(values, step):
    size = lax.axis_size("clip")
    pairs = [
        (t * size + i, (t ^ (step & 1)) * size + (i ^ ((step >> 1) << 1))) for t in range(2) for i in range(size)
    ]
    return lax.ppermute(values, ("tm", "clip"), pairs)


def sum_cores(keep, send, after):
    _, groups, depth, _ = keep.shape
    got, after = lax.optimization_barrier(([clip_swap(part, 1) for part in send], after))
    return plain(fold_kernel, [shape(groups, depth, LANES)] * 4)(keep, *got)


def spread_near(pieces):
    return [pieces[0]] + [near_swap(pieces[step], step) for step in (1, 2, 3)]


def sum_over_devices(first_pieces, second_pieces, send_far, beside_last, finish):
    far = []
    distance = 4
    while distance < lax.axis_size("clip"):
        far.append(distance)
        distance *= 4
    pieces = [*first_pieces, *second_pieces]
    groups = pieces[0].shape[0]
    depth = pieces[0].shape[1] + pieces[4].shape[1]
    left = groups
    sent = None
    for distance in far:
        left //= 4
        fold = functools.partial(fold_four_kernel, len(pieces) // 4)
        pieces = plain(fold, [shape(left, depth, LANES)] * 4)(*pieces)
        if sent is None:
            sent, pieces = send_far(pieces)
        pieces = [pieces[0]] + [clip_swap(pieces[step], step * distance) for step in (1, 2, 3)]
    total = plain(functools.partial(fold_four_kernel, 1), shape(left, depth, LANES))(*pieces)
    for distance in reversed(far):
        pieces = [total] + [clip_swap(total, step * distance) for step in (1, 2, 3)]
        total = plain(join_kernel, shape(4 * total.shape[0], *total.shape[1:]))(*pieces)
    total, sent = lax.optimization_barrier((total, sent))
    pieces = spread_near([total] * 4)
    last = beside_last(sent)
    *pieces, last = lax.optimization_barrier((*pieces, last))
    got = [clip_swap(piece, 1) for piece in pieces]
    return finish(1, got, finish(0, pieces, ())), last


def join_kernel(*refs):
    for step in range(4):
        for slot in range(refs[step].shape[0]):
            refs[4][4 * slot + step] = refs[step][slot]


def finish_kernel(side, depths, counts, place_ref, *refs):
    sources, refs = refs[:4], refs[4:]
    if side:
        first_kept_ref, refs = refs[4], refs[5:]
        outs, vectors, refs = refs[:4], refs[4 : 4 + sum(counts)], refs[4 + sum(counts) :]
        kept_ref, *refs = refs
    else:
        outs, kept_ref, refs = refs[:4], refs[4], refs[5:]
    stage_a, stage_b, done, *wides = refs
    far_places = sources[0].shape[0]
    stores = []
    for near in range(4):
        eighth = eighth_at(place_ref, near, side)
        for far in range(far_places):
            stage_a[chunk_rows_at(place_ref, far, depths[0]), :] = sources[near][far, : depths[0]]
            stage_b[chunk_rows_at(place_ref, far, depths[1]), :] = sources[near][far, depths[0] :]
        for unit, stage_ref in enumerate((stage_a, stage_b)):
            first = 0
            for at in ((0, 1, 2), (3,))[unit]:
                wide_ref = wides[at].at[near]
                depth, width = wide_ref.shape
                for block in range(width // LANES):
                    wide_ref[:, block * LANES : (block + 1) * LANES] = stage_ref[first : first + depth, :].astype(F32)
                    first += depth
                if at == 1:
                    rows = pl.ds(pl.multiple_of((eighth & 1) * depth, 16), depth)
                    target = outs[at].at[rows, pl.ds(pl.multiple_of((eighth >> 1) * width, LANES), width)]
                else:
                    target = outs[at].at[pl.ds(pl.multiple_of(eighth * depth, 16), depth), :]
                stores.append(pltpu.make_async_copy(wide_ref, target, done.at[len(stores)]))
                stores[-1].start()
            kept_ref[eighth, 16 * unit : 16 * unit + 16] = stage_ref[first : first + 16, :].astype(F32)
    if side:
        for near in range(4):
            eighth = eighth_at(place_ref, near, 0)
            kept_ref[eighth] = first_kept_ref[eighth]
        at = 0
        for unit, count in enumerate(counts):
            blocks = [(ref, block) for ref in vectors[at : at + count] for block in range(ref.shape[0] // LANES)]
            at += count
            each = -(-len(blocks) // 8)
            for number, (ref, block) in enumerate(blocks):
                eighth, row = divmod(number, each)
                ref[block * LANES : (block + 1) * LANES] = kept_ref[eighth, 16 * unit + row]
    else:
        for near in range(4):
            kept_ref[eighth_at(place_ref, near, 1)] = jnp.zeros(kept_ref.shape[1:], F32)
    for store in stores:
        store.wait()


def chunk_rows(count, devices):
    return -(-count // (devices * 16)) * 16


def body(
    tokens,
    masked,
    groups,
    cotangent,
    mask_token,
    gain_one,
    shift_one,
    w_qkv,
    q_bias,
    v_bias,
    w_proj,
    b_proj,
    gain_two,
    shift_two,
    w_up,
    b_up,
    w_down,
    b_down,
):
    copies, half, width = tokens.shape
    hidden = w_up.shape[1]
    hide = masked.shape[1]
    unmasked = 2 * half - hide
    rows = unmasked + EXTRA
    some = unmasked // 2 + EXTRA
    total = rows + some
    tm, clip = lax.axis_index("tm"), lax.axis_index("clip")
    clips = lax.axis_size("clip")
    devices = 2 * clips
    me = (clip & 1) | (tm << 1) | ((clip >> 1) << 2)
    place = jnp.stack([tm, me]).astype(jnp.int32)
    swap = functools.partial(lax.ppermute, axis_name="tm", perm=[(0, 1), (1, 0)])

    def run(kernel, args, outs, scratch=(), scalars=1, limit=20, flops=0, in_hbm=(), out_hbm=(), aliases=None, hides=True):
        moved = sum(math.prod(a.shape) * a.dtype.itemsize for a in list(args) + jax.tree.leaves(outs))
        return pl.pallas_call(
            kernel,
            out_shape=outs,
            in_specs=[
                SMEM if at < scalars else HBM if at in in_hbm else VMEM
                for at in range(len(args))
            ],
            out_specs=[HBM if at in out_hbm else VMEM for at in range(len(outs))] if isinstance(outs, list) else VMEM,
            scratch_shapes=list(scratch),
            input_output_aliases=aliases or {},
            compiler_params=pltpu.CompilerParams(vmem_limit_bytes=limit << 20),
            cost_estimate=pl.CostEstimate(
                flops=flops if hides else 1, bytes_accessed=moved if hides else 1, transcendentals=0
            ),
        )(*args)

    blocks = width // LANES
    counts = ((2 * hidden + width) // 8 * blocks + 16, 3 * width // 8 * blocks + 16)
    depths = [chunk_rows(count, devices // 8) for count in counts]

    def chunked(unit, parts):
        halves = [shape(near, devices // 8, depths[unit], LANES) for near in [4] + [4 // parts] * parts]
        return halves, [pltpu.VMEM((8, devices // 8 * depths[unit], LANES), BF)]

    small = jnp.stack(
        [mask_token, gain_one, shift_one, q_bias, v_bias, b_proj, gain_two, shift_two, b_down]
    ).astype(F32)
    bias_up = b_up.astype(F32).reshape(1, hidden)

    block = shape(rows, width)
    everyone = jnp.concatenate([groups, clip_swap(groups, 1)])
    theirs, rank = run(
        functools.partial(prep_theirs_kernel, unmasked),
        (place, *(pltpu.with_memory_space_constraint(each, pltpu.HBM) for each in (masked, tokens))),
        [shape(unmasked, width), shape(16 * copies, LANES, kind=F32)],
        [pltpu.VMEM(masked.shape, jnp.int32), pltpu.VMEM((half, width), BF), pltpu.SemaphoreType.DMA((2,))],
        flops=2 * rows * half * width,
        in_hbm=(1, 2),
    )
    got_mine = swap(theirs)
    everyone, theirs, rank = lax.optimization_barrier((everyone, theirs, rank))
    everyone = jnp.concatenate([everyone, clip_swap(everyone, 2)])
    shared = run(
        functools.partial(prep_shared_kernel, unmasked),
        (rank, tokens),
        shape(unmasked, width),
        scalars=0,
        flops=2 * rows * half * width,
    )
    got_shared = swap(shared)
    everyone, shared, rank = lax.optimization_barrier((everyone, shared, rank))
    everyone = jnp.concatenate([everyone, clip_swap(everyone, 4)])
    cot_own, cot_send = run(
        functools.partial(prep_grads_kernel, unmasked),
        (place, rank, cotangent),
        [shape(total, width), shape(total - EXTRA, width)],
        flops=2 * copies * rows * half * width,
    )
    everyone, cot_own, cot_send = lax.optimization_barrier((everyone, cot_own, cot_send))
    cot_got = swap(cot_send)

    def attend(sources, got, split):
        queries = some if split else rows
        outs = [
            shape(queries, width), shape(queries, width), block, block,
            shape(HEADS, queries, rows), shape(queries, width, kind=F32), shape(queries, width),
        ]
        if split:
            outs.append(block)
        return run(
            functools.partial(attention_kernel, unmasked, hide, split),
            (place, *sources, got, small, w_qkv),
            outs,
            flops=6 * rows * width * width + 4 * queries * rows * width,
        )

    x_a, q_a, k_a, v_a, e_a, inverse_a, att_a = attend((rank, tokens), got_mine, False)
    everyone, att_a = lax.optimization_barrier((everyone, att_a))
    distance = 8
    while distance < clips:
        everyone = jnp.concatenate([everyone, clip_swap(everyone, distance)])
        distance *= 2
    x_b, q_b, k_b, v_b, e_b, inverse_b, att_b, x_whole = attend((shared,), got_shared, True)

    out_rows, middle, normed_two, active, slope = run(
        forward_kernel,
        (att_a, att_b, x_a, x_b, small, bias_up, w_proj, w_up, w_down),
        [
            shape(total, width), shape(total, width, kind=F32), shape(total, width), shape(total, hidden),
            shape(total, hidden),
        ],
        scalars=0,
        flops=2 * total * width * (width + 2 * hidden),
    )
    out_got = swap(out_rows)
    halves, stage = chunked(0, 4)
    grad_middle, grad_att, keep, *send = run(
        backward_kernel,
        (
            place, groups, everyone.reshape(1, -1), cot_own, cot_got, middle, normed_two, active, slope, att_a, att_b,
            small, w_proj, w_up, w_down,
        ),
        [shape(total, width, kind=F32), shape(total, width)] + halves,
        stage,
        scalars=2,
        hides=False,
    )

    def attend_back(row_from, grads, att, q, k, v, e, inverse):
        return run(
            functools.partial(attention_back_kernel, row_from),
            (grads, att, q, k, v, e, inverse),
            [shape(q.shape[0], width), block, block],
            scalars=0,
            hides=False,
        )

    dq_b, dk_b, dv_b = attend_back(rows, grad_att, att_b, q_b, k_b, v_b, e_b, inverse_b)
    pieces, grad_att = lax.optimization_barrier((sum_cores(keep, send, dq_b), grad_att))
    first_pieces = spread_near(pieces)
    dq_a, dk_a, dv_a = attend_back(0, grad_att, att_a, q_a, k_a, v_a, e_a, inverse_a)
    dq_a, out_got = lax.optimization_barrier((dq_a, out_got))
    halves, stage = chunked(1, 2)
    grad_rows, keep, *send = run(
        functools.partial(inputs_back_kernel, unmasked),
        (place, x_a, x_whole, dq_a, dq_b, dk_a, dk_b, dv_a, dv_b, grad_middle, small, w_qkv),
        [shape(2 * unmasked, width)] + halves,
        stage,
        hides=False,
    )
    pieces, first_pieces = lax.optimization_barrier((sum_cores(keep, send, ()), first_pieces))
    second_pieces = spread_near(pieces)

    def send_rows(pieces):
        *pieces, grads = lax.optimization_barrier((*pieces, grad_rows))
        return swap(grads), pieces

    def place_rows(got):
        return (
            run(functools.partial(outputs_kernel, unmasked), (place, rank, out_rows, out_got), shape(*tokens.shape)),
            run(functools.partial(grads_out_kernel, unmasked), (place, rank, grad_rows, got), shape(*tokens.shape)),
        )

    weights = [(hidden, width), (width, hidden), (width, width), (width, 3 * width)]
    slabs = [(hidden // 8, width), (width // 2, hidden // 4), (width // 8, width), (width // 8, 3 * width)]
    vectors = [shape(dim, kind=F32) for dim in [hidden] + [width] * 9]

    def finish(side, sources, earlier):
        kept = pltpu.VMEM((8, 32, LANES), F32)
        return run(
            functools.partial(finish_kernel, side, depths, (5, 5)),
            (place, *sources, *earlier),
            [shape(*dims, kind=F32) for dims in weights] + (vectors if side else [shape(8, 32, LANES, kind=F32)]),
            [kept] * side
            + [pltpu.VMEM((devices // 8 * depth, LANES), BF) for depth in depths]
            + [pltpu.SemaphoreType.DMA((16,))]
            + [pltpu.VMEM((4, *dims), F32) for dims in slabs],
            in_hbm=range(1 + len(sources), 5 + len(sources)) if side else (),
            out_hbm=range(4),
            aliases={1 + len(sources) + at: at for at in range(4)} if side else {},
            hides=False,
        )

    (
        (
            grad_w_down, grad_w_up, grad_w_proj, grad_w_qkv,
            grad_b_up, grad_gain_two, grad_shift_two, grad_b_proj, grad_b_down,
            grad_q_bias, grad_v_bias, grad_gain_one, grad_shift_one, grad_mask_token,
        ),
        (block_out, grad_tokens),
    ) = sum_over_devices(first_pieces, second_pieces, send_rows, place_rows, finish)
    return (
        block_out,
        grad_tokens,
        grad_mask_token,
        grad_gain_one,
        grad_shift_one,
        grad_w_qkv,
        grad_q_bias,
        grad_v_bias,
        grad_w_proj,
        grad_b_proj,
        grad_gain_two,
        grad_shift_two,
        grad_w_up,
        grad_b_up,
        grad_w_down,
        grad_b_down,
    )


def solution(mesh):
    return jax.shard_map(
        body,
        mesh=mesh,
        in_specs=(P("clip", "tm", None), P("clip", None), P("clip"), P("clip", "tm", None)) + (P(),) * 14,
        out_specs=(P("clip", "tm", None), P("clip", "tm", None)) + (P(),) * 14,
        check_vma=False,
    )
```

```python
import functools
import math

import jax
import jax.numpy as jnp
import numpy as np
from jax import lax
from jax.experimental import pallas as pl
from jax.experimental.pallas import tpu as pltpu
from jax.sharding import PartitionSpec as P

HEADS = 6
HEAD_DIM = 64
LANES = 128
EXTRA = 16
EPSILON = 1e-06

BF = jnp.bfloat16
F32 = jnp.float32
VMEM = pl.BlockSpec(memory_space=pltpu.VMEM)
SMEM = pl.BlockSpec(memory_space=pltpu.SMEM)
HBM = pl.BlockSpec(memory_space=pltpu.HBM)


def dot(left, right):
    return jnp.dot(left, right, preferred_element_type=F32)


def dot_last(left, right):
    return lax.dot_general(left, right, (((1,), (1,)), ((), ())), preferred_element_type=F32)


def dot_rows(left, right):
    return lax.dot_general(left, right, (((0,), (0,)), ((), ())), preferred_element_type=F32)


def iota(shape, axis):
    return lax.broadcasted_iota(jnp.int32, shape, axis)


def ones_where(condition):
    return jnp.where(condition, 1.0, 0.0).astype(BF)


def column_sums(values):
    return jnp.sum(values, axis=0, keepdims=True)


def shape(*dims, kind=BF):
    return jax.ShapeDtypeStruct(dims, kind)


def plain(kernel, outs):
    return pl.pallas_call(kernel, out_shape=outs, compiler_params=pltpu.CompilerParams(vmem_limit_bytes=8 << 20))


def all_ranks(masked_ref, tm, half, unmasked):
    copies, hide = masked_ref.shape
    blocks = half // LANES
    marks = []
    for copy in range(copies):
        row = masked_ref[copy : copy + 1, :]
        low = ones_where(iota((LANES, hide), 0) == (row & (LANES - 1)))
        high = ones_where(iota((16, hide), 0) == (row >> 7))
        marks.append(dot_last(high, low))
    marks = jnp.concatenate(marks, axis=0)
    count = 16 * copies
    block = iota((count, LANES), 0)
    free = jnp.where((block & 15) < 2 * blocks, 1.0 - marks, 0.0).astype(BF)
    before = ones_where(iota((LANES, LANES), 0) < iota((LANES, LANES), 1))
    within = dot(free, before)
    totals = dot(free, jnp.ones((LANES, LANES), BF)).astype(BF)
    row, column = iota((count, count), 0), iota((count, count), 1)
    earlier = ones_where(jnp.logical_and(column < row, (column >> 4) == (row >> 4)))
    rank = within + dot(earlier, totals)
    rank = jnp.where(marks > 0.5, float(unmasked), rank)
    across = []
    for first in range(0, count, 16):
        mine = jnp.where(tm == 0, rank[first : first + blocks], rank[first + blocks : first + 2 * blocks])
        across.append(jnp.concatenate([mine, jnp.zeros((16 - blocks, LANES), F32)], axis=0))
    return jnp.concatenate(across, axis=0)


def picks(rank, labels):
    wide = jnp.broadcast_to(labels.astype(F32), (labels.shape[0], LANES))
    return jnp.concatenate([ones_where(wide == rank[b : b + 1, :]) for b in range(rank.shape[0])], axis=1)


def ranks_of(rank_ref, copy, half):
    return rank_ref[pl.ds(pl.multiple_of(16 * copy, 16), 16), :][: half // LANES]


def prep_theirs_kernel(
    unmasked, place_ref, masked_ref, tokens_ref, theirs_ref, rank_ref, marks_ref, half_ref, arrived
):
    tm = place_ref[0]
    half = tokens_ref.shape[1]
    load_marks = pltpu.make_async_copy(masked_ref, marks_ref, arrived.at[0])
    load_marks.start()
    load = pltpu.make_async_copy(tokens_ref.at[1 - tm], half_ref, arrived.at[1])
    load.start()
    load_marks.wait()
    rank_ref[...] = all_ranks(marks_ref, tm, half, unmasked)
    chosen = picks(ranks_of(rank_ref, 1 - tm, half), iota((unmasked, 1), 0))
    load.wait()
    theirs_ref[...] = dot(chosen, half_ref[...]).astype(BF)


def prep_shared_kernel(unmasked, rank_ref, tokens_ref, shared_ref):
    chosen = picks(ranks_of(rank_ref, 2, tokens_ref.shape[1]), iota((unmasked, 1), 0))
    shared_ref[...] = dot(chosen, tokens_ref[2]).astype(BF)


def prep_grads_kernel(unmasked, place_ref, rank_ref, cotangent_ref, keep_ref, send_ref):
    tm = place_ref[0]
    half = cotangent_ref.shape[1]
    rows = unmasked + EXTRA
    part = unmasked // 2
    labels = iota((rows, 1), 0)
    small = iota((part + EXTRA, 1), 0)
    theirs = iota((part, 1), 0) + part * (1 - tm)
    own = jnp.where(small < part, small + part * tm, small + part)
    send_ref[:rows, :] = dot(picks(ranks_of(rank_ref, 1 - tm, half), labels), cotangent_ref[1 - tm]).astype(BF)
    chosen = picks(ranks_of(rank_ref, 2, half), jnp.concatenate([theirs, own], axis=0))
    both = dot(chosen, cotangent_ref[2]).astype(BF)
    send_ref[rows:, :] = both[:part]
    keep_ref[rows:, :] = both[part:]
    keep_ref[:rows, :] = dot(picks(ranks_of(rank_ref, tm, half), labels), cotangent_ref[tm]).astype(BF)


def normalise(values):
    centred = values - jnp.mean(values, axis=-1, keepdims=True)
    scale = lax.rsqrt(jnp.mean(centred * centred, axis=-1, keepdims=True) + EPSILON)
    return centred * scale, scale


def bias_terms(count):
    terms, rest = [], math.log(count)
    for _ in range(3):
        terms.append(float(np.asarray(rest).astype(jnp.bfloat16)))
        rest -= terms[-1]
    return terms


def attention_kernel(unmasked, count, split, place_ref, *refs):
    tm = place_ref[0]
    if split:
        own_ref, got_ref, small_ref, w_ref, x_ref, q_ref, k_ref, v_ref, e_ref, inverse_ref, att_ref, whole_ref = refs
        own = own_ref[...].astype(F32)
    else:
        rank_ref, tokens_ref, got_ref, small_ref, w_ref, x_ref, q_ref, k_ref, v_ref, e_ref, inverse_ref, att_ref = refs
        chosen = picks(ranks_of(rank_ref, tm, tokens_ref.shape[1]), iota((unmasked, 1), 0))
        own = dot(chosen, tokens_ref[tm])
    rows, width = k_ref.shape
    extra = jnp.where(iota((EXTRA, width), 0) == 0, small_ref[0:1, :], 0.0)
    x = jnp.concatenate([own + got_ref[...].astype(F32), extra], axis=0)
    hat, _ = normalise(x)
    normed = (hat * small_ref[1:2, :] + small_ref[2:3, :]).astype(BF)
    mixed = dot(normed, w_ref[...])
    query = ((mixed[:, :width] + small_ref[3:4, :]).astype(BF).astype(F32) * HEAD_DIM ** (-0.5)).astype(BF)
    key = mixed[:, width : 2 * width].astype(BF)
    value = (mixed[:, 2 * width :] + small_ref[4:5, :]).astype(BF)
    k_ref[...] = key
    v_ref[...] = value
    x = x.astype(BF)
    if split:
        part = unmasked // 2

        def take(values):
            chosen = jnp.where(tm == 0, values[:part].astype(F32), values[part:unmasked].astype(F32)).astype(BF)
            return jnp.concatenate([chosen, values[unmasked:]], axis=0)

        whole_ref[...] = x
        x, query = take(x), take(query)
    x_ref[...] = x
    q_ref[...] = query
    lane = iota((1, LANES), 1)
    first = lane < HEAD_DIM
    at = iota((rows, LANES), 0)
    place = iota((rows, LANES), 1) & (HEAD_DIM - 1)
    log_count = jnp.zeros((rows, LANES), F32)
    for which, term in enumerate(bias_terms(count)):
        log_count = jnp.where(place == which, term, log_count)
    bias = jnp.where(at < unmasked, 0.0, jnp.where(at == unmasked, log_count, jnp.where(place == 0, -1e30, 0.0)))
    bias = bias.astype(BF)
    ones = jnp.where((lane & (HEAD_DIM - 1)) < 3, 1.0, 0.0).astype(BF)
    all_ones = jnp.ones((rows, LANES), BF)
    for pair in range(width // LANES):
        cols = slice(pair * LANES, (pair + 1) * LANES)
        q_pair, k_pair, v_pair = query[:, cols], key[:, cols], value[:, cols]
        v_wide = jnp.concatenate([v_pair, all_ones], axis=1)
        parts = []
        for side in range(2):
            mine = first if side == 0 else jnp.logical_not(first)
            scores = dot_last(jnp.where(mine, q_pair, ones), jnp.where(mine, k_pair, bias))
            expo = jnp.exp(scores - jnp.max(scores, axis=1, keepdims=True)).astype(BF)
            e_ref[2 * pair + side] = expo
            parts.append(dot(expo, v_wide))
        inverse = 1.0 / jnp.where(first, parts[0][:, LANES:], parts[1][:, LANES:])
        inverse_ref[:, cols] = inverse
        att_ref[:, cols] = (jnp.where(first, parts[0][:, :LANES], parts[1][:, :LANES]) * inverse).astype(BF)


def gelu_terms(hidden):
    below = 0.5 * lax.erf(hidden * 0.5**0.5) + 0.5
    bell = jnp.exp2(hidden * hidden * (-0.5 * math.log2(math.e)))
    return hidden * below, below + hidden * bell * (1.0 / math.sqrt(2.0 * math.pi))


def stacked(refs):
    return jnp.concatenate([ref[...] for ref in refs], axis=0)


def eighth_at(place_ref, near, side):
    me = place_ref[1]
    return ((near ^ ((me >> 1) & 3)) << 1) | (side ^ (me & 1))


def chunk_rows_at(place_ref, far, depth):
    return pl.ds(pl.multiple_of((far ^ (place_ref[1] >> 3)) * depth, 16), depth)


def scatter_chunks(place_ref, stage_ref, keep_ref, send_refs):
    near_places, far_places, depth, _ = keep_ref.shape
    each = send_refs[0].shape[0]
    for near in range(near_places):
        for side in range(2):
            eighth = eighth_at(place_ref, near, side)
            for far in range(far_places):
                chunk = stage_ref[eighth, chunk_rows_at(place_ref, far, depth), :]
                if side:
                    send_refs[near // each][near % each, far] = chunk
                else:
                    keep_ref[near, far] = chunk


def stage_rows(stage_ref, base, grad, total, first=0):
    slab = total // 8
    step = math.gcd(slab, grad.shape[0])
    grad = grad.astype(BF)
    for row in range(0, grad.shape[0], step):
        eighth, offset = divmod(first + row, slab)
        for block in range(grad.shape[1] // LANES):
            at = base + block * slab + offset
            stage_ref[eighth, at : at + step, :] = grad[row : row + step, block * LANES : (block + 1) * LANES]


def stage_columns(stage_ref, base, grad, total, first):
    slab = grad.shape[0] // 2
    grad = grad.astype(BF)
    for block in range(grad.shape[1] // LANES):
        quarter, offset = divmod(first // LANES + block, total // 4 // LANES)
        at = base + offset * slab
        for half in range(2):
            stage_ref[2 * quarter + half, at : at + slab, :] = grad[
                half * slab : (half + 1) * slab, block * LANES : (block + 1) * LANES
            ]


def stage_vectors(stage_ref, base, vectors):
    pieces = [v[:, b * LANES : (b + 1) * LANES] for v in vectors for b in range(v.shape[1] // LANES)]
    each = -(-len(pieces) // 8)
    for eighth in range(8):
        rows = pieces[eighth * each : (eighth + 1) * each]
        rows = rows + [jnp.zeros((16 - len(rows), LANES), F32)]
        stage_ref[eighth, base : base + 16, :] = jnp.concatenate(rows, axis=0).astype(BF)
        rest = stage_ref.shape[1] - base - 16
        if rest:
            stage_ref[eighth, base + 16 :, :] = jnp.zeros((rest, LANES), BF)


def forward_kernel(
    att_a, att_b, x_a, x_b, small_ref, bias_up_ref, w_proj_ref, w_up_ref, w_down_ref,
    out_ref, middle_ref, normed_ref, active_ref, slope_ref
):
    attended = stacked((att_a, att_b))
    x = stacked((x_a, x_b)).astype(F32)
    middle = x + dot(attended, w_proj_ref[...]) + small_ref[5:6, :]
    middle_ref[...] = middle
    hat, _ = normalise(middle)
    normed = (hat * small_ref[6:7, :] + small_ref[7:8, :]).astype(BF)
    normed_ref[...] = normed
    result = middle + small_ref[8:9, :]
    width, step = w_up_ref.shape[1], 512
    ahead = dot(normed, w_up_ref[:, :step])
    for first in range(0, width, step):
        cols = slice(first, first + step)
        hidden = ahead + bias_up_ref[:, cols]
        if first + step < width:
            ahead = dot(normed, w_up_ref[:, first + step : first + 2 * step])
        active, slope = gelu_terms(hidden)
        active = active.astype(BF)
        active_ref[:, cols] = active
        slope_ref[:, cols] = slope.astype(BF)
        result = result + dot(active, w_down_ref[cols, :])
    out_ref[...] = result.astype(BF)


def norm_back(grad, hat, scale, gain):
    inner = grad * gain
    mean = jnp.mean(inner, axis=-1, keepdims=True)
    along = jnp.mean(inner * hat, axis=-1, keepdims=True)
    return scale * (inner - mean - hat * along)


def backward_kernel(
    place_ref, groups_ref, everyone_ref, cot_own, cot_got, middle_ref, normed_ref, active_ref, slope_ref, att_a, att_b,
    small_ref, w_proj_ref, w_up_ref, w_down_ref,
    grad_middle_ref, grad_att_ref, keep_ref, *send_refs
):
    *send_refs, stage_ref = send_refs
    rows_a, total = att_a.shape[0], cot_own.shape[0]
    everyone = everyone_ref[...]

    def weight_of(group):
        return 1.0 / jnp.sum(jnp.where(everyone == group, 1.0, 0.0), axis=1, keepdims=True)

    weight = jnp.where(
        iota((total, 1), 0) < rows_a, weight_of(groups_ref[place_ref[0]]), weight_of(groups_ref[2])
    )
    got = jnp.concatenate([cot_got[...].astype(F32), jnp.zeros((EXTRA, cot_got.shape[1]), F32)], axis=0)
    upstream = (cot_own[...].astype(F32) + got) * weight
    grad_result = upstream.astype(BF)
    normed = normed_ref[...]
    hidden, step = active_ref.shape[1], 512
    grad_normed = None
    sums = []
    slab = hidden // 8 * (grad_result.shape[1] // LANES)
    for first in range(0, hidden, step):
        cols = slice(first, first + step)
        grad_hidden = (dot_last(grad_result, w_down_ref[cols, :]) * slope_ref[:, cols].astype(F32)).astype(BF)
        stage_rows(stage_ref, 0, dot_rows(active_ref[:, cols], grad_result), hidden, first)
        part = dot_last(grad_hidden, w_up_ref[:, cols])
        grad_normed = part if grad_normed is None else grad_normed + part
        sums.append(column_sums(grad_hidden.astype(F32)))
        stage_columns(stage_ref, slab, dot_rows(normed, grad_hidden), hidden, first)
    hat, scale = normalise(middle_ref[...])
    grad_middle = upstream + norm_back(grad_normed, hat, scale, small_ref[6:7, :])
    grad_middle_ref[...] = grad_middle
    grad_branch = grad_middle.astype(BF)
    grad_att_ref[...] = dot_last(grad_branch, w_proj_ref[...]).astype(BF)
    width = grad_branch.shape[1]
    stage_rows(stage_ref, 2 * slab, dot_rows(stacked((att_a, att_b)), grad_branch), width)
    vectors = sums + [
        column_sums(grad_normed * hat),
        column_sums(grad_normed),
        column_sums(grad_branch.astype(F32)),
        column_sums(grad_result.astype(F32)),
    ]
    stage_vectors(stage_ref, 2 * slab + width // 8 * (width // LANES), vectors)
    scatter_chunks(place_ref, stage_ref, keep_ref, send_refs)


def attention_back_kernel(row_from, g_ref, att_ref, q_ref, k_ref, v_ref, e_ref, inverse_ref, dq_ref, dk_ref, dv_ref):
    rows, width = q_ref.shape
    first = iota((1, LANES), 1) < HEAD_DIM
    for pair in range(width // LANES):
        cols = slice(pair * LANES, (pair + 1) * LANES)
        q_pair, k_pair, v_pair = q_ref[:, cols], k_ref[:, cols], v_ref[:, cols]
        g_pair = (g_ref[row_from : row_from + rows, cols].astype(F32) * inverse_ref[:, cols]).astype(BF)
        agree = g_pair.astype(F32) * att_ref[:, cols].astype(F32)
        dq, dk, dv = [], [], []
        for side in range(2):
            mine = first if side == 0 else jnp.logical_not(first)
            correction = jnp.sum(jnp.where(mine, agree, 0.0), axis=1, keepdims=True)
            expo = e_ref[2 * pair + side]
            grad_probs = dot_last(jnp.where(mine, g_pair, jnp.zeros_like(g_pair)), v_pair)
            grad_scores = expo * (grad_probs - correction).astype(BF)
            dq.append(dot(grad_scores, k_pair))
            dk.append(dot_rows(grad_scores, q_pair))
            dv.append(dot_rows(expo, g_pair))
        dq_ref[:, cols] = (jnp.where(first, dq[0], dq[1]) * HEAD_DIM ** (-0.5)).astype(BF)
        dk_ref[:, cols] = jnp.where(first, dk[0], dk[1]).astype(BF)
        dv_ref[:, cols] = jnp.where(first, dv[0], dv[1]).astype(BF)


def inputs_back_kernel(
    unmasked, place_ref, x_a, x_b, dq_a, dq_b, dk_a, dk_b, dv_a, dv_b, grad_middle_ref, small_ref, w_ref,
    grad_ref, keep_ref, *send_refs
):
    *send_refs, stage_ref = send_refs
    rows, width = x_a.shape
    part = unmasked // 2
    tm = place_ref[0]

    def spread(block):
        wide = block.astype(F32)
        left = jnp.where(tm == 0, wide[:part], 0.0)
        right = jnp.where(tm == 0, 0.0, wide[:part])
        return jnp.concatenate([left, right, wide[part:]], axis=0)

    x = stacked((x_a, x_b)).astype(F32)
    hat, scale = normalise(x)
    gain = small_ref[1:2, :]
    normed = (hat * gain + small_ref[2:3, :]).astype(BF)
    dq = jnp.concatenate([dq_a[...], spread(dq_b[...]).astype(BF)], axis=0)
    mixed = jnp.concatenate([dq, stacked((dk_a, dk_b)), stacked((dv_a, dv_b))], axis=1)
    stage_rows(stage_ref, 0, dot_rows(normed, mixed), width)
    grad_normed = dot_last(mixed, w_ref[...])
    grad = norm_back(grad_normed, hat, scale, gain)
    grad = grad + jnp.concatenate([grad_middle_ref[:rows], spread(grad_middle_ref[rows:])], axis=0)
    grad_ref[:unmasked] = grad[:unmasked].astype(BF)
    grad_ref[unmasked:] = grad[rows : rows + unmasked].astype(BF)
    vectors = (
        column_sums(mixed[:, :width].astype(F32)),
        column_sums(mixed[:, 2 * width :].astype(F32)),
        column_sums(grad_normed * hat),
        column_sums(grad_normed),
        grad[unmasked : unmasked + 1] + grad[rows + unmasked : rows + unmasked + 1],
    )
    stage_vectors(stage_ref, width // 8 * (mixed.shape[1] // LANES), vectors)
    scatter_chunks(place_ref, stage_ref, keep_ref, send_refs)


def place_back(rank_ref, copy, rows, half):
    down = jnp.transpose(ranks_of(rank_ref, copy, 16 * LANES))
    labels = jnp.broadcast_to(iota((1, rows), 1).astype(F32), (LANES, rows))
    return jnp.concatenate([ones_where(labels == down[:, b : b + 1]) for b in range(half // LANES)], axis=0)


def outputs_kernel(unmasked, place_ref, rank_ref, own_ref, got_ref, out_ref):
    tm = place_ref[0]
    half = out_ref.shape[1]
    rows = unmasked + EXTRA
    part = unmasked // 2
    out_ref[tm] = dot(place_back(rank_ref, tm, rows, half), own_ref[:rows]).astype(BF)
    out_ref[1 - tm] = dot(place_back(rank_ref, 1 - tm, rows, half), got_ref[:rows]).astype(BF)
    own = own_ref[rows:].astype(F32)
    got = got_ref[rows:].astype(F32)
    left = jnp.where(tm == 0, own[:part], got[:part])
    right = jnp.where(tm == 0, got[:part], own[:part])
    whole = jnp.concatenate([left, right, own[part:]], axis=0).astype(BF)
    out_ref[2] = dot(place_back(rank_ref, 2, rows, half), whole).astype(BF)


def grads_out_kernel(unmasked, place_ref, rank_ref, own_ref, got_ref, out_ref):
    tm = place_ref[0]
    half = out_ref.shape[1]
    out_ref[tm] = dot(place_back(rank_ref, tm, unmasked, half), own_ref[:unmasked]).astype(BF)
    out_ref[1 - tm] = dot(place_back(rank_ref, 1 - tm, unmasked, half), got_ref[:unmasked]).astype(BF)
    whole = (own_ref[unmasked:].astype(F32) + got_ref[unmasked:].astype(F32)).astype(BF)
    out_ref[2] = dot(place_back(rank_ref, 2, unmasked, half), whole).astype(BF)


def fold_kernel(keep_ref, *refs):
    got_refs, out_refs = refs[:-4], refs[-4:]
    each = got_refs[0].shape[0]
    for step, out_ref in enumerate(out_refs):
        got = got_refs[step // each][step % each]
        out_ref[...] = (keep_ref[step].astype(F32) + got.astype(F32)).astype(BF)


def fold_four_kernel(units, *refs):
    outs = refs[4 * units :]
    first = 0
    for unit in range(units):
        total = refs[4 * unit][...].astype(F32)
        for ref in refs[4 * unit + 1 : 4 * unit + 4]:
            total = total + ref[...].astype(F32)
        total = total.astype(BF)
        rows = slice(first, first + total.shape[1])
        first += total.shape[1]
        if len(outs) == 1:
            outs[0][:, rows] = total
        else:
            for step, out_ref in enumerate(outs):
                for slot in range(out_ref.shape[0]):
                    out_ref[slot, rows] = total[4 * slot + step]


def clip_swap(values, distance):
    size = lax.axis_size("clip")
    return lax.ppermute(values, "clip", [(i, i ^ distance) for i in range(size)])


def near_swap(values, step):
    size = lax.axis_size("clip")
    pairs = [
        (t * size + i, (t ^ (step & 1)) * size + (i ^ ((step >> 1) << 1))) for t in range(2) for i in range(size)
    ]
    return lax.ppermute(values, ("tm", "clip"), pairs)


def sum_cores(keep, send, after):
    _, groups, depth, _ = keep.shape
    got, after = lax.optimization_barrier(([clip_swap(part, 1) for part in send], after))
    return plain(fold_kernel, [shape(groups, depth, LANES)] * 4)(keep, *got)


def spread_near(pieces):
    return [pieces[0]] + [near_swap(pieces[step], step) for step in (1, 2, 3)]


def sum_over_devices(first_pieces, second_pieces, send_far, beside_last, finish):
    far = []
    distance = 4
    while distance < lax.axis_size("clip"):
        far.append(distance)
        distance *= 4
    pieces = [*first_pieces, *second_pieces]
    groups = pieces[0].shape[0]
    depth = pieces[0].shape[1] + pieces[4].shape[1]
    left = groups
    sent = None
    for distance in far:
        left //= 4
        fold = functools.partial(fold_four_kernel, len(pieces) // 4)
        pieces = plain(fold, [shape(left, depth, LANES)] * 4)(*pieces)
        if sent is None:
            sent, pieces = send_far(pieces)
        pieces = [pieces[0]] + [clip_swap(pieces[step], step * distance) for step in (1, 2, 3)]
    total = plain(functools.partial(fold_four_kernel, 1), shape(left, depth, LANES))(*pieces)
    for distance in reversed(far):
        pieces = [total] + [clip_swap(total, step * distance) for step in (1, 2, 3)]
        total = plain(join_kernel, shape(4 * total.shape[0], *total.shape[1:]))(*pieces)
    total, sent = lax.optimization_barrier((total, sent))
    pieces = spread_near([total] * 4)
    last = beside_last(sent)
    early, last = lax.optimization_barrier((total, last))
    middle = total.shape[1] // 32 * 16
    parts = [early[:, :middle], early[:, middle:]]
    done = finish(((0, 0), (0, 1)), [parts, [clip_swap(part, 1) for part in parts]], ())
    *pieces, done = lax.optimization_barrier((*pieces, done))
    got = [clip_swap(piece, 1) for piece in pieces[1:]]
    done = finish(((1, 0), (2, 0), (3, 0)), [[piece] for piece in pieces[1:]], done)
    return finish(((1, 1), (2, 1), (3, 1)), [[piece] for piece in got], done), last


def join_kernel(*refs):
    for step in range(4):
        for slot in range(refs[step].shape[0]):
            refs[4][4 * slot + step] = refs[step][slot]


def finish_kernel(jobs, first_call, depths, counts, place_ref, *refs):
    parts = len(jobs) if not first_call else 2 * len(jobs)
    sources, refs = refs[:parts], refs[parts:]
    if not first_call:
        earlier_ref, refs = refs[4], refs[5:]
    outs, refs = refs[:4], refs[4:]
    vectors, refs = refs[: sum(counts)], refs[sum(counts) :]
    kept_ref, stage_a, stage_b, done, *wides = refs
    kept_ref[...] = jnp.zeros(kept_ref.shape, F32) if first_call else earlier_ref[...]
    stores = []
    each = parts // len(jobs)
    for job, (near, side) in enumerate(jobs):
        eighth = eighth_at(place_ref, near, side)
        for far in range(sources[0].shape[0]):
            start = 0
            for source in sources[job * each : (job + 1) * each]:
                stop = start + source.shape[1]
                for stage_ref, low, depth in ((stage_a, 0, depths[0]), (stage_b, depths[0], depths[1])):
                    top, end = max(start, low), min(stop, low + depth)
                    if top < end:
                        first = pl.multiple_of((far ^ (place_ref[1] >> 3)) * depth + (top - low), 16)
                        stage_ref[pl.ds(first, end - top), :] = source[far, top - start : end - start]
                start = stop
        for unit, stage_ref in enumerate((stage_a, stage_b)):
            first = 0
            for at in ((0, 1, 2), (3,))[unit]:
                wide_ref = wides[at].at[job]
                depth, width = wide_ref.shape
                for block in range(width // LANES):
                    wide_ref[:, block * LANES : (block + 1) * LANES] = stage_ref[first : first + depth, :].astype(F32)
                    first += depth
                if at == 1:
                    rows = pl.ds(pl.multiple_of((eighth & 1) * depth, 16), depth)
                    target = outs[at].at[rows, pl.ds(pl.multiple_of((eighth >> 1) * width, LANES), width)]
                else:
                    target = outs[at].at[pl.ds(pl.multiple_of(eighth * depth, 16), depth), :]
                stores.append(pltpu.make_async_copy(wide_ref, target, done.at[len(stores)]))
                stores[-1].start()
            kept_ref[eighth, 16 * unit : 16 * unit + 16] = stage_ref[first : first + 16, :].astype(F32)
    at = 0
    for unit, count in enumerate(counts):
        blocks = [(ref, block) for ref in vectors[at : at + count] for block in range(ref.shape[0] // LANES)]
        at += count
        each = -(-len(blocks) // 8)
        for number, (ref, block) in enumerate(blocks):
            eighth, row = divmod(number, each)
            ref[block * LANES : (block + 1) * LANES] = kept_ref[eighth, 16 * unit + row]
    for store in stores:
        store.wait()


def chunk_rows(count, devices):
    return -(-count // (devices * 16)) * 16


def body(
    tokens,
    masked,
    groups,
    cotangent,
    mask_token,
    gain_one,
    shift_one,
    w_qkv,
    q_bias,
    v_bias,
    w_proj,
    b_proj,
    gain_two,
    shift_two,
    w_up,
    b_up,
    w_down,
    b_down,
):
    copies, half, width = tokens.shape
    hidden = w_up.shape[1]
    hide = masked.shape[1]
    unmasked = 2 * half - hide
    rows = unmasked + EXTRA
    some = unmasked // 2 + EXTRA
    total = rows + some
    tm, clip = lax.axis_index("tm"), lax.axis_index("clip")
    clips = lax.axis_size("clip")
    devices = 2 * clips
    me = (clip & 1) | (tm << 1) | ((clip >> 1) << 2)
    place = jnp.stack([tm, me]).astype(jnp.int32)
    swap = functools.partial(lax.ppermute, axis_name="tm", perm=[(0, 1), (1, 0)])

    def run(kernel, args, outs, scratch=(), scalars=1, limit=20, flops=0, in_hbm=(), out_hbm=(), aliases=None, hides=True):
        moved = sum(math.prod(a.shape) * a.dtype.itemsize for a in list(args) + jax.tree.leaves(outs))
        return pl.pallas_call(
            kernel,
            out_shape=outs,
            in_specs=[
                SMEM if at < scalars else HBM if at in in_hbm else VMEM
                for at in range(len(args))
            ],
            out_specs=[HBM if at in out_hbm else VMEM for at in range(len(outs))] if isinstance(outs, list) else VMEM,
            scratch_shapes=list(scratch),
            input_output_aliases=aliases or {},
            compiler_params=pltpu.CompilerParams(vmem_limit_bytes=limit << 20),
            cost_estimate=pl.CostEstimate(
                flops=flops if hides else 1, bytes_accessed=moved if hides else 1, transcendentals=0
            ),
        )(*args)

    blocks = width // LANES
    counts = ((2 * hidden + width) // 8 * blocks + 16, 3 * width // 8 * blocks + 16)
    depths = [chunk_rows(count, devices // 8) for count in counts]

    def chunked(unit, parts):
        halves = [shape(near, devices // 8, depths[unit], LANES) for near in [4] + [4 // parts] * parts]
        return halves, [pltpu.VMEM((8, devices // 8 * depths[unit], LANES), BF)]

    small = jnp.stack(
        [mask_token, gain_one, shift_one, q_bias, v_bias, b_proj, gain_two, shift_two, b_down]
    ).astype(F32)
    bias_up = b_up.astype(F32).reshape(1, hidden)

    block = shape(rows, width)
    everyone = jnp.concatenate([groups, clip_swap(groups, 1)])
    theirs, rank = run(
        functools.partial(prep_theirs_kernel, unmasked),
        (place, *(pltpu.with_memory_space_constraint(each, pltpu.HBM) for each in (masked, tokens))),
        [shape(unmasked, width), shape(16 * copies, LANES, kind=F32)],
        [pltpu.VMEM(masked.shape, jnp.int32), pltpu.VMEM((half, width), BF), pltpu.SemaphoreType.DMA((2,))],
        flops=2 * rows * half * width,
        in_hbm=(1, 2),
    )
    got_mine = swap(theirs)
    everyone, theirs, rank = lax.optimization_barrier((everyone, theirs, rank))
    everyone = jnp.concatenate([everyone, clip_swap(everyone, 2)])
    shared = run(
        functools.partial(prep_shared_kernel, unmasked),
        (rank, tokens),
        shape(unmasked, width),
        scalars=0,
        flops=2 * rows * half * width,
    )
    got_shared = swap(shared)
    everyone, shared, rank = lax.optimization_barrier((everyone, shared, rank))
    everyone = jnp.concatenate([everyone, clip_swap(everyone, 4)])
    cot_own, cot_send = run(
        functools.partial(prep_grads_kernel, unmasked),
        (place, rank, cotangent),
        [shape(total, width), shape(total - EXTRA, width)],
        flops=2 * copies * rows * half * width,
    )
    everyone, cot_own, cot_send = lax.optimization_barrier((everyone, cot_own, cot_send))
    cot_got = swap(cot_send)

    def attend(sources, got, split):
        queries = some if split else rows
        outs = [
            shape(queries, width), shape(queries, width), block, block,
            shape(HEADS, queries, rows), shape(queries, width, kind=F32), shape(queries, width),
        ]
        if split:
            outs.append(block)
        return run(
            functools.partial(attention_kernel, unmasked, hide, split),
            (place, *sources, got, small, w_qkv),
            outs,
            flops=6 * rows * width * width + 4 * queries * rows * width,
        )

    x_a, q_a, k_a, v_a, e_a, inverse_a, att_a = attend((rank, tokens), got_mine, False)
    everyone, att_a = lax.optimization_barrier((everyone, att_a))
    distance = 8
    while distance < clips:
        everyone = jnp.concatenate([everyone, clip_swap(everyone, distance)])
        distance *= 2
    x_b, q_b, k_b, v_b, e_b, inverse_b, att_b, x_whole = attend((shared,), got_shared, True)

    out_rows, middle, normed_two, active, slope = run(
        forward_kernel,
        (att_a, att_b, x_a, x_b, small, bias_up, w_proj, w_up, w_down),
        [
            shape(total, width), shape(total, width, kind=F32), shape(total, width), shape(total, hidden),
            shape(total, hidden),
        ],
        scalars=0,
        flops=2 * total * width * (width + 2 * hidden),
    )
    out_got = swap(out_rows)
    halves, stage = chunked(0, 4)
    grad_middle, grad_att, keep, *send = run(
        backward_kernel,
        (
            place, groups, everyone.reshape(1, -1), cot_own, cot_got, middle, normed_two, active, slope, att_a, att_b,
            small, w_proj, w_up, w_down,
        ),
        [shape(total, width, kind=F32), shape(total, width)] + halves,
        stage,
        scalars=2,
        hides=False,
    )

    def attend_back(row_from, grads, att, q, k, v, e, inverse):
        return run(
            functools.partial(attention_back_kernel, row_from),
            (grads, att, q, k, v, e, inverse),
            [shape(q.shape[0], width), block, block],
            scalars=0,
            hides=False,
        )

    dq_b, dk_b, dv_b = attend_back(rows, grad_att, att_b, q_b, k_b, v_b, e_b, inverse_b)
    pieces, grad_att = lax.optimization_barrier((sum_cores(keep, send, dq_b), grad_att))
    first_pieces = spread_near(pieces)
    dq_a, dk_a, dv_a = attend_back(0, grad_att, att_a, q_a, k_a, v_a, e_a, inverse_a)
    dq_a, out_got = lax.optimization_barrier((dq_a, out_got))
    halves, stage = chunked(1, 2)
    grad_rows, keep, *send = run(
        functools.partial(inputs_back_kernel, unmasked),
        (place, x_a, x_whole, dq_a, dq_b, dk_a, dk_b, dv_a, dv_b, grad_middle, small, w_qkv),
        [shape(2 * unmasked, width)] + halves,
        stage,
        hides=False,
    )
    pieces, first_pieces = lax.optimization_barrier((sum_cores(keep, send, ()), first_pieces))
    second_pieces = spread_near(pieces)

    def send_rows(pieces):
        *pieces, grads = lax.optimization_barrier((*pieces, grad_rows))
        return swap(grads), pieces

    def place_rows(got):
        return (
            run(functools.partial(outputs_kernel, unmasked), (place, rank, out_rows, out_got), shape(*tokens.shape), hides=False),
            run(functools.partial(grads_out_kernel, unmasked), (place, rank, grad_rows, got), shape(*tokens.shape), hides=False),
        )

    weights = [(hidden, width), (width, hidden), (width, width), (width, 3 * width)]
    slabs = [(hidden // 8, width), (width // 2, hidden // 4), (width // 8, width), (width // 8, 3 * width)]
    vectors = [shape(dim, kind=F32) for dim in [hidden] + [width] * 9]

    def finish(jobs, sources, earlier):
        sources = [part for parts in sources for part in parts]
        last = bool(earlier) and jobs[0][1] == 1
        kept = (8, 32, LANES)
        return run(
            functools.partial(finish_kernel, jobs, not earlier, depths, (5, 5) if last else ()),
            (place, *sources, *earlier),
            [shape(*dims, kind=F32) for dims in weights] + (vectors if last else [shape(*kept, kind=F32)]),
            [pltpu.VMEM(kept, F32)] * last
            + [pltpu.VMEM((devices // 8 * depth, LANES), BF) for depth in depths]
            + [pltpu.SemaphoreType.DMA((4 * len(jobs),))]
            + [pltpu.VMEM((len(jobs), *dims), F32) for dims in slabs],
            in_hbm=range(1 + len(sources), 5 + len(sources)) if earlier else (),
            out_hbm=range(4),
            aliases={1 + len(sources) + at: at for at in range(4)} if earlier else {},
            hides=False,
        )

    (
        (
            grad_w_down, grad_w_up, grad_w_proj, grad_w_qkv,
            grad_b_up, grad_gain_two, grad_shift_two, grad_b_proj, grad_b_down,
            grad_q_bias, grad_v_bias, grad_gain_one, grad_shift_one, grad_mask_token,
        ),
        (block_out, grad_tokens),
    ) = sum_over_devices(first_pieces, second_pieces, send_rows, place_rows, finish)
    return (
        block_out,
        grad_tokens,
        grad_mask_token,
        grad_gain_one,
        grad_shift_one,
        grad_w_qkv,
        grad_q_bias,
        grad_v_bias,
        grad_w_proj,
        grad_b_proj,
        grad_gain_two,
        grad_shift_two,
        grad_w_up,
        grad_b_up,
        grad_w_down,
        grad_b_down,
    )


def solution(mesh):
    return jax.shard_map(
        body,
        mesh=mesh,
        in_specs=(P("clip", "tm", None), P("clip", None), P("clip"), P("clip", "tm", None)) + (P(),) * 14,
        out_specs=(P("clip", "tm", None), P("clip", "tm", None)) + (P(),) * 14,
        check_vma=False,
    )
```

```python
import functools
import math

import jax
import jax.numpy as jnp
import numpy as np
from jax import lax
from jax.experimental import pallas as pl
from jax.experimental.pallas import tpu as pltpu
from jax.sharding import PartitionSpec as P

HEADS = 6
HEAD_DIM = 64
LANES = 128
EXTRA = 16
EPSILON = 1e-06

BF = jnp.bfloat16
F32 = jnp.float32
VMEM = pl.BlockSpec(memory_space=pltpu.VMEM)
SMEM = pl.BlockSpec(memory_space=pltpu.SMEM)
HBM = pl.BlockSpec(memory_space=pltpu.HBM)


def dot(left, right):
    return jnp.dot(left, right, preferred_element_type=F32)


def dot_last(left, right):
    return lax.dot_general(left, right, (((1,), (1,)), ((), ())), preferred_element_type=F32)


def dot_rows(left, right):
    return lax.dot_general(left, right, (((0,), (0,)), ((), ())), preferred_element_type=F32)


def iota(shape, axis):
    return lax.broadcasted_iota(jnp.int32, shape, axis)


def ones_where(condition):
    return jnp.where(condition, 1.0, 0.0).astype(BF)


def column_sums(values):
    return jnp.sum(values, axis=0, keepdims=True)


def shape(*dims, kind=BF):
    return jax.ShapeDtypeStruct(dims, kind)


def plain(kernel, outs):
    return pl.pallas_call(kernel, out_shape=outs, compiler_params=pltpu.CompilerParams(vmem_limit_bytes=8 << 20))


def all_ranks(masked_ref, tm, half, unmasked):
    copies, hide = masked_ref.shape
    blocks = half // LANES
    marks = []
    for copy in range(copies):
        row = masked_ref[copy : copy + 1, :]
        low = ones_where(iota((LANES, hide), 0) == (row & (LANES - 1)))
        high = ones_where(iota((16, hide), 0) == (row >> 7))
        marks.append(dot_last(high, low))
    marks = jnp.concatenate(marks, axis=0)
    count = 16 * copies
    block = iota((count, LANES), 0)
    free = jnp.where((block & 15) < 2 * blocks, 1.0 - marks, 0.0).astype(BF)
    before = ones_where(iota((LANES, LANES), 0) < iota((LANES, LANES), 1))
    within = dot(free, before)
    totals = dot(free, jnp.ones((LANES, LANES), BF)).astype(BF)
    row, column = iota((count, count), 0), iota((count, count), 1)
    earlier = ones_where(jnp.logical_and(column < row, (column >> 4) == (row >> 4)))
    rank = within + dot(earlier, totals)
    rank = jnp.where(marks > 0.5, float(unmasked), rank)
    across = []
    for first in range(0, count, 16):
        mine = jnp.where(tm == 0, rank[first : first + blocks], rank[first + blocks : first + 2 * blocks])
        across.append(jnp.concatenate([mine, jnp.zeros((16 - blocks, LANES), F32)], axis=0))
    return jnp.concatenate(across, axis=0)


def picks(rank, labels):
    wide = jnp.broadcast_to(labels.astype(F32), (labels.shape[0], LANES))
    return jnp.concatenate([ones_where(wide == rank[b : b + 1, :]) for b in range(rank.shape[0])], axis=1)


def ranks_of(rank_ref, copy, half):
    return rank_ref[pl.ds(pl.multiple_of(16 * copy, 16), 16), :][: half // LANES]


def prep_theirs_kernel(
    unmasked, place_ref, masked_ref, tokens_ref, theirs_ref, rank_ref, marks_ref, half_ref, arrived
):
    tm = place_ref[0]
    half = tokens_ref.shape[1]
    load_marks = pltpu.make_async_copy(masked_ref, marks_ref, arrived.at[0])
    load_marks.start()
    load = pltpu.make_async_copy(tokens_ref.at[1 - tm], half_ref, arrived.at[1])
    load.start()
    load_marks.wait()
    rank_ref[...] = all_ranks(marks_ref, tm, half, unmasked)
    chosen = picks(ranks_of(rank_ref, 1 - tm, half), iota((unmasked, 1), 0))
    load.wait()
    theirs_ref[...] = dot(chosen, half_ref[...]).astype(BF)


def prep_shared_kernel(unmasked, rank_ref, tokens_ref, shared_ref):
    chosen = picks(ranks_of(rank_ref, 2, tokens_ref.shape[1]), iota((unmasked, 1), 0))
    shared_ref[...] = dot(chosen, tokens_ref[2]).astype(BF)


def prep_grads_kernel(unmasked, place_ref, rank_ref, cotangent_ref, keep_ref, send_ref):
    tm = place_ref[0]
    half = cotangent_ref.shape[1]
    rows = unmasked + EXTRA
    part = unmasked // 2
    labels = iota((rows, 1), 0)
    small = iota((part + EXTRA, 1), 0)
    theirs = iota((part, 1), 0) + part * (1 - tm)
    own = jnp.where(small < part, small + part * tm, small + part)
    send_ref[:rows, :] = dot(picks(ranks_of(rank_ref, 1 - tm, half), labels), cotangent_ref[1 - tm]).astype(BF)
    chosen = picks(ranks_of(rank_ref, 2, half), jnp.concatenate([theirs, own], axis=0))
    both = dot(chosen, cotangent_ref[2]).astype(BF)
    send_ref[rows:, :] = both[:part]
    keep_ref[rows:, :] = both[part:]
    keep_ref[:rows, :] = dot(picks(ranks_of(rank_ref, tm, half), labels), cotangent_ref[tm]).astype(BF)


def normalise(values):
    centred = values - jnp.mean(values, axis=-1, keepdims=True)
    scale = lax.rsqrt(jnp.mean(centred * centred, axis=-1, keepdims=True) + EPSILON)
    return centred * scale, scale


def bias_terms(count):
    terms, rest = [], math.log(count)
    for _ in range(3):
        terms.append(float(np.asarray(rest).astype(jnp.bfloat16)))
        rest -= terms[-1]
    return terms


def attention_kernel(unmasked, count, split, place_ref, *refs):
    tm = place_ref[0]
    if split:
        own_ref, got_ref, small_ref, w_ref, x_ref, q_ref, k_ref, v_ref, e_ref, inverse_ref, att_ref, whole_ref = refs
        own = own_ref[...].astype(F32)
    else:
        rank_ref, tokens_ref, got_ref, small_ref, w_ref, x_ref, q_ref, k_ref, v_ref, e_ref, inverse_ref, att_ref = refs
        chosen = picks(ranks_of(rank_ref, tm, tokens_ref.shape[1]), iota((unmasked, 1), 0))
        own = dot(chosen, tokens_ref[tm])
    rows, width = k_ref.shape
    extra = jnp.where(iota((EXTRA, width), 0) == 0, small_ref[0:1, :], 0.0)
    x = jnp.concatenate([own + got_ref[...].astype(F32), extra], axis=0)
    hat, _ = normalise(x)
    normed = (hat * small_ref[1:2, :] + small_ref[2:3, :]).astype(BF)
    mixed = dot(normed, w_ref[...])
    query = ((mixed[:, :width] + small_ref[3:4, :]).astype(BF).astype(F32) * HEAD_DIM ** (-0.5)).astype(BF)
    key = mixed[:, width : 2 * width].astype(BF)
    value = (mixed[:, 2 * width :] + small_ref[4:5, :]).astype(BF)
    k_ref[...] = key
    v_ref[...] = value
    x = x.astype(BF)
    if split:
        part = unmasked // 2

        def take(values):
            chosen = jnp.where(tm == 0, values[:part].astype(F32), values[part:unmasked].astype(F32)).astype(BF)
            return jnp.concatenate([chosen, values[unmasked:]], axis=0)

        whole_ref[...] = x
        x, query = take(x), take(query)
    x_ref[...] = x
    q_ref[...] = query
    lane = iota((1, LANES), 1)
    first = lane < HEAD_DIM
    at = iota((rows, LANES), 0)
    place = iota((rows, LANES), 1) & (HEAD_DIM - 1)
    log_count = jnp.zeros((rows, LANES), F32)
    for which, term in enumerate(bias_terms(count)):
        log_count = jnp.where(place == which, term, log_count)
    bias = jnp.where(at < unmasked, 0.0, jnp.where(at == unmasked, log_count, jnp.where(place == 0, -1e30, 0.0)))
    bias = bias.astype(BF)
    ones = jnp.where((lane & (HEAD_DIM - 1)) < 3, 1.0, 0.0).astype(BF)
    all_ones = jnp.ones((rows, LANES), BF)
    for pair in range(width // LANES):
        cols = slice(pair * LANES, (pair + 1) * LANES)
        q_pair, k_pair, v_pair = query[:, cols], key[:, cols], value[:, cols]
        v_wide = jnp.concatenate([v_pair, all_ones], axis=1)
        parts = []
        for side in range(2):
            mine = first if side == 0 else jnp.logical_not(first)
            scores = dot_last(jnp.where(mine, q_pair, ones), jnp.where(mine, k_pair, bias))
            expo = jnp.exp(scores - jnp.max(scores, axis=1, keepdims=True)).astype(BF)
            e_ref[2 * pair + side] = expo
            parts.append(dot(expo, v_wide))
        inverse = 1.0 / jnp.where(first, parts[0][:, LANES:], parts[1][:, LANES:])
        inverse_ref[:, cols] = inverse
        att_ref[:, cols] = (jnp.where(first, parts[0][:, :LANES], parts[1][:, :LANES]) * inverse).astype(BF)


def gelu_terms(hidden):
    below = 0.5 * lax.erf(hidden * 0.5**0.5) + 0.5
    bell = jnp.exp2(hidden * hidden * (-0.5 * math.log2(math.e)))
    return hidden * below, below + hidden * bell * (1.0 / math.sqrt(2.0 * math.pi))


def stacked(refs):
    return jnp.concatenate([ref[...] for ref in refs], axis=0)


def eighth_at(place_ref, near, side):
    me = place_ref[1]
    return ((near ^ ((me >> 1) & 3)) << 1) | (side ^ (me & 1))


def chunk_rows_at(place_ref, far, depth):
    return pl.ds(pl.multiple_of((far ^ (place_ref[1] >> 3)) * depth, 16), depth)


def scatter_chunks(place_ref, stage_ref, keep_ref, send_refs):
    near_places, far_places, depth, _ = keep_ref.shape
    each = send_refs[0].shape[0]
    for near in range(near_places):
        for side in range(2):
            eighth = eighth_at(place_ref, near, side)
            for far in range(far_places):
                chunk = stage_ref[eighth, chunk_rows_at(place_ref, far, depth), :]
                if side:
                    send_refs[near // each][near % each, far] = chunk
                else:
                    keep_ref[near, far] = chunk


def stage_rows(stage_ref, base, grad, total, first=0):
    slab = total // 8
    step = math.gcd(slab, grad.shape[0])
    grad = grad.astype(BF)
    for row in range(0, grad.shape[0], step):
        eighth, offset = divmod(first + row, slab)
        for block in range(grad.shape[1] // LANES):
            at = base + block * slab + offset
            stage_ref[eighth, at : at + step, :] = grad[row : row + step, block * LANES : (block + 1) * LANES]


def stage_columns(stage_ref, base, grad, total, first):
    slab = grad.shape[0] // 2
    grad = grad.astype(BF)
    for block in range(grad.shape[1] // LANES):
        quarter, offset = divmod(first // LANES + block, total // 4 // LANES)
        at = base + offset * slab
        for half in range(2):
            stage_ref[2 * quarter + half, at : at + slab, :] = grad[
                half * slab : (half + 1) * slab, block * LANES : (block + 1) * LANES
            ]


def stage_vectors(stage_ref, base, vectors):
    pieces = [v[:, b * LANES : (b + 1) * LANES] for v in vectors for b in range(v.shape[1] // LANES)]
    each = -(-len(pieces) // 8)
    for eighth in range(8):
        rows = pieces[eighth * each : (eighth + 1) * each]
        rows = rows + [jnp.zeros((16 - len(rows), LANES), F32)]
        stage_ref[eighth, base : base + 16, :] = jnp.concatenate(rows, axis=0).astype(BF)
    clear_rest(stage_ref, base + 16)


def clear_rest(stage_ref, base):
    if base < stage_ref.shape[1]:
        stage_ref[:, base:, :] = jnp.zeros((8, stage_ref.shape[1] - base, LANES), BF)


def forward_kernel(
    att_a, att_b, x_a, x_b, small_ref, bias_up_ref, w_proj_ref, w_up_ref, w_down_ref,
    out_ref, middle_ref, normed_ref, active_ref, slope_ref
):
    attended = stacked((att_a, att_b))
    x = stacked((x_a, x_b)).astype(F32)
    middle = x + dot(attended, w_proj_ref[...]) + small_ref[5:6, :]
    middle_ref[...] = middle
    hat, _ = normalise(middle)
    normed = (hat * small_ref[6:7, :] + small_ref[7:8, :]).astype(BF)
    normed_ref[...] = normed
    result = middle + small_ref[8:9, :]
    width, step = w_up_ref.shape[1], 512
    ahead = dot(normed, w_up_ref[:, :step])
    for first in range(0, width, step):
        cols = slice(first, first + step)
        hidden = ahead + bias_up_ref[:, cols]
        if first + step < width:
            ahead = dot(normed, w_up_ref[:, first + step : first + 2 * step])
        active, slope = gelu_terms(hidden)
        active = active.astype(BF)
        active_ref[:, cols] = active
        slope_ref[:, cols] = slope.astype(BF)
        result = result + dot(active, w_down_ref[cols, :])
    out_ref[...] = result.astype(BF)


def norm_back(grad, hat, scale, gain):
    inner = grad * gain
    mean = jnp.mean(inner, axis=-1, keepdims=True)
    along = jnp.mean(inner * hat, axis=-1, keepdims=True)
    return scale * (inner - mean - hat * along)


def hidden_back_kernel(
    place_ref, groups_ref, everyone_ref, cot_own, cot_got, normed_ref, active_ref, slope_ref, w_down_ref,
    upstream_ref, grad_hidden_ref, sums_ref, keep_ref, *send_refs
):
    *send_refs, stage_ref = send_refs
    total = cot_own.shape[0]
    rows_a = total - cot_got.shape[0] // 3 - EXTRA
    everyone = everyone_ref[...]

    def weight_of(group):
        return 1.0 / jnp.sum(jnp.where(everyone == group, 1.0, 0.0), axis=1, keepdims=True)

    weight = jnp.where(
        iota((total, 1), 0) < rows_a, weight_of(groups_ref[place_ref[0]]), weight_of(groups_ref[2])
    )
    got = jnp.concatenate([cot_got[...].astype(F32), jnp.zeros((EXTRA, cot_got.shape[1]), F32)], axis=0)
    upstream = (cot_own[...].astype(F32) + got) * weight
    upstream_ref[...] = upstream
    grad_result = upstream.astype(BF)
    normed = normed_ref[...]
    hidden, step = active_ref.shape[1], 512
    slab = hidden // 8 * (grad_result.shape[1] // LANES)
    for first in range(0, hidden, step):
        cols = slice(first, first + step)
        grad_hidden = (dot_last(grad_result, w_down_ref[cols, :]) * slope_ref[:, cols].astype(F32)).astype(BF)
        grad_hidden_ref[:, cols] = grad_hidden
        stage_rows(stage_ref, 0, dot_rows(active_ref[:, cols], grad_result), hidden, first)
        sums_ref[:, cols] = column_sums(grad_hidden.astype(F32))
        stage_columns(stage_ref, slab, dot_rows(normed, grad_hidden), hidden, first)
    clear_rest(stage_ref, 2 * slab)
    scatter_chunks(place_ref, stage_ref, keep_ref, send_refs)


def middle_back_kernel(
    place_ref, upstream_ref, grad_hidden_ref, middle_ref, att_a, att_b, small_ref, w_proj_ref, w_up_ref,
    grad_middle_ref, grad_att_ref, sums_ref, keep_ref, send_a, send_b, stage_ref
):
    grad_normed = dot_last(grad_hidden_ref[...], w_up_ref[...])
    hat, scale = normalise(middle_ref[...])
    upstream = upstream_ref[...]
    grad_middle = upstream + norm_back(grad_normed, hat, scale, small_ref[6:7, :])
    grad_middle_ref[...] = grad_middle
    grad_branch = grad_middle.astype(BF)
    grad_att_ref[...] = dot_last(grad_branch, w_proj_ref[...]).astype(BF)
    width = grad_branch.shape[1]
    stage_rows(stage_ref, 0, dot_rows(stacked((att_a, att_b)), grad_branch), width)
    clear_rest(stage_ref, width // 8 * (width // LANES))
    scatter_chunks(place_ref, stage_ref, keep_ref, (send_a, send_b))
    sums_ref[0:1, :] = column_sums(grad_normed * hat)
    sums_ref[1:2, :] = column_sums(grad_normed)
    sums_ref[2:3, :] = column_sums(grad_branch.astype(F32))
    sums_ref[3:4, :] = column_sums(upstream.astype(BF).astype(F32))


def attention_back_kernel(row_from, g_ref, att_ref, q_ref, k_ref, v_ref, e_ref, inverse_ref, dq_ref, dk_ref, dv_ref):
    rows, width = q_ref.shape
    first = iota((1, LANES), 1) < HEAD_DIM
    for pair in range(width // LANES):
        cols = slice(pair * LANES, (pair + 1) * LANES)
        q_pair, k_pair, v_pair = q_ref[:, cols], k_ref[:, cols], v_ref[:, cols]
        g_pair = (g_ref[row_from : row_from + rows, cols].astype(F32) * inverse_ref[:, cols]).astype(BF)
        agree = g_pair.astype(F32) * att_ref[:, cols].astype(F32)
        dq, dk, dv = [], [], []
        for side in range(2):
            mine = first if side == 0 else jnp.logical_not(first)
            correction = jnp.sum(jnp.where(mine, agree, 0.0), axis=1, keepdims=True)
            expo = e_ref[2 * pair + side]
            grad_probs = dot_last(jnp.where(mine, g_pair, jnp.zeros_like(g_pair)), v_pair)
            grad_scores = expo * (grad_probs - correction).astype(BF)
            dq.append(dot(grad_scores, k_pair))
            dk.append(dot_rows(grad_scores, q_pair))
            dv.append(dot_rows(expo, g_pair))
        dq_ref[:, cols] = (jnp.where(first, dq[0], dq[1]) * HEAD_DIM ** (-0.5)).astype(BF)
        dk_ref[:, cols] = jnp.where(first, dk[0], dk[1]).astype(BF)
        dv_ref[:, cols] = jnp.where(first, dv[0], dv[1]).astype(BF)


def inputs_back_kernel(
    unmasked, place_ref, x_a, x_b, dq_a, dq_b, dk_a, dk_b, dv_a, dv_b, grad_middle_ref, small_ref, w_ref,
    up_sums_ref, middle_sums_ref,
    grad_ref, keep_ref, *send_refs
):
    *send_refs, stage_ref = send_refs
    rows, width = x_a.shape
    part = unmasked // 2
    tm = place_ref[0]

    def spread(block):
        wide = block.astype(F32)
        left = jnp.where(tm == 0, wide[:part], 0.0)
        right = jnp.where(tm == 0, 0.0, wide[:part])
        return jnp.concatenate([left, right, wide[part:]], axis=0)

    x = stacked((x_a, x_b)).astype(F32)
    hat, scale = normalise(x)
    gain = small_ref[1:2, :]
    normed = (hat * gain + small_ref[2:3, :]).astype(BF)
    dq = jnp.concatenate([dq_a[...], spread(dq_b[...]).astype(BF)], axis=0)
    mixed = jnp.concatenate([dq, stacked((dk_a, dk_b)), stacked((dv_a, dv_b))], axis=1)
    stage_rows(stage_ref, 0, dot_rows(normed, mixed), width)
    grad_normed = dot_last(mixed, w_ref[...])
    grad = norm_back(grad_normed, hat, scale, gain)
    grad = grad + jnp.concatenate([grad_middle_ref[:rows], spread(grad_middle_ref[rows:])], axis=0)
    grad_ref[:unmasked] = grad[:unmasked].astype(BF)
    grad_ref[unmasked:] = grad[rows : rows + unmasked].astype(BF)
    slab = width // 8 * (mixed.shape[1] // LANES)
    vectors = (
        up_sums_ref[...],
        *(middle_sums_ref[row : row + 1, :] for row in range(4)),
        column_sums(mixed[:, :width].astype(F32)),
        column_sums(mixed[:, 2 * width :].astype(F32)),
        column_sums(grad_normed * hat),
        column_sums(grad_normed),
        grad[unmasked : unmasked + 1] + grad[rows + unmasked : rows + unmasked + 1],
    )
    stage_vectors(stage_ref, slab, vectors)
    scatter_chunks(place_ref, stage_ref, keep_ref, send_refs)


def place_back(rank_ref, copy, rows, half):
    down = jnp.transpose(ranks_of(rank_ref, copy, 16 * LANES))
    labels = jnp.broadcast_to(iota((1, rows), 1).astype(F32), (LANES, rows))
    return jnp.concatenate([ones_where(labels == down[:, b : b + 1]) for b in range(half // LANES)], axis=0)


def outputs_kernel(unmasked, place_ref, rank_ref, own_ref, got_ref, out_ref):
    tm = place_ref[0]
    half = out_ref.shape[1]
    rows = unmasked + EXTRA
    part = unmasked // 2
    out_ref[tm] = dot(place_back(rank_ref, tm, rows, half), own_ref[:rows]).astype(BF)
    out_ref[1 - tm] = dot(place_back(rank_ref, 1 - tm, rows, half), got_ref[:rows]).astype(BF)
    own = own_ref[rows:].astype(F32)
    got = got_ref[rows:].astype(F32)
    left = jnp.where(tm == 0, own[:part], got[:part])
    right = jnp.where(tm == 0, got[:part], own[:part])
    whole = jnp.concatenate([left, right, own[part:]], axis=0).astype(BF)
    out_ref[2] = dot(place_back(rank_ref, 2, rows, half), whole).astype(BF)


def grads_out_kernel(unmasked, place_ref, rank_ref, own_ref, got_ref, out_ref):
    tm = place_ref[0]
    half = out_ref.shape[1]
    out_ref[tm] = dot(place_back(rank_ref, tm, unmasked, half), own_ref[:unmasked]).astype(BF)
    out_ref[1 - tm] = dot(place_back(rank_ref, 1 - tm, unmasked, half), got_ref[:unmasked]).astype(BF)
    whole = (own_ref[unmasked:].astype(F32) + got_ref[unmasked:].astype(F32)).astype(BF)
    out_ref[2] = dot(place_back(rank_ref, 2, unmasked, half), whole).astype(BF)


def fold_kernel(parts, *refs):
    out_refs = refs[-4:]
    first = 0
    for count in parts:
        keep_ref, got_refs, refs = refs[0], refs[1 : 1 + count], refs[1 + count :]
        each = 4 // count
        rows = slice(first, first + keep_ref.shape[2])
        first = rows.stop
        for step, out_ref in enumerate(out_refs):
            got = got_refs[step // each][step % each]
            out_ref[:, rows] = (keep_ref[step].astype(F32) + got.astype(F32)).astype(BF)


def fold_four_kernel(units, *refs):
    outs = refs[4 * units :]
    first = 0
    for unit in range(units):
        total = refs[4 * unit][...].astype(F32)
        for ref in refs[4 * unit + 1 : 4 * unit + 4]:
            total = total + ref[...].astype(F32)
        total = total.astype(BF)
        rows = slice(first, first + total.shape[1])
        first += total.shape[1]
        if len(outs) == 1:
            outs[0][:, rows] = total
        else:
            for step, out_ref in enumerate(outs):
                for slot in range(out_ref.shape[0]):
                    out_ref[slot, rows] = total[4 * slot + step]


def clip_swap(values, distance):
    size = lax.axis_size("clip")
    return lax.ppermute(values, "clip", [(i, i ^ distance) for i in range(size)])


def near_swap(values, step):
    size = lax.axis_size("clip")
    pairs = [
        (t * size + i, (t ^ (step & 1)) * size + (i ^ ((step >> 1) << 1))) for t in range(2) for i in range(size)
    ]
    return lax.ppermute(values, ("tm", "clip"), pairs)


def swap_cores(send):
    return [clip_swap(part, 1) for part in send]


def fold_cores(units):
    _, groups, _, _ = units[0][0].shape
    depth = sum(keep.shape[2] for keep, _ in units)
    kernel = functools.partial(fold_kernel, [len(got) for _, got in units])
    refs = [part for keep, got in units for part in (keep, *got)]
    return plain(kernel, [shape(groups, depth, LANES)] * 4)(*refs)


def spread_near(pieces):
    return [pieces[0]] + [near_swap(pieces[step], step) for step in (1, 2, 3)]


def sum_over_devices(first_pieces, second_pieces, send_far, beside_last, finish):
    far = []
    distance = 4
    while distance < lax.axis_size("clip"):
        far.append(distance)
        distance *= 4
    pieces = [*first_pieces, *second_pieces]
    groups = pieces[0].shape[0]
    depth = pieces[0].shape[1] + pieces[4].shape[1]
    left = groups
    sent = None
    for distance in far:
        left //= 4
        fold = functools.partial(fold_four_kernel, len(pieces) // 4)
        pieces = plain(fold, [shape(left, depth, LANES)] * 4)(*pieces)
        if sent is None:
            sent, pieces = send_far(pieces)
        pieces = [pieces[0]] + [clip_swap(pieces[step], step * distance) for step in (1, 2, 3)]
    total = plain(functools.partial(fold_four_kernel, 1), shape(left, depth, LANES))(*pieces)
    for distance in reversed(far):
        pieces = [total] + [clip_swap(total, step * distance) for step in (1, 2, 3)]
        total = plain(join_kernel, shape(4 * total.shape[0], *total.shape[1:]))(*pieces)
    total, sent = lax.optimization_barrier((total, sent))
    pieces = spread_near([total] * 4)
    last = beside_last(sent)
    early, last = lax.optimization_barrier((total, last))
    middle = total.shape[1] // 32 * 16
    parts = [early[:, :middle], early[:, middle:]]
    done = finish(((0, 0), (0, 1)), [parts, [clip_swap(part, 1) for part in parts]], ())
    *pieces, done = lax.optimization_barrier((*pieces, done))
    got = [clip_swap(piece, 1) for piece in pieces[1:]]
    done = finish(((1, 0), (2, 0), (3, 0)), [[piece] for piece in pieces[1:]], done)
    return finish(((1, 1), (2, 1), (3, 1)), [[piece] for piece in got], done), last


def join_kernel(*refs):
    for step in range(4):
        for slot in range(refs[step].shape[0]):
            refs[4][4 * slot + step] = refs[step][slot]


def finish_kernel(jobs, first_call, depths, vectors, place_ref, *refs):
    parts = len(jobs) if not first_call else 2 * len(jobs)
    sources, refs = refs[:parts], refs[parts:]
    if not first_call:
        earlier_ref, refs = refs[4], refs[5:]
    outs, refs = refs[:4], refs[4:]
    vectors, refs = refs[:vectors], refs[vectors:]
    kept_ref, *stage_refs = refs[: 1 + len(depths)]
    done, *wides = refs[1 + len(depths) :]
    kept_ref[...] = jnp.zeros(kept_ref.shape, F32) if first_call else earlier_ref[...]
    stores = []
    each = parts // len(jobs)
    for job, (near, side) in enumerate(jobs):
        eighth = eighth_at(place_ref, near, side)
        for far in range(sources[0].shape[0]):
            start = 0
            for source in sources[job * each : (job + 1) * each]:
                stop = start + source.shape[1]
                for unit, (stage_ref, depth) in enumerate(zip(stage_refs, depths)):
                    low = sum(depths[:unit])
                    top, end = max(start, low), min(stop, low + depth)
                    if top < end:
                        first = pl.multiple_of((far ^ (place_ref[1] >> 3)) * depth + (top - low), 16)
                        stage_ref[pl.ds(first, end - top), :] = source[far, top - start : end - start]
                start = stop
        for unit, stage_ref in enumerate(stage_refs):
            first = 0
            for at in ((0, 1), (3,), (2,))[unit]:
                wide_ref = wides[at].at[job]
                depth, width = wide_ref.shape
                for block in range(width // LANES):
                    wide_ref[:, block * LANES : (block + 1) * LANES] = stage_ref[first : first + depth, :].astype(F32)
                    first += depth
                if at == 1:
                    rows = pl.ds(pl.multiple_of((eighth & 1) * depth, 16), depth)
                    target = outs[at].at[rows, pl.ds(pl.multiple_of((eighth >> 1) * width, LANES), width)]
                else:
                    target = outs[at].at[pl.ds(pl.multiple_of(eighth * depth, 16), depth), :]
                stores.append(pltpu.make_async_copy(wide_ref, target, done.at[len(stores)]))
                stores[-1].start()
            if unit == 1:
                kept_ref[eighth] = stage_ref[first : first + 16, :].astype(F32)
    blocks = [(ref, block) for ref in vectors for block in range(ref.shape[0] // LANES)]
    each = -(-len(blocks) // 8)
    for number, (ref, block) in enumerate(blocks):
        eighth, row = divmod(number, each)
        ref[block * LANES : (block + 1) * LANES] = kept_ref[eighth, row]
    for store in stores:
        store.wait()


def chunk_rows(count, devices):
    return -(-count // (devices * 16)) * 16


def body(
    tokens,
    masked,
    groups,
    cotangent,
    mask_token,
    gain_one,
    shift_one,
    w_qkv,
    q_bias,
    v_bias,
    w_proj,
    b_proj,
    gain_two,
    shift_two,
    w_up,
    b_up,
    w_down,
    b_down,
):
    copies, half, width = tokens.shape
    hidden = w_up.shape[1]
    hide = masked.shape[1]
    unmasked = 2 * half - hide
    rows = unmasked + EXTRA
    some = unmasked // 2 + EXTRA
    total = rows + some
    tm, clip = lax.axis_index("tm"), lax.axis_index("clip")
    clips = lax.axis_size("clip")
    devices = 2 * clips
    me = (clip & 1) | (tm << 1) | ((clip >> 1) << 2)
    place = jnp.stack([tm, me]).astype(jnp.int32)
    swap = functools.partial(lax.ppermute, axis_name="tm", perm=[(0, 1), (1, 0)])

    def run(kernel, args, outs, scratch=(), scalars=1, limit=20, flops=0, in_hbm=(), out_hbm=(), aliases=None, hides=True):
        moved = sum(math.prod(a.shape) * a.dtype.itemsize for a in list(args) + jax.tree.leaves(outs))
        return pl.pallas_call(
            kernel,
            out_shape=outs,
            in_specs=[
                SMEM if at < scalars else HBM if at in in_hbm else VMEM
                for at in range(len(args))
            ],
            out_specs=[HBM if at in out_hbm else VMEM for at in range(len(outs))] if isinstance(outs, list) else VMEM,
            scratch_shapes=list(scratch),
            input_output_aliases=aliases or {},
            compiler_params=pltpu.CompilerParams(vmem_limit_bytes=limit << 20),
            cost_estimate=pl.CostEstimate(
                flops=flops if hides else 1, bytes_accessed=moved if hides else 1, transcendentals=0
            ),
        )(*args)

    blocks = width // LANES
    counts = (2 * hidden // 8 * blocks, 3 * width // 8 * blocks + 16, width // 8 * blocks)
    depths = [chunk_rows(count, devices // 8) for count in counts]

    def chunked(unit, parts):
        halves = [shape(near, devices // 8, depths[unit], LANES) for near in [4] + [4 // parts] * parts]
        return halves, [pltpu.VMEM((8, devices // 8 * depths[unit], LANES), BF)]

    small = jnp.stack(
        [mask_token, gain_one, shift_one, q_bias, v_bias, b_proj, gain_two, shift_two, b_down]
    ).astype(F32)
    bias_up = b_up.astype(F32).reshape(1, hidden)

    block = shape(rows, width)
    everyone = jnp.concatenate([groups, clip_swap(groups, 1)])
    theirs, rank = run(
        functools.partial(prep_theirs_kernel, unmasked),
        (place, *(pltpu.with_memory_space_constraint(each, pltpu.HBM) for each in (masked, tokens))),
        [shape(unmasked, width), shape(16 * copies, LANES, kind=F32)],
        [pltpu.VMEM(masked.shape, jnp.int32), pltpu.VMEM((half, width), BF), pltpu.SemaphoreType.DMA((2,))],
        flops=2 * rows * half * width,
        in_hbm=(1, 2),
    )
    got_mine = swap(theirs)
    everyone, theirs, rank = lax.optimization_barrier((everyone, theirs, rank))
    everyone = jnp.concatenate([everyone, clip_swap(everyone, 2)])
    shared = run(
        functools.partial(prep_shared_kernel, unmasked),
        (rank, tokens),
        shape(unmasked, width),
        scalars=0,
        flops=2 * rows * half * width,
    )
    got_shared = swap(shared)
    everyone, shared, rank = lax.optimization_barrier((everyone, shared, rank))
    everyone = jnp.concatenate([everyone, clip_swap(everyone, 4)])
    cot_own, cot_send = run(
        functools.partial(prep_grads_kernel, unmasked),
        (place, rank, cotangent),
        [shape(total, width), shape(total - EXTRA, width)],
        flops=2 * copies * rows * half * width,
    )
    everyone, cot_own, cot_send = lax.optimization_barrier((everyone, cot_own, cot_send))
    cot_got = swap(cot_send)

    def attend(sources, got, split):
        queries = some if split else rows
        outs = [
            shape(queries, width), shape(queries, width), block, block,
            shape(HEADS, queries, rows), shape(queries, width, kind=F32), shape(queries, width),
        ]
        if split:
            outs.append(block)
        return run(
            functools.partial(attention_kernel, unmasked, hide, split),
            (place, *sources, got, small, w_qkv),
            outs,
            flops=6 * rows * width * width + 4 * queries * rows * width,
        )

    x_a, q_a, k_a, v_a, e_a, inverse_a, att_a = attend((rank, tokens), got_mine, False)
    everyone, att_a = lax.optimization_barrier((everyone, att_a))
    distance = 8
    while distance < clips:
        everyone = jnp.concatenate([everyone, clip_swap(everyone, distance)])
        distance *= 2
    x_b, q_b, k_b, v_b, e_b, inverse_b, att_b, x_whole = attend((shared,), got_shared, True)

    everyone, att_b = lax.optimization_barrier((everyone, att_b))
    out_rows, middle, normed_two, active, slope = run(
        forward_kernel,
        (att_a, att_b, x_a, x_b, small, bias_up, w_proj, w_up, w_down),
        [
            shape(total, width), shape(total, width, kind=F32), shape(total, width), shape(total, hidden),
            shape(total, hidden),
        ],
        scalars=0,
        flops=2 * total * width * (width + 2 * hidden),
    )
    out_got = swap(out_rows)
    halves, stage = chunked(0, 4)
    upstream, grad_hidden, up_sums, keep, *send = run(
        hidden_back_kernel,
        (place, groups, everyone.reshape(1, -1), cot_own, cot_got, normed_two, active, slope, w_down),
        [shape(total, width, kind=F32), shape(total, hidden), shape(1, hidden, kind=F32)] + halves,
        stage,
        scalars=2,
        hides=False,
    )
    halves, stage = chunked(2, 2)
    grad_middle, grad_att, middle_sums, keep_proj, *send_proj = run(
        middle_back_kernel,
        (place, upstream, grad_hidden, middle, att_a, att_b, small, w_proj, w_up),
        [shape(total, width, kind=F32), shape(total, width), shape(8, width, kind=F32)] + halves,
        stage,
        hides=False,
    )
    got, grad_att = lax.optimization_barrier((swap_cores(send), grad_att))
    pieces, grad_att, send_proj = lax.optimization_barrier((fold_cores([(keep, got)]), grad_att, send_proj))
    first_pieces = spread_near(pieces)

    def attend_back(row_from, grads, att, q, k, v, e, inverse):
        return run(
            functools.partial(attention_back_kernel, row_from),
            (grads, att, q, k, v, e, inverse),
            [shape(q.shape[0], width), block, block],
            scalars=0,
            hides=False,
        )

    dq_b, dk_b, dv_b = attend_back(rows, grad_att, att_b, q_b, k_b, v_b, e_b, inverse_b)
    dq_b, out_got = lax.optimization_barrier((dq_b, out_got))
    dq_a, dk_a, dv_a = attend_back(0, grad_att, att_a, q_a, k_a, v_a, e_a, inverse_a)
    dq_a, got_proj = lax.optimization_barrier((dq_a, swap_cores(send_proj)))
    halves, stage = chunked(1, 2)
    grad_rows, keep, *send = run(
        functools.partial(inputs_back_kernel, unmasked),
        (place, x_a, x_whole, dq_a, dq_b, dk_a, dk_b, dv_a, dv_b, grad_middle, small, w_qkv, up_sums, middle_sums),
        [shape(2 * unmasked, width)] + halves,
        stage,
        hides=False,
    )
    pieces = fold_cores([(keep, swap_cores(send)), (keep_proj, got_proj)])
    pieces, first_pieces = lax.optimization_barrier((pieces, first_pieces))
    second_pieces = spread_near(pieces)

    def send_rows(pieces):
        *pieces, grads = lax.optimization_barrier((*pieces, grad_rows))
        return swap(grads), pieces

    def place_rows(got):
        return (
            run(functools.partial(outputs_kernel, unmasked), (place, rank, out_rows, out_got), shape(*tokens.shape), hides=False),
            run(functools.partial(grads_out_kernel, unmasked), (place, rank, grad_rows, got), shape(*tokens.shape), hides=False),
        )

    weights = [(hidden, width), (width, hidden), (width, width), (width, 3 * width)]
    slabs = [(hidden // 8, width), (width // 2, hidden // 4), (width // 8, width), (width // 8, 3 * width)]
    vectors = [shape(dim, kind=F32) for dim in [hidden] + [width] * 9]

    def finish(jobs, sources, earlier):
        sources = [part for parts in sources for part in parts]
        last = bool(earlier) and jobs[0][1] == 1
        kept = (8, 16, LANES)
        return run(
            functools.partial(finish_kernel, jobs, not earlier, depths, len(vectors) if last else 0),
            (place, *sources, *earlier),
            [shape(*dims, kind=F32) for dims in weights] + (vectors if last else [shape(*kept, kind=F32)]),
            [pltpu.VMEM(kept, F32)] * last
            + [pltpu.VMEM((devices // 8 * depth, LANES), BF) for depth in depths]
            + [pltpu.SemaphoreType.DMA((4 * len(jobs),))]
            + [pltpu.VMEM((len(jobs), *dims), F32) for dims in slabs],
            in_hbm=range(1 + len(sources), 5 + len(sources)) if earlier else (),
            out_hbm=range(4),
            aliases={1 + len(sources) + at: at for at in range(4)} if earlier else {},
            hides=False,
        )

    (
        (
            grad_w_down, grad_w_up, grad_w_proj, grad_w_qkv,
            grad_b_up, grad_gain_two, grad_shift_two, grad_b_proj, grad_b_down,
            grad_q_bias, grad_v_bias, grad_gain_one, grad_shift_one, grad_mask_token,
        ),
        (block_out, grad_tokens),
    ) = sum_over_devices(first_pieces, second_pieces, send_rows, place_rows, finish)
    return (
        block_out,
        grad_tokens,
        grad_mask_token,
        grad_gain_one,
        grad_shift_one,
        grad_w_qkv,
        grad_q_bias,
        grad_v_bias,
        grad_w_proj,
        grad_b_proj,
        grad_gain_two,
        grad_shift_two,
        grad_w_up,
        grad_b_up,
        grad_w_down,
        grad_b_down,
    )


def solution(mesh):
    return jax.shard_map(
        body,
        mesh=mesh,
        in_specs=(P("clip", "tm", None), P("clip", None), P("clip"), P("clip", "tm", None)) + (P(),) * 14,
        out_specs=(P("clip", "tm", None), P("clip", "tm", None)) + (P(),) * 14,
        check_vma=False,
    )
```

```python
import functools
import math

import jax
import jax.numpy as jnp
import numpy as np
from jax import lax
from jax.experimental import pallas as pl
from jax.experimental.pallas import tpu as pltpu
from jax.sharding import PartitionSpec as P

HEADS = 6
HEAD_DIM = 64
LANES = 128
EXTRA = 16
EPSILON = 1e-06

BF = jnp.bfloat16
F32 = jnp.float32
VMEM = pl.BlockSpec(memory_space=pltpu.VMEM)
SMEM = pl.BlockSpec(memory_space=pltpu.SMEM)
HBM = pl.BlockSpec(memory_space=pltpu.HBM)


def dot(left, right):
    return jnp.dot(left, right, preferred_element_type=F32)


def dot_last(left, right):
    return lax.dot_general(left, right, (((1,), (1,)), ((), ())), preferred_element_type=F32)


def dot_rows(left, right):
    return lax.dot_general(left, right, (((0,), (0,)), ((), ())), preferred_element_type=F32)


def iota(shape, axis):
    return lax.broadcasted_iota(jnp.int32, shape, axis)


def ones_where(condition):
    return jnp.where(condition, 1.0, 0.0).astype(BF)


def column_sums(values):
    return jnp.sum(values, axis=0, keepdims=True)


def shape(*dims, kind=BF):
    return jax.ShapeDtypeStruct(dims, kind)


def plain(kernel, outs):
    return pl.pallas_call(kernel, out_shape=outs, compiler_params=pltpu.CompilerParams(vmem_limit_bytes=8 << 20))


def ranks(rows, tm, half, unmasked):
    copies, hide = len(rows), rows[0].shape[1]
    blocks = half // LANES
    marks = []
    for row in rows:
        low = ones_where(iota((LANES, hide), 0) == (row & (LANES - 1)))
        high = ones_where(iota((16, hide), 0) == (row >> 7))
        marks.append(dot_last(high, low))
    marks = jnp.concatenate(marks, axis=0)
    count = 16 * copies
    block = iota((count, LANES), 0)
    free = jnp.where((block & 15) < 2 * blocks, 1.0 - marks, 0.0).astype(BF)
    before = ones_where(iota((LANES, LANES), 0) < iota((LANES, LANES), 1))
    within = dot(free, before)
    totals = dot(free, jnp.ones((LANES, LANES), BF)).astype(BF)
    row, column = iota((count, count), 0), iota((count, count), 1)
    earlier = ones_where(jnp.logical_and(column < row, (column >> 4) == (row >> 4)))
    rank = within + dot(earlier, totals)
    rank = jnp.where(marks > 0.5, float(unmasked), rank)
    across = []
    for first in range(0, count, 16):
        mine = jnp.where(tm == 0, rank[first : first + blocks], rank[first + blocks : first + 2 * blocks])
        across.append(jnp.concatenate([mine, jnp.zeros((16 - blocks, LANES), F32)], axis=0))
    return jnp.concatenate(across, axis=0)


def picks(rank, labels):
    wide = jnp.broadcast_to(labels.astype(F32), (labels.shape[0], LANES))
    return jnp.concatenate([ones_where(wide == rank[b : b + 1, :]) for b in range(rank.shape[0])], axis=1)


def ranks_of(rank_ref, at, half):
    return rank_ref[16 * at : 16 * at + half // LANES, :]


def prep_theirs_kernel(
    unmasked, place_ref, masked_ref, tokens_ref, theirs_ref, rank_ref, marks_ref, half_ref, arrived
):
    tm = place_ref[0]
    half = tokens_ref.shape[1]
    load_marks = pltpu.make_async_copy(masked_ref, marks_ref, arrived.at[0])
    load_marks.start()
    load = pltpu.make_async_copy(tokens_ref.at[1 - tm], half_ref, arrived.at[1])
    load.start()
    load_marks.wait()
    rank = ranks([marks_ref[pl.ds(1 - tm, 1), :]], tm, half, unmasked)
    rank_ref[...] = rank
    chosen = picks(rank[: half // LANES], iota((unmasked, 1), 0))
    load.wait()
    theirs_ref[...] = dot(chosen, half_ref[...]).astype(BF)


def prep_shared_kernel(unmasked, place_ref, masked_ref, tokens_ref, shared_ref, rank_ref):
    tm = place_ref[0]
    half = tokens_ref.shape[1]
    rank = ranks([masked_ref[2:3, :], masked_ref[pl.ds(tm, 1), :]], tm, half, unmasked)
    rank_ref[...] = rank
    shared_ref[...] = dot(picks(rank[: half // LANES], iota((unmasked, 1), 0)), tokens_ref[2]).astype(BF)


def prep_grads_kernel(unmasked, place_ref, theirs_ref, rank_ref, cotangent_ref, keep_ref, send_ref):
    tm = place_ref[0]
    half = cotangent_ref.shape[1]
    rows = unmasked + EXTRA
    part = unmasked // 2
    labels = iota((rows, 1), 0)
    small = iota((part + EXTRA, 1), 0)
    theirs = iota((part, 1), 0) + part * (1 - tm)
    own = jnp.where(small < part, small + part * tm, small + part)
    send_ref[:rows, :] = dot(picks(ranks_of(theirs_ref, 0, half), labels), cotangent_ref[1 - tm]).astype(BF)
    chosen = picks(ranks_of(rank_ref, 0, half), jnp.concatenate([theirs, own], axis=0))
    both = dot(chosen, cotangent_ref[2]).astype(BF)
    send_ref[rows:, :] = both[:part]
    keep_ref[rows:, :] = both[part:]
    keep_ref[:rows, :] = dot(picks(ranks_of(rank_ref, 1, half), labels), cotangent_ref[tm]).astype(BF)


def normalise(values):
    centred = values - jnp.mean(values, axis=-1, keepdims=True)
    scale = lax.rsqrt(jnp.mean(centred * centred, axis=-1, keepdims=True) + EPSILON)
    return centred * scale, scale


def bias_terms(count):
    terms, rest = [], math.log(count)
    for _ in range(3):
        terms.append(float(np.asarray(rest).astype(jnp.bfloat16)))
        rest -= terms[-1]
    return terms


def attention_kernel(unmasked, count, split, place_ref, *refs):
    tm = place_ref[0]
    if split:
        own_ref, got_ref, small_ref, w_ref, x_ref, q_ref, k_ref, v_ref, e_ref, inverse_ref, att_ref, whole_ref = refs
        own = own_ref[...].astype(F32)
    else:
        rank_ref, tokens_ref, got_ref, small_ref, w_ref, x_ref, q_ref, k_ref, v_ref, e_ref, inverse_ref, att_ref = refs
        chosen = picks(ranks_of(rank_ref, 1, tokens_ref.shape[1]), iota((unmasked, 1), 0))
        own = dot(chosen, tokens_ref[tm])
    rows, width = k_ref.shape
    extra = jnp.where(iota((EXTRA, width), 0) == 0, small_ref[0:1, :], 0.0)
    x = jnp.concatenate([own + got_ref[...].astype(F32), extra], axis=0)
    hat, _ = normalise(x)
    normed = (hat * small_ref[1:2, :] + small_ref[2:3, :]).astype(BF)
    mixed = dot(normed, w_ref[...])
    query = ((mixed[:, :width] + small_ref[3:4, :]).astype(BF).astype(F32) * HEAD_DIM ** (-0.5)).astype(BF)
    key = mixed[:, width : 2 * width].astype(BF)
    value = (mixed[:, 2 * width :] + small_ref[4:5, :]).astype(BF)
    k_ref[...] = key
    v_ref[...] = value
    x = x.astype(BF)
    if split:
        part = unmasked // 2

        def take(values):
            chosen = jnp.where(tm == 0, values[:part].astype(F32), values[part:unmasked].astype(F32)).astype(BF)
            return jnp.concatenate([chosen, values[unmasked:]], axis=0)

        whole_ref[...] = x
        x, query = take(x), take(query)
    x_ref[...] = x
    q_ref[...] = query
    lane = iota((1, LANES), 1)
    first = lane < HEAD_DIM
    at = iota((rows, LANES), 0)
    place = iota((rows, LANES), 1) & (HEAD_DIM - 1)
    log_count = jnp.zeros((rows, LANES), F32)
    for which, term in enumerate(bias_terms(count)):
        log_count = jnp.where(place == which, term, log_count)
    bias = jnp.where(at < unmasked, 0.0, jnp.where(at == unmasked, log_count, jnp.where(place == 0, -1e30, 0.0)))
    bias = bias.astype(BF)
    ones = jnp.where((lane & (HEAD_DIM - 1)) < 3, 1.0, 0.0).astype(BF)
    all_ones = jnp.ones((rows, LANES), BF)
    for pair in range(width // LANES):
        cols = slice(pair * LANES, (pair + 1) * LANES)
        q_pair, k_pair, v_pair = query[:, cols], key[:, cols], value[:, cols]
        v_wide = jnp.concatenate([v_pair, all_ones], axis=1)
        parts = []
        for side in range(2):
            mine = first if side == 0 else jnp.logical_not(first)
            scores = dot_last(jnp.where(mine, q_pair, ones), jnp.where(mine, k_pair, bias))
            expo = jnp.exp(scores - jnp.max(scores, axis=1, keepdims=True)).astype(BF)
            e_ref[2 * pair + side] = expo
            parts.append(dot(expo, v_wide))
        inverse = 1.0 / jnp.where(first, parts[0][:, LANES:], parts[1][:, LANES:])
        inverse_ref[:, cols] = inverse
        att_ref[:, cols] = (jnp.where(first, parts[0][:, :LANES], parts[1][:, :LANES]) * inverse).astype(BF)


def gelu_terms(hidden):
    below = 0.5 * lax.erf(hidden * 0.5**0.5) + 0.5
    bell = jnp.exp2(hidden * hidden * (-0.5 * math.log2(math.e)))
    return hidden * below, below + hidden * bell * (1.0 / math.sqrt(2.0 * math.pi))


def stacked(refs):
    return jnp.concatenate([ref[...] for ref in refs], axis=0)


def eighth_at(place_ref, near, side):
    me = place_ref[1]
    return ((near ^ ((me >> 1) & 3)) << 1) | (side ^ (me & 1))


def chunk_rows_at(place_ref, far, depth):
    return pl.ds(pl.multiple_of((far ^ (place_ref[1] >> 3)) * depth, 16), depth)


def scatter_chunks(place_ref, stage_ref, keep_ref, send_refs):
    near_places, far_places, depth, _ = keep_ref.shape
    each = send_refs[0].shape[0]
    for near in range(near_places):
        for side in range(2):
            eighth = eighth_at(place_ref, near, side)
            for far in range(far_places):
                chunk = stage_ref[eighth, chunk_rows_at(place_ref, far, depth), :]
                if side:
                    send_refs[near // each][near % each, far] = chunk
                else:
                    keep_ref[near, far] = chunk


def stage_rows(stage_ref, base, grad, total, first=0):
    slab = total // 8
    step = math.gcd(slab, grad.shape[0])
    grad = grad.astype(BF)
    for row in range(0, grad.shape[0], step):
        eighth, offset = divmod(first + row, slab)
        for block in range(grad.shape[1] // LANES):
            at = base + block * slab + offset
            stage_ref[eighth, at : at + step, :] = grad[row : row + step, block * LANES : (block + 1) * LANES]


def stage_columns(stage_ref, base, grad, total, first):
    slab = grad.shape[0] // 2
    grad = grad.astype(BF)
    for block in range(grad.shape[1] // LANES):
        quarter, offset = divmod(first // LANES + block, total // 4 // LANES)
        at = base + offset * slab
        for half in range(2):
            stage_ref[2 * quarter + half, at : at + slab, :] = grad[
                half * slab : (half + 1) * slab, block * LANES : (block + 1) * LANES
            ]


def stage_vectors(stage_ref, base, vectors):
    pieces = [v[:, b * LANES : (b + 1) * LANES] for v in vectors for b in range(v.shape[1] // LANES)]
    each = -(-len(pieces) // 8)
    for eighth in range(8):
        rows = pieces[eighth * each : (eighth + 1) * each]
        rows = rows + [jnp.zeros((16 - len(rows), LANES), F32)]
        stage_ref[eighth, base : base + 16, :] = jnp.concatenate(rows, axis=0).astype(BF)
    clear_rest(stage_ref, base + 16)


def clear_rest(stage_ref, base):
    if base < stage_ref.shape[1]:
        stage_ref[:, base:, :] = jnp.zeros((8, stage_ref.shape[1] - base, LANES), BF)


def forward_kernel(
    att_a, att_b, x_a, x_b, small_ref, bias_up_ref, w_proj_ref, w_up_ref, w_down_ref,
    out_ref, middle_ref, normed_ref, active_ref, slope_ref
):
    attended = stacked((att_a, att_b))
    x = stacked((x_a, x_b)).astype(F32)
    middle = x + dot(attended, w_proj_ref[...]) + small_ref[5:6, :]
    middle_ref[...] = middle
    hat, _ = normalise(middle)
    normed = (hat * small_ref[6:7, :] + small_ref[7:8, :]).astype(BF)
    normed_ref[...] = normed
    result = middle + small_ref[8:9, :]
    width, step = w_up_ref.shape[1], 512
    ahead = dot(normed, w_up_ref[:, :step])
    for first in range(0, width, step):
        cols = slice(first, first + step)
        hidden = ahead + bias_up_ref[:, cols]
        if first + step < width:
            ahead = dot(normed, w_up_ref[:, first + step : first + 2 * step])
        active, slope = gelu_terms(hidden)
        active = active.astype(BF)
        active_ref[:, cols] = active
        slope_ref[:, cols] = slope.astype(BF)
        result = result + dot(active, w_down_ref[cols, :])
    out_ref[...] = result.astype(BF)


def norm_back(grad, hat, scale, gain):
    inner = grad * gain
    mean = jnp.mean(inner, axis=-1, keepdims=True)
    along = jnp.mean(inner * hat, axis=-1, keepdims=True)
    return scale * (inner - mean - hat * along)


def hidden_back_kernel(
    place_ref, groups_ref, everyone_ref, cot_own, cot_got, normed_ref, active_ref, slope_ref, w_down_ref,
    upstream_ref, grad_hidden_ref, sums_ref, keep_ref, *send_refs
):
    *send_refs, stage_ref = send_refs
    total = cot_own.shape[0]
    rows_a = total - cot_got.shape[0] // 3 - EXTRA
    everyone = everyone_ref[...]

    def weight_of(group):
        return 1.0 / jnp.sum(jnp.where(everyone == group, 1.0, 0.0), axis=1, keepdims=True)

    weight = jnp.where(
        iota((total, 1), 0) < rows_a, weight_of(groups_ref[place_ref[0]]), weight_of(groups_ref[2])
    )
    got = jnp.concatenate([cot_got[...].astype(F32), jnp.zeros((EXTRA, cot_got.shape[1]), F32)], axis=0)
    upstream = (cot_own[...].astype(F32) + got) * weight
    upstream_ref[...] = upstream
    grad_result = upstream.astype(BF)
    normed = normed_ref[...]
    hidden, step = active_ref.shape[1], 512
    slab = hidden // 8 * (grad_result.shape[1] // LANES)
    for first in range(0, hidden, step):
        cols = slice(first, first + step)
        grad_hidden = (dot_last(grad_result, w_down_ref[cols, :]) * slope_ref[:, cols].astype(F32)).astype(BF)
        grad_hidden_ref[:, cols] = grad_hidden
        stage_rows(stage_ref, 0, dot_rows(active_ref[:, cols], grad_result), hidden, first)
        sums_ref[:, cols] = column_sums(grad_hidden.astype(F32))
        stage_columns(stage_ref, slab, dot_rows(normed, grad_hidden), hidden, first)
    clear_rest(stage_ref, 2 * slab)
    scatter_chunks(place_ref, stage_ref, keep_ref, send_refs)


def middle_back_kernel(
    place_ref, upstream_ref, grad_hidden_ref, middle_ref, att_a, att_b, small_ref, w_proj_ref, w_up_ref,
    grad_middle_ref, grad_att_ref, sums_ref, keep_ref, send_a, send_b, stage_ref
):
    grad_normed = dot_last(grad_hidden_ref[...], w_up_ref[...])
    hat, scale = normalise(middle_ref[...])
    upstream = upstream_ref[...]
    grad_middle = upstream + norm_back(grad_normed, hat, scale, small_ref[6:7, :])
    grad_middle_ref[...] = grad_middle
    grad_branch = grad_middle.astype(BF)
    grad_att_ref[...] = dot_last(grad_branch, w_proj_ref[...]).astype(BF)
    width = grad_branch.shape[1]
    stage_rows(stage_ref, 0, dot_rows(stacked((att_a, att_b)), grad_branch), width)
    clear_rest(stage_ref, width // 8 * (width // LANES))
    scatter_chunks(place_ref, stage_ref, keep_ref, (send_a, send_b))
    sums_ref[0:1, :] = column_sums(grad_normed * hat)
    sums_ref[1:2, :] = column_sums(grad_normed)
    sums_ref[2:3, :] = column_sums(grad_branch.astype(F32))
    sums_ref[3:4, :] = column_sums(upstream.astype(BF).astype(F32))


def attention_back_kernel(row_from, g_ref, att_ref, q_ref, k_ref, v_ref, e_ref, inverse_ref, dq_ref, dk_ref, dv_ref):
    rows, width = q_ref.shape
    first = iota((1, LANES), 1) < HEAD_DIM
    for pair in range(width // LANES):
        cols = slice(pair * LANES, (pair + 1) * LANES)
        q_pair, k_pair, v_pair = q_ref[:, cols], k_ref[:, cols], v_ref[:, cols]
        g_pair = (g_ref[row_from : row_from + rows, cols].astype(F32) * inverse_ref[:, cols]).astype(BF)
        agree = g_pair.astype(F32) * att_ref[:, cols].astype(F32)
        dq, dk, dv = [], [], []
        for side in range(2):
            mine = first if side == 0 else jnp.logical_not(first)
            correction = jnp.sum(jnp.where(mine, agree, 0.0), axis=1, keepdims=True)
            expo = e_ref[2 * pair + side]
            grad_probs = dot_last(jnp.where(mine, g_pair, jnp.zeros_like(g_pair)), v_pair)
            grad_scores = expo * (grad_probs - correction).astype(BF)
            dq.append(dot(grad_scores, k_pair))
            dk.append(dot_rows(grad_scores, q_pair))
            dv.append(dot_rows(expo, g_pair))
        dq_ref[:, cols] = (jnp.where(first, dq[0], dq[1]) * HEAD_DIM ** (-0.5)).astype(BF)
        dk_ref[:, cols] = jnp.where(first, dk[0], dk[1]).astype(BF)
        dv_ref[:, cols] = jnp.where(first, dv[0], dv[1]).astype(BF)


def inputs_back_kernel(
    unmasked, place_ref, x_a, x_b, dq_a, dq_b, dk_a, dk_b, dv_a, dv_b, grad_middle_ref, small_ref, w_ref,
    up_sums_ref, middle_sums_ref,
    grad_ref, keep_ref, *send_refs
):
    *send_refs, stage_ref = send_refs
    rows, width = x_a.shape
    part = unmasked // 2
    tm = place_ref[0]

    def spread(block):
        wide = block.astype(F32)
        left = jnp.where(tm == 0, wide[:part], 0.0)
        right = jnp.where(tm == 0, 0.0, wide[:part])
        return jnp.concatenate([left, right, wide[part:]], axis=0)

    x = stacked((x_a, x_b)).astype(F32)
    hat, scale = normalise(x)
    gain = small_ref[1:2, :]
    normed = (hat * gain + small_ref[2:3, :]).astype(BF)
    dq = jnp.concatenate([dq_a[...], spread(dq_b[...]).astype(BF)], axis=0)
    mixed = jnp.concatenate([dq, stacked((dk_a, dk_b)), stacked((dv_a, dv_b))], axis=1)
    stage_rows(stage_ref, 0, dot_rows(normed, mixed), width)
    grad_normed = dot_last(mixed, w_ref[...])
    grad = norm_back(grad_normed, hat, scale, gain)
    grad = grad + jnp.concatenate([grad_middle_ref[:rows], spread(grad_middle_ref[rows:])], axis=0)
    grad_ref[:unmasked] = grad[:unmasked].astype(BF)
    grad_ref[unmasked:] = grad[rows : rows + unmasked].astype(BF)
    slab = width // 8 * (mixed.shape[1] // LANES)
    vectors = (
        up_sums_ref[...],
        *(middle_sums_ref[row : row + 1, :] for row in range(4)),
        column_sums(mixed[:, :width].astype(F32)),
        column_sums(mixed[:, 2 * width :].astype(F32)),
        column_sums(grad_normed * hat),
        column_sums(grad_normed),
        grad[unmasked : unmasked + 1] + grad[rows + unmasked : rows + unmasked + 1],
    )
    stage_vectors(stage_ref, slab, vectors)
    scatter_chunks(place_ref, stage_ref, keep_ref, send_refs)


def place_back(rank_ref, at, rows, half):
    down = jnp.transpose(ranks_of(rank_ref, at, 16 * LANES))
    labels = jnp.broadcast_to(iota((1, rows), 1).astype(F32), (LANES, rows))
    return jnp.concatenate([ones_where(labels == down[:, b : b + 1]) for b in range(half // LANES)], axis=0)


def outputs_kernel(unmasked, place_ref, theirs_ref, rank_ref, own_ref, got_ref, out_ref):
    tm = place_ref[0]
    half = out_ref.shape[1]
    rows = unmasked + EXTRA
    part = unmasked // 2
    out_ref[tm] = dot(place_back(rank_ref, 1, rows, half), own_ref[:rows]).astype(BF)
    out_ref[1 - tm] = dot(place_back(theirs_ref, 0, rows, half), got_ref[:rows]).astype(BF)
    own = own_ref[rows:].astype(F32)
    got = got_ref[rows:].astype(F32)
    left = jnp.where(tm == 0, own[:part], got[:part])
    right = jnp.where(tm == 0, got[:part], own[:part])
    whole = jnp.concatenate([left, right, own[part:]], axis=0).astype(BF)
    out_ref[2] = dot(place_back(rank_ref, 0, rows, half), whole).astype(BF)


def grads_out_kernel(unmasked, place_ref, theirs_ref, rank_ref, own_ref, got_ref, out_ref):
    tm = place_ref[0]
    half = out_ref.shape[1]
    out_ref[tm] = dot(place_back(rank_ref, 1, unmasked, half), own_ref[:unmasked]).astype(BF)
    out_ref[1 - tm] = dot(place_back(theirs_ref, 0, unmasked, half), got_ref[:unmasked]).astype(BF)
    whole = (own_ref[unmasked:].astype(F32) + got_ref[unmasked:].astype(F32)).astype(BF)
    out_ref[2] = dot(place_back(rank_ref, 0, unmasked, half), whole).astype(BF)


def fold_kernel(parts, *refs):
    out_refs = refs[-4:]
    first = 0
    for count in parts:
        keep_ref, got_refs, refs = refs[0], refs[1 : 1 + count], refs[1 + count :]
        each = 4 // count
        rows = slice(first, first + keep_ref.shape[2])
        first = rows.stop
        for step, out_ref in enumerate(out_refs):
            got = got_refs[step // each][step % each]
            out_ref[:, rows] = (keep_ref[step].astype(F32) + got.astype(F32)).astype(BF)


def fold_four_kernel(units, *refs):
    outs = refs[4 * units :]
    first = 0
    for unit in range(units):
        total = refs[4 * unit][...].astype(F32)
        for ref in refs[4 * unit + 1 : 4 * unit + 4]:
            total = total + ref[...].astype(F32)
        total = total.astype(BF)
        rows = slice(first, first + total.shape[1])
        first += total.shape[1]
        if len(outs) == 1:
            outs[0][:, rows] = total
        else:
            for step, out_ref in enumerate(outs):
                for slot in range(out_ref.shape[0]):
                    out_ref[slot, rows] = total[4 * slot + step]


def clip_swap(values, distance):
    size = lax.axis_size("clip")
    return lax.ppermute(values, "clip", [(i, i ^ distance) for i in range(size)])


def near_swap(values, step):
    size = lax.axis_size("clip")
    pairs = [
        (t * size + i, (t ^ (step & 1)) * size + (i ^ ((step >> 1) << 1))) for t in range(2) for i in range(size)
    ]
    return lax.ppermute(values, ("tm", "clip"), pairs)


def swap_cores(send):
    return [clip_swap(part, 1) for part in send]


def fold_cores(units):
    _, groups, _, _ = units[0][0].shape
    depth = sum(keep.shape[2] for keep, _ in units)
    kernel = functools.partial(fold_kernel, [len(got) for _, got in units])
    refs = [part for keep, got in units for part in (keep, *got)]
    return plain(kernel, [shape(groups, depth, LANES)] * 4)(*refs)


def spread_near(pieces):
    return [pieces[0]] + [near_swap(pieces[step], step) for step in (1, 2, 3)]


def sum_over_devices(first_pieces, second_pieces, send_far, beside_last, finish):
    far = []
    distance = 4
    while distance < lax.axis_size("clip"):
        far.append(distance)
        distance *= 4
    pieces = [*first_pieces, *second_pieces]
    groups = pieces[0].shape[0]
    depth = pieces[0].shape[1] + pieces[4].shape[1]
    left = groups
    sent = None
    for distance in far:
        left //= 4
        fold = functools.partial(fold_four_kernel, len(pieces) // 4)
        pieces = plain(fold, [shape(left, depth, LANES)] * 4)(*pieces)
        if sent is None:
            sent, pieces = send_far(pieces)
        pieces = [pieces[0]] + [clip_swap(pieces[step], step * distance) for step in (3, 2, 1)]
    total = plain(functools.partial(fold_four_kernel, 1), shape(left, depth, LANES))(*pieces)
    for distance in reversed(far):
        pieces = [total] + [clip_swap(total, step * distance) for step in (1, 2, 3)]
        total = plain(join_kernel, shape(4 * total.shape[0], *total.shape[1:]))(*pieces)
    total, sent = lax.optimization_barrier((total, sent))
    pieces = spread_near([total] * 4)
    last = beside_last(sent)
    early, last = lax.optimization_barrier((total, last))
    middle = total.shape[1] // 32 * 16
    parts = [early[:, :middle], early[:, middle:]]
    done = finish(((0, 0), (0, 1)), [parts, [clip_swap(part, 1) for part in parts]], ())
    *pieces, done = lax.optimization_barrier((*pieces, done))
    got = [clip_swap(piece, 1) for piece in pieces[1:]]
    done = finish(((1, 0), (2, 0), (3, 0)), [[piece] for piece in pieces[1:]], done)
    return finish(((1, 1), (2, 1), (3, 1)), [[piece] for piece in got], done), last


def join_kernel(*refs):
    for step in range(4):
        for slot in range(refs[step].shape[0]):
            refs[4][4 * slot + step] = refs[step][slot]


def finish_kernel(jobs, first_call, depths, vectors, place_ref, *refs):
    parts = len(jobs) if not first_call else 2 * len(jobs)
    sources, refs = refs[:parts], refs[parts:]
    if not first_call:
        earlier_ref, refs = refs[4], refs[5:]
    outs, refs = refs[:4], refs[4:]
    vectors, refs = refs[:vectors], refs[vectors:]
    kept_ref, *stage_refs = refs[: 1 + len(depths)]
    done, *wides = refs[1 + len(depths) :]
    kept_ref[...] = jnp.zeros(kept_ref.shape, F32) if first_call else earlier_ref[...]
    stores = []
    each = parts // len(jobs)
    for job, (near, side) in enumerate(jobs):
        eighth = eighth_at(place_ref, near, side)
        for far in range(sources[0].shape[0]):
            start = 0
            for source in sources[job * each : (job + 1) * each]:
                stop = start + source.shape[1]
                for unit, (stage_ref, depth) in enumerate(zip(stage_refs, depths)):
                    low = sum(depths[:unit])
                    top, end = max(start, low), min(stop, low + depth)
                    if top < end:
                        first = pl.multiple_of((far ^ (place_ref[1] >> 3)) * depth + (top - low), 16)
                        stage_ref[pl.ds(first, end - top), :] = source[far, top - start : end - start]
                start = stop
        for unit, stage_ref in enumerate(stage_refs):
            first = 0
            for at in ((0, 1), (3,), (2,))[unit]:
                wide_ref = wides[at].at[job]
                depth, width = wide_ref.shape
                for block in range(width // LANES):
                    wide_ref[:, block * LANES : (block + 1) * LANES] = stage_ref[first : first + depth, :].astype(F32)
                    first += depth
                if at == 1:
                    rows = pl.ds(pl.multiple_of((eighth & 1) * depth, 16), depth)
                    target = outs[at].at[rows, pl.ds(pl.multiple_of((eighth >> 1) * width, LANES), width)]
                else:
                    target = outs[at].at[pl.ds(pl.multiple_of(eighth * depth, 16), depth), :]
                stores.append(pltpu.make_async_copy(wide_ref, target, done.at[len(stores)]))
                stores[-1].start()
            if unit == 1:
                kept_ref[eighth] = stage_ref[first : first + 16, :].astype(F32)
    blocks = [(ref, block) for ref in vectors for block in range(ref.shape[0] // LANES)]
    each = -(-len(blocks) // 8)
    for number, (ref, block) in enumerate(blocks):
        eighth, row = divmod(number, each)
        ref[block * LANES : (block + 1) * LANES] = kept_ref[eighth, row]
    for store in stores:
        store.wait()


def chunk_rows(count, devices):
    return -(-count // (devices * 16)) * 16


def body(
    tokens,
    masked,
    groups,
    cotangent,
    mask_token,
    gain_one,
    shift_one,
    w_qkv,
    q_bias,
    v_bias,
    w_proj,
    b_proj,
    gain_two,
    shift_two,
    w_up,
    b_up,
    w_down,
    b_down,
):
    copies, half, width = tokens.shape
    hidden = w_up.shape[1]
    hide = masked.shape[1]
    unmasked = 2 * half - hide
    rows = unmasked + EXTRA
    some = unmasked // 2 + EXTRA
    total = rows + some
    tm, clip = lax.axis_index("tm"), lax.axis_index("clip")
    clips = lax.axis_size("clip")
    devices = 2 * clips
    me = (clip & 1) | (tm << 1) | ((clip >> 1) << 2)
    place = jnp.stack([tm, me]).astype(jnp.int32)
    swap = functools.partial(lax.ppermute, axis_name="tm", perm=[(0, 1), (1, 0)])

    def run(kernel, args, outs, scratch=(), scalars=1, limit=20, flops=0, in_hbm=(), out_hbm=(), aliases=None, hides=True):
        moved = sum(math.prod(a.shape) * a.dtype.itemsize for a in list(args) + jax.tree.leaves(outs))
        return pl.pallas_call(
            kernel,
            out_shape=outs,
            in_specs=[
                SMEM if at < scalars else HBM if at in in_hbm else VMEM
                for at in range(len(args))
            ],
            out_specs=[HBM if at in out_hbm else VMEM for at in range(len(outs))] if isinstance(outs, list) else VMEM,
            scratch_shapes=list(scratch),
            input_output_aliases=aliases or {},
            compiler_params=pltpu.CompilerParams(vmem_limit_bytes=limit << 20),
            cost_estimate=pl.CostEstimate(
                flops=flops if hides else 1, bytes_accessed=moved if hides else 1, transcendentals=0
            ),
        )(*args)

    blocks = width // LANES
    counts = (2 * hidden // 8 * blocks, 3 * width // 8 * blocks + 16, width // 8 * blocks)
    depths = [chunk_rows(count, devices // 8) for count in counts]

    def chunked(unit, parts):
        halves = [shape(near, devices // 8, depths[unit], LANES) for near in [4] + [4 // parts] * parts]
        return halves, [pltpu.VMEM((8, devices // 8 * depths[unit], LANES), BF)]

    small = jnp.stack(
        [mask_token, gain_one, shift_one, q_bias, v_bias, b_proj, gain_two, shift_two, b_down]
    ).astype(F32)
    bias_up = b_up.astype(F32).reshape(1, hidden)

    block = shape(rows, width)
    everyone = jnp.concatenate([groups, clip_swap(groups, 1)])
    theirs, rank_theirs = run(
        functools.partial(prep_theirs_kernel, unmasked),
        (place, *(pltpu.with_memory_space_constraint(each, pltpu.HBM) for each in (masked, tokens))),
        [shape(unmasked, width), shape(16, LANES, kind=F32)],
        [pltpu.VMEM(masked.shape, jnp.int32), pltpu.VMEM((half, width), BF), pltpu.SemaphoreType.DMA((2,))],
        flops=2 * rows * half * width,
        in_hbm=(1, 2),
    )
    got_mine = swap(theirs)
    everyone, theirs, rank_theirs, masked = lax.optimization_barrier((everyone, theirs, rank_theirs, masked))
    everyone = jnp.concatenate([everyone, clip_swap(everyone, 2)])
    shared, rank = run(
        functools.partial(prep_shared_kernel, unmasked),
        (place, masked, tokens),
        [shape(unmasked, width), shape(32, LANES, kind=F32)],
        flops=2 * rows * half * width,
    )
    got_shared = swap(shared)
    everyone, shared, rank = lax.optimization_barrier((everyone, shared, rank))
    everyone = jnp.concatenate([everyone, clip_swap(everyone, 4)])
    cot_own, cot_send = run(
        functools.partial(prep_grads_kernel, unmasked),
        (place, rank_theirs, rank, cotangent),
        [shape(total, width), shape(total - EXTRA, width)],
        flops=2 * copies * rows * half * width,
    )
    everyone, cot_own, cot_send = lax.optimization_barrier((everyone, cot_own, cot_send))
    cot_got = swap(cot_send)

    def attend(sources, got, split):
        queries = some if split else rows
        outs = [
            shape(queries, width), shape(queries, width), block, block,
            shape(HEADS, queries, rows), shape(queries, width, kind=F32), shape(queries, width),
        ]
        if split:
            outs.append(block)
        return run(
            functools.partial(attention_kernel, unmasked, hide, split),
            (place, *sources, got, small, w_qkv),
            outs,
            flops=6 * rows * width * width + 4 * queries * rows * width,
        )

    x_a, q_a, k_a, v_a, e_a, inverse_a, att_a = attend((rank, tokens), got_mine, False)
    everyone, att_a = lax.optimization_barrier((everyone, att_a))
    distance = 8
    while distance < clips:
        everyone = jnp.concatenate([everyone, clip_swap(everyone, distance)])
        distance *= 2
    x_b, q_b, k_b, v_b, e_b, inverse_b, att_b, x_whole = attend((shared,), got_shared, True)

    everyone, att_b = lax.optimization_barrier((everyone, att_b))
    out_rows, middle, normed_two, active, slope = run(
        forward_kernel,
        (att_a, att_b, x_a, x_b, small, bias_up, w_proj, w_up, w_down),
        [
            shape(total, width), shape(total, width, kind=F32), shape(total, width), shape(total, hidden),
            shape(total, hidden),
        ],
        scalars=0,
        flops=2 * total * width * (width + 2 * hidden),
    )
    out_got = swap(out_rows)
    halves, stage = chunked(0, 4)
    upstream, grad_hidden, up_sums, keep, *send = run(
        hidden_back_kernel,
        (place, groups, everyone.reshape(1, -1), cot_own, cot_got, normed_two, active, slope, w_down),
        [shape(total, width, kind=F32), shape(total, hidden), shape(1, hidden, kind=F32)] + halves,
        stage,
        scalars=2,
        hides=False,
    )
    halves, stage = chunked(2, 2)
    grad_middle, grad_att, middle_sums, keep_proj, *send_proj = run(
        middle_back_kernel,
        (place, upstream, grad_hidden, middle, att_a, att_b, small, w_proj, w_up),
        [shape(total, width, kind=F32), shape(total, width), shape(8, width, kind=F32)] + halves,
        stage,
        hides=False,
    )
    got, grad_att = lax.optimization_barrier((swap_cores(send), grad_att))
    pieces, grad_att, send_proj = lax.optimization_barrier((fold_cores([(keep, got)]), grad_att, send_proj))
    first_pieces = spread_near(pieces)

    def attend_back(row_from, grads, att, q, k, v, e, inverse):
        return run(
            functools.partial(attention_back_kernel, row_from),
            (grads, att, q, k, v, e, inverse),
            [shape(q.shape[0], width), block, block],
            scalars=0,
            hides=False,
        )

    dq_b, dk_b, dv_b = attend_back(rows, grad_att, att_b, q_b, k_b, v_b, e_b, inverse_b)
    dq_b, out_got = lax.optimization_barrier((dq_b, out_got))
    dq_a, dk_a, dv_a = attend_back(0, grad_att, att_a, q_a, k_a, v_a, e_a, inverse_a)
    dq_a, got_proj = lax.optimization_barrier((dq_a, swap_cores(send_proj)))
    halves, stage = chunked(1, 2)
    grad_rows, keep, *send = run(
        functools.partial(inputs_back_kernel, unmasked),
        (place, x_a, x_whole, dq_a, dq_b, dk_a, dk_b, dv_a, dv_b, grad_middle, small, w_qkv, up_sums, middle_sums),
        [shape(2 * unmasked, width)] + halves,
        stage,
        hides=False,
    )
    pieces = fold_cores([(keep, swap_cores(send)), (keep_proj, got_proj)])
    pieces, first_pieces = lax.optimization_barrier((pieces, first_pieces))
    second_pieces = spread_near(pieces)

    def send_rows(pieces):
        *pieces, grads = lax.optimization_barrier((*pieces, grad_rows))
        return swap(grads), pieces

    def place_rows(got):
        return (
            run(functools.partial(outputs_kernel, unmasked), (place, rank_theirs, rank, out_rows, out_got), shape(*tokens.shape), hides=False),
            run(functools.partial(grads_out_kernel, unmasked), (place, rank_theirs, rank, grad_rows, got), shape(*tokens.shape), hides=False),
        )

    weights = [(hidden, width), (width, hidden), (width, width), (width, 3 * width)]
    slabs = [(hidden // 8, width), (width // 2, hidden // 4), (width // 8, width), (width // 8, 3 * width)]
    vectors = [shape(dim, kind=F32) for dim in [hidden] + [width] * 9]

    def finish(jobs, sources, earlier):
        sources = [part for parts in sources for part in parts]
        last = bool(earlier) and jobs[0][1] == 1
        kept = (8, 16, LANES)
        return run(
            functools.partial(finish_kernel, jobs, not earlier, depths, len(vectors) if last else 0),
            (place, *sources, *earlier),
            [shape(*dims, kind=F32) for dims in weights] + (vectors if last else [shape(*kept, kind=F32)]),
            [pltpu.VMEM(kept, F32)] * last
            + [pltpu.VMEM((devices // 8 * depth, LANES), BF) for depth in depths]
            + [pltpu.SemaphoreType.DMA((4 * len(jobs),))]
            + [pltpu.VMEM((len(jobs), *dims), F32) for dims in slabs],
            in_hbm=range(1 + len(sources), 5 + len(sources)) if earlier else (),
            out_hbm=range(4),
            aliases={1 + len(sources) + at: at for at in range(4)} if earlier else {},
            hides=False,
        )

    (
        (
            grad_w_down, grad_w_up, grad_w_proj, grad_w_qkv,
            grad_b_up, grad_gain_two, grad_shift_two, grad_b_proj, grad_b_down,
            grad_q_bias, grad_v_bias, grad_gain_one, grad_shift_one, grad_mask_token,
        ),
        (block_out, grad_tokens),
    ) = sum_over_devices(first_pieces, second_pieces, send_rows, place_rows, finish)
    return (
        block_out,
        grad_tokens,
        grad_mask_token,
        grad_gain_one,
        grad_shift_one,
        grad_w_qkv,
        grad_q_bias,
        grad_v_bias,
        grad_w_proj,
        grad_b_proj,
        grad_gain_two,
        grad_shift_two,
        grad_w_up,
        grad_b_up,
        grad_w_down,
        grad_b_down,
    )


def solution(mesh):
    return jax.shard_map(
        body,
        mesh=mesh,
        in_specs=(P("clip", "tm", None), P("clip", None), P("clip"), P("clip", "tm", None)) + (P(),) * 14,
        out_specs=(P("clip", "tm", None), P("clip", "tm", None)) + (P(),) * 14,
        check_vma=False,
    )
```

```python
import functools
import math

import jax
import jax.numpy as jnp
import numpy as np
from jax import lax
from jax.experimental import pallas as pl
from jax.experimental.pallas import tpu as pltpu
from jax.sharding import PartitionSpec as P

HEADS = 6
HEAD_DIM = 64
LANES = 128
EXTRA = 16
EPSILON = 1e-06

BF = jnp.bfloat16
F32 = jnp.float32
VMEM = pl.BlockSpec(memory_space=pltpu.VMEM)
SMEM = pl.BlockSpec(memory_space=pltpu.SMEM)
HBM = pl.BlockSpec(memory_space=pltpu.HBM)


def dot(left, right):
    return jnp.dot(left, right, preferred_element_type=F32)


def dot_last(left, right):
    return lax.dot_general(left, right, (((1,), (1,)), ((), ())), preferred_element_type=F32)


def dot_rows(left, right):
    return lax.dot_general(left, right, (((0,), (0,)), ((), ())), preferred_element_type=F32)


def iota(shape, axis):
    return lax.broadcasted_iota(jnp.int32, shape, axis)


def ones_where(condition):
    return jnp.where(condition, 1.0, 0.0).astype(BF)


def column_sums(values):
    return jnp.sum(values, axis=0, keepdims=True)


def shape(*dims, kind=BF):
    return jax.ShapeDtypeStruct(dims, kind)


def plain(kernel, outs):
    return pl.pallas_call(kernel, out_shape=outs, compiler_params=pltpu.CompilerParams(vmem_limit_bytes=8 << 20))


def ranks(rows, tm, half, unmasked):
    copies, hide = len(rows), rows[0].shape[1]
    blocks = half // LANES
    marks = []
    for row in rows:
        low = ones_where(iota((LANES, hide), 0) == (row & (LANES - 1)))
        high = ones_where(iota((16, hide), 0) == (row >> 7))
        marks.append(dot_last(high, low))
    marks = jnp.concatenate(marks, axis=0)
    count = 16 * copies
    block = iota((count, LANES), 0)
    free = jnp.where((block & 15) < 2 * blocks, 1.0 - marks, 0.0).astype(BF)
    before = ones_where(iota((LANES, LANES), 0) < iota((LANES, LANES), 1))
    within = dot(free, before)
    totals = dot(free, jnp.ones((LANES, LANES), BF)).astype(BF)
    row, column = iota((count, count), 0), iota((count, count), 1)
    earlier = ones_where(jnp.logical_and(column < row, (column >> 4) == (row >> 4)))
    rank = within + dot(earlier, totals)
    rank = jnp.where(marks > 0.5, float(unmasked), rank)
    across = []
    for first in range(0, count, 16):
        mine = jnp.where(tm == 0, rank[first : first + blocks], rank[first + blocks : first + 2 * blocks])
        across.append(jnp.concatenate([mine, jnp.zeros((16 - blocks, LANES), F32)], axis=0))
    return jnp.concatenate(across, axis=0)


def picks(rank, labels):
    wide = jnp.broadcast_to(labels.astype(F32), (labels.shape[0], LANES))
    return jnp.concatenate([ones_where(wide == rank[b : b + 1, :]) for b in range(rank.shape[0])], axis=1)


def ranks_of(rank_ref, at, half):
    return rank_ref[16 * at : 16 * at + half // LANES, :]


def prep_theirs_kernel(
    unmasked, place_ref, masked_ref, tokens_ref, theirs_ref, rank_ref, marks_ref, half_ref, arrived
):
    tm = place_ref[0]
    half = tokens_ref.shape[1]
    load_marks = pltpu.make_async_copy(masked_ref, marks_ref, arrived.at[0])
    load_marks.start()
    load = pltpu.make_async_copy(tokens_ref.at[1 - tm], half_ref, arrived.at[1])
    load.start()
    load_marks.wait()
    rank = ranks([marks_ref[pl.ds(1 - tm, 1), :]], tm, half, unmasked)
    rank_ref[...] = rank
    chosen = picks(rank[: half // LANES], iota((unmasked, 1), 0))
    load.wait()
    theirs_ref[...] = dot(chosen, half_ref[...]).astype(BF)


def prep_shared_kernel(unmasked, place_ref, masked_ref, tokens_ref, shared_ref, rank_ref):
    tm = place_ref[0]
    half = tokens_ref.shape[1]
    rank = ranks([masked_ref[2:3, :], masked_ref[pl.ds(tm, 1), :]], tm, half, unmasked)
    rank_ref[...] = rank
    shared_ref[...] = dot(picks(rank[: half // LANES], iota((unmasked, 1), 0)), tokens_ref[2]).astype(BF)


def prep_grads_kernel(unmasked, place_ref, theirs_ref, rank_ref, cotangent_ref, keep_ref, send_ref):
    tm = place_ref[0]
    half = cotangent_ref.shape[1]
    rows = unmasked + EXTRA
    part = unmasked // 2
    labels = iota((rows, 1), 0)
    small = iota((part + EXTRA, 1), 0)
    theirs = iota((part, 1), 0) + part * (1 - tm)
    own = jnp.where(small < part, small + part * tm, small + part)
    send_ref[:rows, :] = dot(picks(ranks_of(theirs_ref, 0, half), labels), cotangent_ref[1 - tm]).astype(BF)
    chosen = picks(ranks_of(rank_ref, 0, half), jnp.concatenate([theirs, own], axis=0))
    both = dot(chosen, cotangent_ref[2]).astype(BF)
    send_ref[rows:, :] = both[:part]
    keep_ref[rows:, :] = both[part:]
    keep_ref[:rows, :] = dot(picks(ranks_of(rank_ref, 1, half), labels), cotangent_ref[tm]).astype(BF)


def normalise(values):
    centred = values - jnp.mean(values, axis=-1, keepdims=True)
    scale = lax.rsqrt(jnp.mean(centred * centred, axis=-1, keepdims=True) + EPSILON)
    return centred * scale, scale


def bias_terms(count):
    terms, rest = [], math.log(count)
    for _ in range(3):
        terms.append(float(np.asarray(rest).astype(jnp.bfloat16)))
        rest -= terms[-1]
    return terms


def attention_kernel(unmasked, count, split, place_ref, *refs):
    tm = place_ref[0]
    if split:
        own_ref, got_ref, small_ref, w_ref, x_ref, q_ref, k_ref, v_ref, e_ref, inverse_ref, att_ref, whole_ref = refs
        own = own_ref[...].astype(F32)
    else:
        rank_ref, tokens_ref, got_ref, small_ref, w_ref, x_ref, q_ref, k_ref, v_ref, e_ref, inverse_ref, att_ref = refs
        chosen = picks(ranks_of(rank_ref, 1, tokens_ref.shape[1]), iota((unmasked, 1), 0))
        own = dot(chosen, tokens_ref[tm])
    rows, width = k_ref.shape
    extra = jnp.where(iota((EXTRA, width), 0) == 0, small_ref[0:1, :], 0.0)
    x = jnp.concatenate([own + got_ref[...].astype(F32), extra], axis=0)
    hat, _ = normalise(x)
    normed = (hat * small_ref[1:2, :] + small_ref[2:3, :]).astype(BF)
    mixed = dot(normed, w_ref[...])
    query = ((mixed[:, :width] + small_ref[3:4, :]).astype(BF).astype(F32) * HEAD_DIM ** (-0.5)).astype(BF)
    key = mixed[:, width : 2 * width].astype(BF)
    value = (mixed[:, 2 * width :] + small_ref[4:5, :]).astype(BF)
    k_ref[...] = key
    v_ref[...] = value
    x = x.astype(BF)
    if split:
        part = unmasked // 2

        def take(values):
            chosen = jnp.where(tm == 0, values[:part].astype(F32), values[part:unmasked].astype(F32)).astype(BF)
            return jnp.concatenate([chosen, values[unmasked:]], axis=0)

        whole_ref[...] = x
        x, query = take(x), take(query)
    x_ref[...] = x
    q_ref[...] = query
    lane = iota((1, LANES), 1)
    first = lane < HEAD_DIM
    at = iota((rows, LANES), 0)
    place = iota((rows, LANES), 1) & (HEAD_DIM - 1)
    log_count = jnp.zeros((rows, LANES), F32)
    for which, term in enumerate(bias_terms(count)):
        log_count = jnp.where(place == which, term, log_count)
    bias = jnp.where(at < unmasked, 0.0, jnp.where(at == unmasked, log_count, jnp.where(place == 0, -1e30, 0.0)))
    bias = bias.astype(BF)
    ones = jnp.where((lane & (HEAD_DIM - 1)) < 3, 1.0, 0.0).astype(BF)
    all_ones = jnp.ones((rows, LANES), BF)
    for pair in range(width // LANES):
        cols = slice(pair * LANES, (pair + 1) * LANES)
        q_pair, k_pair, v_pair = query[:, cols], key[:, cols], value[:, cols]
        v_wide = jnp.concatenate([v_pair, all_ones], axis=1)
        parts = []
        for side in range(2):
            mine = first if side == 0 else jnp.logical_not(first)
            scores = dot_last(jnp.where(mine, q_pair, ones), jnp.where(mine, k_pair, bias))
            expo = jnp.exp(scores - jnp.max(scores, axis=1, keepdims=True)).astype(BF)
            e_ref[2 * pair + side] = expo
            parts.append(dot(expo, v_wide))
        inverse = 1.0 / jnp.where(first, parts[0][:, LANES:], parts[1][:, LANES:])
        inverse_ref[:, cols] = inverse
        att_ref[:, cols] = (jnp.where(first, parts[0][:, :LANES], parts[1][:, :LANES]) * inverse).astype(BF)


def gelu_terms(hidden):
    below = 0.5 * lax.erf(hidden * 0.5**0.5) + 0.5
    bell = jnp.exp2(hidden * hidden * (-0.5 * math.log2(math.e)))
    return hidden * below, below + hidden * bell * (1.0 / math.sqrt(2.0 * math.pi))


def stacked(refs):
    return jnp.concatenate([ref[...] for ref in refs], axis=0)


def eighth_at(place_ref, near, side):
    me = place_ref[1]
    return ((near ^ ((me >> 1) & 3)) << 1) | (side ^ (me & 1))


def chunk_rows_at(place_ref, far, depth):
    return pl.ds(pl.multiple_of((far ^ (place_ref[1] >> 3)) * depth, 16), depth)


def scatter_chunks(place_ref, stage_ref, keep_ref, send_refs):
    near_places, far_places, depth, _ = keep_ref.shape
    each = send_refs[0].shape[0]
    for near in range(near_places):
        for side in range(2):
            eighth = eighth_at(place_ref, near, side)
            for far in range(far_places):
                chunk = stage_ref[eighth, chunk_rows_at(place_ref, far, depth), :]
                if side:
                    send_refs[near // each][near % each, far] = chunk
                else:
                    keep_ref[near, far] = chunk


def stage_rows(stage_ref, base, grad, total, first=0):
    slab = total // 8
    step = math.gcd(slab, grad.shape[0])
    grad = grad.astype(BF)
    for row in range(0, grad.shape[0], step):
        eighth, offset = divmod(first + row, slab)
        for block in range(grad.shape[1] // LANES):
            at = base + block * slab + offset
            stage_ref[eighth, at : at + step, :] = grad[row : row + step, block * LANES : (block + 1) * LANES]


def stage_columns(stage_ref, base, grad, total, first):
    slab = grad.shape[0] // 2
    grad = grad.astype(BF)
    for block in range(grad.shape[1] // LANES):
        quarter, offset = divmod(first // LANES + block, total // 4 // LANES)
        at = base + offset * slab
        for half in range(2):
            stage_ref[2 * quarter + half, at : at + slab, :] = grad[
                half * slab : (half + 1) * slab, block * LANES : (block + 1) * LANES
            ]


def stage_vectors(stage_ref, base, vectors):
    pieces = [v[:, b * LANES : (b + 1) * LANES] for v in vectors for b in range(v.shape[1] // LANES)]
    each = -(-len(pieces) // 8)
    for eighth in range(8):
        rows = pieces[eighth * each : (eighth + 1) * each]
        rows = rows + [jnp.zeros((16 - len(rows), LANES), F32)]
        stage_ref[eighth, base : base + 16, :] = jnp.concatenate(rows, axis=0).astype(BF)
    clear_rest(stage_ref, base + 16)


def clear_rest(stage_ref, base):
    if base < stage_ref.shape[1]:
        stage_ref[:, base:, :] = jnp.zeros((8, stage_ref.shape[1] - base, LANES), BF)


def forward_kernel(
    att_a, att_b, x_a, x_b, small_ref, bias_up_ref, w_proj_ref, w_up_ref, w_down_ref,
    out_ref, middle_ref, normed_ref, active_ref, slope_ref
):
    attended = stacked((att_a, att_b))
    x = stacked((x_a, x_b)).astype(F32)
    middle = x + dot(attended, w_proj_ref[...]) + small_ref[5:6, :]
    middle_ref[...] = middle
    hat, _ = normalise(middle)
    normed = (hat * small_ref[6:7, :] + small_ref[7:8, :]).astype(BF)
    normed_ref[...] = normed
    result = middle + small_ref[8:9, :]
    width, step = w_up_ref.shape[1], 512
    ahead = dot(normed, w_up_ref[:, :step])
    for first in range(0, width, step):
        cols = slice(first, first + step)
        hidden = ahead + bias_up_ref[:, cols]
        if first + step < width:
            ahead = dot(normed, w_up_ref[:, first + step : first + 2 * step])
        active, slope = gelu_terms(hidden)
        active = active.astype(BF)
        active_ref[:, cols] = active
        slope_ref[:, cols] = slope.astype(BF)
        result = result + dot(active, w_down_ref[cols, :])
    out_ref[...] = result.astype(BF)


def norm_back(grad, hat, scale, gain):
    inner = grad * gain
    mean = jnp.mean(inner, axis=-1, keepdims=True)
    along = jnp.mean(inner * hat, axis=-1, keepdims=True)
    return scale * (inner - mean - hat * along)


def hidden_back_kernel(
    place_ref, groups_ref, everyone_ref, cot_own, cot_got, normed_ref, active_ref, slope_ref, w_down_ref,
    upstream_ref, grad_hidden_ref, sums_ref, keep_ref, *send_refs
):
    *send_refs, stage_ref = send_refs
    total = cot_own.shape[0]
    rows_a = total - cot_got.shape[0] // 3 - EXTRA
    everyone = everyone_ref[...]

    def weight_of(group):
        return 1.0 / jnp.sum(jnp.where(everyone == group, 1.0, 0.0), axis=1, keepdims=True)

    weight = jnp.where(
        iota((total, 1), 0) < rows_a, weight_of(groups_ref[place_ref[0]]), weight_of(groups_ref[2])
    )
    got = jnp.concatenate([cot_got[...].astype(F32), jnp.zeros((EXTRA, cot_got.shape[1]), F32)], axis=0)
    upstream = (cot_own[...].astype(F32) + got) * weight
    upstream_ref[...] = upstream
    grad_result = upstream.astype(BF)
    normed = normed_ref[...]
    hidden, step = active_ref.shape[1], 512
    slab = hidden // 8 * (grad_result.shape[1] // LANES)
    for first in range(0, hidden, step):
        cols = slice(first, first + step)
        grad_hidden = (dot_last(grad_result, w_down_ref[cols, :]) * slope_ref[:, cols].astype(F32)).astype(BF)
        grad_hidden_ref[:, cols] = grad_hidden
        stage_rows(stage_ref, 0, dot_rows(active_ref[:, cols], grad_result), hidden, first)
        sums_ref[:, cols] = column_sums(grad_hidden.astype(F32))
        stage_columns(stage_ref, slab, dot_rows(normed, grad_hidden), hidden, first)
    clear_rest(stage_ref, 2 * slab)
    scatter_chunks(place_ref, stage_ref, keep_ref, send_refs)


def middle_back_kernel(
    place_ref, upstream_ref, grad_hidden_ref, middle_ref, att_a, att_b, small_ref, w_proj_ref, w_up_ref,
    grad_middle_ref, grad_att_ref, sums_ref, keep_ref, send_a, send_b, stage_ref
):
    grad_normed = dot_last(grad_hidden_ref[...], w_up_ref[...])
    hat, scale = normalise(middle_ref[...])
    upstream = upstream_ref[...]
    grad_middle = upstream + norm_back(grad_normed, hat, scale, small_ref[6:7, :])
    grad_middle_ref[...] = grad_middle
    grad_branch = grad_middle.astype(BF)
    grad_att_ref[...] = dot_last(grad_branch, w_proj_ref[...]).astype(BF)
    width = grad_branch.shape[1]
    stage_rows(stage_ref, 0, dot_rows(stacked((att_a, att_b)), grad_branch), width)
    clear_rest(stage_ref, width // 8 * (width // LANES))
    scatter_chunks(place_ref, stage_ref, keep_ref, (send_a, send_b))
    sums_ref[0:1, :] = column_sums(grad_normed * hat)
    sums_ref[1:2, :] = column_sums(grad_normed)
    sums_ref[2:3, :] = column_sums(grad_branch.astype(F32))
    sums_ref[3:4, :] = column_sums(upstream.astype(BF).astype(F32))


def attention_back_kernel(row_from, g_ref, att_ref, q_ref, k_ref, v_ref, e_ref, inverse_ref, dq_ref, dk_ref, dv_ref):
    rows, width = q_ref.shape
    first = iota((1, LANES), 1) < HEAD_DIM
    for pair in range(width // LANES):
        cols = slice(pair * LANES, (pair + 1) * LANES)
        q_pair, k_pair, v_pair = q_ref[:, cols], k_ref[:, cols], v_ref[:, cols]
        g_pair = (g_ref[row_from : row_from + rows, cols].astype(F32) * inverse_ref[:, cols]).astype(BF)
        agree = g_pair.astype(F32) * att_ref[:, cols].astype(F32)
        dq, dk, dv = [], [], []
        for side in range(2):
            mine = first if side == 0 else jnp.logical_not(first)
            correction = jnp.sum(jnp.where(mine, agree, 0.0), axis=1, keepdims=True)
            expo = e_ref[2 * pair + side]
            grad_probs = dot_last(jnp.where(mine, g_pair, jnp.zeros_like(g_pair)), v_pair)
            grad_scores = expo * (grad_probs - correction).astype(BF)
            dq.append(dot(grad_scores, k_pair))
            dk.append(dot_rows(grad_scores, q_pair))
            dv.append(dot_rows(expo, g_pair))
        dq_ref[:, cols] = (jnp.where(first, dq[0], dq[1]) * HEAD_DIM ** (-0.5)).astype(BF)
        dk_ref[:, cols] = jnp.where(first, dk[0], dk[1]).astype(BF)
        dv_ref[:, cols] = jnp.where(first, dv[0], dv[1]).astype(BF)


def inputs_back_kernel(
    unmasked, place_ref, x_a, x_b, dq_a, dq_b, dk_a, dk_b, dv_a, dv_b, grad_middle_ref, small_ref, w_ref,
    up_sums_ref, middle_sums_ref,
    grad_ref, keep_ref, *send_refs
):
    *send_refs, stage_ref = send_refs
    rows, width = x_a.shape
    part = unmasked // 2
    tm = place_ref[0]

    def spread(block):
        wide = block.astype(F32)
        left = jnp.where(tm == 0, wide[:part], 0.0)
        right = jnp.where(tm == 0, 0.0, wide[:part])
        return jnp.concatenate([left, right, wide[part:]], axis=0)

    x = stacked((x_a, x_b)).astype(F32)
    hat, scale = normalise(x)
    gain = small_ref[1:2, :]
    normed = (hat * gain + small_ref[2:3, :]).astype(BF)
    dq = jnp.concatenate([dq_a[...], spread(dq_b[...]).astype(BF)], axis=0)
    mixed = jnp.concatenate([dq, stacked((dk_a, dk_b)), stacked((dv_a, dv_b))], axis=1)
    stage_rows(stage_ref, 0, dot_rows(normed, mixed), width)
    grad_normed = dot_last(mixed, w_ref[...])
    grad = norm_back(grad_normed, hat, scale, gain)
    grad = grad + jnp.concatenate([grad_middle_ref[:rows], spread(grad_middle_ref[rows:])], axis=0)
    grad_ref[:unmasked] = grad[:unmasked].astype(BF)
    grad_ref[unmasked:] = grad[rows : rows + unmasked].astype(BF)
    slab = width // 8 * (mixed.shape[1] // LANES)
    vectors = (
        up_sums_ref[...],
        *(middle_sums_ref[row : row + 1, :] for row in range(4)),
        column_sums(mixed[:, :width].astype(F32)),
        column_sums(mixed[:, 2 * width :].astype(F32)),
        column_sums(grad_normed * hat),
        column_sums(grad_normed),
        grad[unmasked : unmasked + 1] + grad[rows + unmasked : rows + unmasked + 1],
    )
    stage_vectors(stage_ref, slab, vectors)
    scatter_chunks(place_ref, stage_ref, keep_ref, send_refs)


def place_back(rank_ref, at, rows, half):
    down = jnp.transpose(ranks_of(rank_ref, at, 16 * LANES))
    labels = jnp.broadcast_to(iota((1, rows), 1).astype(F32), (LANES, rows))
    return jnp.concatenate([ones_where(labels == down[:, b : b + 1]) for b in range(half // LANES)], axis=0)


def outputs_kernel(unmasked, place_ref, theirs_ref, rank_ref, own_ref, got_ref, out_ref):
    tm = place_ref[0]
    half = out_ref.shape[1]
    rows = unmasked + EXTRA
    part = unmasked // 2
    out_ref[tm] = dot(place_back(rank_ref, 1, rows, half), own_ref[:rows]).astype(BF)
    out_ref[1 - tm] = dot(place_back(theirs_ref, 0, rows, half), got_ref[:rows]).astype(BF)
    own = own_ref[rows:].astype(F32)
    got = got_ref[rows:].astype(F32)
    left = jnp.where(tm == 0, own[:part], got[:part])
    right = jnp.where(tm == 0, got[:part], own[:part])
    whole = jnp.concatenate([left, right, own[part:]], axis=0).astype(BF)
    out_ref[2] = dot(place_back(rank_ref, 0, rows, half), whole).astype(BF)


def grads_out_kernel(unmasked, place_ref, theirs_ref, rank_ref, own_ref, got_ref, out_ref):
    tm = place_ref[0]
    half = out_ref.shape[1]
    out_ref[tm] = dot(place_back(rank_ref, 1, unmasked, half), own_ref[:unmasked]).astype(BF)
    out_ref[1 - tm] = dot(place_back(theirs_ref, 0, unmasked, half), got_ref[:unmasked]).astype(BF)
    whole = (own_ref[unmasked:].astype(F32) + got_ref[unmasked:].astype(F32)).astype(BF)
    out_ref[2] = dot(place_back(rank_ref, 0, unmasked, half), whole).astype(BF)


def fold_kernel(parts, *refs):
    out_refs = refs[-4:]
    first = 0
    for count in parts:
        keep_ref, got_refs, refs = refs[0], refs[1 : 1 + count], refs[1 + count :]
        each = 4 // count
        rows = slice(first, first + keep_ref.shape[2])
        first = rows.stop
        for step, out_ref in enumerate(out_refs):
            got = got_refs[step // each][step % each]
            out_ref[:, rows] = (keep_ref[step].astype(F32) + got.astype(F32)).astype(BF)


def fold_four_kernel(units, *refs):
    outs = refs[4 * units :]
    first = 0
    for unit in range(units):
        total = refs[4 * unit][...].astype(F32)
        for ref in refs[4 * unit + 1 : 4 * unit + 4]:
            total = total + ref[...].astype(F32)
        total = total.astype(BF)
        rows = slice(first, first + total.shape[1])
        first += total.shape[1]
        if len(outs) == 1:
            outs[0][:, rows] = total
        else:
            for step, out_ref in enumerate(outs):
                for slot in range(out_ref.shape[0]):
                    out_ref[slot, rows] = total[4 * slot + step]


def clip_swap(values, distance):
    size = lax.axis_size("clip")
    return lax.ppermute(values, "clip", [(i, i ^ distance) for i in range(size)])


def near_swap(values, step):
    size = lax.axis_size("clip")
    pairs = [
        (t * size + i, (t ^ (step & 1)) * size + (i ^ ((step >> 1) << 1))) for t in range(2) for i in range(size)
    ]
    return lax.ppermute(values, ("tm", "clip"), pairs)


def swap_cores(send):
    return [clip_swap(part, 1) for part in send]


def fold_cores(units):
    _, groups, _, _ = units[0][0].shape
    depth = sum(keep.shape[2] for keep, _ in units)
    kernel = functools.partial(fold_kernel, [len(got) for _, got in units])
    refs = [part for keep, got in units for part in (keep, *got)]
    return plain(kernel, [shape(groups, depth, LANES)] * 4)(*refs)


def spread_near(pieces):
    return [pieces[0]] + [near_swap(pieces[step], step) for step in (1, 2, 3)]


def sum_over_devices(first_pieces, second_pieces, send_far, beside_last, finish):
    far = []
    distance = 4
    while distance < lax.axis_size("clip"):
        far.append(distance)
        distance *= 4
    pieces = [*first_pieces, *second_pieces]
    groups = pieces[0].shape[0]
    depth = pieces[0].shape[1] + pieces[4].shape[1]
    left = groups
    sent = None
    for distance in far:
        left //= 4
        fold = functools.partial(fold_four_kernel, len(pieces) // 4)
        pieces = plain(fold, [shape(left, depth, LANES)] * 4)(*pieces)
        if sent is None:
            sent, pieces = send_far(pieces)
        pieces = [pieces[0]] + [clip_swap(pieces[step], step * distance) for step in (3, 2, 1)]
    total = plain(functools.partial(fold_four_kernel, 1), shape(left, depth, LANES))(*pieces)
    for distance in reversed(far):
        pieces = [total] + [clip_swap(total, step * distance) for step in (1, 2, 3)]
        total = plain(join_kernel, shape(4 * total.shape[0], *total.shape[1:]))(*pieces)
    total, sent = lax.optimization_barrier((total, sent))
    pieces = spread_near([total] * 4)
    last = beside_last(sent)
    early, last = lax.optimization_barrier((total, last))
    middle = total.shape[1] // 32 * 16
    parts = [early[:, :middle], early[:, middle:]]
    got_parts = [clip_swap(part, 1) for part in parts]
    done = finish(((0, 0), (0, 1)), [parts, got_parts], (), ())
    *pieces, done = lax.optimization_barrier((*pieces, done))
    own = [[piece] for piece in pieces[1:]]
    got = [[clip_swap(piece, 1)] for piece in pieces[1:]]
    done = finish(((1, 0), (2, 0), (3, 0)), own, done, ())
    return finish(((1, 1), (2, 1), (3, 1)), got, done, [parts, got_parts, *own]), last


def join_kernel(*refs):
    for step in range(4):
        for slot in range(refs[step].shape[0]):
            refs[4][4 * slot + step] = refs[step][slot]


def finish_kernel(jobs, counts, extra_jobs, extra_counts, first_call, depths, base, vectors, place_ref, *refs):
    def take(counts):
        nonlocal refs
        taken = []
        for count in counts:
            taken.append(refs[:count])
            refs = refs[count:]
        return taken

    sources, extra_sources = take(counts), take(extra_counts)
    if not first_call:
        take((4,))
    outs, vector_outs, stage_refs, (done,), wides, (kept_ref,), flat_refs = take(
        (4, vectors, len(depths), 1, 4, 1, vectors)
    )
    stores = []

    def store(source, target):
        stores.append(pltpu.make_async_copy(source, target, done.at[len(stores)]))
        stores[-1].start()

    if vectors:
        number, offset = divmod(base, depths[1])
        for (near, side), parts in zip(jobs + extra_jobs, sources + extra_sources):
            start = 0
            for part in parts:
                row = depths[0] + offset - start
                if 0 <= row < part.shape[1]:
                    rows = part[number ^ (place_ref[1] >> 3), row : row + 16]
                    kept_ref[eighth_at(place_ref, near, side)] = rows.astype(F32)
                start += part.shape[1]
        blocks = [(ref, block) for ref in flat_refs for block in range(ref.shape[0] // LANES)]
        each = -(-len(blocks) // 8)
        for at, (ref, block) in enumerate(blocks):
            eighth, row = divmod(at, each)
            ref[block * LANES : (block + 1) * LANES] = kept_ref[eighth, row]
        for flat_ref, out_ref in zip(flat_refs, vector_outs):
            store(flat_ref, out_ref)
    for job, ((near, side), parts) in enumerate(zip(jobs, sources)):
        eighth = eighth_at(place_ref, near, side)
        for far in range(parts[0].shape[0]):
            start = 0
            for part in parts:
                stop = start + part.shape[1]
                for unit, (stage_ref, depth) in enumerate(zip(stage_refs, depths)):
                    low = sum(depths[:unit])
                    top, end = max(start, low), min(stop, low + depth)
                    if top < end:
                        first = pl.multiple_of((far ^ (place_ref[1] >> 3)) * depth + (top - low), 16)
                        stage_ref[pl.ds(first, end - top), :] = part[far, top - start : end - start]
                start = stop
        for unit, stage_ref in enumerate(stage_refs):
            first = 0
            for at in ((0, 1), (3,), (2,))[unit]:
                wide_ref = wides[at].at[job]
                depth, width = wide_ref.shape
                for block in range(width // LANES):
                    wide_ref[:, block * LANES : (block + 1) * LANES] = stage_ref[first : first + depth, :].astype(F32)
                    first += depth
                if at == 1:
                    rows = pl.ds(pl.multiple_of((eighth & 1) * depth, 16), depth)
                    target = outs[at].at[rows, pl.ds(pl.multiple_of((eighth >> 1) * width, LANES), width)]
                else:
                    target = outs[at].at[pl.ds(pl.multiple_of(eighth * depth, 16), depth), :]
                store(wide_ref, target)
    for each in stores:
        each.wait()


def chunk_rows(count, devices):
    return -(-count // (devices * 16)) * 16


def body(
    tokens,
    masked,
    groups,
    cotangent,
    mask_token,
    gain_one,
    shift_one,
    w_qkv,
    q_bias,
    v_bias,
    w_proj,
    b_proj,
    gain_two,
    shift_two,
    w_up,
    b_up,
    w_down,
    b_down,
):
    copies, half, width = tokens.shape
    hidden = w_up.shape[1]
    hide = masked.shape[1]
    unmasked = 2 * half - hide
    rows = unmasked + EXTRA
    some = unmasked // 2 + EXTRA
    total = rows + some
    tm, clip = lax.axis_index("tm"), lax.axis_index("clip")
    clips = lax.axis_size("clip")
    devices = 2 * clips
    me = (clip & 1) | (tm << 1) | ((clip >> 1) << 2)
    place = jnp.stack([tm, me]).astype(jnp.int32)
    swap = functools.partial(lax.ppermute, axis_name="tm", perm=[(0, 1), (1, 0)])

    def run(kernel, args, outs, scratch=(), scalars=1, limit=20, flops=0, in_hbm=(), out_hbm=(), aliases=None, hides=True):
        moved = sum(math.prod(a.shape) * a.dtype.itemsize for a in list(args) + jax.tree.leaves(outs))
        return pl.pallas_call(
            kernel,
            out_shape=outs,
            in_specs=[
                SMEM if at < scalars else HBM if at in in_hbm else VMEM
                for at in range(len(args))
            ],
            out_specs=[HBM if at in out_hbm else VMEM for at in range(len(outs))] if isinstance(outs, list) else VMEM,
            scratch_shapes=list(scratch),
            input_output_aliases=aliases or {},
            compiler_params=pltpu.CompilerParams(vmem_limit_bytes=limit << 20),
            cost_estimate=pl.CostEstimate(
                flops=flops if hides else 1, bytes_accessed=moved if hides else 1, transcendentals=0
            ),
        )(*args)

    blocks = width // LANES
    counts = (2 * hidden // 8 * blocks, 3 * width // 8 * blocks + 16, width // 8 * blocks)
    depths = [chunk_rows(count, devices // 8) for count in counts]

    def chunked(unit, parts):
        halves = [shape(near, devices // 8, depths[unit], LANES) for near in [4] + [4 // parts] * parts]
        return halves, [pltpu.VMEM((8, devices // 8 * depths[unit], LANES), BF)]

    small = jnp.stack(
        [mask_token, gain_one, shift_one, q_bias, v_bias, b_proj, gain_two, shift_two, b_down]
    ).astype(F32)
    bias_up = b_up.astype(F32).reshape(1, hidden)

    block = shape(rows, width)
    everyone = jnp.concatenate([groups, clip_swap(groups, 1)])
    theirs, rank_theirs = run(
        functools.partial(prep_theirs_kernel, unmasked),
        (place, *(pltpu.with_memory_space_constraint(each, pltpu.HBM) for each in (masked, tokens))),
        [shape(unmasked, width), shape(16, LANES, kind=F32)],
        [pltpu.VMEM(masked.shape, jnp.int32), pltpu.VMEM((half, width), BF), pltpu.SemaphoreType.DMA((2,))],
        flops=2 * rows * half * width,
        in_hbm=(1, 2),
    )
    got_mine = swap(theirs)
    everyone, theirs, rank_theirs, masked = lax.optimization_barrier((everyone, theirs, rank_theirs, masked))
    everyone = jnp.concatenate([everyone, clip_swap(everyone, 2)])
    shared, rank = run(
        functools.partial(prep_shared_kernel, unmasked),
        (place, masked, tokens),
        [shape(unmasked, width), shape(32, LANES, kind=F32)],
        flops=2 * rows * half * width,
    )
    got_shared = swap(shared)
    everyone, shared, rank = lax.optimization_barrier((everyone, shared, rank))
    everyone = jnp.concatenate([everyone, clip_swap(everyone, 4)])
    cot_own, cot_send = run(
        functools.partial(prep_grads_kernel, unmasked),
        (place, rank_theirs, rank, cotangent),
        [shape(total, width), shape(total - EXTRA, width)],
        flops=2 * copies * rows * half * width,
    )
    everyone, cot_own, cot_send = lax.optimization_barrier((everyone, cot_own, cot_send))
    cot_got = swap(cot_send)

    def attend(sources, got, split):
        queries = some if split else rows
        outs = [
            shape(queries, width), shape(queries, width), block, block,
            shape(HEADS, queries, rows), shape(queries, width, kind=F32), shape(queries, width),
        ]
        if split:
            outs.append(block)
        return run(
            functools.partial(attention_kernel, unmasked, hide, split),
            (place, *sources, got, small, w_qkv),
            outs,
            flops=6 * rows * width * width + 4 * queries * rows * width,
        )

    x_a, q_a, k_a, v_a, e_a, inverse_a, att_a = attend((rank, tokens), got_mine, False)
    everyone, att_a = lax.optimization_barrier((everyone, att_a))
    distance = 8
    while distance < clips:
        everyone = jnp.concatenate([everyone, clip_swap(everyone, distance)])
        distance *= 2
    x_b, q_b, k_b, v_b, e_b, inverse_b, att_b, x_whole = attend((shared,), got_shared, True)

    everyone, att_b = lax.optimization_barrier((everyone, att_b))
    out_rows, middle, normed_two, active, slope = run(
        forward_kernel,
        (att_a, att_b, x_a, x_b, small, bias_up, w_proj, w_up, w_down),
        [
            shape(total, width), shape(total, width, kind=F32), shape(total, width), shape(total, hidden),
            shape(total, hidden),
        ],
        scalars=0,
        flops=2 * total * width * (width + 2 * hidden),
    )
    out_got = swap(out_rows)
    halves, stage = chunked(0, 4)
    upstream, grad_hidden, up_sums, keep, *send = run(
        hidden_back_kernel,
        (place, groups, everyone.reshape(1, -1), cot_own, cot_got, normed_two, active, slope, w_down),
        [shape(total, width, kind=F32), shape(total, hidden), shape(1, hidden, kind=F32)] + halves,
        stage,
        scalars=2,
        hides=False,
    )
    halves, stage = chunked(2, 2)
    grad_middle, grad_att, middle_sums, keep_proj, *send_proj = run(
        middle_back_kernel,
        (place, upstream, grad_hidden, middle, att_a, att_b, small, w_proj, w_up),
        [shape(total, width, kind=F32), shape(total, width), shape(8, width, kind=F32)] + halves,
        stage,
        hides=False,
    )
    got, grad_att = lax.optimization_barrier((swap_cores(send), grad_att))
    pieces, grad_att, send_proj = lax.optimization_barrier((fold_cores([(keep, got)]), grad_att, send_proj))
    first_pieces = spread_near(pieces)

    def attend_back(row_from, grads, att, q, k, v, e, inverse):
        return run(
            functools.partial(attention_back_kernel, row_from),
            (grads, att, q, k, v, e, inverse),
            [shape(q.shape[0], width), block, block],
            scalars=0,
            hides=False,
        )

    dq_b, dk_b, dv_b = attend_back(rows, grad_att, att_b, q_b, k_b, v_b, e_b, inverse_b)
    dq_b, out_got = lax.optimization_barrier((dq_b, out_got))
    dq_a, dk_a, dv_a = attend_back(0, grad_att, att_a, q_a, k_a, v_a, e_a, inverse_a)
    dq_a, got_proj = lax.optimization_barrier((dq_a, swap_cores(send_proj)))
    halves, stage = chunked(1, 2)
    grad_rows, keep, *send = run(
        functools.partial(inputs_back_kernel, unmasked),
        (place, x_a, x_whole, dq_a, dq_b, dk_a, dk_b, dv_a, dv_b, grad_middle, small, w_qkv, up_sums, middle_sums),
        [shape(2 * unmasked, width)] + halves,
        stage,
        hides=False,
    )
    pieces = fold_cores([(keep, swap_cores(send)), (keep_proj, got_proj)])
    pieces, first_pieces = lax.optimization_barrier((pieces, first_pieces))
    second_pieces = spread_near(pieces)

    def send_rows(pieces):
        *pieces, grads = lax.optimization_barrier((*pieces, grad_rows))
        return swap(grads), pieces

    def place_rows(got):
        return (
            run(functools.partial(outputs_kernel, unmasked), (place, rank_theirs, rank, out_rows, out_got), shape(*tokens.shape), hides=False),
            run(functools.partial(grads_out_kernel, unmasked), (place, rank_theirs, rank, grad_rows, got), shape(*tokens.shape), hides=False),
        )

    weights = [(hidden, width), (width, hidden), (width, width), (width, 3 * width)]
    slabs = [(hidden // 8, width), (width // 2, hidden // 4), (width // 8, width), (width // 8, 3 * width)]
    vectors = [shape(dim, kind=F32) for dim in [hidden] + [width] * 9]

    def finish(jobs, sources, earlier, extra_sources):
        extra_jobs = ((0, 0), (0, 1), (1, 0), (2, 0), (3, 0)) if extra_sources else ()
        refs = [part for parts in [*sources, *extra_sources] for part in parts]
        flat = vectors if extra_sources else []
        kernel = functools.partial(
            finish_kernel,
            jobs,
            [len(parts) for parts in sources],
            extra_jobs,
            [len(parts) for parts in extra_sources],
            not earlier,
            depths,
            counts[1] - 16,
            len(flat),
        )
        return run(
            kernel,
            (place, *refs, *earlier),
            [shape(*dims, kind=F32) for dims in weights] + flat,
            [pltpu.VMEM((devices // 8 * depth, LANES), BF) for depth in depths]
            + [pltpu.SemaphoreType.DMA((4 * len(jobs) + len(flat),))]
            + [pltpu.VMEM((len(jobs), *dims), F32) for dims in slabs]
            + [pltpu.VMEM((8, 16, LANES), F32)]
            + [pltpu.VMEM(each.shape, F32) for each in flat],
            in_hbm=range(1 + len(refs), 5 + len(refs)) if earlier else (),
            out_hbm=range(4 + len(flat)),
            aliases={1 + len(refs) + at: at for at in range(4)} if earlier else {},
            hides=False,
        )

    (
        (
            grad_w_down, grad_w_up, grad_w_proj, grad_w_qkv,
            grad_b_up, grad_gain_two, grad_shift_two, grad_b_proj, grad_b_down,
            grad_q_bias, grad_v_bias, grad_gain_one, grad_shift_one, grad_mask_token,
        ),
        (block_out, grad_tokens),
    ) = sum_over_devices(first_pieces, second_pieces, send_rows, place_rows, finish)
    return (
        block_out,
        grad_tokens,
        grad_mask_token,
        grad_gain_one,
        grad_shift_one,
        grad_w_qkv,
        grad_q_bias,
        grad_v_bias,
        grad_w_proj,
        grad_b_proj,
        grad_gain_two,
        grad_shift_two,
        grad_w_up,
        grad_b_up,
        grad_w_down,
        grad_b_down,
    )


def solution(mesh):
    return jax.shard_map(
        body,
        mesh=mesh,
        in_specs=(P("clip", "tm", None), P("clip", None), P("clip"), P("clip", "tm", None)) + (P(),) * 14,
        out_specs=(P("clip", "tm", None), P("clip", "tm", None)) + (P(),) * 14,
        check_vma=False,
    )
```

```python
import functools
import math

import jax
import jax.numpy as jnp
import numpy as np
from jax import lax
from jax.experimental import pallas as pl
from jax.experimental.pallas import tpu as pltpu
from jax.sharding import PartitionSpec as P

HEADS = 6
HEAD_DIM = 64
LANES = 128
EXTRA = 16
EPSILON = 1e-06

BF = jnp.bfloat16
F32 = jnp.float32
VMEM = pl.BlockSpec(memory_space=pltpu.VMEM)
SMEM = pl.BlockSpec(memory_space=pltpu.SMEM)
HBM = pl.BlockSpec(memory_space=pltpu.HBM)


def dot(left, right):
    return jnp.dot(left, right, preferred_element_type=F32)


def dot_last(left, right):
    return lax.dot_general(left, right, (((1,), (1,)), ((), ())), preferred_element_type=F32)


def dot_rows(left, right):
    return lax.dot_general(left, right, (((0,), (0,)), ((), ())), preferred_element_type=F32)


def iota(shape, axis):
    return lax.broadcasted_iota(jnp.int32, shape, axis)


def ones_where(condition):
    return jnp.where(condition, 1.0, 0.0).astype(BF)


def column_sums(values):
    return jnp.sum(values, axis=0, keepdims=True)


def shape(*dims, kind=BF):
    return jax.ShapeDtypeStruct(dims, kind)


def plain(kernel, outs):
    return pl.pallas_call(kernel, out_shape=outs, compiler_params=pltpu.CompilerParams(vmem_limit_bytes=8 << 20))


def ranks(rows, tm, half, unmasked):
    copies, hide = len(rows), rows[0].shape[1]
    blocks = half // LANES
    marks = []
    for row in rows:
        low = ones_where(iota((LANES, hide), 0) == (row & (LANES - 1)))
        high = ones_where(iota((16, hide), 0) == (row >> 7))
        marks.append(dot_last(high, low))
    marks = jnp.concatenate(marks, axis=0)
    count = 16 * copies
    block = iota((count, LANES), 0)
    free = jnp.where((block & 15) < 2 * blocks, 1.0 - marks, 0.0).astype(BF)
    before = ones_where(iota((LANES, LANES), 0) < iota((LANES, LANES), 1))
    within = dot(free, before)
    totals = dot(free, jnp.ones((LANES, LANES), BF)).astype(BF)
    row, column = iota((count, count), 0), iota((count, count), 1)
    earlier = ones_where(jnp.logical_and(column < row, (column >> 4) == (row >> 4)))
    rank = within + dot(earlier, totals)
    rank = jnp.where(marks > 0.5, float(unmasked), rank)
    across = []
    for first in range(0, count, 16):
        mine = jnp.where(tm == 0, rank[first : first + blocks], rank[first + blocks : first + 2 * blocks])
        across.append(jnp.concatenate([mine, jnp.zeros((16 - blocks, LANES), F32)], axis=0))
    return jnp.concatenate(across, axis=0)


def picks(rank, labels):
    wide = jnp.broadcast_to(labels.astype(F32), (labels.shape[0], LANES))
    return jnp.concatenate([ones_where(wide == rank[b : b + 1, :]) for b in range(rank.shape[0])], axis=1)


def ranks_of(rank_ref, at, half):
    return rank_ref[16 * at : 16 * at + half // LANES, :]


def prep_theirs_kernel(
    unmasked, place_ref, masked_ref, tokens_ref, theirs_ref, rank_ref, marks_ref, half_ref, arrived
):
    tm = place_ref[0]
    half = tokens_ref.shape[1]
    load_marks = pltpu.make_async_copy(masked_ref, marks_ref, arrived.at[0])
    load_marks.start()
    load = pltpu.make_async_copy(tokens_ref.at[1 - tm], half_ref, arrived.at[1])
    load.start()
    load_marks.wait()
    rank = ranks([marks_ref[pl.ds(1 - tm, 1), :]], tm, half, unmasked)
    rank_ref[...] = rank
    chosen = picks(rank[: half // LANES], iota((unmasked, 1), 0))
    load.wait()
    theirs_ref[...] = dot(chosen, half_ref[...]).astype(BF)


def prep_shared_kernel(unmasked, place_ref, masked_ref, tokens_ref, shared_ref, rank_ref):
    tm = place_ref[0]
    half = tokens_ref.shape[1]
    rank = ranks([masked_ref[2:3, :], masked_ref[pl.ds(tm, 1), :]], tm, half, unmasked)
    rank_ref[...] = rank
    shared_ref[...] = dot(picks(rank[: half // LANES], iota((unmasked, 1), 0)), tokens_ref[2]).astype(BF)


def prep_grads_kernel(unmasked, place_ref, theirs_ref, rank_ref, cotangent_ref, keep_ref, send_ref):
    tm = place_ref[0]
    half = cotangent_ref.shape[1]
    rows = unmasked + EXTRA
    part = unmasked // 2
    labels = iota((rows, 1), 0)
    small = iota((part + EXTRA, 1), 0)
    theirs = iota((part, 1), 0) + part * (1 - tm)
    own = jnp.where(small < part, small + part * tm, small + part)
    send_ref[:rows, :] = dot(picks(ranks_of(theirs_ref, 0, half), labels), cotangent_ref[1 - tm]).astype(BF)
    chosen = picks(ranks_of(rank_ref, 0, half), jnp.concatenate([theirs, own], axis=0))
    both = dot(chosen, cotangent_ref[2]).astype(BF)
    send_ref[rows:, :] = both[:part]
    keep_ref[rows:, :] = both[part:]
    keep_ref[:rows, :] = dot(picks(ranks_of(rank_ref, 1, half), labels), cotangent_ref[tm]).astype(BF)


def normalise(values):
    centred = values - jnp.mean(values, axis=-1, keepdims=True)
    scale = lax.rsqrt(jnp.mean(centred * centred, axis=-1, keepdims=True) + EPSILON)
    return centred * scale, scale


def bias_terms(count):
    terms, rest = [], math.log(count)
    for _ in range(3):
        terms.append(float(np.asarray(rest).astype(jnp.bfloat16)))
        rest -= terms[-1]
    return terms


def attention_kernel(unmasked, count, split, place_ref, *refs):
    tm = place_ref[0]
    if split:
        own_ref, got_ref, small_ref, w_ref, x_ref, q_ref, k_ref, v_ref, e_ref, inverse_ref, att_ref, whole_ref = refs
        own = own_ref[...].astype(F32)
    else:
        rank_ref, tokens_ref, got_ref, small_ref, w_ref, x_ref, q_ref, k_ref, v_ref, e_ref, inverse_ref, att_ref = refs
        chosen = picks(ranks_of(rank_ref, 1, tokens_ref.shape[1]), iota((unmasked, 1), 0))
        own = dot(chosen, tokens_ref[tm])
    rows, width = k_ref.shape
    extra = jnp.where(iota((EXTRA, width), 0) == 0, small_ref[0:1, :], 0.0)
    x = jnp.concatenate([own + got_ref[...].astype(F32), extra], axis=0)
    hat, _ = normalise(x)
    normed = (hat * small_ref[1:2, :] + small_ref[2:3, :]).astype(BF)
    mixed = dot(normed, w_ref[...])
    query = ((mixed[:, :width] + small_ref[3:4, :]).astype(BF).astype(F32) * HEAD_DIM ** (-0.5)).astype(BF)
    key = mixed[:, width : 2 * width].astype(BF)
    value = (mixed[:, 2 * width :] + small_ref[4:5, :]).astype(BF)
    k_ref[...] = key
    v_ref[...] = value
    x = x.astype(BF)
    if split:
        part = unmasked // 2

        def take(values):
            chosen = jnp.where(tm == 0, values[:part].astype(F32), values[part:unmasked].astype(F32)).astype(BF)
            return jnp.concatenate([chosen, values[unmasked:]], axis=0)

        whole_ref[...] = x
        x, query = take(x), take(query)
    x_ref[...] = x
    q_ref[...] = query
    lane = iota((1, LANES), 1)
    first = lane < HEAD_DIM
    at = iota((rows, LANES), 0)
    place = iota((rows, LANES), 1) & (HEAD_DIM - 1)
    log_count = jnp.zeros((rows, LANES), F32)
    for which, term in enumerate(bias_terms(count)):
        log_count = jnp.where(place == which, term, log_count)
    bias = jnp.where(at < unmasked, 0.0, jnp.where(at == unmasked, log_count, jnp.where(place == 0, -1e30, 0.0)))
    bias = bias.astype(BF)
    ones = jnp.where((lane & (HEAD_DIM - 1)) < 3, 1.0, 0.0).astype(BF)
    all_ones = jnp.ones((rows, LANES), BF)
    for pair in range(width // LANES):
        cols = slice(pair * LANES, (pair + 1) * LANES)
        q_pair, k_pair, v_pair = query[:, cols], key[:, cols], value[:, cols]
        v_wide = jnp.concatenate([v_pair, all_ones], axis=1)
        parts = []
        for side in range(2):
            mine = first if side == 0 else jnp.logical_not(first)
            scores = dot_last(jnp.where(mine, q_pair, ones), jnp.where(mine, k_pair, bias))
            expo = jnp.exp(scores - jnp.max(scores, axis=1, keepdims=True)).astype(BF)
            e_ref[2 * pair + side] = expo
            parts.append(dot(expo, v_wide))
        inverse = 1.0 / jnp.where(first, parts[0][:, LANES:], parts[1][:, LANES:])
        inverse_ref[:, cols] = inverse
        att_ref[:, cols] = (jnp.where(first, parts[0][:, :LANES], parts[1][:, :LANES]) * inverse).astype(BF)


def gelu_terms(hidden):
    below = 0.5 * lax.erf(hidden * 0.5**0.5) + 0.5
    bell = jnp.exp2(hidden * hidden * (-0.5 * math.log2(math.e)))
    return hidden * below, below + hidden * bell * (1.0 / math.sqrt(2.0 * math.pi))


def stacked(refs):
    return jnp.concatenate([ref[...] for ref in refs], axis=0)


def eighth_at(place_ref, near, side):
    me = place_ref[1]
    return ((near ^ ((me >> 1) & 3)) << 1) | (side ^ (me & 1))


def chunk_rows_at(place_ref, far, depth):
    return pl.ds(pl.multiple_of((far ^ (place_ref[1] >> 3)) * depth, 16), depth)


def scatter_chunks(place_ref, stage_ref, keep_ref, send_refs):
    near_places, far_places, depth, _ = keep_ref.shape
    each = send_refs[0].shape[0]
    for near in range(near_places):
        for side in range(2):
            eighth = eighth_at(place_ref, near, side)
            for far in range(far_places):
                chunk = stage_ref[eighth, chunk_rows_at(place_ref, far, depth), :]
                if side:
                    send_refs[near // each][near % each, far] = chunk
                else:
                    keep_ref[near, far] = chunk


def stage_rows(stage_ref, base, grad, total, first=0):
    slab = total // 8
    step = math.gcd(slab, grad.shape[0])
    grad = grad.astype(BF)
    for row in range(0, grad.shape[0], step):
        eighth, offset = divmod(first + row, slab)
        for block in range(grad.shape[1] // LANES):
            at = base + block * slab + offset
            stage_ref[eighth, at : at + step, :] = grad[row : row + step, block * LANES : (block + 1) * LANES]


def stage_columns(stage_ref, base, grad, total, first):
    slab = grad.shape[0] // 2
    grad = grad.astype(BF)
    for block in range(grad.shape[1] // LANES):
        quarter, offset = divmod(first // LANES + block, total // 4 // LANES)
        at = base + offset * slab
        for half in range(2):
            stage_ref[2 * quarter + half, at : at + slab, :] = grad[
                half * slab : (half + 1) * slab, block * LANES : (block + 1) * LANES
            ]


def stage_vectors(stage_ref, base, vectors):
    pieces = [v[:, b * LANES : (b + 1) * LANES] for v in vectors for b in range(v.shape[1] // LANES)]
    each = -(-len(pieces) // 8)
    for eighth in range(8):
        rows = pieces[eighth * each : (eighth + 1) * each]
        rows = rows + [jnp.zeros((16 - len(rows), LANES), F32)]
        stage_ref[eighth, base : base + 16, :] = jnp.concatenate(rows, axis=0).astype(BF)
    clear_rest(stage_ref, base + 16)


def clear_rest(stage_ref, base):
    if base < stage_ref.shape[1]:
        stage_ref[:, base:, :] = jnp.zeros((8, stage_ref.shape[1] - base, LANES), BF)


def forward_kernel(
    att_a, att_b, x_a, x_b, small_ref, bias_up_ref, w_proj_ref, w_up_ref, w_down_ref,
    out_ref, middle_ref, normed_ref, active_ref, slope_ref
):
    attended = stacked((att_a, att_b))
    x = stacked((x_a, x_b)).astype(F32)
    middle = x + dot(attended, w_proj_ref[...]) + small_ref[5:6, :]
    middle_ref[...] = middle
    hat, _ = normalise(middle)
    normed = (hat * small_ref[6:7, :] + small_ref[7:8, :]).astype(BF)
    normed_ref[...] = normed
    result = middle + small_ref[8:9, :]
    width, step = w_up_ref.shape[1], 512
    ahead = dot(normed, w_up_ref[:, :step])
    for first in range(0, width, step):
        cols = slice(first, first + step)
        hidden = ahead + bias_up_ref[:, cols]
        if first + step < width:
            ahead = dot(normed, w_up_ref[:, first + step : first + 2 * step])
        active, slope = gelu_terms(hidden)
        active = active.astype(BF)
        active_ref[:, cols] = active
        slope_ref[:, cols] = slope.astype(BF)
        result = result + dot(active, w_down_ref[cols, :])
    out_ref[...] = result.astype(BF)


def norm_back(grad, hat, scale, gain):
    inner = grad * gain
    mean = jnp.mean(inner, axis=-1, keepdims=True)
    along = jnp.mean(inner * hat, axis=-1, keepdims=True)
    return scale * (inner - mean - hat * along)


def hidden_back_kernel(
    place_ref, groups_ref, everyone_ref, cot_own, cot_got, normed_ref, active_ref, slope_ref, w_down_ref,
    upstream_ref, grad_hidden_ref, sums_ref, keep_ref, *send_refs
):
    *send_refs, stage_ref = send_refs
    total = cot_own.shape[0]
    rows_a = total - cot_got.shape[0] // 3 - EXTRA
    everyone = everyone_ref[...]

    def weight_of(group):
        return 1.0 / jnp.sum(jnp.where(everyone == group, 1.0, 0.0), axis=1, keepdims=True)

    weight = jnp.where(
        iota((total, 1), 0) < rows_a, weight_of(groups_ref[place_ref[0]]), weight_of(groups_ref[2])
    )
    got = jnp.concatenate([cot_got[...].astype(F32), jnp.zeros((EXTRA, cot_got.shape[1]), F32)], axis=0)
    upstream = (cot_own[...].astype(F32) + got) * weight
    upstream_ref[...] = upstream
    grad_result = upstream.astype(BF)
    normed = normed_ref[...]
    hidden, step = active_ref.shape[1], 512
    slab = hidden // 8 * (grad_result.shape[1] // LANES)
    for first in range(0, hidden, step):
        cols = slice(first, first + step)
        grad_hidden = (dot_last(grad_result, w_down_ref[cols, :]) * slope_ref[:, cols].astype(F32)).astype(BF)
        grad_hidden_ref[:, cols] = grad_hidden
        stage_rows(stage_ref, 0, dot_rows(active_ref[:, cols], grad_result), hidden, first)
        sums_ref[:, cols] = column_sums(grad_hidden.astype(F32))
        stage_columns(stage_ref, slab, dot_rows(normed, grad_hidden), hidden, first)
    clear_rest(stage_ref, 2 * slab)
    scatter_chunks(place_ref, stage_ref, keep_ref, send_refs)


def middle_back_kernel(
    place_ref, upstream_ref, grad_hidden_ref, middle_ref, att_a, att_b, small_ref, w_proj_ref, w_up_ref,
    grad_middle_ref, grad_att_ref, sums_ref, keep_ref, send_a, send_b, stage_ref
):
    grad_normed = dot_last(grad_hidden_ref[...], w_up_ref[...])
    hat, scale = normalise(middle_ref[...])
    upstream = upstream_ref[...]
    grad_middle = upstream + norm_back(grad_normed, hat, scale, small_ref[6:7, :])
    grad_middle_ref[...] = grad_middle
    grad_branch = grad_middle.astype(BF)
    grad_att_ref[...] = dot_last(grad_branch, w_proj_ref[...]).astype(BF)
    width = grad_branch.shape[1]
    stage_rows(stage_ref, 0, dot_rows(stacked((att_a, att_b)), grad_branch), width)
    clear_rest(stage_ref, width // 8 * (width // LANES))
    scatter_chunks(place_ref, stage_ref, keep_ref, (send_a, send_b))
    sums_ref[0:1, :] = column_sums(grad_normed * hat)
    sums_ref[1:2, :] = column_sums(grad_normed)
    sums_ref[2:3, :] = column_sums(grad_branch.astype(F32))
    sums_ref[3:4, :] = column_sums(upstream.astype(BF).astype(F32))


def attention_back_kernel(row_from, g_ref, att_ref, q_ref, k_ref, v_ref, e_ref, inverse_ref, dq_ref, dk_ref, dv_ref):
    rows, width = q_ref.shape
    first = iota((1, LANES), 1) < HEAD_DIM
    for pair in range(width // LANES):
        cols = slice(pair * LANES, (pair + 1) * LANES)
        q_pair, k_pair, v_pair = q_ref[:, cols], k_ref[:, cols], v_ref[:, cols]
        g_pair = (g_ref[row_from : row_from + rows, cols].astype(F32) * inverse_ref[:, cols]).astype(BF)
        agree = g_pair.astype(F32) * att_ref[:, cols].astype(F32)
        dq, dk, dv = [], [], []
        for side in range(2):
            mine = first if side == 0 else jnp.logical_not(first)
            correction = jnp.sum(jnp.where(mine, agree, 0.0), axis=1, keepdims=True)
            expo = e_ref[2 * pair + side]
            grad_probs = dot_last(jnp.where(mine, g_pair, jnp.zeros_like(g_pair)), v_pair)
            grad_scores = expo * (grad_probs - correction).astype(BF)
            dq.append(dot(grad_scores, k_pair))
            dk.append(dot_rows(grad_scores, q_pair))
            dv.append(dot_rows(expo, g_pair))
        dq_ref[:, cols] = (jnp.where(first, dq[0], dq[1]) * HEAD_DIM ** (-0.5)).astype(BF)
        dk_ref[:, cols] = jnp.where(first, dk[0], dk[1]).astype(BF)
        dv_ref[:, cols] = jnp.where(first, dv[0], dv[1]).astype(BF)


def inputs_back_kernel(
    unmasked, place_ref, x_a, x_b, dq_a, dq_b, dk_a, dk_b, dv_a, dv_b, grad_middle_ref, small_ref, w_ref,
    up_sums_ref, middle_sums_ref,
    grad_ref, keep_ref, *send_refs
):
    *send_refs, stage_ref = send_refs
    rows, width = x_a.shape
    part = unmasked // 2
    tm = place_ref[0]

    def spread(block):
        wide = block.astype(F32)
        left = jnp.where(tm == 0, wide[:part], 0.0)
        right = jnp.where(tm == 0, 0.0, wide[:part])
        return jnp.concatenate([left, right, wide[part:]], axis=0)

    x = stacked((x_a, x_b)).astype(F32)
    hat, scale = normalise(x)
    gain = small_ref[1:2, :]
    normed = (hat * gain + small_ref[2:3, :]).astype(BF)
    dq = jnp.concatenate([dq_a[...], spread(dq_b[...]).astype(BF)], axis=0)
    mixed = jnp.concatenate([dq, stacked((dk_a, dk_b)), stacked((dv_a, dv_b))], axis=1)
    stage_rows(stage_ref, 0, dot_rows(normed, mixed), width)
    grad_normed = dot_last(mixed, w_ref[...])
    grad = norm_back(grad_normed, hat, scale, gain)
    grad = grad + jnp.concatenate([grad_middle_ref[:rows], spread(grad_middle_ref[rows:])], axis=0)
    grad_ref[:unmasked] = grad[:unmasked].astype(BF)
    grad_ref[unmasked:] = grad[rows : rows + unmasked].astype(BF)
    slab = width // 8 * (mixed.shape[1] // LANES)
    vectors = (
        up_sums_ref[...],
        *(middle_sums_ref[row : row + 1, :] for row in range(4)),
        column_sums(mixed[:, :width].astype(F32)),
        column_sums(mixed[:, 2 * width :].astype(F32)),
        column_sums(grad_normed * hat),
        column_sums(grad_normed),
        grad[unmasked : unmasked + 1] + grad[rows + unmasked : rows + unmasked + 1],
    )
    stage_vectors(stage_ref, slab, vectors)
    scatter_chunks(place_ref, stage_ref, keep_ref, send_refs)


def place_back(rank_ref, at, rows, half):
    down = jnp.transpose(ranks_of(rank_ref, at, 16 * LANES))
    labels = jnp.broadcast_to(iota((1, rows), 1).astype(F32), (LANES, rows))
    return jnp.concatenate([ones_where(labels == down[:, b : b + 1]) for b in range(half // LANES)], axis=0)


def outputs_kernel(unmasked, place_ref, theirs_ref, rank_ref, own_ref, got_ref, out_ref):
    tm = place_ref[0]
    half = out_ref.shape[1]
    rows = unmasked + EXTRA
    part = unmasked // 2
    out_ref[tm] = dot(place_back(rank_ref, 1, rows, half), own_ref[:rows]).astype(BF)
    out_ref[1 - tm] = dot(place_back(theirs_ref, 0, rows, half), got_ref[:rows]).astype(BF)
    own = own_ref[rows:].astype(F32)
    got = got_ref[rows:].astype(F32)
    left = jnp.where(tm == 0, own[:part], got[:part])
    right = jnp.where(tm == 0, got[:part], own[:part])
    whole = jnp.concatenate([left, right, own[part:]], axis=0).astype(BF)
    out_ref[2] = dot(place_back(rank_ref, 0, rows, half), whole).astype(BF)


def grads_out_kernel(unmasked, place_ref, theirs_ref, rank_ref, own_ref, got_ref, out_ref):
    tm = place_ref[0]
    half = out_ref.shape[1]
    out_ref[tm] = dot(place_back(rank_ref, 1, unmasked, half), own_ref[:unmasked]).astype(BF)
    out_ref[1 - tm] = dot(place_back(theirs_ref, 0, unmasked, half), got_ref[:unmasked]).astype(BF)
    whole = (own_ref[unmasked:].astype(F32) + got_ref[unmasked:].astype(F32)).astype(BF)
    out_ref[2] = dot(place_back(rank_ref, 0, unmasked, half), whole).astype(BF)


def fold_kernel(parts, *refs):
    out_refs = refs[-4:]
    first = 0
    for count in parts:
        keep_ref, got_refs, refs = refs[0], refs[1 : 1 + count], refs[1 + count :]
        each = 4 // count
        rows = slice(first, first + keep_ref.shape[2])
        first = rows.stop
        for step, out_ref in enumerate(out_refs):
            got = got_refs[step // each][step % each]
            out_ref[:, rows] = (keep_ref[step].astype(F32) + got.astype(F32)).astype(BF)


def fold_four_kernel(units, *refs):
    outs = refs[4 * units :]
    first = 0
    for unit in range(units):
        total = refs[4 * unit][...].astype(F32)
        for ref in refs[4 * unit + 1 : 4 * unit + 4]:
            total = total + ref[...].astype(F32)
        total = total.astype(BF)
        rows = slice(first, first + total.shape[1])
        first += total.shape[1]
        if len(outs) == 1:
            outs[0][:, rows] = total
        else:
            for step, out_ref in enumerate(outs):
                for slot in range(out_ref.shape[0]):
                    out_ref[slot, rows] = total[4 * slot + step]


def clip_swap(values, distance):
    size = lax.axis_size("clip")
    return lax.ppermute(values, "clip", [(i, i ^ distance) for i in range(size)])


def near_swap(values, step):
    size = lax.axis_size("clip")
    pairs = [
        (t * size + i, (t ^ (step & 1)) * size + (i ^ ((step >> 1) << 1))) for t in range(2) for i in range(size)
    ]
    return lax.ppermute(values, ("tm", "clip"), pairs)


def swap_cores(send):
    return [clip_swap(part, 1) for part in send]


def fold_cores(units):
    _, groups, _, _ = units[0][0].shape
    depth = sum(keep.shape[2] for keep, _ in units)
    kernel = functools.partial(fold_kernel, [len(got) for _, got in units])
    refs = [part for keep, got in units for part in (keep, *got)]
    return plain(kernel, [shape(groups, depth, LANES)] * 4)(*refs)


def spread_near(pieces, steps=(1, 2, 3)):
    return [pieces[0]] + [near_swap(pieces[step], step) for step in steps]


def sum_over_devices(first_pieces, second_pieces, send_far, beside_last, finish):
    far = []
    distance = 4
    while distance < lax.axis_size("clip"):
        far.append(distance)
        distance *= 4
    pieces = [*first_pieces, *second_pieces]
    groups = pieces[0].shape[0]
    depth = pieces[0].shape[1] + pieces[4].shape[1]
    left = groups
    sent = None
    for distance in far:
        left //= 4
        fold = functools.partial(fold_four_kernel, len(pieces) // 4)
        pieces = plain(fold, [shape(left, depth, LANES)] * 4)(*pieces)
        if sent is None:
            sent, pieces = send_far(pieces)
        pieces = [pieces[0]] + [clip_swap(pieces[step], step * distance) for step in (3, 2, 1)]
    total = plain(functools.partial(fold_four_kernel, 1), shape(left, depth, LANES))(*pieces)
    for distance in reversed(far):
        pieces = [total] + [clip_swap(total, step * distance) for step in (1, 2, 3)]
        total = plain(join_kernel, shape(4 * total.shape[0], *total.shape[1:]))(*pieces)
    total, sent = lax.optimization_barrier((total, sent))
    pieces = spread_near([total] * 4)
    last = beside_last(sent)
    early, last = lax.optimization_barrier((total, last))
    middle = total.shape[1] // 32 * 16
    parts = [early[:, :middle], early[:, middle:]]
    got_parts = [clip_swap(part, 1) for part in parts]
    done = finish(((0, 0), (0, 1)), [parts, got_parts], (), ())
    *pieces, done = lax.optimization_barrier((*pieces, done))
    own = [[piece] for piece in pieces[1:]]
    got = [[clip_swap(piece, 1)] for piece in pieces[1:]]
    done = finish(((1, 0), (2, 0), (3, 0)), own, done, ())
    return finish(((1, 1), (2, 1), (3, 1)), got, done, [parts, got_parts, *own]), last


def join_kernel(*refs):
    for step in range(4):
        for slot in range(refs[step].shape[0]):
            refs[4][4 * slot + step] = refs[step][slot]


def finish_kernel(jobs, counts, extra_jobs, extra_counts, first_call, depths, base, vectors, place_ref, *refs):
    def take(counts):
        nonlocal refs
        taken = []
        for count in counts:
            taken.append(refs[:count])
            refs = refs[count:]
        return taken

    sources, extra_sources = take(counts), take(extra_counts)
    if not first_call:
        take((4,))
    outs, vector_outs, stage_refs, (done,), wides, (kept_ref,), flat_refs = take(
        (4, vectors, len(depths), 1, 4, 1, vectors)
    )
    stores = []

    def store(source, target):
        stores.append(pltpu.make_async_copy(source, target, done.at[len(stores)]))
        stores[-1].start()

    if vectors:
        number, offset = divmod(base, depths[1])
        for (near, side), parts in zip(jobs + extra_jobs, sources + extra_sources):
            start = 0
            for part in parts:
                row = depths[0] + offset - start
                if 0 <= row < part.shape[1]:
                    rows = part[number ^ (place_ref[1] >> 3), row : row + 16]
                    kept_ref[eighth_at(place_ref, near, side)] = rows.astype(F32)
                start += part.shape[1]
        blocks = [(ref, block) for ref in flat_refs for block in range(ref.shape[0] // LANES)]
        each = -(-len(blocks) // 8)
        for at, (ref, block) in enumerate(blocks):
            eighth, row = divmod(at, each)
            ref[block * LANES : (block + 1) * LANES] = kept_ref[eighth, row]
        for flat_ref, out_ref in zip(flat_refs, vector_outs):
            store(flat_ref, out_ref)
    for job, ((near, side), parts) in enumerate(zip(jobs, sources)):
        eighth = eighth_at(place_ref, near, side)
        for far in range(parts[0].shape[0]):
            start = 0
            for part in parts:
                stop = start + part.shape[1]
                for unit, (stage_ref, depth) in enumerate(zip(stage_refs, depths)):
                    low = sum(depths[:unit])
                    top, end = max(start, low), min(stop, low + depth)
                    if top < end:
                        first = pl.multiple_of((far ^ (place_ref[1] >> 3)) * depth + (top - low), 16)
                        stage_ref[pl.ds(first, end - top), :] = part[far, top - start : end - start]
                start = stop
        for unit, stage_ref in enumerate(stage_refs):
            first = 0
            for at in ((0, 1), (3,), (2,))[unit]:
                wide_ref = wides[at].at[job]
                depth, width = wide_ref.shape
                for block in range(width // LANES):
                    wide_ref[:, block * LANES : (block + 1) * LANES] = stage_ref[first : first + depth, :].astype(F32)
                    first += depth
                if at == 1:
                    rows = pl.ds(pl.multiple_of((eighth & 1) * depth, 16), depth)
                    target = outs[at].at[rows, pl.ds(pl.multiple_of((eighth >> 1) * width, LANES), width)]
                else:
                    target = outs[at].at[pl.ds(pl.multiple_of(eighth * depth, 16), depth), :]
                store(wide_ref, target)
    for each in stores:
        each.wait()


def chunk_rows(count, devices):
    return -(-count // (devices * 16)) * 16


def body(
    tokens,
    masked,
    groups,
    cotangent,
    mask_token,
    gain_one,
    shift_one,
    w_qkv,
    q_bias,
    v_bias,
    w_proj,
    b_proj,
    gain_two,
    shift_two,
    w_up,
    b_up,
    w_down,
    b_down,
):
    copies, half, width = tokens.shape
    hidden = w_up.shape[1]
    hide = masked.shape[1]
    unmasked = 2 * half - hide
    rows = unmasked + EXTRA
    some = unmasked // 2 + EXTRA
    total = rows + some
    tm, clip = lax.axis_index("tm"), lax.axis_index("clip")
    clips = lax.axis_size("clip")
    devices = 2 * clips
    me = (clip & 1) | (tm << 1) | ((clip >> 1) << 2)
    place = jnp.stack([tm, me]).astype(jnp.int32)
    swap = functools.partial(lax.ppermute, axis_name="tm", perm=[(0, 1), (1, 0)])

    def run(kernel, args, outs, scratch=(), scalars=1, limit=20, flops=0, in_hbm=(), out_hbm=(), aliases=None, hides=True):
        moved = sum(math.prod(a.shape) * a.dtype.itemsize for a in list(args) + jax.tree.leaves(outs))
        return pl.pallas_call(
            kernel,
            out_shape=outs,
            in_specs=[
                SMEM if at < scalars else HBM if at in in_hbm else VMEM
                for at in range(len(args))
            ],
            out_specs=[HBM if at in out_hbm else VMEM for at in range(len(outs))] if isinstance(outs, list) else VMEM,
            scratch_shapes=list(scratch),
            input_output_aliases=aliases or {},
            compiler_params=pltpu.CompilerParams(vmem_limit_bytes=limit << 20),
            cost_estimate=pl.CostEstimate(
                flops=flops if hides else 1, bytes_accessed=moved if hides else 1, transcendentals=0
            ),
        )(*args)

    blocks = width // LANES
    counts = (2 * hidden // 8 * blocks, 3 * width // 8 * blocks + 16, width // 8 * blocks)
    depths = [chunk_rows(count, devices // 8) for count in counts]

    def chunked(unit, parts):
        halves = [shape(near, devices // 8, depths[unit], LANES) for near in [4] + [4 // parts] * parts]
        return halves, [pltpu.VMEM((8, devices // 8 * depths[unit], LANES), BF)]

    small = jnp.stack(
        [mask_token, gain_one, shift_one, q_bias, v_bias, b_proj, gain_two, shift_two, b_down]
    ).astype(F32)
    bias_up = b_up.astype(F32).reshape(1, hidden)

    block = shape(rows, width)
    everyone = jnp.concatenate([groups, clip_swap(groups, 1)])
    theirs, rank_theirs = run(
        functools.partial(prep_theirs_kernel, unmasked),
        (place, *(pltpu.with_memory_space_constraint(each, pltpu.HBM) for each in (masked, tokens))),
        [shape(unmasked, width), shape(16, LANES, kind=F32)],
        [pltpu.VMEM(masked.shape, jnp.int32), pltpu.VMEM((half, width), BF), pltpu.SemaphoreType.DMA((2,))],
        flops=2 * rows * half * width,
        in_hbm=(1, 2),
    )
    got_mine = swap(theirs)
    everyone, theirs, rank_theirs, masked = lax.optimization_barrier((everyone, theirs, rank_theirs, masked))
    everyone = jnp.concatenate([everyone, clip_swap(everyone, 2)])
    shared, rank = run(
        functools.partial(prep_shared_kernel, unmasked),
        (place, masked, tokens),
        [shape(unmasked, width), shape(32, LANES, kind=F32)],
        flops=2 * rows * half * width,
    )
    got_shared = swap(shared)
    everyone, shared, rank = lax.optimization_barrier((everyone, shared, rank))
    everyone = jnp.concatenate([everyone, clip_swap(everyone, 4)])
    cot_own, cot_send = run(
        functools.partial(prep_grads_kernel, unmasked),
        (place, rank_theirs, rank, cotangent),
        [shape(total, width), shape(total - EXTRA, width)],
        flops=2 * copies * rows * half * width,
    )
    everyone, cot_own, cot_send = lax.optimization_barrier((everyone, cot_own, cot_send))
    cot_got = swap(cot_send)

    def attend(sources, got, split):
        queries = some if split else rows
        outs = [
            shape(queries, width), shape(queries, width), block, block,
            shape(HEADS, queries, rows), shape(queries, width, kind=F32), shape(queries, width),
        ]
        if split:
            outs.append(block)
        return run(
            functools.partial(attention_kernel, unmasked, hide, split),
            (place, *sources, got, small, w_qkv),
            outs,
            flops=6 * rows * width * width + 4 * queries * rows * width,
        )

    x_a, q_a, k_a, v_a, e_a, inverse_a, att_a = attend((rank, tokens), got_mine, False)
    everyone, att_a = lax.optimization_barrier((everyone, att_a))
    distance = 8
    while distance < clips:
        everyone = jnp.concatenate([everyone, clip_swap(everyone, distance)])
        distance *= 2
    x_b, q_b, k_b, v_b, e_b, inverse_b, att_b, x_whole = attend((shared,), got_shared, True)

    everyone, att_b = lax.optimization_barrier((everyone, att_b))
    out_rows, middle, normed_two, active, slope = run(
        forward_kernel,
        (att_a, att_b, x_a, x_b, small, bias_up, w_proj, w_up, w_down),
        [
            shape(total, width), shape(total, width, kind=F32), shape(total, width), shape(total, hidden),
            shape(total, hidden),
        ],
        scalars=0,
        flops=2 * total * width * (width + 2 * hidden),
    )
    out_got = swap(out_rows)
    halves, stage = chunked(0, 4)
    upstream, grad_hidden, up_sums, keep, *send = run(
        hidden_back_kernel,
        (place, groups, everyone.reshape(1, -1), cot_own, cot_got, normed_two, active, slope, w_down),
        [shape(total, width, kind=F32), shape(total, hidden), shape(1, hidden, kind=F32)] + halves,
        stage,
        scalars=2,
        hides=False,
    )
    halves, stage = chunked(2, 2)
    grad_middle, grad_att, middle_sums, keep_proj, *send_proj = run(
        middle_back_kernel,
        (place, upstream, grad_hidden, middle, att_a, att_b, small, w_proj, w_up),
        [shape(total, width, kind=F32), shape(total, width), shape(8, width, kind=F32)] + halves,
        stage,
        hides=False,
    )
    got, grad_att = lax.optimization_barrier((swap_cores(send), grad_att))
    pieces, grad_att, send_proj = lax.optimization_barrier((fold_cores([(keep, got)]), grad_att, send_proj))
    first_pieces = spread_near(pieces, (2, 1, 3))

    def attend_back(row_from, grads, att, q, k, v, e, inverse):
        return run(
            functools.partial(attention_back_kernel, row_from),
            (grads, att, q, k, v, e, inverse),
            [shape(q.shape[0], width), block, block],
            scalars=0,
            hides=False,
        )

    dq_b, dk_b, dv_b = attend_back(rows, grad_att, att_b, q_b, k_b, v_b, e_b, inverse_b)
    dq_b, out_got = lax.optimization_barrier((dq_b, out_got))
    dq_a, dk_a, dv_a = attend_back(0, grad_att, att_a, q_a, k_a, v_a, e_a, inverse_a)
    dq_a, got_proj = lax.optimization_barrier((dq_a, swap_cores(send_proj)))
    halves, stage = chunked(1, 2)
    grad_rows, keep, *send = run(
        functools.partial(inputs_back_kernel, unmasked),
        (place, x_a, x_whole, dq_a, dq_b, dk_a, dk_b, dv_a, dv_b, grad_middle, small, w_qkv, up_sums, middle_sums),
        [shape(2 * unmasked, width)] + halves,
        stage,
        hides=False,
    )
    pieces = fold_cores([(keep, swap_cores(send)), (keep_proj, got_proj)])
    pieces, first_pieces = lax.optimization_barrier((pieces, first_pieces))
    second_pieces = spread_near(pieces, (2, 1, 3))

    def send_rows(pieces):
        *pieces, grads = lax.optimization_barrier((*pieces, grad_rows))
        return swap(grads), pieces

    def place_rows(got):
        return (
            run(functools.partial(outputs_kernel, unmasked), (place, rank_theirs, rank, out_rows, out_got), shape(*tokens.shape), hides=False),
            run(functools.partial(grads_out_kernel, unmasked), (place, rank_theirs, rank, grad_rows, got), shape(*tokens.shape), hides=False),
        )

    weights = [(hidden, width), (width, hidden), (width, width), (width, 3 * width)]
    slabs = [(hidden // 8, width), (width // 2, hidden // 4), (width // 8, width), (width // 8, 3 * width)]
    vectors = [shape(dim, kind=F32) for dim in [hidden] + [width] * 9]

    def finish(jobs, sources, earlier, extra_sources):
        extra_jobs = ((0, 0), (0, 1), (1, 0), (2, 0), (3, 0)) if extra_sources else ()
        refs = [part for parts in [*sources, *extra_sources] for part in parts]
        flat = vectors if extra_sources else []
        kernel = functools.partial(
            finish_kernel,
            jobs,
            [len(parts) for parts in sources],
            extra_jobs,
            [len(parts) for parts in extra_sources],
            not earlier,
            depths,
            counts[1] - 16,
            len(flat),
        )
        return run(
            kernel,
            (place, *refs, *earlier),
            [shape(*dims, kind=F32) for dims in weights] + flat,
            [pltpu.VMEM((devices // 8 * depth, LANES), BF) for depth in depths]
            + [pltpu.SemaphoreType.DMA((4 * len(jobs) + len(flat),))]
            + [pltpu.VMEM((len(jobs), *dims), F32) for dims in slabs]
            + [pltpu.VMEM((8, 16, LANES), F32)]
            + [pltpu.VMEM(each.shape, F32) for each in flat],
            in_hbm=range(1 + len(refs), 5 + len(refs)) if earlier else (),
            out_hbm=range(4 + len(flat)),
            aliases={1 + len(refs) + at: at for at in range(4)} if earlier else {},
            hides=False,
        )

    (
        (
            grad_w_down, grad_w_up, grad_w_proj, grad_w_qkv,
            grad_b_up, grad_gain_two, grad_shift_two, grad_b_proj, grad_b_down,
            grad_q_bias, grad_v_bias, grad_gain_one, grad_shift_one, grad_mask_token,
        ),
        (block_out, grad_tokens),
    ) = sum_over_devices(first_pieces, second_pieces, send_rows, place_rows, finish)
    return (
        block_out,
        grad_tokens,
        grad_mask_token,
        grad_gain_one,
        grad_shift_one,
        grad_w_qkv,
        grad_q_bias,
        grad_v_bias,
        grad_w_proj,
        grad_b_proj,
        grad_gain_two,
        grad_shift_two,
        grad_w_up,
        grad_b_up,
        grad_w_down,
        grad_b_down,
    )


def solution(mesh):
    return jax.shard_map(
        body,
        mesh=mesh,
        in_specs=(P("clip", "tm", None), P("clip", None), P("clip"), P("clip", "tm", None)) + (P(),) * 14,
        out_specs=(P("clip", "tm", None), P("clip", "tm", None)) + (P(),) * 14,
        check_vma=False,
    )
```

```python
import functools
import math

import jax
import jax.numpy as jnp
import numpy as np
from jax import lax
from jax.experimental import pallas as pl
from jax.experimental.pallas import tpu as pltpu
from jax.sharding import PartitionSpec as P

HEADS = 6
HEAD_DIM = 64
LANES = 128
EXTRA = 16
EPSILON = 1e-06

BF = jnp.bfloat16
F32 = jnp.float32
VMEM = pl.BlockSpec(memory_space=pltpu.VMEM)
SMEM = pl.BlockSpec(memory_space=pltpu.SMEM)
HBM = pl.BlockSpec(memory_space=pltpu.HBM)


def dot(left, right):
    return jnp.dot(left, right, preferred_element_type=F32)


def dot_last(left, right):
    return lax.dot_general(left, right, (((1,), (1,)), ((), ())), preferred_element_type=F32)


def dot_rows(left, right):
    return lax.dot_general(left, right, (((0,), (0,)), ((), ())), preferred_element_type=F32)


def iota(shape, axis):
    return lax.broadcasted_iota(jnp.int32, shape, axis)


def ones_where(condition):
    return jnp.where(condition, 1.0, 0.0).astype(BF)


def column_sums(values):
    return jnp.sum(values, axis=0, keepdims=True)


def shape(*dims, kind=BF):
    return jax.ShapeDtypeStruct(dims, kind)


def plain(kernel, outs):
    return pl.pallas_call(kernel, out_shape=outs, compiler_params=pltpu.CompilerParams(vmem_limit_bytes=8 << 20))


def ranks(rows, tm, half, unmasked):
    copies, hide = len(rows), rows[0].shape[1]
    blocks = half // LANES
    marks = []
    for row in rows:
        low = ones_where(iota((LANES, hide), 0) == (row & (LANES - 1)))
        high = ones_where(iota((16, hide), 0) == (row >> 7))
        marks.append(dot_last(high, low))
    marks = jnp.concatenate(marks, axis=0)
    count = 16 * copies
    block = iota((count, LANES), 0)
    free = jnp.where((block & 15) < 2 * blocks, 1.0 - marks, 0.0).astype(BF)
    before = ones_where(iota((LANES, LANES), 0) < iota((LANES, LANES), 1))
    within = dot(free, before)
    totals = dot(free, jnp.ones((LANES, LANES), BF)).astype(BF)
    row, column = iota((count, count), 0), iota((count, count), 1)
    earlier = ones_where(jnp.logical_and(column < row, (column >> 4) == (row >> 4)))
    rank = within + dot(earlier, totals)
    rank = jnp.where(marks > 0.5, float(unmasked), rank)
    across = []
    for first in range(0, count, 16):
        mine = jnp.where(tm == 0, rank[first : first + blocks], rank[first + blocks : first + 2 * blocks])
        across.append(jnp.concatenate([mine, jnp.zeros((16 - blocks, LANES), F32)], axis=0))
    return jnp.concatenate(across, axis=0)


def picks(rank, labels):
    wide = jnp.broadcast_to(labels.astype(F32), (labels.shape[0], LANES))
    return jnp.concatenate([ones_where(wide == rank[b : b + 1, :]) for b in range(rank.shape[0])], axis=1)


def ranks_of(rank_ref, at, half):
    return rank_ref[16 * at : 16 * at + half // LANES, :]


def prep_theirs_kernel(
    unmasked, place_ref, masked_ref, tokens_ref, theirs_ref, rank_ref, marks_ref, half_ref, arrived
):
    tm = place_ref[0]
    half = tokens_ref.shape[1]
    load_marks = pltpu.make_async_copy(masked_ref, marks_ref, arrived.at[0])
    load_marks.start()
    step = half // 3
    loads = [
        pltpu.make_async_copy(
            tokens_ref.at[1 - tm, block * step : (block + 1) * step],
            half_ref.at[block * step : (block + 1) * step],
            arrived.at[1 + block],
        )
        for block in range(3)
    ]
    for load in loads:
        load.start()
    load_marks.wait()
    rank = ranks([marks_ref[pl.ds(1 - tm, 1), :]], tm, half, unmasked)
    rank_ref[...] = rank
    chosen = picks(rank[: half // LANES], iota((unmasked, 1), 0))
    total = None
    for block, load in enumerate(loads):
        load.wait()
        rows = slice(block * step, (block + 1) * step)
        part = dot(chosen[:, rows], half_ref[rows, :])
        total = part if total is None else total + part
    theirs_ref[...] = total.astype(BF)


def prep_shared_kernel(unmasked, place_ref, masked_ref, tokens_ref, shared_ref, rank_ref):
    tm = place_ref[0]
    half = tokens_ref.shape[1]
    rank = ranks([masked_ref[2:3, :], masked_ref[pl.ds(tm, 1), :]], tm, half, unmasked)
    rank_ref[...] = rank
    shared_ref[...] = dot(picks(rank[: half // LANES], iota((unmasked, 1), 0)), tokens_ref[2]).astype(BF)


def prep_grads_kernel(unmasked, place_ref, theirs_ref, rank_ref, cotangent_ref, keep_ref, send_ref):
    tm = place_ref[0]
    half = cotangent_ref.shape[1]
    rows = unmasked + EXTRA
    part = unmasked // 2
    labels = iota((rows, 1), 0)
    small = iota((part + EXTRA, 1), 0)
    theirs = iota((part, 1), 0) + part * (1 - tm)
    own = jnp.where(small < part, small + part * tm, small + part)
    send_ref[:rows, :] = dot(picks(ranks_of(theirs_ref, 0, half), labels), cotangent_ref[1 - tm]).astype(BF)
    chosen = picks(ranks_of(rank_ref, 0, half), jnp.concatenate([theirs, own], axis=0))
    both = dot(chosen, cotangent_ref[2]).astype(BF)
    send_ref[rows:, :] = both[:part]
    keep_ref[rows:, :] = both[part:]
    keep_ref[:rows, :] = dot(picks(ranks_of(rank_ref, 1, half), labels), cotangent_ref[tm]).astype(BF)


def normalise(values):
    centred = values - jnp.mean(values, axis=-1, keepdims=True)
    scale = lax.rsqrt(jnp.mean(centred * centred, axis=-1, keepdims=True) + EPSILON)
    return centred * scale, scale


def bias_terms(count):
    terms, rest = [], math.log(count)
    for _ in range(3):
        terms.append(float(np.asarray(rest).astype(jnp.bfloat16)))
        rest -= terms[-1]
    return terms


def attention_kernel(unmasked, count, split, place_ref, *refs):
    tm = place_ref[0]
    if split:
        own_ref, got_ref, small_ref, w_ref, x_ref, q_ref, k_ref, v_ref, e_ref, inverse_ref, att_ref, whole_ref = refs
        own = own_ref[...].astype(F32)
    else:
        rank_ref, tokens_ref, got_ref, small_ref, w_ref, x_ref, q_ref, k_ref, v_ref, e_ref, inverse_ref, att_ref = refs
        chosen = picks(ranks_of(rank_ref, 1, tokens_ref.shape[1]), iota((unmasked, 1), 0))
        own = dot(chosen, tokens_ref[tm])
    rows, width = k_ref.shape
    extra = jnp.where(iota((EXTRA, width), 0) == 0, small_ref[0:1, :], 0.0)
    x = jnp.concatenate([own + got_ref[...].astype(F32), extra], axis=0)
    hat, _ = normalise(x)
    normed = (hat * small_ref[1:2, :] + small_ref[2:3, :]).astype(BF)
    mixed = dot(normed, w_ref[...])
    query = ((mixed[:, :width] + small_ref[3:4, :]).astype(BF).astype(F32) * HEAD_DIM ** (-0.5)).astype(BF)
    key = mixed[:, width : 2 * width].astype(BF)
    value = (mixed[:, 2 * width :] + small_ref[4:5, :]).astype(BF)
    k_ref[...] = key
    v_ref[...] = value
    x = x.astype(BF)
    if split:
        part = unmasked // 2

        def take(values):
            chosen = jnp.where(tm == 0, values[:part].astype(F32), values[part:unmasked].astype(F32)).astype(BF)
            return jnp.concatenate([chosen, values[unmasked:]], axis=0)

        whole_ref[...] = x
        x, query = take(x), take(query)
    x_ref[...] = x
    q_ref[...] = query
    lane = iota((1, LANES), 1)
    first = lane < HEAD_DIM
    at = iota((rows, LANES), 0)
    place = iota((rows, LANES), 1) & (HEAD_DIM - 1)
    log_count = jnp.zeros((rows, LANES), F32)
    for which, term in enumerate(bias_terms(count)):
        log_count = jnp.where(place == which, term, log_count)
    bias = jnp.where(at < unmasked, 0.0, jnp.where(at == unmasked, log_count, jnp.where(place == 0, -1e30, 0.0)))
    bias = bias.astype(BF)
    ones = jnp.where((lane & (HEAD_DIM - 1)) < 3, 1.0, 0.0).astype(BF)
    all_ones = jnp.ones((rows, LANES), BF)
    for pair in range(width // LANES):
        cols = slice(pair * LANES, (pair + 1) * LANES)
        q_pair, k_pair, v_pair = query[:, cols], key[:, cols], value[:, cols]
        v_wide = jnp.concatenate([v_pair, all_ones], axis=1)
        parts = []
        for side in range(2):
            mine = first if side == 0 else jnp.logical_not(first)
            scores = dot_last(jnp.where(mine, q_pair, ones), jnp.where(mine, k_pair, bias))
            expo = jnp.exp(scores - jnp.max(scores, axis=1, keepdims=True)).astype(BF)
            e_ref[2 * pair + side] = expo
            parts.append(dot(expo, v_wide))
        inverse = 1.0 / jnp.where(first, parts[0][:, LANES:], parts[1][:, LANES:])
        inverse_ref[:, cols] = inverse
        att_ref[:, cols] = (jnp.where(first, parts[0][:, :LANES], parts[1][:, :LANES]) * inverse).astype(BF)


def gelu_terms(hidden):
    below = 0.5 * lax.erf(hidden * 0.5**0.5) + 0.5
    bell = jnp.exp2(hidden * hidden * (-0.5 * math.log2(math.e)))
    return hidden * below, below + hidden * bell * (1.0 / math.sqrt(2.0 * math.pi))


def stacked(refs):
    return jnp.concatenate([ref[...] for ref in refs], axis=0)


def eighth_at(place_ref, near, side):
    me = place_ref[1]
    return ((near ^ ((me >> 1) & 3)) << 1) | (side ^ (me & 1))


def chunk_rows_at(place_ref, far, depth):
    return pl.ds(pl.multiple_of((far ^ (place_ref[1] >> 3)) * depth, 16), depth)


def scatter_chunks(place_ref, stage_ref, keep_ref, send_refs):
    near_places, far_places, depth, _ = keep_ref.shape
    each = send_refs[0].shape[0]
    for near in range(near_places):
        for side in range(2):
            eighth = eighth_at(place_ref, near, side)
            for far in range(far_places):
                chunk = stage_ref[eighth, chunk_rows_at(place_ref, far, depth), :]
                if side:
                    send_refs[near // each][near % each, far] = chunk
                else:
                    keep_ref[near, far] = chunk


def stage_rows(stage_ref, base, grad, total, first=0):
    slab = total // 8
    step = math.gcd(slab, grad.shape[0])
    grad = grad.astype(BF)
    for row in range(0, grad.shape[0], step):
        eighth, offset = divmod(first + row, slab)
        for block in range(grad.shape[1] // LANES):
            at = base + block * slab + offset
            stage_ref[eighth, at : at + step, :] = grad[row : row + step, block * LANES : (block + 1) * LANES]


def stage_columns(stage_ref, base, grad, total, first):
    slab = grad.shape[0] // 2
    grad = grad.astype(BF)
    for block in range(grad.shape[1] // LANES):
        quarter, offset = divmod(first // LANES + block, total // 4 // LANES)
        at = base + offset * slab
        for half in range(2):
            stage_ref[2 * quarter + half, at : at + slab, :] = grad[
                half * slab : (half + 1) * slab, block * LANES : (block + 1) * LANES
            ]


def stage_vectors(stage_ref, base, vectors):
    pieces = [v[:, b * LANES : (b + 1) * LANES] for v in vectors for b in range(v.shape[1] // LANES)]
    each = -(-len(pieces) // 8)
    for eighth in range(8):
        rows = pieces[eighth * each : (eighth + 1) * each]
        rows = rows + [jnp.zeros((16 - len(rows), LANES), F32)]
        stage_ref[eighth, base : base + 16, :] = jnp.concatenate(rows, axis=0).astype(BF)
    clear_rest(stage_ref, base + 16)


def clear_rest(stage_ref, base):
    if base < stage_ref.shape[1]:
        stage_ref[:, base:, :] = jnp.zeros((8, stage_ref.shape[1] - base, LANES), BF)


def forward_kernel(
    att_a, att_b, x_a, x_b, small_ref, bias_up_ref, w_proj_ref, w_up_ref, w_down_ref,
    out_ref, middle_ref, normed_ref, active_ref, slope_ref
):
    attended = stacked((att_a, att_b))
    x = stacked((x_a, x_b)).astype(F32)
    middle = x + dot(attended, w_proj_ref[...]) + small_ref[5:6, :]
    middle_ref[...] = middle
    hat, _ = normalise(middle)
    normed = (hat * small_ref[6:7, :] + small_ref[7:8, :]).astype(BF)
    normed_ref[...] = normed
    result = middle + small_ref[8:9, :]
    width, step = w_up_ref.shape[1], 512
    ahead = dot(normed, w_up_ref[:, :step])
    for first in range(0, width, step):
        cols = slice(first, first + step)
        hidden = ahead + bias_up_ref[:, cols]
        if first + step < width:
            ahead = dot(normed, w_up_ref[:, first + step : first + 2 * step])
        active, slope = gelu_terms(hidden)
        active = active.astype(BF)
        active_ref[:, cols] = active
        slope_ref[:, cols] = slope.astype(BF)
        result = result + dot(active, w_down_ref[cols, :])
    out_ref[...] = result.astype(BF)


def norm_back(grad, hat, scale, gain):
    inner = grad * gain
    mean = jnp.mean(inner, axis=-1, keepdims=True)
    along = jnp.mean(inner * hat, axis=-1, keepdims=True)
    return scale * (inner - mean - hat * along)


def hidden_back_kernel(
    place_ref, groups_ref, everyone_ref, cot_own, cot_got, normed_ref, active_ref, slope_ref, w_down_ref,
    upstream_ref, grad_hidden_ref, sums_ref, keep_ref, *send_refs
):
    *send_refs, stage_ref = send_refs
    total = cot_own.shape[0]
    rows_a = total - cot_got.shape[0] // 3 - EXTRA
    everyone = everyone_ref[...]

    def weight_of(group):
        return 1.0 / jnp.sum(jnp.where(everyone == group, 1.0, 0.0), axis=1, keepdims=True)

    weight = jnp.where(
        iota((total, 1), 0) < rows_a, weight_of(groups_ref[place_ref[0]]), weight_of(groups_ref[2])
    )
    got = jnp.concatenate([cot_got[...].astype(F32), jnp.zeros((EXTRA, cot_got.shape[1]), F32)], axis=0)
    upstream = (cot_own[...].astype(F32) + got) * weight
    upstream_ref[...] = upstream
    grad_result = upstream.astype(BF)
    normed = normed_ref[...]
    hidden, step = active_ref.shape[1], 512
    slab = hidden // 8 * (grad_result.shape[1] // LANES)
    for first in range(0, hidden, step):
        cols = slice(first, first + step)
        grad_hidden = (dot_last(grad_result, w_down_ref[cols, :]) * slope_ref[:, cols].astype(F32)).astype(BF)
        grad_hidden_ref[:, cols] = grad_hidden
        stage_rows(stage_ref, 0, dot_rows(active_ref[:, cols], grad_result), hidden, first)
        sums_ref[:, cols] = column_sums(grad_hidden.astype(F32))
        stage_columns(stage_ref, slab, dot_rows(normed, grad_hidden), hidden, first)
    clear_rest(stage_ref, 2 * slab)
    scatter_chunks(place_ref, stage_ref, keep_ref, send_refs)


def middle_back_kernel(
    place_ref, upstream_ref, grad_hidden_ref, middle_ref, att_a, att_b, small_ref, w_proj_ref, w_up_ref,
    grad_middle_ref, grad_att_ref, sums_ref, keep_ref, send_a, send_b, stage_ref
):
    grad_normed = dot_last(grad_hidden_ref[...], w_up_ref[...])
    hat, scale = normalise(middle_ref[...])
    upstream = upstream_ref[...]
    grad_middle = upstream + norm_back(grad_normed, hat, scale, small_ref[6:7, :])
    grad_middle_ref[...] = grad_middle
    grad_branch = grad_middle.astype(BF)
    grad_att_ref[...] = dot_last(grad_branch, w_proj_ref[...]).astype(BF)
    width = grad_branch.shape[1]
    stage_rows(stage_ref, 0, dot_rows(stacked((att_a, att_b)), grad_branch), width)
    clear_rest(stage_ref, width // 8 * (width // LANES))
    scatter_chunks(place_ref, stage_ref, keep_ref, (send_a, send_b))
    sums_ref[0:1, :] = column_sums(grad_normed * hat)
    sums_ref[1:2, :] = column_sums(grad_normed)
    sums_ref[2:3, :] = column_sums(grad_branch.astype(F32))
    sums_ref[3:4, :] = column_sums(upstream.astype(BF).astype(F32))


def attention_back_kernel(row_from, g_ref, att_ref, q_ref, k_ref, v_ref, e_ref, inverse_ref, dq_ref, dk_ref, dv_ref):
    rows, width = q_ref.shape
    first = iota((1, LANES), 1) < HEAD_DIM
    for pair in range(width // LANES):
        cols = slice(pair * LANES, (pair + 1) * LANES)
        q_pair, k_pair, v_pair = q_ref[:, cols], k_ref[:, cols], v_ref[:, cols]
        g_pair = (g_ref[row_from : row_from + rows, cols].astype(F32) * inverse_ref[:, cols]).astype(BF)
        agree = g_pair.astype(F32) * att_ref[:, cols].astype(F32)
        dq, dk, dv = [], [], []
        for side in range(2):
            mine = first if side == 0 else jnp.logical_not(first)
            correction = jnp.sum(jnp.where(mine, agree, 0.0), axis=1, keepdims=True)
            expo = e_ref[2 * pair + side]
            grad_probs = dot_last(jnp.where(mine, g_pair, jnp.zeros_like(g_pair)), v_pair)
            grad_scores = expo * (grad_probs - correction).astype(BF)
            dq.append(dot(grad_scores, k_pair))
            dk.append(dot_rows(grad_scores, q_pair))
            dv.append(dot_rows(expo, g_pair))
        dq_ref[:, cols] = (jnp.where(first, dq[0], dq[1]) * HEAD_DIM ** (-0.5)).astype(BF)
        dk_ref[:, cols] = jnp.where(first, dk[0], dk[1]).astype(BF)
        dv_ref[:, cols] = jnp.where(first, dv[0], dv[1]).astype(BF)


def inputs_back_kernel(
    unmasked, place_ref, x_a, x_b, dq_a, dq_b, dk_a, dk_b, dv_a, dv_b, grad_middle_ref, small_ref, w_ref,
    up_sums_ref, middle_sums_ref,
    grad_ref, keep_ref, *send_refs
):
    *send_refs, stage_ref = send_refs
    rows, width = x_a.shape
    part = unmasked // 2
    tm = place_ref[0]

    def spread(block):
        wide = block.astype(F32)
        left = jnp.where(tm == 0, wide[:part], 0.0)
        right = jnp.where(tm == 0, 0.0, wide[:part])
        return jnp.concatenate([left, right, wide[part:]], axis=0)

    x = stacked((x_a, x_b)).astype(F32)
    hat, scale = normalise(x)
    gain = small_ref[1:2, :]
    normed = (hat * gain + small_ref[2:3, :]).astype(BF)
    dq = jnp.concatenate([dq_a[...], spread(dq_b[...]).astype(BF)], axis=0)
    mixed = jnp.concatenate([dq, stacked((dk_a, dk_b)), stacked((dv_a, dv_b))], axis=1)
    stage_rows(stage_ref, 0, dot_rows(normed, mixed), width)
    grad_normed = dot_last(mixed, w_ref[...])
    grad = norm_back(grad_normed, hat, scale, gain)
    grad = grad + jnp.concatenate([grad_middle_ref[:rows], spread(grad_middle_ref[rows:])], axis=0)
    grad_ref[:unmasked] = grad[:unmasked].astype(BF)
    grad_ref[unmasked:] = grad[rows : rows + unmasked].astype(BF)
    slab = width // 8 * (mixed.shape[1] // LANES)
    vectors = (
        up_sums_ref[...],
        *(middle_sums_ref[row : row + 1, :] for row in range(4)),
        column_sums(mixed[:, :width].astype(F32)),
        column_sums(mixed[:, 2 * width :].astype(F32)),
        column_sums(grad_normed * hat),
        column_sums(grad_normed),
        grad[unmasked : unmasked + 1] + grad[rows + unmasked : rows + unmasked + 1],
    )
    stage_vectors(stage_ref, slab, vectors)
    scatter_chunks(place_ref, stage_ref, keep_ref, send_refs)


def place_back(rank_ref, at, rows, half):
    down = jnp.transpose(ranks_of(rank_ref, at, 16 * LANES))
    labels = jnp.broadcast_to(iota((1, rows), 1).astype(F32), (LANES, rows))
    return jnp.concatenate([ones_where(labels == down[:, b : b + 1]) for b in range(half // LANES)], axis=0)


def outputs_kernel(unmasked, place_ref, theirs_ref, rank_ref, own_ref, got_ref, out_ref):
    tm = place_ref[0]
    half = out_ref.shape[1]
    rows = unmasked + EXTRA
    part = unmasked // 2
    out_ref[tm] = dot(place_back(rank_ref, 1, rows, half), own_ref[:rows]).astype(BF)
    out_ref[1 - tm] = dot(place_back(theirs_ref, 0, rows, half), got_ref[:rows]).astype(BF)
    own = own_ref[rows:].astype(F32)
    got = got_ref[rows:].astype(F32)
    left = jnp.where(tm == 0, own[:part], got[:part])
    right = jnp.where(tm == 0, got[:part], own[:part])
    whole = jnp.concatenate([left, right, own[part:]], axis=0).astype(BF)
    out_ref[2] = dot(place_back(rank_ref, 0, rows, half), whole).astype(BF)


def grads_out_kernel(unmasked, place_ref, theirs_ref, rank_ref, own_ref, got_ref, out_ref):
    tm = place_ref[0]
    half = out_ref.shape[1]
    out_ref[tm] = dot(place_back(rank_ref, 1, unmasked, half), own_ref[:unmasked]).astype(BF)
    out_ref[1 - tm] = dot(place_back(theirs_ref, 0, unmasked, half), got_ref[:unmasked]).astype(BF)
    whole = (own_ref[unmasked:].astype(F32) + got_ref[unmasked:].astype(F32)).astype(BF)
    out_ref[2] = dot(place_back(rank_ref, 0, unmasked, half), whole).astype(BF)


def fold_kernel(parts, *refs):
    out_refs = refs[-4:]
    first = 0
    for count in parts:
        keep_ref, got_refs, refs = refs[0], refs[1 : 1 + count], refs[1 + count :]
        each = 4 // count
        rows = slice(first, first + keep_ref.shape[2])
        first = rows.stop
        for step, out_ref in enumerate(out_refs):
            got = got_refs[step // each][step % each]
            out_ref[:, rows] = (keep_ref[step].astype(F32) + got.astype(F32)).astype(BF)


def fold_four_kernel(units, *refs):
    outs = refs[4 * units :]
    first = 0
    for unit in range(units):
        total = refs[4 * unit][...].astype(F32)
        for ref in refs[4 * unit + 1 : 4 * unit + 4]:
            total = total + ref[...].astype(F32)
        total = total.astype(BF)
        rows = slice(first, first + total.shape[1])
        first += total.shape[1]
        if len(outs) == 1:
            outs[0][:, rows] = total
        else:
            for step, out_ref in enumerate(outs):
                for slot in range(out_ref.shape[0]):
                    out_ref[slot, rows] = total[4 * slot + step]


def clip_swap(values, distance):
    size = lax.axis_size("clip")
    return lax.ppermute(values, "clip", [(i, i ^ distance) for i in range(size)])


def near_swap(values, step):
    size = lax.axis_size("clip")
    pairs = [
        (t * size + i, (t ^ (step & 1)) * size + (i ^ ((step >> 1) << 1))) for t in range(2) for i in range(size)
    ]
    return lax.ppermute(values, ("tm", "clip"), pairs)


def swap_cores(send):
    return [clip_swap(part, 1) for part in send]


def fold_cores(units):
    _, groups, _, _ = units[0][0].shape
    depth = sum(keep.shape[2] for keep, _ in units)
    kernel = functools.partial(fold_kernel, [len(got) for _, got in units])
    refs = [part for keep, got in units for part in (keep, *got)]
    return plain(kernel, [shape(groups, depth, LANES)] * 4)(*refs)


def spread_near(pieces, steps=(1, 2, 3)):
    return [pieces[0]] + [near_swap(pieces[step], step) for step in steps]


def sum_over_devices(first_pieces, second_pieces, send_far, beside_last, finish):
    far = []
    distance = 4
    while distance < lax.axis_size("clip"):
        far.append(distance)
        distance *= 4
    pieces = [*first_pieces, *second_pieces]
    groups = pieces[0].shape[0]
    depth = pieces[0].shape[1] + pieces[4].shape[1]
    left = groups
    sent = None
    for distance in far:
        left //= 4
        fold = functools.partial(fold_four_kernel, len(pieces) // 4)
        pieces = plain(fold, [shape(left, depth, LANES)] * 4)(*pieces)
        if sent is None:
            sent, pieces = send_far(pieces)
        pieces = [pieces[0]] + [clip_swap(pieces[step], step * distance) for step in (3, 2, 1)]
    total = plain(functools.partial(fold_four_kernel, 1), shape(left, depth, LANES))(*pieces)
    for distance in reversed(far):
        pieces = [total] + [clip_swap(total, step * distance) for step in (1, 2, 3)]
        total = plain(join_kernel, shape(4 * total.shape[0], *total.shape[1:]))(*pieces)
    total, sent = lax.optimization_barrier((total, sent))
    pieces = spread_near([total] * 4)
    last = beside_last(sent)
    early, last = lax.optimization_barrier((total, last))
    middle = total.shape[1] // 32 * 16
    parts = [early[:, :middle], early[:, middle:]]
    got_parts = [clip_swap(part, 1) for part in parts]
    done = finish(((0, 0), (0, 1)), [parts, got_parts], (), ())
    *pieces, done = lax.optimization_barrier((*pieces, done))
    own = [[piece] for piece in pieces[1:]]
    got = [[clip_swap(piece, 1)] for piece in pieces[1:]]
    done = finish(((1, 0), (2, 0), (3, 0)), own, done, ())
    return finish(((1, 1), (2, 1), (3, 1)), got, done, [parts, got_parts, *own]), last


def join_kernel(*refs):
    for step in range(4):
        for slot in range(refs[step].shape[0]):
            refs[4][4 * slot + step] = refs[step][slot]


def finish_kernel(jobs, counts, extra_jobs, extra_counts, first_call, depths, base, vectors, place_ref, *refs):
    def take(counts):
        nonlocal refs
        taken = []
        for count in counts:
            taken.append(refs[:count])
            refs = refs[count:]
        return taken

    sources, extra_sources = take(counts), take(extra_counts)
    if not first_call:
        take((4,))
    outs, vector_outs, stage_refs, (done,), wides, (kept_ref,), flat_refs = take(
        (4, vectors, len(depths), 1, 4, 1, vectors)
    )
    stores = []

    def store(source, target):
        stores.append(pltpu.make_async_copy(source, target, done.at[len(stores)]))
        stores[-1].start()

    if vectors:
        number, offset = divmod(base, depths[1])
        for (near, side), parts in zip(jobs + extra_jobs, sources + extra_sources):
            start = 0
            for part in parts:
                row = depths[0] + offset - start
                if 0 <= row < part.shape[1]:
                    rows = part[number ^ (place_ref[1] >> 3), row : row + 16]
                    kept_ref[eighth_at(place_ref, near, side)] = rows.astype(F32)
                start += part.shape[1]
        blocks = [(ref, block) for ref in flat_refs for block in range(ref.shape[0] // LANES)]
        each = -(-len(blocks) // 8)
        for at, (ref, block) in enumerate(blocks):
            eighth, row = divmod(at, each)
            ref[block * LANES : (block + 1) * LANES] = kept_ref[eighth, row]
        for flat_ref, out_ref in zip(flat_refs, vector_outs):
            store(flat_ref, out_ref)
    for job, ((near, side), parts) in enumerate(zip(jobs, sources)):
        eighth = eighth_at(place_ref, near, side)
        for far in range(parts[0].shape[0]):
            start = 0
            for part in parts:
                stop = start + part.shape[1]
                for unit, (stage_ref, depth) in enumerate(zip(stage_refs, depths)):
                    low = sum(depths[:unit])
                    top, end = max(start, low), min(stop, low + depth)
                    if top < end:
                        first = pl.multiple_of((far ^ (place_ref[1] >> 3)) * depth + (top - low), 16)
                        stage_ref[pl.ds(first, end - top), :] = part[far, top - start : end - start]
                start = stop
        for unit, stage_ref in enumerate(stage_refs):
            first = 0
            for at in ((0, 1), (3,), (2,))[unit]:
                wide_ref = wides[at].at[job]
                depth, width = wide_ref.shape
                for block in range(width // LANES):
                    wide_ref[:, block * LANES : (block + 1) * LANES] = stage_ref[first : first + depth, :].astype(F32)
                    first += depth
                if at == 1:
                    rows = pl.ds(pl.multiple_of((eighth & 1) * depth, 16), depth)
                    target = outs[at].at[rows, pl.ds(pl.multiple_of((eighth >> 1) * width, LANES), width)]
                else:
                    target = outs[at].at[pl.ds(pl.multiple_of(eighth * depth, 16), depth), :]
                store(wide_ref, target)
    for each in stores:
        each.wait()


def chunk_rows(count, devices):
    return -(-count // (devices * 16)) * 16


def body(
    tokens,
    masked,
    groups,
    cotangent,
    mask_token,
    gain_one,
    shift_one,
    w_qkv,
    q_bias,
    v_bias,
    w_proj,
    b_proj,
    gain_two,
    shift_two,
    w_up,
    b_up,
    w_down,
    b_down,
):
    copies, half, width = tokens.shape
    hidden = w_up.shape[1]
    hide = masked.shape[1]
    unmasked = 2 * half - hide
    rows = unmasked + EXTRA
    some = unmasked // 2 + EXTRA
    total = rows + some
    tm, clip = lax.axis_index("tm"), lax.axis_index("clip")
    clips = lax.axis_size("clip")
    devices = 2 * clips
    me = (clip & 1) | (tm << 1) | ((clip >> 1) << 2)
    place = jnp.stack([tm, me]).astype(jnp.int32)
    swap = functools.partial(lax.ppermute, axis_name="tm", perm=[(0, 1), (1, 0)])

    def run(kernel, args, outs, scratch=(), scalars=1, limit=20, flops=0, in_hbm=(), out_hbm=(), aliases=None, hides=True):
        moved = sum(math.prod(a.shape) * a.dtype.itemsize for a in list(args) + jax.tree.leaves(outs))
        return pl.pallas_call(
            kernel,
            out_shape=outs,
            in_specs=[
                SMEM if at < scalars else HBM if at in in_hbm else VMEM
                for at in range(len(args))
            ],
            out_specs=[HBM if at in out_hbm else VMEM for at in range(len(outs))] if isinstance(outs, list) else VMEM,
            scratch_shapes=list(scratch),
            input_output_aliases=aliases or {},
            compiler_params=pltpu.CompilerParams(vmem_limit_bytes=limit << 20),
            cost_estimate=pl.CostEstimate(
                flops=flops if hides else 1, bytes_accessed=moved if hides else 1, transcendentals=0
            ),
        )(*args)

    blocks = width // LANES
    counts = (2 * hidden // 8 * blocks, 3 * width // 8 * blocks + 16, width // 8 * blocks)
    depths = [chunk_rows(count, devices // 8) for count in counts]

    def chunked(unit, parts):
        halves = [shape(near, devices // 8, depths[unit], LANES) for near in [4] + [4 // parts] * parts]
        return halves, [pltpu.VMEM((8, devices // 8 * depths[unit], LANES), BF)]

    small = jnp.stack(
        [mask_token, gain_one, shift_one, q_bias, v_bias, b_proj, gain_two, shift_two, b_down]
    ).astype(F32)
    bias_up = b_up.astype(F32).reshape(1, hidden)

    block = shape(rows, width)
    everyone = jnp.concatenate([groups, clip_swap(groups, 1)])
    theirs, rank_theirs = run(
        functools.partial(prep_theirs_kernel, unmasked),
        (place, *(pltpu.with_memory_space_constraint(each, pltpu.HBM) for each in (masked, tokens))),
        [shape(unmasked, width), shape(16, LANES, kind=F32)],
        [pltpu.VMEM(masked.shape, jnp.int32), pltpu.VMEM((half, width), BF), pltpu.SemaphoreType.DMA((4,))],
        flops=2 * rows * half * width,
        in_hbm=(1, 2),
    )
    got_mine = swap(theirs)
    everyone, theirs, rank_theirs, masked = lax.optimization_barrier((everyone, theirs, rank_theirs, masked))
    everyone = jnp.concatenate([everyone, clip_swap(everyone, 2)])
    shared, rank = run(
        functools.partial(prep_shared_kernel, unmasked),
        (place, masked, tokens),
        [shape(unmasked, width), shape(32, LANES, kind=F32)],
        flops=2 * rows * half * width,
    )
    got_shared = swap(shared)
    everyone, shared, rank = lax.optimization_barrier((everyone, shared, rank))
    everyone = jnp.concatenate([everyone, clip_swap(everyone, 4)])
    cot_own, cot_send = run(
        functools.partial(prep_grads_kernel, unmasked),
        (place, rank_theirs, rank, cotangent),
        [shape(total, width), shape(total - EXTRA, width)],
        flops=2 * copies * rows * half * width,
    )
    everyone, cot_own, cot_send = lax.optimization_barrier((everyone, cot_own, cot_send))
    cot_got = swap(cot_send)

    def attend(sources, got, split):
        queries = some if split else rows
        outs = [
            shape(queries, width), shape(queries, width), block, block,
            shape(HEADS, queries, rows), shape(queries, width, kind=F32), shape(queries, width),
        ]
        if split:
            outs.append(block)
        return run(
            functools.partial(attention_kernel, unmasked, hide, split),
            (place, *sources, got, small, w_qkv),
            outs,
            flops=6 * rows * width * width + 4 * queries * rows * width,
        )

    x_a, q_a, k_a, v_a, e_a, inverse_a, att_a = attend((rank, tokens), got_mine, False)
    everyone, att_a = lax.optimization_barrier((everyone, att_a))
    distance = 8
    while distance < clips:
        everyone = jnp.concatenate([everyone, clip_swap(everyone, distance)])
        distance *= 2
    x_b, q_b, k_b, v_b, e_b, inverse_b, att_b, x_whole = attend((shared,), got_shared, True)

    everyone, att_b = lax.optimization_barrier((everyone, att_b))
    out_rows, middle, normed_two, active, slope = run(
        forward_kernel,
        (att_a, att_b, x_a, x_b, small, bias_up, w_proj, w_up, w_down),
        [
            shape(total, width), shape(total, width, kind=F32), shape(total, width), shape(total, hidden),
            shape(total, hidden),
        ],
        scalars=0,
        flops=2 * total * width * (width + 2 * hidden),
    )
    out_got = swap(out_rows)
    halves, stage = chunked(0, 4)
    upstream, grad_hidden, up_sums, keep, *send = run(
        hidden_back_kernel,
        (place, groups, everyone.reshape(1, -1), cot_own, cot_got, normed_two, active, slope, w_down),
        [shape(total, width, kind=F32), shape(total, hidden), shape(1, hidden, kind=F32)] + halves,
        stage,
        scalars=2,
        hides=False,
    )
    halves, stage = chunked(2, 2)
    grad_middle, grad_att, middle_sums, keep_proj, *send_proj = run(
        middle_back_kernel,
        (place, upstream, grad_hidden, middle, att_a, att_b, small, w_proj, w_up),
        [shape(total, width, kind=F32), shape(total, width), shape(8, width, kind=F32)] + halves,
        stage,
        hides=False,
    )
    got, grad_att = lax.optimization_barrier((swap_cores(send), grad_att))
    pieces, grad_att, send_proj = lax.optimization_barrier((fold_cores([(keep, got)]), grad_att, send_proj))
    first_pieces = spread_near(pieces, (2, 1, 3))

    def attend_back(row_from, grads, att, q, k, v, e, inverse):
        return run(
            functools.partial(attention_back_kernel, row_from),
            (grads, att, q, k, v, e, inverse),
            [shape(q.shape[0], width), block, block],
            scalars=0,
            hides=False,
        )

    dq_b, dk_b, dv_b = attend_back(rows, grad_att, att_b, q_b, k_b, v_b, e_b, inverse_b)
    dq_b, out_got = lax.optimization_barrier((dq_b, out_got))
    dq_a, dk_a, dv_a = attend_back(0, grad_att, att_a, q_a, k_a, v_a, e_a, inverse_a)
    dq_a, got_proj = lax.optimization_barrier((dq_a, swap_cores(send_proj)))
    halves, stage = chunked(1, 2)
    grad_rows, keep, *send = run(
        functools.partial(inputs_back_kernel, unmasked),
        (place, x_a, x_whole, dq_a, dq_b, dk_a, dk_b, dv_a, dv_b, grad_middle, small, w_qkv, up_sums, middle_sums),
        [shape(2 * unmasked, width)] + halves,
        stage,
        hides=False,
    )
    pieces = fold_cores([(keep, swap_cores(send)), (keep_proj, got_proj)])
    pieces, first_pieces = lax.optimization_barrier((pieces, first_pieces))
    second_pieces = spread_near(pieces, (2, 1, 3))

    def send_rows(pieces):
        *pieces, grads = lax.optimization_barrier((*pieces, grad_rows))
        return swap(grads), pieces

    def place_rows(got):
        return (
            run(functools.partial(outputs_kernel, unmasked), (place, rank_theirs, rank, out_rows, out_got), shape(*tokens.shape), hides=False),
            run(functools.partial(grads_out_kernel, unmasked), (place, rank_theirs, rank, grad_rows, got), shape(*tokens.shape), hides=False),
        )

    weights = [(hidden, width), (width, hidden), (width, width), (width, 3 * width)]
    slabs = [(hidden // 8, width), (width // 2, hidden // 4), (width // 8, width), (width // 8, 3 * width)]
    vectors = [shape(dim, kind=F32) for dim in [hidden] + [width] * 9]

    def finish(jobs, sources, earlier, extra_sources):
        extra_jobs = ((0, 0), (0, 1), (1, 0), (2, 0), (3, 0)) if extra_sources else ()
        refs = [part for parts in [*sources, *extra_sources] for part in parts]
        flat = vectors if extra_sources else []
        kernel = functools.partial(
            finish_kernel,
            jobs,
            [len(parts) for parts in sources],
            extra_jobs,
            [len(parts) for parts in extra_sources],
            not earlier,
            depths,
            counts[1] - 16,
            len(flat),
        )
        return run(
            kernel,
            (place, *refs, *earlier),
            [shape(*dims, kind=F32) for dims in weights] + flat,
            [pltpu.VMEM((devices // 8 * depth, LANES), BF) for depth in depths]
            + [pltpu.SemaphoreType.DMA((4 * len(jobs) + len(flat),))]
            + [pltpu.VMEM((len(jobs), *dims), F32) for dims in slabs]
            + [pltpu.VMEM((8, 16, LANES), F32)]
            + [pltpu.VMEM(each.shape, F32) for each in flat],
            in_hbm=range(1 + len(refs), 5 + len(refs)) if earlier else (),
            out_hbm=range(4 + len(flat)),
            aliases={1 + len(refs) + at: at for at in range(4)} if earlier else {},
            hides=False,
        )

    (
        (
            grad_w_down, grad_w_up, grad_w_proj, grad_w_qkv,
            grad_b_up, grad_gain_two, grad_shift_two, grad_b_proj, grad_b_down,
            grad_q_bias, grad_v_bias, grad_gain_one, grad_shift_one, grad_mask_token,
        ),
        (block_out, grad_tokens),
    ) = sum_over_devices(first_pieces, second_pieces, send_rows, place_rows, finish)
    return (
        block_out,
        grad_tokens,
        grad_mask_token,
        grad_gain_one,
        grad_shift_one,
        grad_w_qkv,
        grad_q_bias,
        grad_v_bias,
        grad_w_proj,
        grad_b_proj,
        grad_gain_two,
        grad_shift_two,
        grad_w_up,
        grad_b_up,
        grad_w_down,
        grad_b_down,
    )


def solution(mesh):
    return jax.shard_map(
        body,
        mesh=mesh,
        in_specs=(P("clip", "tm", None), P("clip", None), P("clip"), P("clip", "tm", None)) + (P(),) * 14,
        out_specs=(P("clip", "tm", None), P("clip", "tm", None)) + (P(),) * 14,
        check_vma=False,
    )
```
